32 devices in a mesh: dp: 8 (over y, x, core), tensor: 4 (over z).
Axes of the slice: x: 2, y: 2, z: 4, core: 2. Of those that a mesh axis runs over, the one named last changes fastest.
Arguments:
- inputs: bfloat16 [2, 16384, 768], P(None, 'dp'), may hold values from -6 to 6
- cotangent: bfloat16 [2, 16384, 768], P(None, 'dp'), may hold values from -6 to 6
- bucket: int32 [2, 32], P(None, 'dp'), may hold values from 0 to 1, as said below
- lengths: int32 [2, 32, 4], P(None, 'dp'), may hold values from 64 to 512, as said below
- counts: int32 [2, 32], P(None, 'dp'), may hold values from 1 to 4, as said below
- w_qkv: bfloat16 [3, 768, 768], P(None, 'dp', 'tensor'), may hold values from -0.21875 to 0.21875
- w_out: bfloat16 [768, 768], P('tensor', 'dp'), may hold values from -2.5 to 2.5
- w_in: bfloat16 [768, 3072], P('dp', 'tensor'), may hold values from -0.21875 to 0.21875
- w_down: bfloat16 [3072, 768], P('tensor', 'dp'), may hold values from -0.109375 to 0.109375
- head_bias: bfloat16 [2, 768], P(None, 'tensor'), may hold values from -2 to 2
- ffn_bias: bfloat16 [3072], P('tensor'), may hold values from -2 to 2
- norm_gains: bfloat16 [2, 768], P(None, 'dp'), may hold values from 0.25 to 1.75
- row_biases: bfloat16 [4, 768], P(None, 'dp'), may hold values from -2 to 2
Outputs:
- layer_output: bfloat16 [2, 16384, 768], P(None, 'dp')
- input_grad: bfloat16 [2, 16384, 768], P(None, 'dp')
- grad_w_qkv: float32 [3, 768, 768], P(None, 'dp', 'tensor')
- grad_w_out: float32 [768, 768], P('tensor', 'dp')
- grad_w_in: float32 [768, 3072], P('dp', 'tensor')
- grad_w_down: float32 [3072, 768], P('tensor', 'dp')
- grad_head_bias: float32 [2, 768], P(None, 'tensor')
- grad_ffn_bias: float32 [3072], P('tensor')
- grad_norm_gains: float32 [2, 768], P(None, 'dp')
- grad_row_biases: float32 [4, 768], P(None, 'dp')
The draws below stay inside these ranges and needn't reach their ends.
Inputs may be any that keep to these rules, and one draw needn't show every extreme that they name: `bucket`: 1 marks a block of one item of 512 slots, 0 a block of four items of 128 slots; every micro-batch has blocks of both kinds. `lengths`: entry i is the length of item i of the block; a one-item block uses entry 0 only, within 128 to 512; a four-item block's entries lie within 64 to 128. `counts`: 1 in a one-item block, 2 to 4 in a four-item block.
All inputs are finite; a program needn't handle non-finite values.
Results may differ from the reference program's by a relative error of at most 0.018.
Values may be sent and summed in bfloat16 or wider, within the bound.
A program may use at most 256 MiB of HBM per device.

```python
import jax
import jax.numpy as jnp
from jax import lax

HEADS = 12
HEAD_DIM = 64
FF = 3072
D = 768
SLOTS = 512
MICRO = 2
GROUPS = 32
TOKENS_MB = 16384


def block_layout(key):
    key_bucket, key_short, key_long, key_count, key_full, key_other = jax.random.split(key, 6)
    group_index = jnp.arange(GROUPS, dtype=jnp.int32)
    drawn_bucket = jax.random.randint(key_bucket, (MICRO, GROUPS), 0, 2, dtype=jnp.int32)
    full_at = jax.random.randint(key_full, (MICRO, 1), 0, GROUPS, dtype=jnp.int32)
    other_at = (full_at + 1 + jax.random.randint(key_other, (MICRO, 1), 0, GROUPS - 1, dtype=jnp.int32)) % GROUPS
    is_full = group_index[None, :] == full_at
    is_other = group_index[None, :] == other_at
    bucket = jnp.where(is_full, 1, jnp.where(is_other, 0, drawn_bucket)).astype(jnp.int32)
    short_lengths = jax.random.randint(key_short, (MICRO, GROUPS, 4), SLOTS // 8, SLOTS // 4 + 1, dtype=jnp.int32)
    long_lengths = jax.random.randint(key_long, (MICRO, GROUPS, 1), SLOTS // 4, SLOTS + 1, dtype=jnp.int32)
    long_lengths = jnp.where(is_full[..., None], SLOTS, long_lengths)
    lengths = jnp.where(bucket[..., None] == 1, long_lengths, short_lengths).astype(jnp.int32)
    drawn_counts = jax.random.randint(key_count, (MICRO, GROUPS), 2, 5, dtype=jnp.int32)
    counts = jnp.where(bucket == 1, 1, jnp.where(is_other, 4, drawn_counts)).astype(jnp.int32)
    return (bucket, lengths, counts)


def draw_bucket(key, part):
    layout = block_layout(key)
    return layout[0]


def draw_lengths(key, part):
    layout = block_layout(key)
    return layout[1]


def draw_counts(key, part):
    layout = block_layout(key)
    return layout[2]


def spiked(values, rng, source, target, shards_of, factor):
    def block_of(dim):
        return (jnp.arange(values.shape[dim]) // (values.shape[dim] // shards_of)).reshape((-1,) + (1,) * (values.ndim - 1 - dim))

    near = jax.random.permutation(rng, shards_of)[block_of(target)]
    second = (block_of(target) + shards_of // 2) % shards_of
    return jnp.where((block_of(source) == near) | (block_of(source) == second), factor * values, values)


def level_of(stream_key, dims, cuts, least, high):
    def one(dim, parts):
        draws = jax.random.uniform(jax.random.fold_in(jax.random.fold_in(stream_key, 6), dim), (parts,), jnp.float32, least / len(cuts), high / len(cuts))
        return jnp.repeat(jnp.exp(draws), dims[dim] // parts).reshape((-1,) + (1,) * (len(dims) - dim - 1))

    loudness = one(*cuts[0])
    for cut in cuts[1:]:
        loudness = loudness * one(*cut)
    return loudness


def noise(rng, shape, scale, bound, shards=(), kind=jnp.bfloat16):
    values = jax.random.normal(rng, shape, jnp.float32) * scale
    if len(shards) > 0:
        values = level_of(rng, shape, shards, -0.22, 0.18) * values
    return jnp.clip(values, min=-bound, max=bound).astype(kind)


def bell_draw_with(key, shape, deviation, limit, shards, heavy, kind=jnp.bfloat16):
    entries = deviation * jax.random.normal(key, shape, jnp.float32)
    if shards:
        entries = entries * level_of(key, shape, shards, -0.22, 0.18)
    return jnp.clip(spiked(entries, jax.random.fold_in(key, 3), *heavy), -limit, limit).astype(kind)


def setup_inputs(seed: int = 0) -> dict:
    streams_of = jax.random.split(jax.random.key(seed), 14)
    return {
        "inputs": bell_draw_with(streams_of[0], (MICRO, TOKENS_MB, D), 1.0, 6.0, ((1, 8),), (1, 2, 8, 2.0)),
        "cotangent": bell_draw_with(streams_of[1], (MICRO, TOKENS_MB, D), 1.0, 6.0, ((1, 8),), (1, 2, 8, 2.0)),
        "bucket": draw_bucket(jax.random.fold_in(streams_of[13], 71), 0),
        "lengths": draw_lengths(jax.random.fold_in(streams_of[13], 71), 0),
        "counts": draw_counts(jax.random.fold_in(streams_of[13], 71), 0),
        "w_qkv": noise(streams_of[5], (3, D, D), D ** -0.5, 0.21875, ((1, 8), (2, 4))),
        "w_out": noise(streams_of[6], (D, D), (D * 4 // SLOTS) ** -0.5, 2.5, ((0, 4), (1, 8))),
        "w_in": noise(streams_of[7], (D, FF), D ** -0.5, 0.21875, ((0, 8), (1, 4))),
        "w_down": noise(streams_of[8], (FF, D), FF ** -0.5, 0.109375, ((0, 4), (1, 8))),
        "head_bias": noise(streams_of[9], (2, D), 0.3, 2.0, ((1, 4),)),
        "ffn_bias": noise(streams_of[10], (FF,), 0.3, 2.0, ((0, 4),)),
        "norm_gains": jnp.clip(1.0 + 0.15 * jax.random.normal(streams_of[11], (2, D), jnp.float32), 0.25, 1.75).astype(jnp.bfloat16),
        "row_biases": noise(streams_of[12], (4, D), 0.3, 2.0, ((1, 8),)),
    }


EPSILON = 1e-12
HIGHEST_PRECISION = lax.Precision.HIGHEST

@jax.custom_vjp
def low(v):
    return lax.optimization_barrier(v.astype(jnp.bfloat16)).astype(jnp.float32)

@jax.custom_vjp
def low_back(v):
    return v

def low_keep(v):
    return (low(v), None)

def low_pass(kept, grad):
    return (grad,)

def back_keep(v):
    return (v, None)

def back_low(kept, grad):
    return (low(grad),)
low.defvjp(low_keep, low_pass)
low_back.defvjp(back_keep, back_low)

def token_masks(bucket_id, item_lengths, item_count, slot_count):
    position = jnp.arange(slot_count, dtype=jnp.int32)
    item_size = jnp.where(bucket_id == 1, slot_count, slot_count // 4).astype(jnp.int32)
    item_index = position // item_size
    within = position % item_size
    picked = item_index[:, None] == jnp.arange(4, dtype=jnp.int32)[None, :]
    length_of = lax.optimization_barrier(jnp.sum(jnp.where(picked, item_lengths[None, :], 0), axis=1))
    is_live = (item_index < item_count) & (within < length_of)
    keymask = (item_index[:, None] == item_index[None, :]) & is_live[None, :]
    return (is_live, keymask)

def hdot(left_side, right_side):
    return jnp.dot(left_side, right_side, precision=HIGHEST_PRECISION, preferred_element_type=jnp.float32)

def norm_rows(hidden, gain_row, shift_row):
    center = hidden - lax.optimization_barrier(jnp.mean(hidden, axis=-1, keepdims=True))
    return center * lax.rsqrt(lax.optimization_barrier(jnp.mean(center * center, axis=-1, keepdims=True)) + EPSILON) * gain_row + shift_row

def block_forward(tokens, keymask, w_qkv, w_out, w_in, w_down, head_bias, ffn_bias, norm_gains, row_biases):
    slot_count = tokens.shape[0]
    query_rows = low(low_back(hdot(tokens, w_qkv[0]) + head_bias[0]))
    key_rows = low(low_back(hdot(tokens, w_qkv[1])))
    values = low(low_back(hdot(tokens, w_qkv[2]) + head_bias[1]))
    query_heads = query_rows.reshape(slot_count, HEADS, HEAD_DIM)
    key_heads = key_rows.reshape(slot_count, HEADS, HEAD_DIM)
    value_heads = values.reshape(slot_count, HEADS, HEAD_DIM)
    scores = low_back(jnp.einsum('qhd,khd->hqk', query_heads, key_heads, precision=HIGHEST_PRECISION) * HEAD_DIM ** (-0.5))
    scores = jnp.where(keymask[None], scores, -10000.0)
    row_peak = lax.optimization_barrier(jnp.max(scores, axis=-1, keepdims=True))
    exp_scores = jnp.exp(scores - row_peak)
    attn_probs = low(exp_scores / lax.optimization_barrier(jnp.sum(exp_scores, axis=-1, keepdims=True)))
    context = jnp.einsum('hqk,khd->qhd', attn_probs, value_heads, precision=HIGHEST_PRECISION)
    context = low(low_back(context.reshape(slot_count, HEADS * HEAD_DIM)))
    attention = low_back(hdot(context, w_out))
    first_norm = norm_rows(tokens + attention + row_biases[0], norm_gains[0], row_biases[1])
    upward = low_back(hdot(low(first_norm), w_in) + ffn_bias)
    activated = low(jax.nn.gelu(upward, approximate=False))
    down_sum = low_back(hdot(activated, w_down))
    return norm_rows(first_norm + down_sum + row_biases[2], norm_gains[1], row_biases[3])

def reference(inputs, cotangent, bucket, lengths, counts, w_qkv, w_out, w_in, w_down, head_bias, ffn_bias, norm_gains, row_biases):
    weights = tuple((weight_array.astype(jnp.float32) for weight_array in (w_qkv, w_out, w_in, w_down, head_bias, ffn_bias, norm_gains, row_biases)))
    width = inputs.shape[-1]
    block_tokens = inputs.astype(jnp.float32).reshape(-1, SLOTS, width)
    block_cot = cotangent.astype(jnp.float32).reshape(-1, SLOTS, width)
    flat_bucket = bucket.reshape(-1)
    flat_lengths = lengths.reshape(-1, 4)
    flat_counts = counts.reshape(-1)

    def block_step(running, carried):
        tokens, grad_out, bucket_id, item_lengths, item_count = carried
        is_live, keymask = token_masks(bucket_id, item_lengths, item_count, SLOTS)

        def forward(tokens, *params):
            return block_forward(tokens, keymask, *params)
        result, pullback = jax.vjp(forward, tokens, *weights)
        gradients = pullback(grad_out * is_live.astype(jnp.float32)[:, None])
        running = tuple((total_now + gradient for total_now, gradient in zip(running, gradients[1:])))
        return (running, (result.astype(jnp.bfloat16), gradients[0].astype(jnp.bfloat16)))
    start_totals = tuple((jnp.zeros_like(weight_array) for weight_array in weights))
    totals, (results, input_grads) = lax.scan(block_step, start_totals, (block_tokens, block_cot, flat_bucket, flat_lengths, flat_counts))
    return (results.reshape(inputs.shape), input_grads.reshape(inputs.shape), totals[0], totals[1], totals[2], totals[3], totals[4], totals[5], totals[6], totals[7])
```

```python
import jax
import jax.numpy as jnp
from jax import lax
from jax.sharding import PartitionSpec as P

HEAD_DIM = 64


EPSILON = 1e-12


def token_masks(bucket_id, item_lengths, item_count, slot_count):
    position = jnp.arange(slot_count, dtype=jnp.int32)
    item_size = jnp.where(bucket_id == 1, slot_count, slot_count // 4).astype(jnp.int32)
    item_index = position // item_size
    within = position % item_size
    picked = item_index[:, None] == jnp.arange(4, dtype=jnp.int32)[None, :]
    length_of = jnp.sum(jnp.where(picked, item_lengths[None, :], 0), axis=1)
    is_live = (item_index < item_count) & (within < length_of)
    keymask = (item_index[:, None] == item_index[None, :]) & is_live[None, :]
    return (is_live, keymask)


def gelu_exact(argument):
    return jax.nn.gelu(argument, approximate=False)


def norm_forward(hidden, gain_row, shift_row):
    center = hidden - jnp.mean(hidden, axis=-1, keepdims=True)
    inverse = lax.rsqrt(jnp.mean(center * center, axis=-1, keepdims=True) + EPSILON)
    normed = center * inverse
    return (normed * gain_row + shift_row, normed, inverse)


def norm_backward(grad_rows, normed, inverse, gain_row):
    grad_normed = grad_rows * gain_row
    grad_input = inverse * (
        grad_normed
        - jnp.mean(grad_normed, axis=-1, keepdims=True)
        - normed * jnp.mean(grad_normed * normed, axis=-1, keepdims=True)
    )
    return (grad_input, jnp.sum(grad_rows * normed, axis=0), jnp.sum(grad_rows, axis=0))


def block_scores(query_rows, key_rows, keymask):
    slot_count = query_rows.shape[0]
    query_heads = query_rows.reshape(slot_count, -1, HEAD_DIM)
    key_heads = key_rows.reshape(slot_count, -1, HEAD_DIM)
    scores = jnp.einsum(
        "qhd,khd->hqk", query_heads, key_heads, preferred_element_type=jnp.float32
    ) * HEAD_DIM ** (-0.5)
    return jnp.where(keymask[None], scores, -10000.0)


def add_tuples(earlier, latest):
    return tuple((first_term + second_term for first_term, second_term in zip(earlier, latest)))


def packed_shards(w_qkv, w_out, w_in, w_down):
    head_slab = jnp.concatenate([w_qkv[0], w_qkv[1], w_qkv[2], w_out.T], axis=1)
    return (head_slab, w_in, w_down.T)


def body(
    inputs,
    cotangent,
    bucket,
    lengths,
    counts,
    w_qkv,
    w_out,
    w_in,
    w_down,
    head_bias,
    ffn_bias,
    norm_gains,
    row_biases,
):
    micro_count = inputs.shape[0]
    blocks_all = bucket.shape[1]
    slot_count = inputs.shape[1] // blocks_all
    score_scale = HEAD_DIM ** (-0.5)
    parts = lax.axis_size("tensor")
    rank = lax.axis_index("tensor")
    width = inputs.shape[2]
    head_cols = w_out.shape[0]
    share_blocks = blocks_all // parts
    share_count = share_blocks * slot_count
    share_start = rank * share_count

    slabs = packed_shards(w_qkv, w_out, w_in, w_down)
    full = [lax.all_gather(s, ("tensor", "dp"), axis=0, tiled=True).reshape(parts, width, s.shape[1]) for s in slabs]
    mat_head, mat_in, mat_down = full
    mat_in = mat_in.transpose(1, 0, 2).reshape(width, -1)
    mat_down = mat_down.transpose(1, 0, 2).reshape(width, -1)
    split = mat_head.reshape(parts, width, 4, head_cols).transpose(2, 1, 0, 3).reshape(4, width, width)
    gain_rows = lax.all_gather(norm_gains, "dp", axis=1, tiled=True).astype(jnp.float32)
    shifts = lax.all_gather(row_biases, "dp", axis=1, tiled=True).astype(jnp.float32)
    column_bias = lax.all_gather(head_bias, "tensor", axis=1, tiled=True).astype(jnp.float32)
    hidden_bias = lax.all_gather(ffn_bias, "tensor", axis=0, tiled=True).astype(jnp.float32)

    results = []
    input_grads = []
    kept = None
    for micro_index in range(micro_count):
        tokens = lax.dynamic_slice_in_dim(inputs[micro_index], share_start, share_count, 0)
        cot_rows = lax.dynamic_slice_in_dim(cotangent[micro_index], share_start, share_count, 0)
        bucket_rows = lax.dynamic_slice_in_dim(bucket[micro_index], rank * share_blocks, share_blocks, 0)
        length_rows = lax.dynamic_slice_in_dim(lengths[micro_index], rank * share_blocks, share_blocks, 0)
        count_rows = lax.dynamic_slice_in_dim(counts[micro_index], rank * share_blocks, share_blocks, 0)
        query_rows = (jnp.dot(tokens, split[0], preferred_element_type=jnp.float32) + column_bias[0]).astype(jnp.bfloat16)
        key_rows = jnp.dot(tokens, split[1], preferred_element_type=jnp.float32).astype(jnp.bfloat16)
        values = (jnp.dot(tokens, split[2], preferred_element_type=jnp.float32) + column_bias[1]).astype(jnp.bfloat16)
        live_parts, mask_parts, prob_parts, context_parts = ([], [], [], [])
        for block_index in range(share_blocks):
            rows = slice(block_index * slot_count, (block_index + 1) * slot_count)
            is_live, keymask = token_masks(
                bucket_rows[block_index], length_rows[block_index], count_rows[block_index], slot_count
            )
            scores = block_scores(query_rows[rows], key_rows[rows], keymask)
            row_peak = jnp.max(scores, axis=-1, keepdims=True)
            exp_scores = jnp.exp(scores - row_peak)
            totals = jnp.sum(exp_scores, axis=-1, keepdims=True)
            attn_probs = (exp_scores / totals).astype(jnp.bfloat16)
            value_heads = values[rows].reshape(slot_count, -1, HEAD_DIM)
            context = jnp.einsum("hqk,khd->qhd", attn_probs, value_heads, preferred_element_type=jnp.float32)
            context_parts.append(context.reshape(slot_count, -1).astype(jnp.bfloat16))
            live_parts.append(is_live)
            mask_parts.append(keymask)
            prob_parts.append(attn_probs)
        context_all = jnp.concatenate(context_parts, axis=0)
        live_share = jnp.concatenate(live_parts, axis=0).astype(jnp.float32)
        attention = jnp.einsum("rc,dc->rd", context_all, split[3], preferred_element_type=jnp.float32)
        first_norm, normed_one, inverse_one = norm_forward(
            tokens.astype(jnp.float32) + attention + shifts[0], gain_rows[0], shifts[1]
        )
        first_low = first_norm.astype(jnp.bfloat16)
        upward = jnp.dot(first_low, mat_in, preferred_element_type=jnp.float32) + hidden_bias
        activated = gelu_exact(upward).astype(jnp.bfloat16)
        down_sum = jnp.einsum("rf,df->rd", activated, mat_down, preferred_element_type=jnp.float32)
        result, normed_two, inverse_two = norm_forward(
            first_norm + down_sum + shifts[2], gain_rows[1], shifts[3]
        )
        results.append(lax.all_gather(result.astype(jnp.bfloat16), "tensor", axis=0, tiled=True))
        grad_out = cot_rows.astype(jnp.float32) * live_share[:, None]
        grad_second, gain_two, shift_two = norm_backward(grad_out, normed_two, inverse_two, gain_rows[1])
        second_low = grad_second.astype(jnp.bfloat16)
        grad_down_w = jnp.einsum("rd,rf->df", second_low, activated, preferred_element_type=jnp.float32)
        grad_act = jnp.einsum("rd,df->rf", second_low, mat_down, preferred_element_type=jnp.float32)
        pullback = jax.vjp(gelu_exact, upward)[1]
        grad_up = pullback(grad_act)[0].astype(jnp.bfloat16)
        grad_in_w = jnp.einsum("rd,rf->df", first_low, grad_up, preferred_element_type=jnp.float32)
        back_total = jnp.einsum("rf,df->rd", grad_up, mat_in, preferred_element_type=jnp.float32)
        grad_first = grad_second + back_total
        grad_hidden, gain_one, shift_one = norm_backward(grad_first, normed_one, inverse_one, gain_rows[0])
        hidden_low = grad_hidden.astype(jnp.bfloat16)
        grad_out_w = jnp.einsum("rd,rc->dc", hidden_low, context_all, preferred_element_type=jnp.float32)
        grad_context = jnp.dot(hidden_low, split[3], preferred_element_type=jnp.float32).astype(jnp.bfloat16)
        query_parts, key_parts, value_parts = ([], [], [])
        for block_index in range(share_blocks):
            rows = slice(block_index * slot_count, (block_index + 1) * slot_count)
            attn_probs = prob_parts[block_index].astype(jnp.float32)
            context_heads = grad_context[rows].reshape(slot_count, -1, HEAD_DIM)
            value_heads = values[rows].reshape(slot_count, -1, HEAD_DIM)
            query_heads = query_rows[rows].reshape(slot_count, -1, HEAD_DIM)
            key_heads = key_rows[rows].reshape(slot_count, -1, HEAD_DIM)
            grad_values = jnp.einsum("hqk,qhd->khd", prob_parts[block_index], context_heads, preferred_element_type=jnp.float32)
            grad_probs = jnp.einsum("qhd,khd->hqk", context_heads, value_heads, preferred_element_type=jnp.float32)
            row_inner = jnp.sum(attn_probs * grad_probs, axis=-1, keepdims=True)
            grad_scores = jnp.where(
                mask_parts[block_index][None], attn_probs * (grad_probs - row_inner), 0.0
            ).astype(jnp.bfloat16)
            grad_query = jnp.einsum("hqk,khd->qhd", grad_scores, key_heads, preferred_element_type=jnp.float32) * score_scale
            grad_keys = jnp.einsum("hqk,qhd->khd", grad_scores, query_heads, preferred_element_type=jnp.float32) * score_scale
            query_parts.append(grad_query.reshape(slot_count, -1))
            key_parts.append(grad_keys.reshape(slot_count, -1))
            value_parts.append(grad_values.reshape(slot_count, -1))
        grad_qkv = jnp.stack(
            [jnp.concatenate(query_parts, axis=0), jnp.concatenate(key_parts, axis=0), jnp.concatenate(value_parts, axis=0)]
        ).astype(jnp.bfloat16)
        grad_qkv_w = jnp.einsum("rd,trc->tdc", tokens, grad_qkv, preferred_element_type=jnp.float32)
        token_total = jnp.einsum("trc,tdc->rd", grad_qkv, split[:3], preferred_element_type=jnp.float32)
        grad_tokens = (grad_hidden + token_total).astype(jnp.bfloat16)
        input_grads.append(lax.all_gather(grad_tokens, "tensor", axis=0, tiled=True))
        grad_qkv_wide = grad_qkv.astype(jnp.float32)
        now = (
            grad_qkv_w,
            grad_out_w,
            grad_in_w,
            grad_down_w,
            jnp.stack([gain_one, gain_two]),
            jnp.stack([jnp.sum(grad_hidden, axis=0), shift_one, jnp.sum(grad_second, axis=0), shift_two]),
            jnp.stack([jnp.sum(grad_qkv_wide[0], axis=0), jnp.sum(grad_qkv_wide[2], axis=0)]),
            jnp.sum(grad_up.astype(jnp.float32), axis=0),
        )
        kept = now if kept is None else add_tuples(kept, now)
    both = ("tensor", "dp")
    heads = jnp.concatenate([kept[0], kept[1][None]], axis=0)
    heads = heads.reshape(4, width, parts, head_cols).transpose(2, 1, 0, 3).reshape(parts * width, 4 * head_cols)
    ins = kept[2].reshape(width, parts, -1).transpose(1, 0, 2).reshape(parts * width, -1)
    downs = kept[3].reshape(width, parts, -1).transpose(1, 0, 2).reshape(parts * width, -1)
    heads, ins, downs = [
        lax.psum_scatter(v.astype(jnp.bfloat16), both, scatter_dimension=0, tiled=True).astype(jnp.float32)
        for v in (heads, ins, downs)
    ]
    gains_sum = lax.psum_scatter(lax.psum(kept[4], "tensor"), "dp", scatter_dimension=1, tiled=True)
    shifts_sum = lax.psum_scatter(lax.psum(kept[5], "tensor"), "dp", scatter_dimension=1, tiled=True)
    head_sum = lax.psum_scatter(lax.psum(kept[6], "dp"), "tensor", scatter_dimension=1, tiled=True)
    ffn_sum = lax.psum_scatter(lax.psum(kept[7], "dp"), "tensor", scatter_dimension=0, tiled=True)
    heads = heads.reshape(-1, 4, head_cols).transpose(1, 0, 2)
    return (
        jnp.stack(results),
        jnp.stack(input_grads),
        heads[:3],
        heads[3].T,
        ins,
        downs.T,
        head_sum,
        ffn_sum,
        gains_sum,
        shifts_sum,
    )


def solution(mesh):
    in_specs = (
        P(None, "dp", None),
        P(None, "dp", None),
        P(None, "dp"),
        P(None, "dp", None),
        P(None, "dp"),
        P(None, "dp", "tensor"),
        P("tensor", "dp"),
        P("dp", "tensor"),
        P("tensor", "dp"),
        P(None, "tensor"),
        P("tensor"),
        P(None, "dp"),
        P(None, "dp"),
    )
    out_specs = (
        P(None, "dp", None),
        P(None, "dp", None),
        P(None, "dp", "tensor"),
        P("tensor", "dp"),
        P("dp", "tensor"),
        P("tensor", "dp"),
        P(None, "tensor"),
        P("tensor"),
        P(None, "dp"),
        P(None, "dp"),
    )
    return jax.shard_map(body, mesh=mesh, in_specs=in_specs, out_specs=out_specs, check_vma=False)
```

```python
import functools

import jax
import jax.numpy as jnp
from jax import lax
from jax.experimental import pallas as pl
from jax.experimental.pallas import tpu as pltpu
from jax.sharding import PartitionSpec as P

HEAD_DIM = 64
EPSILON = 1e-12
VMEM_LIMIT = 60 * 1024 * 1024
MESH = pl.DeviceIdType.MESH
GATHER_LAG = 1
REDUCE_LAG = 1
LOW = jnp.bfloat16
WIDE = jnp.float32
CHUNK_HEADS = 3
VALUE_AT = (6, 7, 10)
OUT_AT = (8, 9, 11)


def dot_nn(left, right):
    return lax.dot_general(left, right, (((1,), (0,)), ((), ())), preferred_element_type=WIDE)


def dot_nt(left, right):
    return lax.dot_general(left, right, (((1,), (1,)), ((), ())), preferred_element_type=WIDE)


def dot_tn(left, right):
    return lax.dot_general(left, right, (((0,), (0,)), ((), ())), preferred_element_type=WIDE)


def piece(tile, at):
    return tile[:, at * HEAD_DIM : (at + 1) * HEAD_DIM]


def slot_codes(layout, micro, block, slot_count, shape, axis):
    bucket, lengths, counts = layout
    position = lax.broadcasted_iota(jnp.int32, shape, axis)
    quarter = slot_count // 4
    whole = bucket[micro, block] == 1
    item = jnp.where(whole, 0, position // quarter)
    place = position - item * quarter
    length = jnp.where(
        item == 0,
        lengths[micro, block, 0],
        jnp.where(
            item == 1,
            lengths[micro, block, 1],
            jnp.where(item == 2, lengths[micro, block, 2], lengths[micro, block, 3]),
        ),
    )
    return item, (item < counts[micro, block]) & (place < length)


def normalize(hidden):
    center = hidden - jnp.mean(hidden, axis=-1, keepdims=True)
    inverse = lax.rsqrt(jnp.mean(center * center, axis=-1, keepdims=True) + EPSILON)
    return center * inverse, inverse


def norm_pullback(grad_rows, normed, inverse, gain_row):
    grad_normed = grad_rows * gain_row
    return inverse * (
        grad_normed
        - jnp.mean(grad_normed, axis=-1, keepdims=True)
        - normed * jnp.mean(grad_normed * normed, axis=-1, keepdims=True)
    )


def row_sum(values):
    return jnp.sum(values, axis=0, keepdims=True)


def attend_kernel(micro, place, bucket, lengths, counts, x_ref, w_ref, bias_ref, vec_ref,
                  normed_ref, inverse_ref, proj_ref, prob_ref, context_ref, total):
    step = pl.program_id(0)
    slot_count = x_ref.shape[1]
    layout = (bucket, lengths, counts)
    tokens = x_ref[0]
    proj = (dot_nn(tokens, w_ref[0, 0]) + bias_ref[0]).astype(LOW)
    proj_ref[0] = proj
    row_item, _ = slot_codes(layout, micro, place[0], slot_count, (slot_count, 1), 0)
    key_item, key_live = slot_codes(layout, micro, place[0], slot_count, (1, slot_count), 1)
    key_code = jnp.where(key_live, key_item, -1)
    parts = []
    for head in range(CHUNK_HEADS):
        query = piece(proj, 2 * head) * jnp.asarray(HEAD_DIM ** (-0.5), LOW)
        scores = dot_nt(query, piece(proj, 2 * head + 1))
        scores = jnp.where(row_item == key_code, scores, -10000.0)
        grown = jnp.exp(scores - jnp.max(scores, axis=-1, keepdims=True))
        probs = (grown * (1.0 / jnp.sum(grown, axis=-1, keepdims=True))).astype(LOW)
        prob_ref[head] = probs
        parts.append(dot_nn(probs, piece(proj, VALUE_AT[head])).astype(LOW))
    context = jnp.concatenate([parts[0], parts[1], jnp.zeros_like(parts[0]), parts[2]], axis=1)
    context_ref[0] = context
    attention = dot_nt(context, w_ref[0, 0, :, 8 * HEAD_DIM :])

    @pl.when(step == 0)
    def _():
        total[...] = attention

    @pl.when(step > 0)
    def _():
        total[...] += attention

    @pl.when(step == pl.num_programs(0) - 1)
    def _():
        normed, inverse = normalize(tokens.astype(WIDE) + total[...] + vec_ref[2:3])
        normed_ref[...] = normed
        inverse_ref[...] = jnp.broadcast_to(inverse, inverse_ref.shape)


def ffn_kernel(micro, place, bucket, lengths, counts, normed_ref, cot_ref, w_in_ref, w_down_ref, bias_ref, vec_ref,
               act_ref, slope_ref, out_ref, second_ref, second_low_ref, stat_ref, first_low, total):
    step = pl.program_id(0)
    slot_count = normed_ref.shape[0]

    @pl.when(step == 0)
    def _():
        first_low[...] = (normed_ref[...] * vec_ref[0:1] + vec_ref[3:4]).astype(LOW)

    upward = dot_nn(first_low[...], w_in_ref[0, 0]) + bias_ref[0]
    share = 0.5 + 0.5 * lax.erf(upward * (0.5**0.5))
    activated = (upward * share).astype(LOW)
    act_ref[0] = activated
    bell = jnp.exp(-0.5 * upward * upward) * 0.3989422804014327
    slope_ref[0] = (share + upward * bell).astype(LOW)
    down = dot_nt(activated, w_down_ref[0, 0])

    @pl.when(step == 0)
    def _():
        total[...] = down

    @pl.when(step > 0)
    def _():
        total[...] += down

    @pl.when(step == pl.num_programs(0) - 1)
    def _():
        _, live = slot_codes((bucket, lengths, counts), micro, place[0], slot_count, (slot_count, 1), 0)
        first = normed_ref[...] * vec_ref[0:1] + vec_ref[3:4]
        normed, inverse = normalize(first + total[...] + vec_ref[4:5])
        out_ref[...] = (normed * vec_ref[1:2] + vec_ref[5:6]).astype(LOW)
        grad_out = jnp.where(live, cot_ref[0].astype(WIDE), 0.0)
        second = norm_pullback(grad_out, normed, inverse, vec_ref[1:2])
        second_ref[...] = second
        second_low_ref[...] = second.astype(LOW)
        stat_ref[...] = jnp.concatenate(
            [row_sum(grad_out * normed), row_sum(grad_out), row_sum(second), jnp.zeros((5, second.shape[1]), WIDE)], axis=0
        )


def ffn_back_kernel(second_ref, second_low_ref, slope_ref, w_in_ref, w_down_ref, normed_ref, inverse_ref, vec_ref,
                    up_ref, hidden_ref, hidden_low_ref, up_stat_ref, stat_ref, total):
    step = pl.program_id(0)
    grad_act = dot_nn(second_low_ref[...], w_down_ref[0, 0])
    grad_up = (grad_act * slope_ref[0].astype(WIDE)).astype(LOW)
    up_ref[0] = grad_up
    up_stat_ref[0] = jnp.broadcast_to(row_sum(grad_up.astype(WIDE)), up_stat_ref.shape[1:])
    back = dot_nt(grad_up, w_in_ref[0, 0])

    @pl.when(step == 0)
    def _():
        total[...] = back + second_ref[...]

    @pl.when(step > 0)
    def _():
        total[...] += back

    @pl.when(step == pl.num_programs(0) - 1)
    def _():
        grad_first = total[...]
        normed = normed_ref[...]
        hidden = norm_pullback(grad_first, normed, inverse_ref[:, :1], vec_ref[0:1])
        hidden_ref[...] = hidden
        hidden_low_ref[...] = hidden.astype(LOW)
        stat_ref[...] = jnp.concatenate(
            [row_sum(grad_first * normed), row_sum(grad_first), row_sum(hidden), jnp.zeros((5, hidden.shape[1]), WIDE)],
            axis=0,
        )


def attend_back_kernel(micro, place, bucket, lengths, counts, hidden_ref, hidden_low_ref, w_ref, proj_ref, prob_ref,
                       context_ref, grad_ref, out_ref, stat_ref, total):
    step = pl.program_id(0)
    slot_count = hidden_ref.shape[0]
    layout = (bucket, lengths, counts)
    row_item, _ = slot_codes(layout, micro, place[0], slot_count, (slot_count, 1), 0)
    key_item, key_live = slot_codes(layout, micro, place[0], slot_count, (1, slot_count), 1)
    key_code = jnp.where(key_live, key_item, -1)
    proj = proj_ref[0]
    grad_context = dot_nn(hidden_low_ref[...], w_ref[0, 0, :, 8 * HEAD_DIM :]).astype(LOW)
    scale = HEAD_DIM ** (-0.5)
    grads = [None] * 12
    for head in range(CHUNK_HEADS):
        query, key = piece(proj, 2 * head), piece(proj, 2 * head + 1)
        probs = prob_ref[head]
        grad_head = piece(grad_context, OUT_AT[head] - 8)
        grads[VALUE_AT[head]] = dot_tn(probs, grad_head).astype(LOW)
        grad_probs = dot_nt(grad_head, piece(proj, VALUE_AT[head]))
        wide = probs.astype(WIDE)
        inner = jnp.sum(wide * grad_probs, axis=-1, keepdims=True)
        grad_scores = jnp.where(row_item == key_code, wide * (grad_probs - inner), 0.0).astype(LOW)
        grads[2 * head] = (dot_nn(grad_scores, key) * scale).astype(LOW)
        grads[2 * head + 1] = (dot_tn(grad_scores, query) * scale).astype(LOW)
    context = context_ref[0]
    zero = jnp.zeros_like(grads[0])
    for at in OUT_AT:
        grads[at] = zero
    slab = jnp.concatenate(grads, axis=1)
    back = dot_nt(slab, w_ref[0, 0])
    for at in OUT_AT:
        grads[at] = piece(context, at - 8)
    grad_ref[0] = jnp.concatenate(grads, axis=1)
    stat_ref[0] = jnp.broadcast_to(row_sum(slab.astype(WIDE)), stat_ref.shape[1:])

    @pl.when(step == 0)
    def _():
        total[...] = back + hidden_ref[...]

    @pl.when(step > 0)
    def _():
        total[...] += back

    @pl.when(step == pl.num_programs(0) - 1)
    def _():
        out_ref[...] = total[...].astype(LOW)


def in_vmem(shape, index_map):
    return pl.BlockSpec(shape, index_map)


def params(vmem=VMEM_LIMIT):
    return pltpu.CompilerParams(dimension_semantics=("arbitrary",), vmem_limit_bytes=vmem)


def attend(micro, place, bucket, lengths, counts, inputs, weights, bias, vectors, slot_count):
    parts, width = weights.shape[1], weights.shape[2]
    wide_slab = weights.shape[3]
    heads = parts * CHUNK_HEADS
    whole = lambda *shape: pl.BlockSpec(shape, lambda j, p, b, l, c: (0,) * len(shape))
    return pl.pallas_call(
        functools.partial(attend_kernel, micro),
        grid_spec=pltpu.PrefetchScalarGridSpec(
            num_scalar_prefetch=4,
            grid=(parts,),
            in_specs=[
                pl.BlockSpec((1, slot_count, width), lambda j, p, b, l, c: (micro, p[0], 0)),
                pl.BlockSpec((1, 1, width, wide_slab), lambda j, p, b, l, c: (0, j, 0, 0)),
                pl.BlockSpec((1, 1, wide_slab), lambda j, p, b, l, c: (j, 0, 0)),
                whole(*vectors.shape),
            ],
            out_specs=[
                whole(slot_count, width),
                whole(slot_count, 128),
                pl.BlockSpec((1, slot_count, wide_slab), lambda j, p, b, l, c: (j, 0, 0)),
                pl.BlockSpec((CHUNK_HEADS, slot_count, slot_count), lambda j, p, b, l, c: (j, 0, 0)),
                pl.BlockSpec((1, slot_count, 4 * HEAD_DIM), lambda j, p, b, l, c: (j, 0, 0)),
            ],
            scratch_shapes=[pltpu.VMEM((slot_count, width), WIDE)],
        ),
        out_shape=[
            jax.ShapeDtypeStruct((slot_count, width), WIDE),
            jax.ShapeDtypeStruct((slot_count, 128), WIDE),
            jax.ShapeDtypeStruct((parts, slot_count, wide_slab), LOW),
            jax.ShapeDtypeStruct((heads, slot_count, slot_count), LOW),
            jax.ShapeDtypeStruct((parts, slot_count, 4 * HEAD_DIM), LOW),
        ],
        compiler_params=params(),
        name="attend",
    )(place, bucket, lengths, counts, inputs, weights, bias, vectors)


def ffn(micro, place, bucket, lengths, counts, normed, cotangent, weights, bias, vectors):
    parts, width, cols = weights.shape[1:]
    slot_count = normed.shape[0]
    whole = lambda *shape: pl.BlockSpec(shape, lambda j, p, b, l, c: (0,) * len(shape))
    each = pl.BlockSpec((1, slot_count, cols), lambda j, p, b, l, c: (j, 0, 0))
    return pl.pallas_call(
        functools.partial(ffn_kernel, micro),
        grid_spec=pltpu.PrefetchScalarGridSpec(
            num_scalar_prefetch=4,
            grid=(parts,),
            in_specs=[
                whole(slot_count, width),
                pl.BlockSpec((1, slot_count, width), lambda j, p, b, l, c: (micro, p[0], 0)),
                pl.BlockSpec((1, 1, width, cols), lambda j, p, b, l, c: (1, j, 0, 0)),
                pl.BlockSpec((1, 1, width, cols), lambda j, p, b, l, c: (2, j, 0, 0)),
                pl.BlockSpec((1, 1, cols), lambda j, p, b, l, c: (j, 0, 0)),
                whole(*vectors.shape),
            ],
            out_specs=[each, each, whole(slot_count, width), whole(slot_count, width), whole(slot_count, width), whole(8, width)],
            scratch_shapes=[pltpu.VMEM((slot_count, width), LOW), pltpu.VMEM((slot_count, width), WIDE)],
        ),
        out_shape=[
            jax.ShapeDtypeStruct((parts, slot_count, cols), LOW),
            jax.ShapeDtypeStruct((parts, slot_count, cols), LOW),
            jax.ShapeDtypeStruct((slot_count, width), LOW),
            jax.ShapeDtypeStruct((slot_count, width), WIDE),
            jax.ShapeDtypeStruct((slot_count, width), LOW),
            jax.ShapeDtypeStruct((8, width), WIDE),
        ],
        compiler_params=params(),
        name="ffn",
    )(place, bucket, lengths, counts, normed, cotangent, weights, weights, bias, vectors)


def ffn_back(second, second_low, slope, weights, normed, inverse, vectors):
    parts, width, cols = weights.shape[1:]
    slot_count = normed.shape[0]
    whole = lambda *shape: pl.BlockSpec(shape, lambda j: (0,) * len(shape))
    each = pl.BlockSpec((1, slot_count, cols), lambda j: (j, 0, 0))
    return pl.pallas_call(
        ffn_back_kernel,
        grid=(parts,),
        in_specs=[
            whole(slot_count, width),
            whole(slot_count, width),
            each,
            pl.BlockSpec((1, 1, width, cols), lambda j: (1, j, 0, 0)),
            pl.BlockSpec((1, 1, width, cols), lambda j: (2, j, 0, 0)),
            whole(slot_count, width),
            whole(slot_count, 128),
            whole(*vectors.shape),
        ],
        out_specs=[each, whole(slot_count, width), whole(slot_count, width),
                   pl.BlockSpec((1, 8, cols), lambda j: (j, 0, 0)), whole(8, width)],
        scratch_shapes=[pltpu.VMEM((slot_count, width), WIDE)],
        out_shape=[
            jax.ShapeDtypeStruct((parts, slot_count, cols), LOW),
            jax.ShapeDtypeStruct((slot_count, width), WIDE),
            jax.ShapeDtypeStruct((slot_count, width), LOW),
            jax.ShapeDtypeStruct((parts, 8, cols), WIDE),
            jax.ShapeDtypeStruct((8, width), WIDE),
        ],
        compiler_params=params(),
        name="ffn_back",
    )(second, second_low, slope, weights, weights, normed, inverse, vectors)


def attend_back(micro, place, bucket, lengths, counts, hidden, hidden_low, weights, proj, probs, context):
    parts, width = weights.shape[1], weights.shape[2]
    wide_slab = weights.shape[3]
    slot_count = hidden.shape[0]
    whole = lambda *shape: pl.BlockSpec(shape, lambda j, p, b, l, c: (0,) * len(shape))
    each = pl.BlockSpec((1, slot_count, wide_slab), lambda j, p, b, l, c: (j, 0, 0))
    return pl.pallas_call(
        functools.partial(attend_back_kernel, micro),
        grid_spec=pltpu.PrefetchScalarGridSpec(
            num_scalar_prefetch=4,
            grid=(parts,),
            in_specs=[
                whole(slot_count, width),
                whole(slot_count, width),
                pl.BlockSpec((1, 1, width, wide_slab), lambda j, p, b, l, c: (0, j, 0, 0)),
                each,
                pl.BlockSpec((CHUNK_HEADS, slot_count, slot_count), lambda j, p, b, l, c: (j, 0, 0)),
                pl.BlockSpec((1, slot_count, 4 * HEAD_DIM), lambda j, p, b, l, c: (j, 0, 0)),
            ],
            out_specs=[each, whole(slot_count, width), pl.BlockSpec((1, 8, wide_slab), lambda j, p, b, l, c: (j, 0, 0))],
            scratch_shapes=[pltpu.VMEM((slot_count, width), WIDE)],
        ),
        out_shape=[
            jax.ShapeDtypeStruct((parts, slot_count, wide_slab), LOW),
            jax.ShapeDtypeStruct((slot_count, width), LOW),
            jax.ShapeDtypeStruct((parts, 8, wide_slab), WIDE),
        ],
        compiler_params=params(),
        name="attend_back",
    )(place, bucket, lengths, counts, hidden, hidden_low, weights, proj, probs, context)


def weight_grads_kernel(blocks, place, *refs):
    normed = refs[:blocks]
    second_low, hidden_low, act, grad_up, head_grads, tokens = [refs[(k + 1) * blocks : (k + 2) * blocks] for k in range(6)]
    vec_ref, out_ref = refs[7 * blocks], refs[7 * blocks + 1]
    turned = refs[7 * blocks + 2]
    step = pl.program_id(0)
    slot_count = second_low[0].shape[0]

    @pl.when(step == 0)
    def _():
        for b in range(blocks):
            span = slice(b * slot_count, (b + 1) * slot_count)
            first = (normed[b][...] * vec_ref[0:1] + vec_ref[3:4]).astype(LOW)
            turned[0, :, span] = tokens[b][0].T
            turned[1, :, span] = first.T
            turned[2, :, span] = second_low[b][...].T
            turned[3, :, span] = hidden_low[b][...].T

    grads = jnp.concatenate([ref[0] for ref in head_grads], axis=0)
    qkv = dot_nn(turned[0], grads)
    outs = dot_nn(turned[3], grads[:, 8 * HEAD_DIM :])
    lane = lax.broadcasted_iota(jnp.int32, (1, 2 * HEAD_DIM), 1)
    last = jnp.where(lane < HEAD_DIM, qkv[:, 10 * HEAD_DIM :], outs[:, 2 * HEAD_DIM :])
    out_ref[0, 0] = jnp.concatenate([qkv[:, : 8 * HEAD_DIM], outs[:, : 2 * HEAD_DIM], last], axis=1).astype(LOW)
    out_ref[1, 0] = dot_nn(turned[1], jnp.concatenate([ref[0] for ref in grad_up], axis=0)).astype(LOW)
    out_ref[2, 0] = dot_nn(turned[2], jnp.concatenate([ref[0] for ref in act], axis=0)).astype(LOW)


def weight_grads(place, inputs, normed, second_low, hidden_low, act, grad_up, head_grads, vectors):
    blocks = len(normed)
    micro_count = inputs.shape[0]
    per_micro = blocks // micro_count
    parts, slot_count, cols = act[0].shape
    width = normed[0].shape[1]
    whole = lambda *shape: pl.BlockSpec(shape, lambda j, p: (0,) * len(shape))
    each = pl.BlockSpec((1, slot_count, cols), lambda j, p: (j, 0, 0))
    token_specs = [
        pl.BlockSpec((1, slot_count, width), lambda j, p, m=b // per_micro, k=b % per_micro: (m, p[0] + k, 0))
        for b in range(blocks)
    ]
    return pl.pallas_call(
        functools.partial(weight_grads_kernel, blocks),
        grid_spec=pltpu.PrefetchScalarGridSpec(
            num_scalar_prefetch=1,
            grid=(parts,),
            in_specs=[whole(slot_count, width)] * (3 * blocks) + [each] * (3 * blocks) + token_specs + [whole(*vectors.shape)],
            out_specs=pl.BlockSpec((3, 1, width, cols), lambda j, p: (0, j, 0, 0)),
            scratch_shapes=[pltpu.VMEM((4, width, blocks * slot_count), LOW)],
        ),
        out_shape=jax.ShapeDtypeStruct((3, parts, width, cols), LOW),
        compiler_params=params(),
        name="weight_grads",
    )(place, *normed, *second_low, *hidden_low, *act, *grad_up, *head_grads, *([inputs] * blocks), vectors)


def mesh_place(bits):
    d = lax.axis_index("dp")
    t = lax.axis_index("tensor")
    digits = [(d // (1 << k)) % 2 for k in range(bits)]
    mates = [d + (1 - 2 * digits[k]) * (1 << k) for k in range(bits)]
    return d, t, digits, mates


def digit_index(bits, digits, open_bits):
    return tuple(slice(None) if k in open_bits else digits[k] for k in reversed(range(bits)))


def greet(d, t, mates, parts):
    barrier = pltpu.get_barrier_semaphore()
    for mate in mates:
        pl.semaphore_signal(barrier, inc=1, device_id=(mate, t), device_id_type=MESH)
    for hop in range(1, parts):
        pl.semaphore_signal(barrier, inc=1, device_id=(d, (t + hop) % parts), device_id_type=MESH)
    pl.semaphore_wait(barrier, len(mates) + parts - 1)


def bit_order(bits, flip):
    far = list(range(1, bits))
    return (far[::-1] if flip else far) + [0]


def gather_kernel(parts, bits, own, small, full, small_dp, small_t, z_send, z_recv, h_send, h_recv, s_send, s_recv, keep):
    d, t, digits, mates = mesh_place(bits)
    slab_count = own.shape[0]
    mine = digit_index(bits, digits, ())
    greet(d, t, mates, parts)
    offsets = [0] + [sign * hop for hop in range(1, parts) for sign in (1, -1)]
    pending = []

    def remote(src, dst, send, recv, to):
        return pltpu.make_async_remote_copy(src, dst, send, recv, device_id=to, device_id_type=MESH)

    local = [pltpu.make_async_copy(own.at[s], full.at[(s, t) + mine], keep.at[s]) for s in range(slab_count)]
    local.append(pltpu.make_async_copy(small.at[0], small_dp.at[mine], keep.at[slab_count]))
    local.append(pltpu.make_async_copy(small.at[1], small_t.at[t], keep.at[slab_count + 1]))
    for copy in local:
        copy.start()

    def z_copy(s, at, src, up):
        to = (d, t + 1) if up else (d, t - 1)
        way = 0 if up else 1
        return remote(src, full.at[(s, at) + mine], z_send.at[s, at, way], z_recv.at[s, at], to)

    def h_copy(s, index, step):
        offset = offsets[index]
        order = bit_order(bits, (abs(offset) + s) % 2 == 1)
        blocks = (s, t + offset) + digit_index(bits, digits, order[:step])
        src = own.at[s] if offset == 0 and step == 0 else full.at[blocks]
        return remote(src, full.at[blocks], h_send.at[s, index, step], h_recv.at[s, index, step], (mates[order[step]], t))

    def exists(offset):
        return (t + offset >= 0) & (t + offset < parts)

    def begin(s, index):
        offset = offsets[index]
        if offset == 0:
            h_copy(s, index, 0).start()
            return

        @pl.when(exists(offset))
        def _():
            up = offset < 0
            z_copy(s, t + offset, own.at[s], up).wait_recv()

            @pl.when((t < parts - 1) if up else (t > 0))
            def _():
                z_copy(s, t + offset, full.at[(s, t + offset) + mine], up).start()

            h_copy(s, index, 0).start()

    def advance(s, index, step):
        @pl.when(exists(offsets[index]))
        def _():
            h_copy(s, index, step - 1).wait_recv()
            if step < bits:
                h_copy(s, index, step).start()

    def small_step(step):
        blocks = digit_index(bits, digits, range(step))
        src = small.at[0] if step == 0 else small_dp.at[blocks]
        return remote(src, small_dp.at[blocks], s_send.at[step], s_recv.at[step], (mates[step], t))

    def small_hop(hop):
        peer = (d, (t + hop) % parts)
        return remote(small.at[1], small_t.at[t], s_send.at[bits + hop - 1], s_recv.at[bits + hop - 1], peer)

    for s in range(slab_count):
        @pl.when(t < parts - 1)
        def _():
            z_copy(s, t, own.at[s], True).start()

        @pl.when(t > 0)
        def _():
            z_copy(s, t, own.at[s], False).start()
        if s == 0:
            begin(0, 0)
            for hop in range(1, parts):
                small_hop(hop).start()
            small_step(0).start()
    for copy in local:
        copy.wait()

    groups = [(s, [index for index, offset in enumerate(offsets) if abs(offset) == hop])
              for s in range(slab_count) for hop in range(parts)]
    for wave in range(len(groups) + bits * GATHER_LAG):
        for step in range(bits + 1):
            if 0 <= wave - step * GATHER_LAG < len(groups):
                s, indices = groups[wave - step * GATHER_LAG]
                for index in indices:
                    if step:
                        advance(s, index, step)
                    elif (s, index) != (0, 0):
                        begin(s, index)
        if wave < bits:
            small_step(wave).wait_recv()
            if wave + 1 < bits:
                small_step(wave + 1).start()

    for hop in range(1, parts):
        small_hop(hop).wait()
    for step in range(bits):
        small_step(step).wait_send()
    for s, indices in groups:
        for index in indices:
            offset = offsets[index]

            @pl.when(exists(offset))
            def _():
                for step in range(bits):
                    h_copy(s, index, step).wait_send()
                if offset <= 0:
                    @pl.when(t < parts - 1)
                    def _():
                        z_copy(s, t + offset, own.at[s], True).wait_send()
                if offset >= 0:
                    @pl.when(t > 0)
                    def _():
                        z_copy(s, t + offset, own.at[s], False).wait_send()


def gather_weights(own, small, parts, dp_count):
    bits = dp_count.bit_length() - 1
    slab_count, rows, columns = own.shape
    places = 2 * parts - 1
    low = jnp.bfloat16
    full, small_dp, small_t = pl.pallas_call(
        functools.partial(gather_kernel, parts, bits),
        out_shape=[
            jax.ShapeDtypeStruct((slab_count, parts) + (2,) * bits + (rows, columns), low),
            jax.ShapeDtypeStruct((2,) * bits + small.shape[1:], low),
            jax.ShapeDtypeStruct((parts,) + small.shape[1:], low),
        ],
        in_specs=[pl.BlockSpec(memory_space=pl.ANY)] * 2,
        out_specs=[pl.BlockSpec(memory_space=pl.ANY)] * 3,
        scratch_shapes=[
            pltpu.SemaphoreType.DMA((slab_count, parts, 2)),
            pltpu.SemaphoreType.DMA((slab_count, parts)),
            pltpu.SemaphoreType.DMA((slab_count, places, bits)),
            pltpu.SemaphoreType.DMA((slab_count, places, bits)),
            pltpu.SemaphoreType.DMA((bits + parts - 1,)),
            pltpu.SemaphoreType.DMA((bits + parts - 1,)),
            pltpu.SemaphoreType.DMA((slab_count + 2,)),
        ],
        compiler_params=pltpu.CompilerParams(collective_id=0, has_side_effects=True, vmem_limit_bytes=VMEM_LIMIT),
        name="gather_weights",
    )(own, small)
    full = full.reshape(slab_count, parts, dp_count * rows, columns)
    return full, small_dp.reshape((dp_count,) + small.shape[1:]), small_t


def add_rows(target, first, second, rows):
    lead = target.shape[:-2]
    chunk = 16 if rows % 16 == 0 else rows
    steps = rows // chunk
    count = 1
    for extent in lead:
        count *= extent

    def one(i, carry):
        at, rest = [], i // steps
        for extent in reversed(lead):
            at.insert(0, rest % extent)
            rest = rest // extent
        where = tuple(at) + (pl.ds(pl.multiple_of((i % steps) * chunk, chunk), chunk),)
        total = first[where].astype(jnp.float32) + second[where].astype(jnp.float32)
        target[where] = total.astype(target.dtype)
        return carry

    lax.fori_loop(0, count * steps, one, 0)


def reduce_kernel(parts, bits, grads, small, out, small_out, *scratch):
    bufs = scratch[:bits]
    z_up, z_down, small_buf, small_sum = scratch[bits:bits + 4]
    h_send, h_recv, up_send, up_recv, down_send, down_recv, s_send, s_recv = scratch[bits + 4:]
    d, t, digits, mates = mesh_place(bits)
    slab_count = grads.shape[0]
    rows = grads.shape[-2]
    greet(d, t, mates, parts)
    items = [(s, at) for s in range(slab_count) for at in range(parts)]
    small_bits = bits + parts.bit_length() - 1

    def remote(src, dst, send, recv, to):
        return pltpu.make_async_remote_copy(src, dst, send, recv, device_id=to, device_id_type=MESH)

    def order_of(number):
        s, at = items[number]
        return bit_order(bits, (s + at) % 2 == 1)[::-1]

    def held(number, step):
        s, at = items[number]
        return grads.at[s, at] if step == 0 else bufs[step - 1].at[number]

    def part_of(number, step, side):
        order = order_of(number)
        left = [k for k in reversed(range(bits)) if k not in order[:step]]
        pick = tuple(side if k == order[step] else slice(None) for k in left)
        return held(number, step).at[pick]

    def h_copy(number, step):
        order = order_of(number)
        digit = digits[order[step]]
        return remote(part_of(number, step, 1 - digit), bufs[step].at[number],
                      h_send.at[number, step], h_recv.at[number, step], (mates[order[step]], t))

    def fold(number, step):
        h_copy(number, step).wait_recv()
        digit = digits[order_of(number)[step]]
        add_rows(bufs[step].at[number], bufs[step].at[number], part_of(number, step, digit), rows)

    def summed(s, at):
        return bufs[bits - 1].at[s * parts + at]

    def z_copy(s, at, up, src):
        buf, send, recv = (z_up, up_send, up_recv) if up else (z_down, down_send, down_recv)
        to = (d, t + 1) if up else (d, t - 1)
        return remote(src, buf.at[s, at], send.at[s, at], recv.at[s, at], to)

    def z_pass(s, hop, up):
        at = t + hop if up else t - hop
        edge = (t == 0) if up else (t == parts - 1)
        buf = z_up if up else z_down

        @pl.when((at < parts) if up else (at >= 0))
        def _():
            @pl.when(edge)
            def _():
                z_copy(s, at, up, summed(s, at)).start()

            @pl.when(jnp.logical_not(edge))
            def _():
                z_copy(s, at, up, summed(s, at)).wait_recv()
                add_rows(buf.at[s, at], buf.at[s, at], summed(s, at), rows)
                z_copy(s, at, up, buf.at[s, at]).start()

    def z_finish(s):
        add_rows(out.at[s], summed(s, t), summed(s, t), rows)

        def scaled(i, carry):
            out[s] = out[s] * 0.5
            return carry
        lax.fori_loop(0, 1, scaled, 0)
        for up, buf in ((True, z_up), (False, z_down)):
            @pl.when((t > 0) if up else (t < parts - 1))
            def _():
                z_copy(s, t, up, summed(s, t)).wait_recv()
                add_rows(out.at[s], out.at[s], buf.at[s, t], rows)

    def small_copy(step):
        if step < bits:
            to = (mates[step], t)
        else:
            gap = 1 << (step - bits)
            to = (d, t + (1 - 2 * ((t // gap) % 2)) * gap)
        src = small if step == 0 else small_sum.at[step - 1]
        return remote(src, small_buf.at[step], s_send.at[step], s_recv.at[step], to)

    def small_fold(step):
        small_copy(step).wait_recv()
        before = small[...] if step == 0 else small_sum[step - 1]
        small_sum[step] = before + small_buf[step]
        if step + 1 < small_bits:
            small_copy(step + 1).start()

    for number in range(len(items)):
        h_copy(number, 0).start()
        if number == 0:
            small_copy(0).start()
    for wave in range(len(items) + bits * REDUCE_LAG + parts + 1):
        for step in range(bits):
            number = wave - step * REDUCE_LAG
            if 0 <= number < len(items):
                fold(number, step)
                if step + 1 < bits:
                    h_copy(number, step + 1).start()
        for s in range(slab_count):
            phase = wave - ((s + 1) * parts - 1 + bits * REDUCE_LAG)
            if 0 <= phase < parts - 1:
                z_pass(s, parts - 1 - phase, True)
                z_pass(s, parts - 1 - phase, False)
            elif phase == parts - 1:
                z_finish(s)
        if wave < small_bits:
            small_fold(wave)
    small_out[...] = small_sum[small_bits - 1]

    for step in range(small_bits):
        small_copy(step).wait_send()
    for number in range(len(items)):
        for step in range(bits):
            h_copy(number, step).wait_send()
    for s in range(slab_count):
        for hop in range(1, parts):
            @pl.when(t + hop < parts)
            def _():
                z_copy(s, t + hop, True, summed(s, t)).wait_send()

            @pl.when(t - hop >= 0)
            def _():
                z_copy(s, t - hop, False, summed(s, t)).wait_send()


def reduce_grads(grads, small, parts, dp_count):
    bits = dp_count.bit_length() - 1
    slab_count, columns = grads.shape[0], grads.shape[-1]
    rows = grads.shape[2] // dp_count
    grads = grads.reshape((slab_count, parts) + (2,) * bits + (rows, columns))
    low = jnp.bfloat16
    count = slab_count * parts
    small_bits = bits + parts.bit_length() - 1
    dma = pltpu.SemaphoreType.DMA
    return pl.pallas_call(
        functools.partial(reduce_kernel, parts, bits),
        out_shape=[
            jax.ShapeDtypeStruct((slab_count, rows, columns), jnp.float32),
            jax.ShapeDtypeStruct(small.shape, jnp.float32),
        ],
        in_specs=[pl.BlockSpec(memory_space=pltpu.VMEM)] * 2,
        out_specs=[pl.BlockSpec(memory_space=pltpu.VMEM)] * 2,
        scratch_shapes=[pltpu.VMEM((count,) + (2,) * (bits - 1 - step) + (rows, columns), low) for step in range(bits)]
        + [pltpu.VMEM((slab_count, parts, rows, columns), low)] * 2
        + [pltpu.VMEM((small_bits,) + small.shape, jnp.float32)] * 2
        + [dma((count, bits)), dma((count, bits))]
        + [dma((slab_count, parts))] * 4
        + [dma((small_bits,))] * 2,
        compiler_params=pltpu.CompilerParams(collective_id=1, has_side_effects=True, vmem_limit_bytes=VMEM_LIMIT),
        name="reduce_grads",
    )(grads, small)


def slab_order(query, key, value, out):
    columns = lambda group, head: group[..., head * HEAD_DIM : (head + 1) * HEAD_DIM]
    order = [(query, 0), (key, 0), (query, 1), (key, 1), (query, 2), (key, 2),
             (value, 0), (value, 1), (out, 0), (out, 1), (value, 2), (out, 2)]
    return jnp.concatenate([columns(group, head) for group, head in order], axis=-1)


def slab_parts(slab):
    columns = lambda at: slab[..., at * HEAD_DIM : (at + 1) * HEAD_DIM]
    groups = ((0, 2, 4), (1, 3, 5), VALUE_AT, OUT_AT)
    return [jnp.concatenate([columns(at) for at in group], axis=-1) for group in groups]


def add_all(terms):
    total = terms[0]
    for term in terms[1:]:
        total = total + term
    return total


def body(
    inputs,
    cotangent,
    bucket,
    lengths,
    counts,
    w_qkv,
    w_out,
    w_in,
    w_down,
    head_bias,
    ffn_bias,
    norm_gains,
    row_biases,
):
    micro_count, _, width = inputs.shape
    blocks_all = bucket.shape[1]
    slot_count = inputs.shape[1] // blocks_all
    parts, dp_count = lax.axis_size("tensor"), lax.axis_size("dp")
    rank, dp_rank = lax.axis_index("tensor"), lax.axis_index("dp")
    per_micro = blocks_all // parts
    cols = w_in.shape[1]
    rows = w_in.shape[0]

    own = jnp.stack([slab_order(w_qkv[0], w_qkv[1], w_qkv[2], w_out.T), w_in, w_down.T])
    norm_row = jnp.concatenate([norm_gains, row_biases], axis=0).reshape(1, -1)
    vector_count = norm_gains.shape[0] + row_biases.shape[0]
    no_bias = jnp.zeros_like(head_bias[:1])
    bias_rows = jnp.concatenate([slab_order(head_bias[:1], no_bias, head_bias[1:], no_bias), ffn_bias[None]], axis=0)
    small = jnp.stack([
        jnp.pad(norm_row, ((0, 15), (0, cols - norm_row.shape[1]))),
        jnp.pad(bias_rows, ((0, 14), (0, 0))),
    ])
    weights, small_dp, small_t = gather_weights(own, small, parts, dp_count)
    vectors = small_dp[:, 0, : norm_row.shape[1]].reshape(dp_count, vector_count, rows)
    vectors = vectors.transpose(1, 0, 2).reshape(vector_count, width).astype(jnp.float32)
    vectors = jnp.pad(vectors, ((0, 8 - vector_count), (0, 0)))
    head_rows = small_t[:, 0:1].astype(jnp.float32)
    ffn_rows = small_t[:, 1:2].astype(jnp.float32)

    blocks = [(m, k) for m in range(micro_count) for k in range(per_micro)]
    places = [jnp.full((1,), rank * per_micro + k, jnp.int32) for k in range(per_micro)]
    layout = (bucket, lengths, counts)
    kept = []
    outs = []
    for m, k in blocks:
        normed, inverse, proj, probs, context = attend(m, places[k], *layout, inputs, weights, head_rows, vectors, slot_count)
        act, slope, out, second, second_low, stat = ffn(m, places[k], *layout, normed, cotangent, weights, ffn_rows, vectors)
        kept.append((normed, inverse, proj, probs, context, act, slope, second, second_low, stat))
        outs.append(out)
    results = [
        lax.all_gather(jnp.concatenate(outs[m * per_micro : (m + 1) * per_micro], axis=0), "tensor", axis=0, tiled=True)
        for m in range(micro_count)
    ]
    token_grads, saved = [], []
    for (m, k), (normed, inverse, proj, probs, context, act, slope, second, second_low, stat) in zip(blocks, kept):
        grad_up, hidden, hidden_low, up_stat, first_stat = ffn_back(second, second_low, slope, weights, normed, inverse, vectors)
        head_grads, token_grad, head_stat = attend_back(
            m, places[k], *layout, hidden, hidden_low, weights, proj, probs, context
        )
        token_grads.append(token_grad)
        saved.append((normed, second_low, hidden_low, act, grad_up, head_grads, stat, first_stat, up_stat, head_stat))
    input_grads = [
        lax.all_gather(jnp.concatenate(token_grads[m * per_micro : (m + 1) * per_micro], axis=0), "tensor", axis=0, tiled=True)
        for m in range(micro_count)
    ]
    columns = list(zip(*saved))
    grads = weight_grads(places[0], inputs, *columns[:6], vectors)
    stat, first_stat, up_stat, head_stat = [add_all(column) for column in columns[6:]]
    small_grads = jnp.concatenate(
        [
            jnp.stack([first_stat[0], stat[0], first_stat[2], first_stat[1], stat[2], stat[1]]),
            up_stat[:, 0],
            head_stat[:, 0],
        ],
        axis=0,
    )
    small_grads = jnp.pad(small_grads, ((0, -small_grads.shape[0] % 8), (0, 0)))
    shard, sums = reduce_grads(grads, small_grads, parts, dp_count)
    grad_query, grad_key, grad_value, grad_out = slab_parts(shard[0])
    vector_sums = lax.dynamic_slice_in_dim(sums[:vector_count], dp_rank * rows, rows, 1)
    ffn_sum = lax.dynamic_slice_in_dim(sums, vector_count + rank, 1, 0)[0]
    head_sum = slab_parts(lax.dynamic_slice_in_dim(sums, vector_count + parts + rank, 1, 0))
    return (
        jnp.stack(results),
        jnp.stack(input_grads),
        jnp.stack([grad_query, grad_key, grad_value]),
        grad_out.T,
        shard[1],
        shard[2].T,
        jnp.concatenate([head_sum[0], head_sum[2]], axis=0),
        ffn_sum,
        vector_sums[:2],
        vector_sums[2:],
    )


def solution(mesh):
    in_specs = (
        P(None, "dp", None),
        P(None, "dp", None),
        P(None, "dp"),
        P(None, "dp", None),
        P(None, "dp"),
        P(None, "dp", "tensor"),
        P("tensor", "dp"),
        P("dp", "tensor"),
        P("tensor", "dp"),
        P(None, "tensor"),
        P("tensor"),
        P(None, "dp"),
        P(None, "dp"),
    )
    out_specs = (
        P(None, "dp", None),
        P(None, "dp", None),
        P(None, "dp", "tensor"),
        P("tensor", "dp"),
        P("dp", "tensor"),
        P("tensor", "dp"),
        P(None, "tensor"),
        P("tensor"),
        P(None, "dp"),
        P(None, "dp"),
    )
    return jax.shard_map(body, mesh=mesh, in_specs=in_specs, out_specs=out_specs, check_vma=False)
```

```python
import functools

import jax
import jax.numpy as jnp
from jax import lax
from jax.experimental import pallas as pl
from jax.experimental.pallas import tpu as pltpu
from jax.sharding import PartitionSpec as P

HEAD_DIM = 64
EPSILON = 1e-12
VMEM_LIMIT = 60 * 1024 * 1024
MESH = pl.DeviceIdType.MESH
GATHER_LAG = 2
REDUCE_LAG = 2
def takes(microseconds):
    return pl.CostEstimate(flops=int(microseconds * 1.15e8), bytes_accessed=0, transcendentals=0)


LOW = jnp.bfloat16
WIDE = jnp.float32
CHUNK_HEADS = 3
VALUE_AT = (6, 7, 10)
OUT_AT = (8, 9, 11)


def dot_nn(left, right):
    return lax.dot_general(left, right, (((1,), (0,)), ((), ())), preferred_element_type=WIDE)


def dot_nt(left, right):
    return lax.dot_general(left, right, (((1,), (1,)), ((), ())), preferred_element_type=WIDE)


def dot_tn(left, right):
    return lax.dot_general(left, right, (((0,), (0,)), ((), ())), preferred_element_type=WIDE)


def piece(tile, at):
    return tile[:, at * HEAD_DIM : (at + 1) * HEAD_DIM]


def slot_codes(layout, micro, block, slot_count, shape, axis):
    bucket, lengths, counts = layout
    position = lax.broadcasted_iota(jnp.int32, shape, axis)
    quarter = slot_count // 4
    whole = bucket[micro, block] == 1
    item = jnp.where(whole, 0, position // quarter)
    place = position - item * quarter
    length = jnp.where(
        item == 0,
        lengths[micro, block, 0],
        jnp.where(
            item == 1,
            lengths[micro, block, 1],
            jnp.where(item == 2, lengths[micro, block, 2], lengths[micro, block, 3]),
        ),
    )
    return item, (item < counts[micro, block]) & (place < length)


def normalize(hidden):
    center = hidden - jnp.mean(hidden, axis=-1, keepdims=True)
    inverse = lax.rsqrt(jnp.mean(center * center, axis=-1, keepdims=True) + EPSILON)
    return center * inverse, inverse


def norm_pullback(grad_rows, normed, inverse, gain_row):
    grad_normed = grad_rows * gain_row
    return inverse * (
        grad_normed
        - jnp.mean(grad_normed, axis=-1, keepdims=True)
        - normed * jnp.mean(grad_normed * normed, axis=-1, keepdims=True)
    )


def row_sum(values):
    return jnp.sum(values, axis=0, keepdims=True)


def attend_unit(layout, micro, place, tokens, weights, bias_row, proj_ref, prob_ref, context_ref):
    slot_count = tokens.shape[0]
    proj = (dot_nn(tokens, weights) + bias_row).astype(LOW)
    proj_ref[...] = proj
    row_item, _ = slot_codes(layout, micro, place, slot_count, (slot_count, 1), 0)
    key_item, key_live = slot_codes(layout, micro, place, slot_count, (1, slot_count), 1)
    key_code = jnp.where(key_live, key_item, -1)
    outs = []
    for head in range(CHUNK_HEADS):
        query = piece(proj, 2 * head) * jnp.asarray(HEAD_DIM ** (-0.5), LOW)
        scores = dot_nt(query, piece(proj, 2 * head + 1))
        scores = jnp.where(row_item == key_code, scores, -10000.0)
        grown = jnp.exp(scores - jnp.max(scores, axis=-1, keepdims=True))
        probs = (grown * (1.0 / jnp.sum(grown, axis=-1, keepdims=True))).astype(LOW)
        prob_ref[head] = probs
        outs.append(dot_nn(probs, piece(proj, VALUE_AT[head])).astype(LOW))
    context = jnp.concatenate([outs[0], outs[1], jnp.zeros_like(outs[0]), outs[2]], axis=1)
    context_ref[...] = context
    return dot_nt(context, weights[:, 8 * HEAD_DIM :])


def ffn_unit(first_low, w_in, w_down, bias_row, act_ref, slope_ref):
    upward = dot_nn(first_low, w_in) + bias_row
    share = 0.5 + 0.5 * lax.erf(upward * (0.5**0.5))
    activated = (upward * share).astype(LOW)
    act_ref[...] = activated
    bell = jnp.exp(-0.5 * upward * upward) * 0.3989422804014327
    slope_ref[...] = (share + upward * bell).astype(LOW)
    return dot_nt(activated, w_down)


def second_norm(layout, micro, place, first_normed, down_total, cot_rows, vectors):
    slot_count = first_normed.shape[0]
    _, live = slot_codes(layout, micro, place, slot_count, (slot_count, 1), 0)
    first = first_normed * vectors[0:1] + vectors[3:4]
    normed, inverse = normalize(first + down_total + vectors[4:5])
    out = (normed * vectors[1:2] + vectors[5:6]).astype(LOW)
    grad_out = jnp.where(live, cot_rows.astype(WIDE), 0.0)
    second = norm_pullback(grad_out, normed, inverse, vectors[1:2])
    stat = jnp.concatenate(
        [row_sum(grad_out * normed), row_sum(grad_out), row_sum(second), jnp.zeros((5, second.shape[1]), WIDE)], axis=0
    )
    return out, second, stat


def attend_kernel(micro, place, bucket, lengths, counts, x_ref, w_ref, bias_ref, vec_ref,
                  normed_ref, inverse_ref, proj_ref, prob_ref, context_ref, total):
    step = pl.program_id(0)
    layout = (bucket, lengths, counts)
    tokens = x_ref[0]
    attention = attend_unit(layout, micro, place[0], tokens, w_ref[0, 0], bias_ref[0],
                            proj_ref.at[0], prob_ref, context_ref.at[0])

    @pl.when(step == 0)
    def _():
        total[...] = attention

    @pl.when(step > 0)
    def _():
        total[...] += attention

    @pl.when(step == pl.num_programs(0) - 1)
    def _():
        normed, inverse = normalize(tokens.astype(WIDE) + total[...] + vec_ref[2:3])
        normed_ref[...] = normed
        inverse_ref[...] = jnp.broadcast_to(inverse, inverse_ref.shape)


def ffn_kernel(micro, place, bucket, lengths, counts, normed_ref, cot_ref, w_in_ref, w_down_ref, bias_ref, vec_ref,
               act_ref, slope_ref, out_ref, second_ref, second_low_ref, stat_ref, first_low, total):
    step = pl.program_id(0)

    @pl.when(step == 0)
    def _():
        first_low[...] = (normed_ref[...] * vec_ref[0:1] + vec_ref[3:4]).astype(LOW)

    down = ffn_unit(first_low[...], w_in_ref[0, 0], w_down_ref[0, 0], bias_ref[0], act_ref.at[0], slope_ref.at[0])

    @pl.when(step == 0)
    def _():
        total[...] = down

    @pl.when(step > 0)
    def _():
        total[...] += down

    @pl.when(step == pl.num_programs(0) - 1)
    def _():
        out, second, stat = second_norm(
            (bucket, lengths, counts), micro, place[0], normed_ref[...], total[...], cot_ref[0], vec_ref
        )
        out_ref[...] = out
        second_ref[...] = second
        second_low_ref[...] = second.astype(LOW)
        stat_ref[...] = stat


def ffn_back_kernel(second_ref, second_low_ref, slope_ref, w_in_ref, w_down_ref, normed_ref, inverse_ref, vec_ref,
                    up_ref, hidden_ref, hidden_low_ref, up_stat_ref, stat_ref, total):
    step = pl.program_id(0)
    grad_act = dot_nn(second_low_ref[...], w_down_ref[0, 0])
    grad_up = (grad_act * slope_ref[0].astype(WIDE)).astype(LOW)
    up_ref[0] = grad_up
    up_stat_ref[0] = jnp.broadcast_to(row_sum(grad_up.astype(WIDE)), up_stat_ref.shape[1:])
    back = dot_nt(grad_up, w_in_ref[0, 0])

    @pl.when(step == 0)
    def _():
        total[...] = back + second_ref[...]

    @pl.when(step > 0)
    def _():
        total[...] += back

    @pl.when(step == pl.num_programs(0) - 1)
    def _():
        grad_first = total[...]
        normed = normed_ref[...]
        hidden = norm_pullback(grad_first, normed, inverse_ref[:, :1], vec_ref[0:1])
        hidden_ref[...] = hidden
        hidden_low_ref[...] = hidden.astype(LOW)
        stat_ref[...] = jnp.concatenate(
            [row_sum(grad_first * normed), row_sum(grad_first), row_sum(hidden), jnp.zeros((5, hidden.shape[1]), WIDE)],
            axis=0,
        )


def attend_back_kernel(micro, place, bucket, lengths, counts, hidden_ref, hidden_low_ref, w_ref, proj_ref, prob_ref,
                       context_ref, grad_ref, out_ref, stat_ref, total):
    step = pl.program_id(0)
    slot_count = hidden_ref.shape[0]
    layout = (bucket, lengths, counts)
    row_item, _ = slot_codes(layout, micro, place[0], slot_count, (slot_count, 1), 0)
    key_item, key_live = slot_codes(layout, micro, place[0], slot_count, (1, slot_count), 1)
    key_code = jnp.where(key_live, key_item, -1)
    proj = proj_ref[0]
    grad_context = dot_nn(hidden_low_ref[...], w_ref[0, 0, :, 8 * HEAD_DIM :]).astype(LOW)
    scale = HEAD_DIM ** (-0.5)
    grads = [None] * 12
    for head in range(CHUNK_HEADS):
        query, key = piece(proj, 2 * head), piece(proj, 2 * head + 1)
        probs = prob_ref[head]
        grad_head = piece(grad_context, OUT_AT[head] - 8)
        grads[VALUE_AT[head]] = dot_tn(probs, grad_head).astype(LOW)
        grad_probs = dot_nt(grad_head, piece(proj, VALUE_AT[head]))
        wide = probs.astype(WIDE)
        inner = jnp.sum(wide * grad_probs, axis=-1, keepdims=True)
        grad_scores = jnp.where(row_item == key_code, wide * (grad_probs - inner), 0.0).astype(LOW)
        grads[2 * head] = (dot_nn(grad_scores, key) * scale).astype(LOW)
        grads[2 * head + 1] = (dot_tn(grad_scores, query) * scale).astype(LOW)
    context = context_ref[0]
    zero = jnp.zeros_like(grads[0])
    for at in OUT_AT:
        grads[at] = zero
    slab = jnp.concatenate(grads, axis=1)
    back = dot_nt(slab, w_ref[0, 0])
    for at in OUT_AT:
        grads[at] = piece(context, at - 8)
    grad_ref[0] = jnp.concatenate(grads, axis=1)
    stat_ref[0] = jnp.broadcast_to(row_sum(slab.astype(WIDE)), stat_ref.shape[1:])

    @pl.when(step == 0)
    def _():
        total[...] = back + hidden_ref[...]

    @pl.when(step > 0)
    def _():
        total[...] += back

    @pl.when(step == pl.num_programs(0) - 1)
    def _():
        out_ref[...] = total[...].astype(LOW)


def in_vmem(shape, index_map):
    return pl.BlockSpec(shape, index_map)


def params(vmem=VMEM_LIMIT):
    return pltpu.CompilerParams(dimension_semantics=("arbitrary",), vmem_limit_bytes=vmem)


def attend(micro, place, bucket, lengths, counts, inputs, weights, bias, vectors, slot_count):
    parts, width = weights.shape[1], weights.shape[2]
    wide_slab = weights.shape[3]
    heads = parts * CHUNK_HEADS
    whole = lambda *shape: pl.BlockSpec(shape, lambda j, p, b, l, c: (0,) * len(shape))
    return pl.pallas_call(
        functools.partial(attend_kernel, micro),
        grid_spec=pltpu.PrefetchScalarGridSpec(
            num_scalar_prefetch=4,
            grid=(parts,),
            in_specs=[
                pl.BlockSpec((1, slot_count, width), lambda j, p, b, l, c: (micro, p[0], 0)),
                pl.BlockSpec((1, 1, width, wide_slab), lambda j, p, b, l, c: (0, j, 0, 0)),
                pl.BlockSpec((1, 1, wide_slab), lambda j, p, b, l, c: (j, 0, 0)),
                whole(*vectors.shape),
            ],
            out_specs=[
                whole(slot_count, width),
                whole(slot_count, 128),
                pl.BlockSpec((1, slot_count, wide_slab), lambda j, p, b, l, c: (j, 0, 0)),
                pl.BlockSpec((CHUNK_HEADS, slot_count, slot_count), lambda j, p, b, l, c: (j, 0, 0)),
                pl.BlockSpec((1, slot_count, 4 * HEAD_DIM), lambda j, p, b, l, c: (j, 0, 0)),
            ],
            scratch_shapes=[pltpu.VMEM((slot_count, width), WIDE)],
        ),
        out_shape=[
            jax.ShapeDtypeStruct((slot_count, width), WIDE),
            jax.ShapeDtypeStruct((slot_count, 128), WIDE),
            jax.ShapeDtypeStruct((parts, slot_count, wide_slab), LOW),
            jax.ShapeDtypeStruct((heads, slot_count, slot_count), LOW),
            jax.ShapeDtypeStruct((parts, slot_count, 4 * HEAD_DIM), LOW),
        ],
        compiler_params=params(),
        name="attend",
        cost_estimate=takes(16),
    )(place, bucket, lengths, counts, inputs, weights, bias, vectors)


def ffn(micro, place, bucket, lengths, counts, normed, cotangent, weights, bias, vectors):
    parts, width, cols = weights.shape[1:]
    normed, index = normed
    slot_count = normed.shape[1]
    whole = lambda *shape: pl.BlockSpec(shape, lambda j, p, b, l, c: (0,) * len(shape))
    each = pl.BlockSpec((1, slot_count, cols), lambda j, p, b, l, c: (j, 0, 0))
    return pl.pallas_call(
        functools.partial(ffn_kernel, micro),
        grid_spec=pltpu.PrefetchScalarGridSpec(
            num_scalar_prefetch=4,
            grid=(parts,),
            in_specs=[
                pl.BlockSpec((None, slot_count, width), lambda j, p, b, l, c: (index, 0, 0)),
                pl.BlockSpec((1, slot_count, width), lambda j, p, b, l, c: (micro, p[0], 0)),
                pl.BlockSpec((1, 1, width, cols), lambda j, p, b, l, c: (1, j, 0, 0)),
                pl.BlockSpec((1, 1, width, cols), lambda j, p, b, l, c: (2, j, 0, 0)),
                pl.BlockSpec((1, 1, cols), lambda j, p, b, l, c: (j, 0, 0)),
                whole(*vectors.shape),
            ],
            out_specs=[each, each, whole(slot_count, width), whole(slot_count, width), whole(slot_count, width), whole(8, width)],
            scratch_shapes=[pltpu.VMEM((slot_count, width), LOW), pltpu.VMEM((slot_count, width), WIDE)],
        ),
        out_shape=[
            jax.ShapeDtypeStruct((parts, slot_count, cols), LOW),
            jax.ShapeDtypeStruct((parts, slot_count, cols), LOW),
            jax.ShapeDtypeStruct((slot_count, width), LOW),
            jax.ShapeDtypeStruct((slot_count, width), WIDE),
            jax.ShapeDtypeStruct((slot_count, width), LOW),
            jax.ShapeDtypeStruct((8, width), WIDE),
        ],
        compiler_params=params(),
        name="ffn",
        cost_estimate=takes(16),
    )(place, bucket, lengths, counts, normed, cotangent, weights, weights, bias, vectors)


def ffn_back(second, second_low, slope, weights, normed, inverse, vectors):
    parts, width, cols = weights.shape[1:]
    (normed, index), (inverse, _) = normed, inverse
    slot_count = normed.shape[1]
    whole = lambda *shape: pl.BlockSpec(shape, lambda j: (0,) * len(shape))
    each = pl.BlockSpec((1, slot_count, cols), lambda j: (j, 0, 0))
    return pl.pallas_call(
        ffn_back_kernel,
        grid=(parts,),
        in_specs=[
            whole(slot_count, width),
            whole(slot_count, width),
            each,
            pl.BlockSpec((1, 1, width, cols), lambda j: (1, j, 0, 0)),
            pl.BlockSpec((1, 1, width, cols), lambda j: (2, j, 0, 0)),
            pl.BlockSpec((None, slot_count, width), lambda j: (index, 0, 0)),
            pl.BlockSpec((None, slot_count, 128), lambda j: (index, 0, 0)),
            whole(*vectors.shape),
        ],
        out_specs=[each, whole(slot_count, width), whole(slot_count, width),
                   pl.BlockSpec((1, 8, cols), lambda j: (j, 0, 0)), whole(8, width)],
        scratch_shapes=[pltpu.VMEM((slot_count, width), WIDE)],
        out_shape=[
            jax.ShapeDtypeStruct((parts, slot_count, cols), LOW),
            jax.ShapeDtypeStruct((slot_count, width), WIDE),
            jax.ShapeDtypeStruct((slot_count, width), LOW),
            jax.ShapeDtypeStruct((parts, 8, cols), WIDE),
            jax.ShapeDtypeStruct((8, width), WIDE),
        ],
        compiler_params=params(),
        name="ffn_back",
        cost_estimate=takes(14),
    )(second, second_low, slope, weights, weights, normed, inverse, vectors)


def attend_back(micro, place, bucket, lengths, counts, hidden, hidden_low, weights, proj, probs, context):
    parts, width = weights.shape[1], weights.shape[2]
    wide_slab = weights.shape[3]
    slot_count = hidden.shape[0]
    (proj, index), (probs, _), (context, _) = proj, probs, context
    whole = lambda *shape: pl.BlockSpec(shape, lambda j, p, b, l, c: (0,) * len(shape))
    each = pl.BlockSpec((1, slot_count, wide_slab), lambda j, p, b, l, c: (j, 0, 0))
    return pl.pallas_call(
        functools.partial(attend_back_kernel, micro),
        grid_spec=pltpu.PrefetchScalarGridSpec(
            num_scalar_prefetch=4,
            grid=(parts,),
            in_specs=[
                whole(slot_count, width),
                whole(slot_count, width),
                pl.BlockSpec((1, 1, width, wide_slab), lambda j, p, b, l, c: (0, j, 0, 0)),
                pl.BlockSpec((None, 1, slot_count, wide_slab), lambda j, p, b, l, c: (index, j, 0, 0)),
                pl.BlockSpec((None, CHUNK_HEADS, slot_count, slot_count), lambda j, p, b, l, c: (index, j, 0, 0)),
                pl.BlockSpec((None, 1, slot_count, 4 * HEAD_DIM), lambda j, p, b, l, c: (index, j, 0, 0)),
            ],
            out_specs=[each, whole(slot_count, width), pl.BlockSpec((1, 8, wide_slab), lambda j, p, b, l, c: (j, 0, 0))],
            scratch_shapes=[pltpu.VMEM((slot_count, width), WIDE)],
        ),
        out_shape=[
            jax.ShapeDtypeStruct((parts, slot_count, wide_slab), LOW),
            jax.ShapeDtypeStruct((slot_count, width), LOW),
            jax.ShapeDtypeStruct((parts, 8, wide_slab), WIDE),
        ],
        compiler_params=params(),
        name="attend_back",
        cost_estimate=takes(22),
    )(place, bucket, lengths, counts, hidden, hidden_low, weights, proj, probs, context)


def weight_grads_kernel(blocks, place, *refs):
    normed = refs[:blocks]
    second_low, hidden_low, act, grad_up, head_grads, tokens = [refs[(k + 1) * blocks : (k + 2) * blocks] for k in range(6)]
    vec_ref, out_ref = refs[7 * blocks], refs[7 * blocks + 1]
    turned = refs[7 * blocks + 2]
    step = pl.program_id(0)
    slot_count = second_low[0].shape[0]

    @pl.when(step == 0)
    def _():
        for b in range(blocks):
            span = slice(b * slot_count, (b + 1) * slot_count)
            first = (normed[b][...] * vec_ref[0:1] + vec_ref[3:4]).astype(LOW)
            turned[0, :, span] = tokens[b][0].T
            turned[1, :, span] = first.T
            turned[2, :, span] = second_low[b][...].T
            turned[3, :, span] = hidden_low[b][...].T

    grads = jnp.concatenate([ref[0] for ref in head_grads], axis=0)
    qkv = dot_nn(turned[0], grads)
    outs = dot_nn(turned[3], grads[:, 8 * HEAD_DIM :])
    lane = lax.broadcasted_iota(jnp.int32, (1, 2 * HEAD_DIM), 1)
    last = jnp.where(lane < HEAD_DIM, qkv[:, 10 * HEAD_DIM :], outs[:, 2 * HEAD_DIM :])
    out_ref[0, 0] = jnp.concatenate([qkv[:, : 8 * HEAD_DIM], outs[:, : 2 * HEAD_DIM], last], axis=1).astype(LOW)
    out_ref[1, 0] = dot_nn(turned[1], jnp.concatenate([ref[0] for ref in grad_up], axis=0)).astype(LOW)
    out_ref[2, 0] = dot_nn(turned[2], jnp.concatenate([ref[0] for ref in act], axis=0)).astype(LOW)


def weight_grads(place, inputs, normed, second_low, hidden_low, act, grad_up, head_grads, vectors):
    blocks = len(normed)
    normed_specs = [
        pl.BlockSpec((None,) + array.shape[1:], lambda j, p, index=index: (index, 0, 0)) for array, index in normed
    ]
    normed = [array for array, _ in normed]
    micro_count = inputs.shape[0]
    per_micro = blocks // micro_count
    parts, slot_count, cols = act[0].shape
    width = normed[0].shape[2]
    whole = lambda *shape: pl.BlockSpec(shape, lambda j, p: (0,) * len(shape))
    each = pl.BlockSpec((1, slot_count, cols), lambda j, p: (j, 0, 0))
    token_specs = [
        pl.BlockSpec((1, slot_count, width), lambda j, p, m=b // per_micro, k=b % per_micro: (m, p[0] + k, 0))
        for b in range(blocks)
    ]
    return pl.pallas_call(
        functools.partial(weight_grads_kernel, blocks),
        grid_spec=pltpu.PrefetchScalarGridSpec(
            num_scalar_prefetch=1,
            grid=(parts,),
            in_specs=normed_specs + [whole(slot_count, width)] * (2 * blocks) + [each] * (3 * blocks) + token_specs + [whole(*vectors.shape)],
            out_specs=pl.BlockSpec((3, 1, width, cols), lambda j, p: (0, j, 0, 0)),
            scratch_shapes=[pltpu.VMEM((4, width, blocks * slot_count), LOW)],
        ),
        out_shape=jax.ShapeDtypeStruct((3, parts, width, cols), LOW),
        compiler_params=params(),
        name="weight_grads",
        cost_estimate=takes(26),
    )(place, *normed, *second_low, *hidden_low, *act, *grad_up, *head_grads, *([inputs] * blocks), vectors)


def mesh_place(bits):
    d = lax.axis_index("dp")
    t = lax.axis_index("tensor")
    digits = [(d // (1 << k)) % 2 for k in range(bits)]
    mates = [d + (1 - 2 * digits[k]) * (1 << k) for k in range(bits)]
    return d, t, digits, mates


def digit_index(bits, digits, open_bits):
    return tuple(slice(None) if k in open_bits else digits[k] for k in reversed(range(bits)))


def greet(d, t, mates, parts):
    barrier = pltpu.get_barrier_semaphore()
    for mate in mates:
        pl.semaphore_signal(barrier, inc=1, device_id=(mate, t), device_id_type=MESH)
    for hop in range(1, parts):
        pl.semaphore_signal(barrier, inc=1, device_id=(d, (t + hop) % parts), device_id_type=MESH)
    pl.semaphore_wait(barrier, len(mates) + parts - 1)


def bit_order(bits, flip):
    far = list(range(1, bits))
    return (far[::-1] if flip else far) + [0]


def gather_kernel(parts, bits, own, small, full, small_dp, small_t, z_send, z_recv, h_send, h_recv, s_send, s_recv, keep):
    d, t, digits, mates = mesh_place(bits)
    slab_count = own.shape[0]
    mine = digit_index(bits, digits, ())
    greet(d, t, mates, parts)
    offsets = [0] + [sign * hop for hop in range(1, parts) for sign in (1, -1)]
    pending = []

    def remote(src, dst, send, recv, to):
        return pltpu.make_async_remote_copy(src, dst, send, recv, device_id=to, device_id_type=MESH)

    local = [pltpu.make_async_copy(own.at[s], full.at[(s, t) + mine], keep.at[s]) for s in range(slab_count)]
    local.append(pltpu.make_async_copy(small.at[0], small_dp.at[mine], keep.at[slab_count]))
    local.append(pltpu.make_async_copy(small.at[1], small_t.at[t], keep.at[slab_count + 1]))
    for copy in local:
        copy.start()

    def z_copy(s, at, src, up):
        to = (d, t + 1) if up else (d, t - 1)
        way = 0 if up else 1
        return remote(src, full.at[(s, at) + mine], z_send.at[s, at, way], z_recv.at[s, at], to)

    def h_copy(s, index, step):
        offset = offsets[index]
        order = bit_order(bits, (abs(offset) + s) % 2 == 1)
        blocks = (s, t + offset) + digit_index(bits, digits, order[:step])
        src = own.at[s] if offset == 0 and step == 0 else full.at[blocks]
        return remote(src, full.at[blocks], h_send.at[s, index, step], h_recv.at[s, index, step], (mates[order[step]], t))

    def exists(offset):
        return (t + offset >= 0) & (t + offset < parts)

    def begin(s, index):
        offset = offsets[index]
        if offset == 0:
            h_copy(s, index, 0).start()
            return

        @pl.when(exists(offset))
        def _():
            up = offset < 0
            z_copy(s, t + offset, own.at[s], up).wait_recv()

            @pl.when((t < parts - 1) if up else (t > 0))
            def _():
                z_copy(s, t + offset, full.at[(s, t + offset) + mine], up).start()

            h_copy(s, index, 0).start()

    def advance(s, index, step):
        @pl.when(exists(offsets[index]))
        def _():
            h_copy(s, index, step - 1).wait_recv()
            if step < bits:
                h_copy(s, index, step).start()

    def small_step(step):
        blocks = digit_index(bits, digits, range(step))
        src = small.at[0] if step == 0 else small_dp.at[blocks]
        return remote(src, small_dp.at[blocks], s_send.at[step], s_recv.at[step], (mates[step], t))

    def small_hop(hop):
        peer = (d, (t + hop) % parts)
        return remote(small.at[1], small_t.at[t], s_send.at[bits + hop - 1], s_recv.at[bits + hop - 1], peer)

    for s in range(slab_count):
        @pl.when(t < parts - 1)
        def _():
            z_copy(s, t, own.at[s], True).start()

        @pl.when(t > 0)
        def _():
            z_copy(s, t, own.at[s], False).start()
        if s == 0:
            begin(0, 0)
            for hop in range(1, parts):
                small_hop(hop).start()
            small_step(0).start()
    for copy in local:
        copy.wait()

    groups = [(s, [index for index, offset in enumerate(offsets) if abs(offset) == hop])
              for s in range(slab_count) for hop in range(parts)]
    for wave in range(len(groups) + bits * GATHER_LAG):
        for step in range(bits + 1):
            if 0 <= wave - step * GATHER_LAG < len(groups):
                s, indices = groups[wave - step * GATHER_LAG]
                for index in indices:
                    if step:
                        advance(s, index, step)
                    elif (s, index) != (0, 0):
                        begin(s, index)
        if wave < bits:
            small_step(wave).wait_recv()
            if wave + 1 < bits:
                small_step(wave + 1).start()

    for hop in range(1, parts):
        small_hop(hop).wait()
    for step in range(bits):
        small_step(step).wait_send()
    for s, indices in groups:
        for index in indices:
            offset = offsets[index]

            @pl.when(exists(offset))
            def _():
                for step in range(bits):
                    h_copy(s, index, step).wait_send()
                if offset <= 0:
                    @pl.when(t < parts - 1)
                    def _():
                        z_copy(s, t + offset, own.at[s], True).wait_send()
                if offset >= 0:
                    @pl.when(t > 0)
                    def _():
                        z_copy(s, t + offset, own.at[s], False).wait_send()


def gather_weights(own, small, parts, dp_count):
    bits = dp_count.bit_length() - 1
    slab_count, rows, columns = own.shape
    places = 2 * parts - 1
    low = jnp.bfloat16
    full, small_dp, small_t = pl.pallas_call(
        functools.partial(gather_kernel, parts, bits),
        out_shape=[
            jax.ShapeDtypeStruct((slab_count, parts) + (2,) * bits + (rows, columns), low),
            jax.ShapeDtypeStruct((2,) * bits + small.shape[1:], low),
            jax.ShapeDtypeStruct((parts,) + small.shape[1:], low),
        ],
        in_specs=[pl.BlockSpec(memory_space=pl.ANY)] * 2,
        out_specs=[pl.BlockSpec(memory_space=pl.ANY)] * 3,
        scratch_shapes=[
            pltpu.SemaphoreType.DMA((slab_count, parts, 2)),
            pltpu.SemaphoreType.DMA((slab_count, parts)),
            pltpu.SemaphoreType.DMA((slab_count, places, bits)),
            pltpu.SemaphoreType.DMA((slab_count, places, bits)),
            pltpu.SemaphoreType.DMA((bits + parts - 1,)),
            pltpu.SemaphoreType.DMA((bits + parts - 1,)),
            pltpu.SemaphoreType.DMA((slab_count + 2,)),
        ],
        compiler_params=pltpu.CompilerParams(collective_id=0, has_side_effects=True, vmem_limit_bytes=VMEM_LIMIT),
        name="gather_weights",
        cost_estimate=takes(100),
    )(own, small)
    full = full.reshape(slab_count, parts, dp_count * rows, columns)
    return full, small_dp.reshape((dp_count,) + small.shape[1:]), small_t


def add_rows(target, first, second, rows):
    lead = target.shape[:-2]
    chunk = 16 if rows % 16 == 0 else rows
    steps = rows // chunk
    count = 1
    for extent in lead:
        count *= extent

    def one(i, carry):
        at, rest = [], i // steps
        for extent in reversed(lead):
            at.insert(0, rest % extent)
            rest = rest // extent
        where = tuple(at) + (pl.ds(pl.multiple_of((i % steps) * chunk, chunk), chunk),)
        total = first[where].astype(jnp.float32) + second[where].astype(jnp.float32)
        target[where] = total.astype(target.dtype)
        return carry

    lax.fori_loop(0, count * steps, one, 0)


def reduce_kernel(parts, bits, grads, small, out, small_out, *scratch):
    bufs = scratch[:bits]
    z_up, z_down, small_buf, small_sum = scratch[bits:bits + 4]
    h_send, h_recv, up_send, up_recv, down_send, down_recv, s_send, s_recv = scratch[bits + 4:]
    d, t, digits, mates = mesh_place(bits)
    slab_count = grads.shape[0]
    rows = grads.shape[-2]
    greet(d, t, mates, parts)
    items = [(s, at) for s in range(slab_count) for at in range(parts)]
    small_bits = bits + parts.bit_length() - 1

    def remote(src, dst, send, recv, to):
        return pltpu.make_async_remote_copy(src, dst, send, recv, device_id=to, device_id_type=MESH)

    def order_of(number):
        s, at = items[number]
        return bit_order(bits, (s + at) % 2 == 1)[::-1]

    def held(number, step):
        s, at = items[number]
        return grads.at[s, at] if step == 0 else bufs[step - 1].at[number]

    def part_of(number, step, side):
        order = order_of(number)
        left = [k for k in reversed(range(bits)) if k not in order[:step]]
        pick = tuple(side if k == order[step] else slice(None) for k in left)
        return held(number, step).at[pick]

    def h_copy(number, step):
        order = order_of(number)
        digit = digits[order[step]]
        return remote(part_of(number, step, 1 - digit), bufs[step].at[number],
                      h_send.at[number, step], h_recv.at[number, step], (mates[order[step]], t))

    def fold(number, step):
        h_copy(number, step).wait_recv()
        digit = digits[order_of(number)[step]]
        add_rows(bufs[step].at[number], bufs[step].at[number], part_of(number, step, digit), rows)

    def summed(s, at):
        return bufs[bits - 1].at[s * parts + at]

    def z_copy(s, at, up, src):
        buf, send, recv = (z_up, up_send, up_recv) if up else (z_down, down_send, down_recv)
        to = (d, t + 1) if up else (d, t - 1)
        return remote(src, buf.at[s, at], send.at[s, at], recv.at[s, at], to)

    def z_pass(s, hop, up):
        at = t + hop if up else t - hop
        edge = (t == 0) if up else (t == parts - 1)
        buf = z_up if up else z_down

        @pl.when((at < parts) if up else (at >= 0))
        def _():
            @pl.when(edge)
            def _():
                z_copy(s, at, up, summed(s, at)).start()

            @pl.when(jnp.logical_not(edge))
            def _():
                z_copy(s, at, up, summed(s, at)).wait_recv()
                add_rows(buf.at[s, at], buf.at[s, at], summed(s, at), rows)
                z_copy(s, at, up, buf.at[s, at]).start()

    def z_finish(s):
        add_rows(out.at[s], summed(s, t), summed(s, t), rows)

        def scaled(i, carry):
            out[s] = out[s] * 0.5
            return carry
        lax.fori_loop(0, 1, scaled, 0)
        for up, buf in ((True, z_up), (False, z_down)):
            @pl.when((t > 0) if up else (t < parts - 1))
            def _():
                z_copy(s, t, up, summed(s, t)).wait_recv()
                add_rows(out.at[s], out.at[s], buf.at[s, t], rows)

    def small_copy(step):
        if step < bits:
            to = (mates[step], t)
        else:
            gap = 1 << (step - bits)
            to = (d, t + (1 - 2 * ((t // gap) % 2)) * gap)
        src = small if step == 0 else small_sum.at[step - 1]
        return remote(src, small_buf.at[step], s_send.at[step], s_recv.at[step], to)

    def small_fold(step):
        small_copy(step).wait_recv()
        before = small[...] if step == 0 else small_sum[step - 1]
        small_sum[step] = before + small_buf[step]
        if step + 1 < small_bits:
            small_copy(step + 1).start()

    for number in range(len(items)):
        h_copy(number, 0).start()
        if number == 0:
            small_copy(0).start()
    for wave in range(len(items) + bits * REDUCE_LAG + parts + 1):
        for step in range(bits):
            number = wave - step * REDUCE_LAG
            if 0 <= number < len(items):
                fold(number, step)
                if step + 1 < bits:
                    h_copy(number, step + 1).start()
        for s in range(slab_count):
            phase = wave - ((s + 1) * parts - 1 + bits * REDUCE_LAG)
            if 0 <= phase < parts - 1:
                z_pass(s, parts - 1 - phase, True)
                z_pass(s, parts - 1 - phase, False)
            elif phase == parts - 1:
                z_finish(s)
        if wave < small_bits:
            small_fold(wave)
    small_out[...] = small_sum[small_bits - 1]

    for step in range(small_bits):
        small_copy(step).wait_send()
    for number in range(len(items)):
        for step in range(bits):
            h_copy(number, step).wait_send()
    for s in range(slab_count):
        for hop in range(1, parts):
            @pl.when(t + hop < parts)
            def _():
                z_copy(s, t + hop, True, summed(s, t)).wait_send()

            @pl.when(t - hop >= 0)
            def _():
                z_copy(s, t - hop, False, summed(s, t)).wait_send()


def reduce_grads(grads, small, parts, dp_count):
    bits = dp_count.bit_length() - 1
    slab_count, columns = grads.shape[0], grads.shape[-1]
    rows = grads.shape[2] // dp_count
    grads = grads.reshape((slab_count, parts) + (2,) * bits + (rows, columns))
    low = jnp.bfloat16
    count = slab_count * parts
    small_bits = bits + parts.bit_length() - 1
    dma = pltpu.SemaphoreType.DMA
    return pl.pallas_call(
        functools.partial(reduce_kernel, parts, bits),
        out_shape=[
            jax.ShapeDtypeStruct((slab_count, rows, columns), jnp.float32),
            jax.ShapeDtypeStruct(small.shape, jnp.float32),
        ],
        in_specs=[pl.BlockSpec(memory_space=pltpu.VMEM)] * 2,
        out_specs=[pl.BlockSpec(memory_space=pltpu.VMEM)] * 2,
        scratch_shapes=[pltpu.VMEM((count,) + (2,) * (bits - 1 - step) + (rows, columns), low) for step in range(bits)]
        + [pltpu.VMEM((slab_count, parts, rows, columns), low)] * 2
        + [pltpu.VMEM((small_bits,) + small.shape, jnp.float32)] * 2
        + [dma((count, bits)), dma((count, bits))]
        + [dma((slab_count, parts))] * 4
        + [dma((small_bits,))] * 2,
        compiler_params=pltpu.CompilerParams(collective_id=1, has_side_effects=True, vmem_limit_bytes=VMEM_LIMIT),
        name="reduce_grads",
        cost_estimate=takes(100),
    )(grads, small)


def forward_kernel(parts, bits, micro_count, per_micro, slot_count, own, small, bucket, lengths, counts, inputs, cotangent,
                   weights, vectors, head_rows, ffn_rows, normed_out, inverse_out, proj_out, prob_out, context_out,
                   act_out, slope_out, out_out, second_out, second_low_out, stat_out,
                   full, small_dp, small_t, tokens, cot, total, normed_buf, inverse_buf, proj_buf, prob_buf, context_buf,
                   act_buf, slope_buf, first_low, down_total, out_buf, second_buf, second_low_buf,
                   z_send, z_recv, h_send, h_recv, s_send, s_recv, keep, load, weight_done, unit_done, ffn_done, end_done):
    layout = (bucket, lengths, counts)
    d, t, digits, mates = mesh_place(bits)
    blocks = micro_count * per_micro
    slab_count = own.shape[0]
    width = own.shape[2]
    mine = digit_index(bits, digits, ())

    def block_place(b):
        return b // per_micro, t * per_micro + b % per_micro

    def block_rows(b):
        micro, place = block_place(b)
        return (micro, pl.ds(pl.multiple_of(place * slot_count, slot_count), slot_count))

    loads = [pltpu.make_async_copy(inputs.at[block_rows(b)], tokens.at[b], load.at[b]) for b in range(blocks)]
    loads.append(pltpu.make_async_copy(cotangent.at[block_rows(0)], cot, load.at[blocks]))
    greet(d, t, mates, parts)
    offsets = [0] + [sign * hop for hop in range(1, parts) for sign in (1, -1)]

    def remote(src, dst, send, recv, to):
        return pltpu.make_async_remote_copy(src, dst, send, recv, device_id=to, device_id_type=MESH)

    local = [pltpu.make_async_copy(own.at[s], full.at[(s, t) + mine], keep.at[s]) for s in range(slab_count)]
    local.append(pltpu.make_async_copy(small.at[0], small_dp.at[mine], keep.at[slab_count]))
    local.append(pltpu.make_async_copy(small.at[1], small_t.at[t], keep.at[slab_count + 1]))

    def z_copy(s, at, src, up):
        to = (d, t + 1) if up else (d, t - 1)
        return remote(src, full.at[(s, at) + mine], z_send.at[s, at, 0 if up else 1], z_recv.at[s, at], to)

    def h_copy(s, index, step):
        offset = offsets[index]
        order = bit_order(bits, (abs(offset) + s) % 2 == 1)
        where = (s, t + offset) + digit_index(bits, digits, order[:step])
        src = own.at[s] if offset == 0 and step == 0 else full.at[where]
        return remote(src, full.at[where], h_send.at[s, index, step], h_recv.at[s, index, step], (mates[order[step]], t))

    def exists(offset):
        return (t + offset >= 0) & (t + offset < parts)

    def weight_copy(s, at):
        return pltpu.make_async_copy(full.at[s, at], weights.at[s, at], weight_done.at[s, at])

    def begin(s, index):
        offset = offsets[index]
        if offset == 0:
            h_copy(s, index, 0).start()
            return

        @pl.when(exists(offset))
        def _():
            up = offset < 0
            z_copy(s, t + offset, own.at[s], up).wait_recv()

            @pl.when((t < parts - 1) if up else (t > 0))
            def _():
                z_copy(s, t + offset, full.at[(s, t + offset) + mine], up).start()

            h_copy(s, index, 0).start()

    def advance(s, index, step):
        @pl.when(exists(offsets[index]))
        def _():
            h_copy(s, index, step - 1).wait_recv()
            if step < bits:
                h_copy(s, index, step).start()
            else:
                weight_copy(s, t + offsets[index]).start()

    def small_step(step):
        where = digit_index(bits, digits, range(step))
        src = small.at[0] if step == 0 else small_dp.at[where]
        return remote(src, small_dp.at[where], s_send.at[step], s_recv.at[step], (mates[step], t))

    def small_hop(hop):
        peer = (d, (t + hop) % parts)
        return remote(small.at[1], small_t.at[t], s_send.at[bits + hop - 1], s_recv.at[bits + hop - 1], peer)

    def send_own(s):
        @pl.when(t < parts - 1)
        def _():
            z_copy(s, t, own.at[s], True).start()

        @pl.when(t > 0)
        def _():
            z_copy(s, t, own.at[s], False).start()

    toward = 1 - 2 * ((2 * t) // parts)

    def nearest(k):
        return (t + toward * k + parts) % parts

    def matrix(s, at):
        return full[s, at].reshape(width, full.shape[-1])

    def unit_copies(unit, at, b):
        slot = unit % 2
        heads = pl.ds(at * CHUNK_HEADS, CHUNK_HEADS)
        return [
            pltpu.make_async_copy(proj_buf.at[slot], proj_out.at[b, at], unit_done.at[slot, 0]),
            pltpu.make_async_copy(prob_buf.at[slot], prob_out.at[b, heads], unit_done.at[slot, 1]),
            pltpu.make_async_copy(context_buf.at[slot], context_out.at[b, at], unit_done.at[slot, 2]),
        ]

    def attend_part(b, k):
        unit = b * parts + k
        at = nearest(k)
        if unit >= 2:
            for copy in unit_copies(unit - 2, nearest((unit - 2) % parts), (unit - 2) // parts):
                copy.wait()
        slot = unit % 2
        micro, place = block_place(b)
        attention = attend_unit(layout, micro, place, tokens[b], matrix(0, at), head_rows[at],
                                proj_buf.at[slot], prob_buf.at[slot], context_buf.at[slot])
        if k == 0:
            total[...] = attention
        else:
            total[...] += attention
        for copy in unit_copies(unit, at, b):
            copy.start()
        if k == parts - 1:
            normed, inverse = normalize(tokens[b].astype(WIDE) + total[...] + vectors[2:3])
            normed_buf[b] = normed
            inverse_buf[b] = jnp.broadcast_to(inverse, inverse_buf.shape[1:])
            for copy in norm_copies(b):
                copy.start()

    def norm_copies(b):
        return [pltpu.make_async_copy(normed_buf.at[b], normed_out.at[b], end_done.at[b, 0]),
                pltpu.make_async_copy(inverse_buf.at[b], inverse_out.at[b], end_done.at[b, 1])]

    def ffn_copies(k):
        slot, at = k % 2, nearest(k)
        return [pltpu.make_async_copy(act_buf.at[slot], act_out.at[at], ffn_done.at[slot, 0]),
                pltpu.make_async_copy(slope_buf.at[slot], slope_out.at[at], ffn_done.at[slot, 1])]

    def final_copies():
        return [pltpu.make_async_copy(out_buf, out_out, end_done.at[blocks, 0]),
                pltpu.make_async_copy(second_buf, second_out, end_done.at[blocks, 1]),
                pltpu.make_async_copy(second_low_buf, second_low_out, end_done.at[blocks + 1, 0])]

    def ffn_part(k):
        at = nearest(k)
        if k == 0:
            first_low[...] = (normed_buf[0] * vectors[0:1] + vectors[3:4]).astype(LOW)
        if k >= 2:
            for copy in ffn_copies(k - 2):
                copy.wait()
        slot = k % 2
        down = ffn_unit(first_low[...], matrix(1, at), matrix(2, at), ffn_rows[at], act_buf.at[slot], slope_buf.at[slot])
        for copy in ffn_copies(k):
            copy.start()
        if k == 0:
            down_total[...] = down
        else:
            down_total[...] += down
        if k == parts - 1:
            micro, place = block_place(0)
            out, second, stat = second_norm(layout, micro, place, normed_buf[0], down_total[...], cot[...], vectors)
            out_buf[...] = out
            second_buf[...] = second
            second_low_buf[...] = second.astype(LOW)
            stat_out[...] = stat
            for copy in final_copies():
                copy.start()

    def finish_small():
        lanes = own.shape[1]
        pieces = [small_dp[digit_index(bits, [(i // (1 << k)) % 2 for k in range(bits)], ())][:8, :lanes].astype(WIDE)
                  for i in range(1 << bits)]
        vectors[...] = jnp.concatenate(pieces, axis=1)
        for at in range(parts):
            head_rows[at] = small_t[at, 0:1, :].astype(WIDE)
            ffn_rows[at] = small_t[at, 1:2, :].astype(WIDE)

    send_own(0)
    begin(0, 0)
    for hop in range(1, parts):
        small_hop(hop).start()
    small_step(0).start()
    for copy in local + loads:
        copy.start()
    for s in range(1, slab_count):
        send_own(s)
    for copy in local + loads:
        copy.wait()

    order = [(0, hop) for hop in range(parts)] + [(s, hop) for hop in range(parts) for s in range(1, slab_count)]
    groups = [(s, [index for index, offset in enumerate(offsets) if abs(offset) == hop]) for s, hop in order]
    done_at = {place: number + bits * GATHER_LAG for number, place in enumerate(order)}
    jobs = [(done_at[(0, k)], functools.partial(attend_part, b, k)) for b in range(blocks) for k in range(parts)]
    jobs += [(done_at[(slab_count - 1, k)], functools.partial(ffn_part, k)) for k in range(parts)]
    for wave in range(len(groups) + bits * GATHER_LAG):
        for step in range(bits, -1, -1):
            if 0 <= wave - step * GATHER_LAG < len(groups):
                s, indices = groups[wave - step * GATHER_LAG]
                for index in indices:
                    if step:
                        advance(s, index, step)
                    elif (s, index) != (0, 0):
                        begin(s, index)
        if wave < bits:
            small_step(wave).wait_recv()
            if wave + 1 < bits:
                small_step(wave + 1).start()
            else:
                for hop in range(1, parts):
                    small_hop(hop).wait_recv()
                finish_small()
        if jobs and jobs[0][0] <= wave:
            jobs.pop(0)[1]()
    for _, job in jobs:
        job()

    for hop in range(1, parts):
        small_hop(hop).wait_send()
    for step in range(bits):
        small_step(step).wait_send()
    for s, indices in groups:
        for index in indices:
            offset = offsets[index]

            @pl.when(exists(offset))
            def _():
                for step in range(bits):
                    h_copy(s, index, step).wait_send()
                weight_copy(s, t + offset).wait()
                if offset <= 0:
                    @pl.when(t < parts - 1)
                    def _():
                        z_copy(s, t + offset, own.at[s], True).wait_send()
                if offset >= 0:
                    @pl.when(t > 0)
                    def _():
                        z_copy(s, t + offset, own.at[s], False).wait_send()
    last = blocks * parts
    for unit in range(max(0, last - 2), last):
        for copy in unit_copies(unit, nearest(unit % parts), unit // parts):
            copy.wait()
    for k in range(max(0, parts - 2), parts):
        for copy in ffn_copies(k):
            copy.wait()
    for b in range(blocks):
        for copy in norm_copies(b):
            copy.wait()
    for copy in final_copies():
        copy.wait()


def forward(own, small, layout, inputs, cotangent, parts, dp_count, slot_count, micro_count, per_micro):
    bits = dp_count.bit_length() - 1
    slab_count, rows, cols = own.shape
    width = rows * dp_count
    places = 2 * parts - 1
    blocks = micro_count * per_micro
    heads = parts * CHUNK_HEADS
    spread = (slab_count, parts) + (2,) * bits + (rows, cols)
    shape = jax.ShapeDtypeStruct
    dma = pltpu.SemaphoreType.DMA
    hbm, vmem, smem = [pl.BlockSpec(memory_space=space) for space in (pl.ANY, pltpu.VMEM, pltpu.SMEM)]
    slab = (slot_count, cols)
    rows_of = (slot_count, width)
    outs = [
        (spread, LOW, hbm),
        ((8, width), WIDE, vmem),
        ((parts, 1, cols), WIDE, vmem),
        ((parts, 1, cols), WIDE, vmem),
        ((blocks,) + rows_of, WIDE, hbm),
        ((blocks, slot_count, 128), WIDE, hbm),
        ((blocks, parts) + slab, LOW, hbm),
        ((blocks, heads, slot_count, slot_count), LOW, hbm),
        ((blocks, parts, slot_count, 4 * HEAD_DIM), LOW, hbm),
        ((parts,) + slab, LOW, hbm),
        ((parts,) + slab, LOW, hbm),
        (rows_of, LOW, hbm),
        (rows_of, WIDE, hbm),
        (rows_of, LOW, hbm),
        ((8, width), WIDE, vmem),
    ]
    result = pl.pallas_call(
        functools.partial(forward_kernel, parts, bits, micro_count, per_micro, slot_count),
        out_shape=[shape(dims, kind) for dims, kind, _ in outs],
        in_specs=[hbm, hbm, smem, smem, smem, hbm, hbm],
        out_specs=[space for _, _, space in outs],
        scratch_shapes=[
            pltpu.VMEM(spread, LOW),
            pltpu.VMEM((2,) * bits + small.shape[1:], LOW),
            pltpu.VMEM((parts,) + small.shape[1:], LOW),
            pltpu.VMEM((blocks,) + rows_of, LOW),
            pltpu.VMEM(rows_of, LOW),
            pltpu.VMEM(rows_of, WIDE),
            pltpu.VMEM((blocks,) + rows_of, WIDE),
            pltpu.VMEM((blocks, slot_count, 128), WIDE),
            pltpu.VMEM((2,) + slab, LOW),
            pltpu.VMEM((2, CHUNK_HEADS, slot_count, slot_count), LOW),
            pltpu.VMEM((2, slot_count, 4 * HEAD_DIM), LOW),
            pltpu.VMEM((2,) + slab, LOW),
            pltpu.VMEM((2,) + slab, LOW),
            pltpu.VMEM(rows_of, LOW),
            pltpu.VMEM(rows_of, WIDE),
            pltpu.VMEM(rows_of, LOW),
            pltpu.VMEM(rows_of, WIDE),
            pltpu.VMEM(rows_of, LOW),
            dma((slab_count, parts, 2)),
            dma((slab_count, parts)),
            dma((slab_count, places, bits)),
            dma((slab_count, places, bits)),
            dma((bits + parts - 1,)),
            dma((bits + parts - 1,)),
            dma((slab_count + 2,)),
            dma((blocks + 1,)),
            dma((slab_count, parts)),
            dma((2, 3)),
            dma((2, 2)),
            dma((blocks + 2, 2)),
        ],
        compiler_params=pltpu.CompilerParams(collective_id=2, has_side_effects=True, vmem_limit_bytes=VMEM_LIMIT),
        name="forward",
    )(own, small, *layout, inputs, cotangent)
    return (result[0].reshape(slab_count, parts, width, cols),) + tuple(result[1:])


def slab_order(query, key, value, out):
    columns = lambda group, head: group[..., head * HEAD_DIM : (head + 1) * HEAD_DIM]
    order = [(query, 0), (key, 0), (query, 1), (key, 1), (query, 2), (key, 2),
             (value, 0), (value, 1), (out, 0), (out, 1), (value, 2), (out, 2)]
    return jnp.concatenate([columns(group, head) for group, head in order], axis=-1)


def slab_parts(slab):
    columns = lambda at: slab[..., at * HEAD_DIM : (at + 1) * HEAD_DIM]
    groups = ((0, 2, 4), (1, 3, 5), VALUE_AT, OUT_AT)
    return [jnp.concatenate([columns(at) for at in group], axis=-1) for group in groups]


def add_all(terms):
    total = terms[0]
    for term in terms[1:]:
        total = total + term
    return total


def after(values, *earlier):
    return lax.optimization_barrier((tuple(values), earlier))[0]


def body(
    inputs,
    cotangent,
    bucket,
    lengths,
    counts,
    w_qkv,
    w_out,
    w_in,
    w_down,
    head_bias,
    ffn_bias,
    norm_gains,
    row_biases,
):
    micro_count, _, width = inputs.shape
    blocks_all = bucket.shape[1]
    slot_count = inputs.shape[1] // blocks_all
    parts, dp_count = lax.axis_size("tensor"), lax.axis_size("dp")
    rank, dp_rank = lax.axis_index("tensor"), lax.axis_index("dp")
    per_micro = blocks_all // parts
    cols = w_in.shape[1]
    rows = w_in.shape[0]

    own = jnp.stack([slab_order(w_qkv[0], w_qkv[1], w_qkv[2], w_out.T), w_in, w_down.T])
    norm_rows = jnp.concatenate([norm_gains, row_biases], axis=0)
    vector_count = norm_rows.shape[0]
    no_bias = jnp.zeros_like(head_bias[:1])
    bias_rows = jnp.concatenate([slab_order(head_bias[:1], no_bias, head_bias[1:], no_bias), ffn_bias[None]], axis=0)
    small = jnp.stack([
        jnp.pad(norm_rows, ((0, 16 - vector_count), (0, cols - rows))),
        jnp.pad(bias_rows, ((0, 14), (0, 0))),
    ])
    blocks = [(m, k) for m in range(micro_count) for k in range(per_micro)]
    places = [jnp.full((1,), rank * per_micro + k, jnp.int32) for k in range(per_micro)]
    layout = (bucket, lengths, counts)
    kept = []
    if rows % 16 == 0:
        (weights, vectors, head_rows, ffn_rows, normed, inverse, proj, probs, context, *first_ffn) = forward(
            own, small, layout, inputs, cotangent, parts, dp_count, slot_count, micro_count, per_micro
        )
        attended = [tuple((array, b) for array in (normed, inverse, proj, probs, context)) for b in range(len(blocks))]
        ffns = [first_ffn]
    else:
        weights, small_dp, small_t = gather_weights(own, small, parts, dp_count)
        vectors = small_dp[:, :8, :rows].transpose(1, 0, 2).reshape(8, width).astype(jnp.float32)
        head_rows = small_t[:, 0:1].astype(jnp.float32)
        ffn_rows = small_t[:, 1:2].astype(jnp.float32)
        attended = []
        for m, k in blocks:
            parts_of = attend(m, places[k], *layout, inputs, weights, head_rows, vectors, slot_count)
            attended.append(tuple((array[None], 0) for array in parts_of))
        ffns = []
    for m, k in blocks[len(ffns) :]:
        normed = attended[m * per_micro + k][0]
        ffns.append(ffn(m, places[k], *layout, normed, cotangent, weights, ffn_rows, vectors))
    outs = []
    for (normed, inverse, proj, probs, context), (act, slope, out, second, second_low, stat) in zip(attended, ffns):
        kept.append((normed, inverse, proj, probs, context, act, slope, second, second_low, stat))
        outs.append(out)
    results = [
        lax.all_gather(jnp.concatenate(outs[m * per_micro : (m + 1) * per_micro], axis=0), "tensor", axis=0, tiled=True)
        for m in range(micro_count)
    ]
    token_grads, saved = [], []
    kept[0] = kept[0][:7] + after(kept[0][7:], outs[-1])
    for (m, k), (normed, inverse, proj, probs, context, act, slope, second, second_low, stat) in zip(blocks, kept):
        grad_up, hidden, hidden_low, up_stat, first_stat = ffn_back(second, second_low, slope, weights, normed, inverse, vectors)
        if (m, k) == blocks[-1]:
            hidden, hidden_low = after((hidden, hidden_low), results[0])
        head_grads, token_grad, head_stat = attend_back(
            m, places[k], *layout, hidden, hidden_low, weights, proj, probs, context
        )
        token_grads.append(token_grad)
        saved.append((normed, second_low, hidden_low, act, grad_up, head_grads, stat, first_stat, up_stat, head_stat))
    input_grads = [
        lax.all_gather(jnp.concatenate(token_grads[m * per_micro : (m + 1) * per_micro], axis=0), "tensor", axis=0, tiled=True)
        for m in range(micro_count)
    ]
    columns = list(zip(*saved))
    grads = weight_grads(places[0], inputs, *columns[:6], vectors)
    grads = after((grads,), results[1])[0]
    stat, first_stat, up_stat, head_stat = [add_all(column) for column in columns[6:]]
    small_grads = jnp.concatenate(
        [
            jnp.stack([first_stat[0], stat[0], first_stat[2], first_stat[1], stat[2], stat[1]]),
            up_stat[:, 0],
            head_stat[:, 0],
        ],
        axis=0,
    )
    small_grads = jnp.pad(small_grads, ((0, -small_grads.shape[0] % 8), (0, 0)))
    shard, sums = reduce_grads(grads, small_grads, parts, dp_count)
    grad_query, grad_key, grad_value, grad_out = slab_parts(shard[0])
    vector_sums = lax.dynamic_slice_in_dim(sums[:vector_count], dp_rank * rows, rows, 1)
    ffn_sum = lax.dynamic_slice_in_dim(sums, vector_count + rank, 1, 0)[0]
    head_sum = slab_parts(lax.dynamic_slice_in_dim(sums, vector_count + parts + rank, 1, 0))
    return (
        jnp.stack(results),
        jnp.stack(input_grads),
        jnp.stack([grad_query, grad_key, grad_value]),
        grad_out.T,
        shard[1],
        shard[2].T,
        jnp.concatenate([head_sum[0], head_sum[2]], axis=0),
        ffn_sum,
        vector_sums[:2],
        vector_sums[2:],
    )


def solution(mesh):
    in_specs = (
        P(None, "dp", None),
        P(None, "dp", None),
        P(None, "dp"),
        P(None, "dp", None),
        P(None, "dp"),
        P(None, "dp", "tensor"),
        P("tensor", "dp"),
        P("dp", "tensor"),
        P("tensor", "dp"),
        P(None, "tensor"),
        P("tensor"),
        P(None, "dp"),
        P(None, "dp"),
    )
    out_specs = (
        P(None, "dp", None),
        P(None, "dp", None),
        P(None, "dp", "tensor"),
        P("tensor", "dp"),
        P("dp", "tensor"),
        P("tensor", "dp"),
        P(None, "tensor"),
        P("tensor"),
        P(None, "dp"),
        P(None, "dp"),
    )
    return jax.shard_map(body, mesh=mesh, in_specs=in_specs, out_specs=out_specs, check_vma=False)
```

```python
import functools

import jax
import jax.numpy as jnp
from jax import lax
from jax.experimental import pallas as pl
from jax.experimental.pallas import tpu as pltpu
from jax.sharding import PartitionSpec as P

HEAD_DIM = 64
EPSILON = 1e-12
VMEM_LIMIT = 60 * 1024 * 1024
MESH = pl.DeviceIdType.MESH
GATHER_LAG = 2
Z_WAVES = (2, 3)
LINE_PACE = 1
LINE_CHUNKS = 4
REDUCE_LAG = 2
def takes(microseconds):
    return pl.CostEstimate(flops=int(microseconds * 1.15e8), bytes_accessed=0, transcendentals=0)


LOW = jnp.bfloat16
WIDE = jnp.float32
CHUNK_HEADS = 3
VALUE_AT = (6, 7, 10)
OUT_AT = (8, 9, 11)


def slab_order(query, key, value, out):
    columns = lambda group, head: group[..., head * HEAD_DIM : (head + 1) * HEAD_DIM]
    order = [(query, 0), (key, 0), (query, 1), (key, 1), (query, 2), (key, 2),
             (value, 0), (value, 1), (out, 0), (out, 1), (value, 2), (out, 2)]
    return jnp.concatenate([columns(group, head) for group, head in order], axis=-1)


def slab_parts(slab):
    columns = lambda at: slab[..., at * HEAD_DIM : (at + 1) * HEAD_DIM]
    groups = ((0, 2, 4), (1, 3, 5), VALUE_AT, OUT_AT)
    return [jnp.concatenate([columns(at) for at in group], axis=-1) for group in groups]


def dot_nn(left, right):
    return lax.dot_general(left, right, (((1,), (0,)), ((), ())), preferred_element_type=WIDE)


def dot_nt(left, right):
    return lax.dot_general(left, right, (((1,), (1,)), ((), ())), preferred_element_type=WIDE)


def dot_tn(left, right):
    return lax.dot_general(left, right, (((0,), (0,)), ((), ())), preferred_element_type=WIDE)


def piece(tile, at):
    return tile[:, at * HEAD_DIM : (at + 1) * HEAD_DIM]


def slot_codes(layout, micro, block, slot_count, shape, axis):
    bucket, lengths, counts = layout
    position = lax.broadcasted_iota(jnp.int32, shape, axis)
    quarter = slot_count // 4
    whole = bucket[micro, block] == 1
    item = jnp.where(whole, 0, position // quarter)
    place = position - item * quarter
    length = jnp.where(
        item == 0,
        lengths[micro, block, 0],
        jnp.where(
            item == 1,
            lengths[micro, block, 1],
            jnp.where(item == 2, lengths[micro, block, 2], lengths[micro, block, 3]),
        ),
    )
    return item, (item < counts[micro, block]) & (place < length)


def normalize(hidden):
    center = hidden - jnp.mean(hidden, axis=-1, keepdims=True)
    inverse = lax.rsqrt(jnp.mean(center * center, axis=-1, keepdims=True) + EPSILON)
    return center * inverse, inverse


def norm_pullback(grad_rows, normed, inverse, gain_row):
    grad_normed = grad_rows * gain_row
    return inverse * (
        grad_normed
        - jnp.mean(grad_normed, axis=-1, keepdims=True)
        - normed * jnp.mean(grad_normed * normed, axis=-1, keepdims=True)
    )


def row_sum(values):
    return jnp.sum(values, axis=0, keepdims=True)


def attend_unit(layout, micro, place, tokens, weights, bias_row, proj_ref, prob_ref, context_ref):
    slot_count = tokens.shape[0]
    proj = (dot_nn(tokens, weights) + bias_row).astype(LOW)
    proj_ref[...] = proj
    row_item, _ = slot_codes(layout, micro, place, slot_count, (slot_count, 1), 0)
    key_item, key_live = slot_codes(layout, micro, place, slot_count, (1, slot_count), 1)
    key_code = jnp.where(key_live, key_item, -1)
    outs = []
    for head in range(CHUNK_HEADS):
        query = piece(proj, 2 * head) * jnp.asarray(HEAD_DIM ** (-0.5), LOW)
        scores = dot_nt(query, piece(proj, 2 * head + 1))
        scores = jnp.where(row_item == key_code, scores, -10000.0)
        grown = jnp.exp(scores - jnp.max(scores, axis=-1, keepdims=True))
        probs = (grown * (1.0 / jnp.sum(grown, axis=-1, keepdims=True))).astype(LOW)
        prob_ref[head] = probs
        outs.append(dot_nn(probs, piece(proj, VALUE_AT[head])).astype(LOW))
    context = jnp.concatenate([outs[0], outs[1], jnp.zeros_like(outs[0]), outs[2]], axis=1)
    context_ref[...] = context
    return dot_nt(context, weights[:, 8 * HEAD_DIM :])


def ffn_unit(first_low, w_in, w_down, bias_row, act_ref, slope_ref):
    upward = dot_nn(first_low, w_in) + bias_row
    share = 0.5 + 0.5 * lax.erf(upward * (0.5**0.5))
    activated = (upward * share).astype(LOW)
    act_ref[...] = activated
    bell = jnp.exp(-0.5 * upward * upward) * 0.3989422804014327
    slope_ref[...] = (share + upward * bell).astype(LOW)
    return dot_nt(activated, w_down)


def second_norm(layout, micro, place, first_normed, down_total, cot_rows, vectors):
    slot_count = first_normed.shape[0]
    _, live = slot_codes(layout, micro, place, slot_count, (slot_count, 1), 0)
    first = first_normed * vectors[0:1] + vectors[3:4]
    normed, inverse = normalize(first + down_total + vectors[4:5])
    out = (normed * vectors[1:2] + vectors[5:6]).astype(LOW)
    grad_out = jnp.where(live, cot_rows.astype(WIDE), 0.0)
    second = norm_pullback(grad_out, normed, inverse, vectors[1:2])
    stat = jnp.concatenate(
        [row_sum(grad_out * normed), row_sum(grad_out), row_sum(second), jnp.zeros((5, second.shape[1]), WIDE)], axis=0
    )
    return out, second, stat


def attend_kernel(micro, place, bucket, lengths, counts, x_ref, w_ref, bias_ref, vec_ref,
                  normed_ref, inverse_ref, proj_ref, prob_ref, context_ref, total):
    step = pl.program_id(0)
    layout = (bucket, lengths, counts)
    tokens = x_ref[0]
    attention = attend_unit(layout, micro, place[0], tokens, w_ref[0, 0], bias_ref[0],
                            proj_ref.at[0], prob_ref, context_ref.at[0])

    @pl.when(step == 0)
    def _():
        total[...] = attention

    @pl.when(step > 0)
    def _():
        total[...] += attention

    @pl.when(step == pl.num_programs(0) - 1)
    def _():
        normed, inverse = normalize(tokens.astype(WIDE) + total[...] + vec_ref[2:3])
        normed_ref[...] = normed
        inverse_ref[...] = jnp.broadcast_to(inverse, inverse_ref.shape)


def ffn_kernel(micro, place, bucket, lengths, counts, normed_ref, cot_ref, w_in_ref, w_down_ref, bias_ref, vec_ref,
               act_ref, slope_ref, out_ref, second_ref, second_low_ref, stat_ref, first_low, total):
    step = pl.program_id(0)

    @pl.when(step == 0)
    def _():
        first_low[...] = (normed_ref[...] * vec_ref[0:1] + vec_ref[3:4]).astype(LOW)

    down = ffn_unit(first_low[...], w_in_ref[0, 0], w_down_ref[0, 0], bias_ref[0], act_ref.at[0], slope_ref.at[0])

    @pl.when(step == 0)
    def _():
        total[...] = down

    @pl.when(step > 0)
    def _():
        total[...] += down

    @pl.when(step == pl.num_programs(0) - 1)
    def _():
        out, second, stat = second_norm(
            (bucket, lengths, counts), micro, place[0], normed_ref[...], total[...], cot_ref[0], vec_ref
        )
        out_ref[...] = out
        second_ref[...] = second
        second_low_ref[...] = second.astype(LOW)
        stat_ref[...] = stat


def ffn_back_kernel(second_ref, second_low_ref, slope_ref, w_in_ref, w_down_ref, normed_ref, inverse_ref, vec_ref,
                    up_ref, hidden_ref, hidden_low_ref, up_stat_ref, stat_ref, total):
    step = pl.program_id(0)
    grad_act = dot_nn(second_low_ref[...], w_down_ref[0, 0])
    grad_up = (grad_act * slope_ref[0].astype(WIDE)).astype(LOW)
    up_ref[0] = grad_up
    up_stat_ref[0] = jnp.broadcast_to(row_sum(grad_up.astype(WIDE)), up_stat_ref.shape[1:])
    back = dot_nt(grad_up, w_in_ref[0, 0])

    @pl.when(step == 0)
    def _():
        total[...] = back + second_ref[...]

    @pl.when(step > 0)
    def _():
        total[...] += back

    @pl.when(step == pl.num_programs(0) - 1)
    def _():
        grad_first = total[...]
        normed = normed_ref[...]
        hidden = norm_pullback(grad_first, normed, inverse_ref[:, :1], vec_ref[0:1])
        hidden_ref[...] = hidden
        hidden_low_ref[...] = hidden.astype(LOW)
        stat_ref[...] = jnp.concatenate(
            [row_sum(grad_first * normed), row_sum(grad_first), row_sum(hidden), jnp.zeros((5, hidden.shape[1]), WIDE)],
            axis=0,
        )


def attend_back_kernel(micro, place, bucket, lengths, counts, hidden_ref, hidden_low_ref, w_ref, proj_ref, prob_ref,
                       context_ref, grad_ref, out_ref, stat_ref, total):
    step = pl.program_id(0)
    slot_count = hidden_ref.shape[0]
    layout = (bucket, lengths, counts)
    row_item, _ = slot_codes(layout, micro, place[0], slot_count, (slot_count, 1), 0)
    key_item, key_live = slot_codes(layout, micro, place[0], slot_count, (1, slot_count), 1)
    key_code = jnp.where(key_live, key_item, -1)
    proj = proj_ref[0]
    grad_context = dot_nn(hidden_low_ref[...], w_ref[0, 0, :, 8 * HEAD_DIM :]).astype(LOW)
    scale = HEAD_DIM ** (-0.5)
    grads = [None] * 12
    for head in range(CHUNK_HEADS):
        query, key = piece(proj, 2 * head), piece(proj, 2 * head + 1)
        probs = prob_ref[head]
        grad_head = piece(grad_context, OUT_AT[head] - 8)
        grads[VALUE_AT[head]] = dot_tn(probs, grad_head).astype(LOW)
        grad_probs = dot_nt(grad_head, piece(proj, VALUE_AT[head]))
        wide = probs.astype(WIDE)
        inner = jnp.sum(wide * grad_probs, axis=-1, keepdims=True)
        grad_scores = jnp.where(row_item == key_code, wide * (grad_probs - inner), 0.0).astype(LOW)
        grads[2 * head] = (dot_nn(grad_scores, key) * scale).astype(LOW)
        grads[2 * head + 1] = (dot_tn(grad_scores, query) * scale).astype(LOW)
    context = context_ref[0]
    zero = jnp.zeros_like(grads[0])
    for at in OUT_AT:
        grads[at] = zero
    slab = jnp.concatenate(grads, axis=1)
    back = dot_nt(slab, w_ref[0, 0])
    for at in OUT_AT:
        grads[at] = piece(context, at - 8)
    grad_ref[0] = jnp.concatenate(grads, axis=1)
    stat_ref[0] = jnp.broadcast_to(row_sum(slab.astype(WIDE)), stat_ref.shape[1:])

    @pl.when(step == 0)
    def _():
        total[...] = back + hidden_ref[...]

    @pl.when(step > 0)
    def _():
        total[...] += back

    @pl.when(step == pl.num_programs(0) - 1)
    def _():
        out_ref[...] = total[...].astype(LOW)


def in_vmem(shape, index_map):
    return pl.BlockSpec(shape, index_map)


def params(vmem=VMEM_LIMIT):
    return pltpu.CompilerParams(dimension_semantics=("arbitrary",), vmem_limit_bytes=vmem)


def attend(micro, place, bucket, lengths, counts, inputs, weights, bias, vectors, slot_count):
    parts, width = weights.shape[1], weights.shape[2]
    wide_slab = weights.shape[3]
    heads = parts * CHUNK_HEADS
    whole = lambda *shape: pl.BlockSpec(shape, lambda j, p, b, l, c: (0,) * len(shape))
    return pl.pallas_call(
        functools.partial(attend_kernel, micro),
        grid_spec=pltpu.PrefetchScalarGridSpec(
            num_scalar_prefetch=4,
            grid=(parts,),
            in_specs=[
                pl.BlockSpec((1, slot_count, width), lambda j, p, b, l, c: (micro, p[0], 0)),
                pl.BlockSpec((1, 1, width, wide_slab), lambda j, p, b, l, c: (0, j, 0, 0)),
                pl.BlockSpec((1, 1, wide_slab), lambda j, p, b, l, c: (j, 0, 0)),
                whole(*vectors.shape),
            ],
            out_specs=[
                whole(slot_count, width),
                whole(slot_count, 128),
                pl.BlockSpec((1, slot_count, wide_slab), lambda j, p, b, l, c: (j, 0, 0)),
                pl.BlockSpec((CHUNK_HEADS, slot_count, slot_count), lambda j, p, b, l, c: (j, 0, 0)),
                pl.BlockSpec((1, slot_count, 4 * HEAD_DIM), lambda j, p, b, l, c: (j, 0, 0)),
            ],
            scratch_shapes=[pltpu.VMEM((slot_count, width), WIDE)],
        ),
        out_shape=[
            jax.ShapeDtypeStruct((slot_count, width), WIDE),
            jax.ShapeDtypeStruct((slot_count, 128), WIDE),
            jax.ShapeDtypeStruct((parts, slot_count, wide_slab), LOW),
            jax.ShapeDtypeStruct((heads, slot_count, slot_count), LOW),
            jax.ShapeDtypeStruct((parts, slot_count, 4 * HEAD_DIM), LOW),
        ],
        compiler_params=params(),
        name="attend",
        cost_estimate=takes(16),
    )(place, bucket, lengths, counts, inputs, weights, bias, vectors)


def ffn(micro, place, bucket, lengths, counts, normed, cotangent, weights, bias, vectors):
    parts, width, cols = weights.shape[1:]
    normed, index = normed
    slot_count = normed.shape[1]
    whole = lambda *shape: pl.BlockSpec(shape, lambda j, p, b, l, c: (0,) * len(shape))
    each = pl.BlockSpec((1, slot_count, cols), lambda j, p, b, l, c: (j, 0, 0))
    return pl.pallas_call(
        functools.partial(ffn_kernel, micro),
        grid_spec=pltpu.PrefetchScalarGridSpec(
            num_scalar_prefetch=4,
            grid=(parts,),
            in_specs=[
                pl.BlockSpec((None, slot_count, width), lambda j, p, b, l, c: (index, 0, 0)),
                pl.BlockSpec((1, slot_count, width), lambda j, p, b, l, c: (micro, p[0], 0)),
                pl.BlockSpec((1, 1, width, cols), lambda j, p, b, l, c: (1, j, 0, 0)),
                pl.BlockSpec((1, 1, width, cols), lambda j, p, b, l, c: (2, j, 0, 0)),
                pl.BlockSpec((1, 1, cols), lambda j, p, b, l, c: (j, 0, 0)),
                whole(*vectors.shape),
            ],
            out_specs=[each, each, whole(slot_count, width), whole(slot_count, width), whole(slot_count, width), whole(8, width)],
            scratch_shapes=[pltpu.VMEM((slot_count, width), LOW), pltpu.VMEM((slot_count, width), WIDE)],
        ),
        out_shape=[
            jax.ShapeDtypeStruct((parts, slot_count, cols), LOW),
            jax.ShapeDtypeStruct((parts, slot_count, cols), LOW),
            jax.ShapeDtypeStruct((slot_count, width), LOW),
            jax.ShapeDtypeStruct((slot_count, width), WIDE),
            jax.ShapeDtypeStruct((slot_count, width), LOW),
            jax.ShapeDtypeStruct((8, width), WIDE),
        ],
        compiler_params=params(),
        name="ffn",
        cost_estimate=takes(16),
    )(place, bucket, lengths, counts, normed, cotangent, weights, weights, bias, vectors)


def ffn_back(second, second_low, slope, weights, normed, inverse, vectors):
    parts, width, cols = weights.shape[1:]
    (normed, index), (inverse, _) = normed, inverse
    slot_count = normed.shape[1]
    whole = lambda *shape: pl.BlockSpec(shape, lambda j: (0,) * len(shape))
    each = pl.BlockSpec((1, slot_count, cols), lambda j: (j, 0, 0))
    return pl.pallas_call(
        ffn_back_kernel,
        grid=(parts,),
        in_specs=[
            whole(slot_count, width),
            whole(slot_count, width),
            each,
            pl.BlockSpec((1, 1, width, cols), lambda j: (1, j, 0, 0)),
            pl.BlockSpec((1, 1, width, cols), lambda j: (2, j, 0, 0)),
            pl.BlockSpec((None, slot_count, width), lambda j: (index, 0, 0)),
            pl.BlockSpec((None, slot_count, 128), lambda j: (index, 0, 0)),
            whole(*vectors.shape),
        ],
        out_specs=[each, whole(slot_count, width), whole(slot_count, width),
                   pl.BlockSpec((1, 8, cols), lambda j: (j, 0, 0)), whole(8, width)],
        scratch_shapes=[pltpu.VMEM((slot_count, width), WIDE)],
        out_shape=[
            jax.ShapeDtypeStruct((parts, slot_count, cols), LOW),
            jax.ShapeDtypeStruct((slot_count, width), WIDE),
            jax.ShapeDtypeStruct((slot_count, width), LOW),
            jax.ShapeDtypeStruct((parts, 8, cols), WIDE),
            jax.ShapeDtypeStruct((8, width), WIDE),
        ],
        compiler_params=params(),
        name="ffn_back",
        cost_estimate=takes(14),
    )(second, second_low, slope, weights, weights, normed, inverse, vectors)


def attend_back(micro, place, bucket, lengths, counts, hidden, hidden_low, weights, proj, probs, context):
    parts, width = weights.shape[1], weights.shape[2]
    wide_slab = weights.shape[3]
    slot_count = hidden.shape[0]
    (proj, index), (probs, _), (context, _) = proj, probs, context
    whole = lambda *shape: pl.BlockSpec(shape, lambda j, p, b, l, c: (0,) * len(shape))
    each = pl.BlockSpec((1, slot_count, wide_slab), lambda j, p, b, l, c: (j, 0, 0))
    return pl.pallas_call(
        functools.partial(attend_back_kernel, micro),
        grid_spec=pltpu.PrefetchScalarGridSpec(
            num_scalar_prefetch=4,
            grid=(parts,),
            in_specs=[
                whole(slot_count, width),
                whole(slot_count, width),
                pl.BlockSpec((1, 1, width, wide_slab), lambda j, p, b, l, c: (0, j, 0, 0)),
                pl.BlockSpec((None, 1, slot_count, wide_slab), lambda j, p, b, l, c: (index, j, 0, 0)),
                pl.BlockSpec((None, CHUNK_HEADS, slot_count, slot_count), lambda j, p, b, l, c: (index, j, 0, 0)),
                pl.BlockSpec((None, 1, slot_count, 4 * HEAD_DIM), lambda j, p, b, l, c: (index, j, 0, 0)),
            ],
            out_specs=[each, whole(slot_count, width), pl.BlockSpec((1, 8, wide_slab), lambda j, p, b, l, c: (j, 0, 0))],
            scratch_shapes=[pltpu.VMEM((slot_count, width), WIDE)],
        ),
        out_shape=[
            jax.ShapeDtypeStruct((parts, slot_count, wide_slab), LOW),
            jax.ShapeDtypeStruct((slot_count, width), LOW),
            jax.ShapeDtypeStruct((parts, 8, wide_slab), WIDE),
        ],
        compiler_params=params(),
        name="attend_back",
        cost_estimate=takes(22),
    )(place, bucket, lengths, counts, hidden, hidden_low, weights, proj, probs, context)


def weight_grads_kernel(blocks, place, *refs):
    normed = refs[:blocks]
    second_low, hidden_low, act, grad_up, head_grads, tokens = [refs[(k + 1) * blocks : (k + 2) * blocks] for k in range(6)]
    vec_ref, out_ref = refs[7 * blocks], refs[7 * blocks + 1]
    turned = refs[7 * blocks + 2]
    step = pl.program_id(0)
    slot_count = second_low[0].shape[0]

    @pl.when(step == 0)
    def _():
        for b in range(blocks):
            span = slice(b * slot_count, (b + 1) * slot_count)
            first = (normed[b][...] * vec_ref[0:1] + vec_ref[3:4]).astype(LOW)
            turned[0, :, span] = tokens[b][0].T
            turned[1, :, span] = first.T
            turned[2, :, span] = second_low[b][...].T
            turned[3, :, span] = hidden_low[b][...].T

    grads = jnp.concatenate([ref[0] for ref in head_grads], axis=0)
    qkv = dot_nn(turned[0], grads)
    outs = dot_nn(turned[3], grads[:, 8 * HEAD_DIM :])
    lane = lax.broadcasted_iota(jnp.int32, (1, 2 * HEAD_DIM), 1)
    last = jnp.where(lane < HEAD_DIM, qkv[:, 10 * HEAD_DIM :], outs[:, 2 * HEAD_DIM :])
    out_ref[0, 0] = jnp.concatenate([qkv[:, : 8 * HEAD_DIM], outs[:, : 2 * HEAD_DIM], last], axis=1).astype(LOW)
    out_ref[1, 0] = dot_nn(turned[1], jnp.concatenate([ref[0] for ref in grad_up], axis=0)).astype(LOW)
    out_ref[2, 0] = dot_nn(turned[2], jnp.concatenate([ref[0] for ref in act], axis=0)).astype(LOW)


def weight_grads(place, inputs, normed, second_low, hidden_low, act, grad_up, head_grads, vectors):
    blocks = len(normed)
    normed_specs = [
        pl.BlockSpec((None,) + array.shape[1:], lambda j, p, index=index: (index, 0, 0)) for array, index in normed
    ]
    normed = [array for array, _ in normed]
    micro_count = inputs.shape[0]
    per_micro = blocks // micro_count
    parts, slot_count, cols = act[0].shape
    width = normed[0].shape[2]
    whole = lambda *shape: pl.BlockSpec(shape, lambda j, p: (0,) * len(shape))
    each = pl.BlockSpec((1, slot_count, cols), lambda j, p: (j, 0, 0))
    token_specs = [
        pl.BlockSpec((1, slot_count, width), lambda j, p, m=b // per_micro, k=b % per_micro: (m, p[0] + k, 0))
        for b in range(blocks)
    ]
    return pl.pallas_call(
        functools.partial(weight_grads_kernel, blocks),
        grid_spec=pltpu.PrefetchScalarGridSpec(
            num_scalar_prefetch=1,
            grid=(parts,),
            in_specs=normed_specs + [whole(slot_count, width)] * (2 * blocks) + [each] * (3 * blocks) + token_specs + [whole(*vectors.shape)],
            out_specs=pl.BlockSpec((3, 1, width, cols), lambda j, p: (0, j, 0, 0)),
            scratch_shapes=[pltpu.VMEM((4, width, blocks * slot_count), LOW)],
        ),
        out_shape=jax.ShapeDtypeStruct((3, parts, width, cols), LOW),
        compiler_params=params(),
        name="weight_grads",
        cost_estimate=takes(26),
    )(place, *normed, *second_low, *hidden_low, *act, *grad_up, *head_grads, *([inputs] * blocks), vectors)


def mesh_place(bits):
    d = lax.axis_index("dp")
    t = lax.axis_index("tensor")
    digits = [(d // (1 << k)) % 2 for k in range(bits)]
    mates = [d + (1 - 2 * digits[k]) * (1 << k) for k in range(bits)]
    return d, t, digits, mates


def digit_index(bits, digits, open_bits):
    return tuple(slice(None) if k in open_bits else digits[k] for k in reversed(range(bits)))


def greet(d, t, mates, parts):
    barrier = pltpu.get_barrier_semaphore()
    for mate in mates:
        pl.semaphore_signal(barrier, inc=1, device_id=(mate, t), device_id_type=MESH)
    for hop in range(1, parts):
        pl.semaphore_signal(barrier, inc=1, device_id=(d, (t + hop) % parts), device_id_type=MESH)
    pl.semaphore_wait(barrier, len(mates) + parts - 1)


def bit_order(bits, flip):
    far = list(range(1, bits))
    return (far[::-1] if flip else far) + [0]


def gather_kernel(parts, bits, own, small, full, small_dp, small_t, z_send, z_recv, h_send, h_recv, s_send, s_recv, keep):
    d, t, digits, mates = mesh_place(bits)
    slab_count = own.shape[0]
    mine = digit_index(bits, digits, ())
    greet(d, t, mates, parts)
    offsets = [0] + [sign * hop for hop in range(1, parts) for sign in (1, -1)]
    pending = []

    def remote(src, dst, send, recv, to):
        return pltpu.make_async_remote_copy(src, dst, send, recv, device_id=to, device_id_type=MESH)

    local = [pltpu.make_async_copy(own.at[s], full.at[(s, t) + mine], keep.at[s]) for s in range(slab_count)]
    local.append(pltpu.make_async_copy(small.at[0], small_dp.at[mine], keep.at[slab_count]))
    local.append(pltpu.make_async_copy(small.at[1], small_t.at[t], keep.at[slab_count + 1]))
    for copy in local:
        copy.start()

    def z_copy(s, at, src, up):
        to = (d, t + 1) if up else (d, t - 1)
        way = 0 if up else 1
        return remote(src, full.at[(s, at) + mine], z_send.at[s, at, way], z_recv.at[s, at], to)

    def h_copy(s, index, step):
        offset = offsets[index]
        order = bit_order(bits, (abs(offset) + s) % 2 == 1)
        blocks = (s, t + offset) + digit_index(bits, digits, order[:step])
        src = own.at[s] if offset == 0 and step == 0 else full.at[blocks]
        return remote(src, full.at[blocks], h_send.at[s, index, step], h_recv.at[s, index, step], (mates[order[step]], t))

    def exists(offset):
        return (t + offset >= 0) & (t + offset < parts)

    def begin(s, index):
        offset = offsets[index]
        if offset == 0:
            h_copy(s, index, 0).start()
            return

        @pl.when(exists(offset))
        def _():
            up = offset < 0
            z_copy(s, t + offset, own.at[s], up).wait_recv()

            @pl.when((t < parts - 1) if up else (t > 0))
            def _():
                z_copy(s, t + offset, full.at[(s, t + offset) + mine], up).start()

            h_copy(s, index, 0).start()

    def advance(s, index, step):
        @pl.when(exists(offsets[index]))
        def _():
            h_copy(s, index, step - 1).wait_recv()
            if step < bits:
                h_copy(s, index, step).start()

    def small_step(step):
        blocks = digit_index(bits, digits, range(step))
        src = small.at[0] if step == 0 else small_dp.at[blocks]
        return remote(src, small_dp.at[blocks], s_send.at[step], s_recv.at[step], (mates[step], t))

    def small_hop(hop):
        peer = (d, (t + hop) % parts)
        return remote(small.at[1], small_t.at[t], s_send.at[bits + hop - 1], s_recv.at[bits + hop - 1], peer)

    def send_own(s):
        @pl.when(t < parts - 1)
        def _():
            z_copy(s, t, own.at[s], True).start()

        @pl.when(t > 0)
        def _():
            z_copy(s, t, own.at[s], False).start()

    order = [(s, hop) for s in range(slab_count) for hop in range(parts)]
    groups = [(s, [index for index, offset in enumerate(offsets) if abs(offset) == hop]) for s, hop in order]
    send_own(0)
    begin(0, 0)
    for hop in range(1, parts):
        small_hop(hop).start()
    small_step(0).start()
    for copy in local:
        copy.wait()
    for wave in range(len(groups) + bits * GATHER_LAG):
        for step in range(bits + 1):
            if 0 <= wave - step * GATHER_LAG < len(groups):
                s, indices = groups[wave - step * GATHER_LAG]
                for index in indices:
                    if step:
                        advance(s, index, step)
                    elif (s, index) != (0, 0):
                        begin(s, index)
        if wave in Z_WAVES:
            send_own(1 + Z_WAVES.index(wave))
        if wave < bits:
            small_step(wave).wait_recv()
            if wave + 1 < bits:
                small_step(wave + 1).start()

    for hop in range(1, parts):
        small_hop(hop).wait()
    for step in range(bits):
        small_step(step).wait_send()
    for s, indices in groups:
        for index in indices:
            offset = offsets[index]

            @pl.when(exists(offset))
            def _():
                for step in range(bits):
                    h_copy(s, index, step).wait_send()
                if offset <= 0:
                    @pl.when(t < parts - 1)
                    def _():
                        z_copy(s, t + offset, own.at[s], True).wait_send()
                if offset >= 0:
                    @pl.when(t > 0)
                    def _():
                        z_copy(s, t + offset, own.at[s], False).wait_send()


def gather_weights(own, small, parts, dp_count):
    bits = dp_count.bit_length() - 1
    slab_count, rows, columns = own.shape
    places = 2 * parts - 1
    low = jnp.bfloat16
    full, small_dp, small_t = pl.pallas_call(
        functools.partial(gather_kernel, parts, bits),
        out_shape=[
            jax.ShapeDtypeStruct((slab_count, parts) + (2,) * bits + (rows, columns), low),
            jax.ShapeDtypeStruct((2,) * bits + small.shape[1:], low),
            jax.ShapeDtypeStruct((parts,) + small.shape[1:], low),
        ],
        in_specs=[pl.BlockSpec(memory_space=pl.ANY)] * 2,
        out_specs=[pl.BlockSpec(memory_space=pl.ANY)] * 3,
        scratch_shapes=[
            pltpu.SemaphoreType.DMA((slab_count, parts, 2)),
            pltpu.SemaphoreType.DMA((slab_count, parts)),
            pltpu.SemaphoreType.DMA((slab_count, places, bits)),
            pltpu.SemaphoreType.DMA((slab_count, places, bits)),
            pltpu.SemaphoreType.DMA((bits + parts - 1,)),
            pltpu.SemaphoreType.DMA((bits + parts - 1,)),
            pltpu.SemaphoreType.DMA((slab_count + 2,)),
        ],
        compiler_params=pltpu.CompilerParams(collective_id=0, has_side_effects=True, vmem_limit_bytes=VMEM_LIMIT),
        name="gather_weights",
        cost_estimate=takes(100),
    )(own, small)
    full = full.reshape(slab_count, parts, dp_count * rows, columns)
    return full, small_dp.reshape((dp_count,) + small.shape[1:]), small_t


def add_rows(target, first, second, rows):
    lead = target.shape[:-2]
    chunk = 16 if rows % 16 == 0 else rows
    steps = rows // chunk
    count = 1
    for extent in lead:
        count *= extent

    def one(i, carry):
        at, rest = [], i // steps
        for extent in reversed(lead):
            at.insert(0, rest % extent)
            rest = rest // extent
        where = tuple(at) + (pl.ds(pl.multiple_of((i % steps) * chunk, chunk), chunk),)
        total = first[where].astype(jnp.float32) + second[where].astype(jnp.float32)
        target[where] = total.astype(target.dtype)
        return carry

    lax.fori_loop(0, count * steps, one, 0)


def reduce_kernel(parts, bits, grads, small, out, small_out, *scratch):
    bufs = scratch[:bits]
    z_up, z_down, small_buf, small_sum = scratch[bits:bits + 4]
    h_send, h_recv, up_send, up_recv, down_send, down_recv, s_send, s_recv = scratch[bits + 4:]
    d, t, digits, mates = mesh_place(bits)
    slab_count = grads.shape[0]
    rows = grads.shape[-2]
    greet(d, t, mates, parts)
    items = [(s, at) for s in range(slab_count) for at in range(parts)]
    small_bits = bits + parts.bit_length() - 1

    def remote(src, dst, send, recv, to):
        return pltpu.make_async_remote_copy(src, dst, send, recv, device_id=to, device_id_type=MESH)

    def order_of(number):
        s, at = items[number]
        return bit_order(bits, (s + at) % 2 == 1)[::-1]

    def held(number, step):
        s, at = items[number]
        return grads.at[s, at] if step == 0 else bufs[step - 1].at[number]

    def part_of(number, step, side):
        order = order_of(number)
        left = [k for k in reversed(range(bits)) if k not in order[:step]]
        pick = tuple(side if k == order[step] else slice(None) for k in left)
        return held(number, step).at[pick]

    def h_copy(number, step):
        order = order_of(number)
        digit = digits[order[step]]
        return remote(part_of(number, step, 1 - digit), bufs[step].at[number],
                      h_send.at[number, step], h_recv.at[number, step], (mates[order[step]], t))

    def fold(number, step):
        h_copy(number, step).wait_recv()
        digit = digits[order_of(number)[step]]
        add_rows(bufs[step].at[number], bufs[step].at[number], part_of(number, step, digit), rows)

    def summed(s, at):
        return bufs[bits - 1].at[s * parts + at]

    def z_copy(s, at, up, src):
        buf, send, recv = (z_up, up_send, up_recv) if up else (z_down, down_send, down_recv)
        to = (d, t + 1) if up else (d, t - 1)
        return remote(src, buf.at[s, at], send.at[s, at], recv.at[s, at], to)

    def z_pass(s, hop, up):
        at = t + hop if up else t - hop
        edge = (t == 0) if up else (t == parts - 1)
        buf = z_up if up else z_down

        @pl.when((at < parts) if up else (at >= 0))
        def _():
            @pl.when(edge)
            def _():
                z_copy(s, at, up, summed(s, at)).start()

            @pl.when(jnp.logical_not(edge))
            def _():
                z_copy(s, at, up, summed(s, at)).wait_recv()
                add_rows(buf.at[s, at], buf.at[s, at], summed(s, at), rows)
                z_copy(s, at, up, buf.at[s, at]).start()

    def z_finish(s):
        add_rows(out.at[s], summed(s, t), summed(s, t), rows)

        def scaled(i, carry):
            out[s] = out[s] * 0.5
            return carry
        lax.fori_loop(0, 1, scaled, 0)
        for up, buf in ((True, z_up), (False, z_down)):
            @pl.when((t > 0) if up else (t < parts - 1))
            def _():
                z_copy(s, t, up, summed(s, t)).wait_recv()
                add_rows(out.at[s], out.at[s], buf.at[s, t], rows)

    def small_copy(step):
        if step < bits:
            to = (mates[step], t)
        else:
            gap = 1 << (step - bits)
            to = (d, t + (1 - 2 * ((t // gap) % 2)) * gap)
        src = small if step == 0 else small_sum.at[step - 1]
        return remote(src, small_buf.at[step], s_send.at[step], s_recv.at[step], to)

    def small_fold(step):
        small_copy(step).wait_recv()
        before = small[...] if step == 0 else small_sum[step - 1]
        small_sum[step] = before + small_buf[step]
        if step + 1 < small_bits:
            small_copy(step + 1).start()

    for number in range(len(items)):
        h_copy(number, 0).start()
        if number == 0:
            small_copy(0).start()
    for wave in range(len(items) + bits * REDUCE_LAG + parts + 1):
        for step in range(bits):
            number = wave - step * REDUCE_LAG
            if 0 <= number < len(items):
                fold(number, step)
                if step + 1 < bits:
                    h_copy(number, step + 1).start()
        for s in range(slab_count):
            phase = wave - ((s + 1) * parts - 1 + bits * REDUCE_LAG)
            if 0 <= phase < parts - 1:
                z_pass(s, parts - 1 - phase, True)
                z_pass(s, parts - 1 - phase, False)
            elif phase == parts - 1:
                z_finish(s)
        if wave < small_bits:
            small_fold(wave)
    small_out[...] = small_sum[small_bits - 1]

    for step in range(small_bits):
        small_copy(step).wait_send()
    for number in range(len(items)):
        for step in range(bits):
            h_copy(number, step).wait_send()
    for s in range(slab_count):
        for hop in range(1, parts):
            @pl.when(t + hop < parts)
            def _():
                z_copy(s, t + hop, True, summed(s, t)).wait_send()

            @pl.when(t - hop >= 0)
            def _():
                z_copy(s, t - hop, False, summed(s, t)).wait_send()


def reduce_grads(grads, small, parts, dp_count):
    bits = dp_count.bit_length() - 1
    slab_count, columns = grads.shape[0], grads.shape[-1]
    rows = grads.shape[2] // dp_count
    grads = grads.reshape((slab_count, parts) + (2,) * bits + (rows, columns))
    low = jnp.bfloat16
    count = slab_count * parts
    small_bits = bits + parts.bit_length() - 1
    dma = pltpu.SemaphoreType.DMA
    return pl.pallas_call(
        functools.partial(reduce_kernel, parts, bits),
        out_shape=[
            jax.ShapeDtypeStruct((slab_count, rows, columns), jnp.float32),
            jax.ShapeDtypeStruct(small.shape, jnp.float32),
        ],
        in_specs=[pl.BlockSpec(memory_space=pltpu.VMEM)] * 2,
        out_specs=[pl.BlockSpec(memory_space=pltpu.VMEM)] * 2,
        scratch_shapes=[pltpu.VMEM((count,) + (2,) * (bits - 1 - step) + (rows, columns), low) for step in range(bits)]
        + [pltpu.VMEM((slab_count, parts, rows, columns), low)] * 2
        + [pltpu.VMEM((small_bits,) + small.shape, jnp.float32)] * 2
        + [dma((count, bits)), dma((count, bits))]
        + [dma((slab_count, parts))] * 4
        + [dma((small_bits,))] * 2,
        compiler_params=pltpu.CompilerParams(collective_id=1, has_side_effects=True, vmem_limit_bytes=VMEM_LIMIT),
        name="reduce_grads",
        cost_estimate=takes(100),
    )(grads, small)


def forward_kernel(parts, bits, micro_count, per_micro, slot_count, w_qkv, w_out, w_in, w_down, head_bias, ffn_bias,
                   norm_gains, row_biases, bucket, lengths, counts, inputs, cotangent,
                   weights, vectors, head_rows, ffn_rows, normed_out, inverse_out, proj_out, prob_out, context_out,
                   act_out, slope_out, out_out, second_out, second_low_out, stat_out,
                   own, small, full, small_dp, small_t, tokens, cot, total, normed_buf, inverse_buf, proj_buf, prob_buf, context_buf,
                   act_buf, slope_buf, first_low, down_total, out_buf, second_buf, second_low_buf,
                   z_send, z_recv, h_send, h_recv, s_send, s_recv, keep, load, weight_done, unit_done, ffn_done, end_done):
    layout = (bucket, lengths, counts)
    d, t, digits, mates = mesh_place(bits)
    blocks = micro_count * per_micro
    slab_count = own.shape[0]
    width = own.shape[2]
    mine = digit_index(bits, digits, ())

    def block_place(b):
        return b // per_micro, t * per_micro + b % per_micro

    def block_rows(b):
        micro, place = block_place(b)
        return (micro, pl.ds(pl.multiple_of(place * slot_count, slot_count), slot_count))

    loads = [pltpu.make_async_copy(inputs.at[block_rows(b)], tokens.at[b], load.at[b]) for b in range(blocks)]
    loads.append(pltpu.make_async_copy(cotangent.at[block_rows(0)], cot, load.at[blocks]))
    own[0] = slab_order(w_qkv[0], w_qkv[1], w_qkv[2], w_out[...].T)
    own[1] = w_in[...]
    own[2] = w_down[...]
    small[...] = jnp.zeros_like(small)
    vector_count = norm_gains.shape[0] + row_biases.shape[0]
    small[0, :, : own.shape[1]] = jnp.concatenate(
        [norm_gains[...], row_biases[...], jnp.zeros((16 - vector_count, own.shape[1]), LOW)], axis=0
    )
    no_bias = jnp.zeros((1, head_bias.shape[1]), LOW)
    bias_row = slab_order(head_bias[0:1], no_bias, head_bias[1:2], no_bias)
    small[1] = jnp.concatenate([bias_row, ffn_bias[...], jnp.zeros((14, own.shape[2]), LOW)], axis=0)
    greet(d, t, mates, parts)
    offsets = [0] + [sign * hop for hop in range(1, parts) for sign in (1, -1)]

    def remote(src, dst, send, recv, to):
        return pltpu.make_async_remote_copy(src, dst, send, recv, device_id=to, device_id_type=MESH)

    local = [pltpu.make_async_copy(own.at[s], full.at[(s, t) + mine], keep.at[s]) for s in range(slab_count)]
    local.append(pltpu.make_async_copy(small.at[0], small_dp.at[mine], keep.at[slab_count]))
    local.append(pltpu.make_async_copy(small.at[1], small_t.at[t], keep.at[slab_count + 1]))

    def z_copy(s, at, src, up):
        to = (d, t + 1) if up else (d, t - 1)
        return remote(src, full.at[(s, at) + mine], z_send.at[s, at, 0 if up else 1], z_recv.at[s, at], to)

    def h_copy(s, index, step):
        offset = offsets[index]
        order = bit_order(bits, (abs(offset) + s) % 2 == 1)
        where = (s, t + offset) + digit_index(bits, digits, order[:step])
        src = own.at[s] if offset == 0 and step == 0 else full.at[where]
        return remote(src, full.at[where], h_send.at[s, index, step], h_recv.at[s, index, step], (mates[order[step]], t))

    def exists(offset):
        return (t + offset >= 0) & (t + offset < parts)

    def weight_copy(s, at):
        return pltpu.make_async_copy(full.at[s, at], weights.at[s, at], weight_done.at[s, at])

    def begin(s, index):
        offset = offsets[index]
        if offset == 0:
            h_copy(s, index, 0).start()
            return

        @pl.when(exists(offset))
        def _():
            up = offset < 0
            z_copy(s, t + offset, own.at[s], up).wait_recv()

            @pl.when((t < parts - 1) if up else (t > 0))
            def _():
                z_copy(s, t + offset, full.at[(s, t + offset) + mine], up).start()

            h_copy(s, index, 0).start()

    def advance(s, index, step):
        @pl.when(exists(offsets[index]))
        def _():
            h_copy(s, index, step - 1).wait_recv()
            if step < bits:
                h_copy(s, index, step).start()
            else:
                weight_copy(s, t + offsets[index]).start()

    def small_step(step):
        where = digit_index(bits, digits, range(step))
        src = small.at[0] if step == 0 else small_dp.at[where]
        return remote(src, small_dp.at[where], s_send.at[step], s_recv.at[step], (mates[step], t))

    def small_hop(hop):
        peer = (d, (t + hop) % parts)
        return remote(small.at[1], small_t.at[t], s_send.at[bits + hop - 1], s_recv.at[bits + hop - 1], peer)

    def send_own(s):
        @pl.when(t < parts - 1)
        def _():
            z_copy(s, t, own.at[s], True).start()

        @pl.when(t > 0)
        def _():
            z_copy(s, t, own.at[s], False).start()

    toward = 1 - 2 * ((2 * t) // parts)

    def nearest(k):
        return (t + toward * k + parts) % parts

    def matrix(s, at):
        return full[s, at].reshape(width, full.shape[-1])

    def unit_copies(unit, at, b):
        slot = unit % 2
        heads = pl.ds(at * CHUNK_HEADS, CHUNK_HEADS)
        return [
            pltpu.make_async_copy(proj_buf.at[slot], proj_out.at[b, at], unit_done.at[slot, 0]),
            pltpu.make_async_copy(prob_buf.at[slot], prob_out.at[b, heads], unit_done.at[slot, 1]),
            pltpu.make_async_copy(context_buf.at[slot], context_out.at[b, at], unit_done.at[slot, 2]),
        ]

    def attend_part(b, k):
        unit = b * parts + k
        at = nearest(k)
        if unit >= 2:
            for copy in unit_copies(unit - 2, nearest((unit - 2) % parts), (unit - 2) // parts):
                copy.wait()
        slot = unit % 2
        micro, place = block_place(b)
        attention = attend_unit(layout, micro, place, tokens[b], matrix(0, at), head_rows[at],
                                proj_buf.at[slot], prob_buf.at[slot], context_buf.at[slot])
        if k == 0:
            total[...] = attention
        else:
            total[...] += attention
        for copy in unit_copies(unit, at, b):
            copy.start()
        if k == parts - 1:
            normed, inverse = normalize(tokens[b].astype(WIDE) + total[...] + vectors[2:3])
            normed_buf[b] = normed
            inverse_buf[b] = jnp.broadcast_to(inverse, inverse_buf.shape[1:])
            for copy in norm_copies(b):
                copy.start()

    def norm_copies(b):
        return [pltpu.make_async_copy(normed_buf.at[b], normed_out.at[b], end_done.at[b, 0]),
                pltpu.make_async_copy(inverse_buf.at[b], inverse_out.at[b], end_done.at[b, 1])]

    def ffn_copies(k):
        slot, at = k % 2, nearest(k)
        return [pltpu.make_async_copy(act_buf.at[slot], act_out.at[at], ffn_done.at[slot, 0]),
                pltpu.make_async_copy(slope_buf.at[slot], slope_out.at[at], ffn_done.at[slot, 1])]

    def final_copies():
        return [pltpu.make_async_copy(out_buf, out_out, end_done.at[blocks, 0]),
                pltpu.make_async_copy(second_buf, second_out, end_done.at[blocks, 1]),
                pltpu.make_async_copy(second_low_buf, second_low_out, end_done.at[blocks + 1, 0])]

    def ffn_part(k):
        at = nearest(k)
        if k == 0:
            first_low[...] = (normed_buf[0] * vectors[0:1] + vectors[3:4]).astype(LOW)
        if k >= 2:
            for copy in ffn_copies(k - 2):
                copy.wait()
        slot = k % 2
        down = ffn_unit(first_low[...], matrix(1, at), matrix(2, at), ffn_rows[at], act_buf.at[slot], slope_buf.at[slot])
        for copy in ffn_copies(k):
            copy.start()
        if k == 0:
            down_total[...] = down
        else:
            down_total[...] += down
        if k == parts - 1:
            micro, place = block_place(0)
            out, second, stat = second_norm(layout, micro, place, normed_buf[0], down_total[...], cot[...], vectors)
            out_buf[...] = out
            second_buf[...] = second
            second_low_buf[...] = second.astype(LOW)
            stat_out[...] = stat
            for copy in final_copies():
                copy.start()

    def finish_small():
        lanes = own.shape[1]
        pieces = [small_dp[digit_index(bits, [(i // (1 << k)) % 2 for k in range(bits)], ())][:8, :lanes].astype(WIDE)
                  for i in range(1 << bits)]
        vectors[...] = jnp.concatenate(pieces, axis=1)
        for at in range(parts):
            head_rows[at] = small_t[at, 0:1, :].astype(WIDE)
            ffn_rows[at] = small_t[at, 1:2, :].astype(WIDE)

    send_own(0)
    begin(0, 0)
    for hop in range(1, parts):
        small_hop(hop).start()
    small_step(0).start()
    for copy in local + loads:
        copy.start()
    for copy in local + loads:
        copy.wait()

    order = [(0, hop) for hop in range(parts)] + [(s, hop) for hop in range(parts) for s in range(1, slab_count)]
    groups = [(s, [index for index, offset in enumerate(offsets) if abs(offset) == hop]) for s, hop in order]
    done_at = {place: number + bits * GATHER_LAG for number, place in enumerate(order)}
    jobs = [(done_at[(0, k)], functools.partial(attend_part, b, k)) for b in range(blocks) for k in range(parts)]
    jobs += [(done_at[(slab_count - 1, k)], functools.partial(ffn_part, k)) for k in range(parts)]
    for wave in range(len(groups) + bits * GATHER_LAG):
        for step in range(bits + 1):
            if 0 <= wave - step * GATHER_LAG < len(groups):
                s, indices = groups[wave - step * GATHER_LAG]
                for index in indices:
                    if step:
                        advance(s, index, step)
                    elif (s, index) != (0, 0):
                        begin(s, index)
        if wave in Z_WAVES:
            send_own(1 + Z_WAVES.index(wave))
        if wave < bits:
            small_step(wave).wait_recv()
            if wave + 1 < bits:
                small_step(wave + 1).start()
            else:
                for hop in range(1, parts):
                    small_hop(hop).wait_recv()
                finish_small()
        if jobs and jobs[0][0] <= wave:
            jobs.pop(0)[1]()
    for _, job in jobs:
        job()

    for hop in range(1, parts):
        small_hop(hop).wait_send()
    for step in range(bits):
        small_step(step).wait_send()
    for s, indices in groups:
        for index in indices:
            offset = offsets[index]

            @pl.when(exists(offset))
            def _():
                for step in range(bits):
                    h_copy(s, index, step).wait_send()
                weight_copy(s, t + offset).wait()
                if offset <= 0:
                    @pl.when(t < parts - 1)
                    def _():
                        z_copy(s, t + offset, own.at[s], True).wait_send()
                if offset >= 0:
                    @pl.when(t > 0)
                    def _():
                        z_copy(s, t + offset, own.at[s], False).wait_send()
    last = blocks * parts
    for unit in range(max(0, last - 2), last):
        for copy in unit_copies(unit, nearest(unit % parts), unit // parts):
            copy.wait()
    for k in range(max(0, parts - 2), parts):
        for copy in ffn_copies(k):
            copy.wait()
    for b in range(blocks):
        for copy in norm_copies(b):
            copy.wait()
    for copy in final_copies():
        copy.wait()


def forward(arrays, layout, inputs, cotangent, parts, dp_count, slot_count, micro_count, per_micro):
    bits = dp_count.bit_length() - 1
    slab_count = 3
    rows, cols = arrays[2].shape
    width = rows * dp_count
    places = 2 * parts - 1
    blocks = micro_count * per_micro
    heads = parts * CHUNK_HEADS
    spread = (slab_count, parts) + (2,) * bits + (rows, cols)
    shape = jax.ShapeDtypeStruct
    dma = pltpu.SemaphoreType.DMA
    hbm, vmem, smem = [pl.BlockSpec(memory_space=space) for space in (pl.ANY, pltpu.VMEM, pltpu.SMEM)]
    slab = (slot_count, cols)
    rows_of = (slot_count, width)
    outs = [
        (spread, LOW, hbm),
        ((8, width), WIDE, vmem),
        ((parts, 1, cols), WIDE, vmem),
        ((parts, 1, cols), WIDE, vmem),
        ((blocks,) + rows_of, WIDE, hbm),
        ((blocks, slot_count, 128), WIDE, hbm),
        ((blocks, parts) + slab, LOW, hbm),
        ((blocks, heads, slot_count, slot_count), LOW, hbm),
        ((blocks, parts, slot_count, 4 * HEAD_DIM), LOW, hbm),
        ((parts,) + slab, LOW, hbm),
        ((parts,) + slab, LOW, hbm),
        (rows_of, LOW, hbm),
        (rows_of, WIDE, hbm),
        (rows_of, LOW, hbm),
        ((8, width), WIDE, vmem),
    ]
    result = pl.pallas_call(
        functools.partial(forward_kernel, parts, bits, micro_count, per_micro, slot_count),
        out_shape=[shape(dims, kind) for dims, kind, _ in outs],
        in_specs=[vmem] * len(arrays) + [smem, smem, smem, hbm, hbm],
        out_specs=[space for _, _, space in outs],
        scratch_shapes=[
            pltpu.VMEM((slab_count, rows, cols), LOW),
            pltpu.VMEM((2, 16, cols), LOW),
            pltpu.VMEM(spread, LOW),
            pltpu.VMEM((2,) * bits + (16, cols), LOW),
            pltpu.VMEM((parts, 16, cols), LOW),
            pltpu.VMEM((blocks,) + rows_of, LOW),
            pltpu.VMEM(rows_of, LOW),
            pltpu.VMEM(rows_of, WIDE),
            pltpu.VMEM((blocks,) + rows_of, WIDE),
            pltpu.VMEM((blocks, slot_count, 128), WIDE),
            pltpu.VMEM((2,) + slab, LOW),
            pltpu.VMEM((2, CHUNK_HEADS, slot_count, slot_count), LOW),
            pltpu.VMEM((2, slot_count, 4 * HEAD_DIM), LOW),
            pltpu.VMEM((2,) + slab, LOW),
            pltpu.VMEM((2,) + slab, LOW),
            pltpu.VMEM(rows_of, LOW),
            pltpu.VMEM(rows_of, WIDE),
            pltpu.VMEM(rows_of, LOW),
            pltpu.VMEM(rows_of, WIDE),
            pltpu.VMEM(rows_of, LOW),
            dma((slab_count, parts, 2)),
            dma((slab_count, parts)),
            dma((slab_count, places, bits)),
            dma((slab_count, places, bits)),
            dma((bits + parts - 1,)),
            dma((bits + parts - 1,)),
            dma((slab_count + 2,)),
            dma((blocks + 1,)),
            dma((slab_count, parts)),
            dma((2, 3)),
            dma((2, 2)),
            dma((blocks + 2, 2)),
        ],
        compiler_params=pltpu.CompilerParams(collective_id=2, has_side_effects=True, vmem_limit_bytes=VMEM_LIMIT),
        name="forward",
    )(*arrays, *layout, inputs, cotangent)
    return (result[0].reshape(slab_count, parts, width, cols),) + tuple(result[1:])


def finish_kernel(parts, bits, micro_count, per_micro, slot_count, chunks, vectors, small, inputs, normed, *refs):
    blocks = micro_count * per_micro
    second_low, hidden_low, act, grad_up, head_grads, token_grad = [refs[i * blocks : (i + 1) * blocks] for i in range(6)]
    rest = refs[6 * blocks :]
    gathered, out, small_out = rest[:3]
    (grads, operand, turned, staged, staged_wide, small_buf, small_sum, z_up, z_down) = rest[3:12]
    bufs = rest[12 : 12 + bits]
    (h_send, h_recv, up_send, up_recv, down_send, down_recv, s_send, s_recv, g_send, g_recv, g_keep, load, load_wide, fetch) = rest[
        12 + bits :
    ]
    d, t, digits, mates = mesh_place(bits)
    slab_count = grads.shape[0]
    rows = grads.shape[-2]
    width = inputs.shape[2]
    items = [(s, at) for s in range(slab_count) for at in range(parts)]
    small_bits = bits + parts.bit_length() - 1
    chunk_rows = slot_count // chunks

    def remote(src, dst, send, recv, to):
        return pltpu.make_async_remote_copy(src, dst, send, recv, device_id=to, device_id_type=MESH)

    def token_rows(b):
        place = t * per_micro + b % per_micro
        return inputs.at[b // per_micro, pl.ds(pl.multiple_of(place * slot_count, slot_count), slot_count)]

    def span(b):
        return pl.ds(b * slot_count, slot_count)

    def stage_loads(which):
        if which == 3:
            return [pltpu.make_async_copy(normed.at[b], staged_wide.at[span(b)], load_wide.at[b]) for b in range(blocks)]
        source = ([token_rows(b) for b in range(blocks)], hidden_low, second_low)[which]
        return [pltpu.make_async_copy(source[b], staged.at[which, span(b)], load.at[which, b]) for b in range(blocks)]

    def operand_loads(number):
        s, at = items[number]
        source = (head_grads, grad_up, act)[s]
        slot = number % 3
        return [pltpu.make_async_copy(source[b].at[at], operand.at[slot, span(b)], fetch.at[slot, b]) for b in range(blocks)]

    def grads_job(number):
        s, at = items[number]
        if number == 0:
            for copy in stage_loads(0) + stage_loads(1):
                copy.wait()
            turned[0] = staged[0].T
            turned[1] = staged[1].T
        elif at == 0 and s == 1:
            for copy in stage_loads(3):
                copy.wait()
            turned[0] = (staged_wide[...] * vectors[0:1] + vectors[3:4]).astype(LOW).T
        elif at == 0:
            for copy in stage_loads(2):
                copy.wait()
            turned[1] = staged[2].T
        for copy in operand_loads(number):
            copy.wait()
        right = operand[number % 3]
        if s == 0:
            qkv = dot_nn(turned[0], right)
            outs = dot_nn(turned[1], right[:, 8 * HEAD_DIM :])
            lane = lax.broadcasted_iota(jnp.int32, (1, 2 * HEAD_DIM), 1)
            last = jnp.where(lane < HEAD_DIM, qkv[:, 10 * HEAD_DIM :], outs[:, 2 * HEAD_DIM :])
            total = jnp.concatenate([qkv[:, : 8 * HEAD_DIM], outs[:, : 2 * HEAD_DIM], last], axis=1)
        else:
            total = dot_nn(turned[s - 1], right)
        grads[s, at] = total.astype(LOW).reshape(grads.shape[2:])
        if number + 3 < len(items):
            for copy in operand_loads(number + 3):
                copy.start()

    def order_of(number):
        s, at = items[number]
        return bit_order(bits, (s + at) % 2 == 1)[::-1]

    def held(number, step):
        s, at = items[number]
        return grads.at[s, at] if step == 0 else bufs[step - 1].at[number]

    def part_of(number, step, side):
        order = order_of(number)
        left = [k for k in reversed(range(bits)) if k not in order[:step]]
        pick = tuple(side if k == order[step] else slice(None) for k in left)
        return held(number, step).at[pick]

    def h_copy(number, step):
        order = order_of(number)
        digit = digits[order[step]]
        return remote(part_of(number, step, 1 - digit), bufs[step].at[number],
                      h_send.at[number, step], h_recv.at[number, step], (mates[order[step]], t))

    def fold(number, step):
        h_copy(number, step).wait_recv()
        digit = digits[order_of(number)[step]]
        add_rows(bufs[step].at[number], bufs[step].at[number], part_of(number, step, digit), rows)

    def summed(s, at):
        return bufs[bits - 1].at[s * parts + at]

    def z_copy(s, at, up, src):
        buf, send, recv = (z_up, up_send, up_recv) if up else (z_down, down_send, down_recv)
        to = (d, t + 1) if up else (d, t - 1)
        return remote(src, buf.at[s, at], send.at[s, at], recv.at[s, at], to)

    def z_pass(s, hop, up):
        at = t + hop if up else t - hop
        edge = (t == 0) if up else (t == parts - 1)
        buf = z_up if up else z_down

        @pl.when((at < parts) if up else (at >= 0))
        def _():
            @pl.when(edge)
            def _():
                z_copy(s, at, up, summed(s, at)).start()

            @pl.when(jnp.logical_not(edge))
            def _():
                z_copy(s, at, up, summed(s, at)).wait_recv()
                add_rows(buf.at[s, at], buf.at[s, at], summed(s, at), rows)
                z_copy(s, at, up, buf.at[s, at]).start()

    def z_finish(s):
        @pl.when(t > 0)
        def _():
            z_copy(s, t, True, summed(s, t)).wait_recv()
            add_rows(out.at[s], summed(s, t), z_up.at[s, t], rows)

        @pl.when(t < parts - 1)
        def _():
            z_copy(s, t, False, summed(s, t)).wait_recv()

            @pl.when(t > 0)
            def _():
                add_rows(out.at[s], out.at[s], z_down.at[s, t], rows)

            @pl.when(t == 0)
            def _():
                add_rows(out.at[s], summed(s, t), z_down.at[s, t], rows)

    def small_copy(step):
        if step < bits:
            to = (mates[step], t)
        else:
            gap = 1 << (step - bits)
            to = (d, t + (1 - 2 * ((t // gap) % 2)) * gap)
        src = small if step == 0 else small_sum.at[step - 1]
        return remote(src, small_buf.at[step], s_send.at[step], s_recv.at[step], to)

    def small_fold(step):
        small_copy(step).wait_recv()
        before = small[...] if step == 0 else small_sum[step - 1]
        small_sum[step] = before + small_buf[step]
        if step + 1 < small_bits:
            small_copy(step + 1).start()

    def line_rows(b, at, q):
        place = at * per_micro + b % per_micro
        start = pl.multiple_of(place * slot_count + q * chunk_rows, chunk_rows)
        return gathered.at[b // per_micro, pl.ds(start, chunk_rows)]

    def own_rows(b, q):
        return token_grad[b].at[pl.ds(q * chunk_rows, chunk_rows)]

    def line_copy(b, at, q, src, up):
        to = (d, t + 1) if up else (d, t - 1)
        return remote(src, line_rows(b, at, q), g_send.at[b, at, q, 0 if up else 1], g_recv.at[b, at, q], to)

    def line_send(b, q):
        for up in (True, False):
            @pl.when((t < parts - 1) if up else (t > 0))
            def _():
                line_copy(b, t, q, own_rows(b, q), up).start()

    def line_pass(b, hop, q):
        for up in (True, False):
            at = t - hop if up else t + hop

            @pl.when((at >= 0) if up else (at < parts))
            def _():
                line_copy(b, at, q, own_rows(b, q), up).wait_recv()

                @pl.when((t < parts - 1) if up else (t > 0))
                def _():
                    line_copy(b, at, q, line_rows(b, at, q), up).start()

    def line_settle(b, hop, q):
        for up in (True, False):
            at = t - hop if up else t + hop

            @pl.when(((at >= 0) if up else (at < parts)) & ((t < parts - 1) if up else (t > 0)))
            def _():
                line_copy(b, at, q, own_rows(b, q), up).wait_send()

    keeps = [pltpu.make_async_copy(own_rows(b, q), line_rows(b, t, q), g_keep.at[b, q])
             for b in range(blocks) for q in range(chunks)]
    events = []
    for turn in range(blocks + parts):
        for hop in range(parts + 1):
            b = turn - hop
            if 0 <= b < blocks and hop <= parts - 1:
                for q in range(chunks):
                    events.append(functools.partial(line_send, b, q) if hop == 0 else functools.partial(line_pass, b, hop, q))

    for copy in stage_loads(0) + stage_loads(1):
        copy.start()
    for number in range(min(3, len(items))):
        for copy in operand_loads(number):
            copy.start()
    for copy in stage_loads(3) + stage_loads(2):
        copy.start()
    greet(d, t, mates, parts)
    for copy in keeps:
        copy.start()
    small_copy(0).start()
    ahead = chunks

    waves = len(items) + bits * REDUCE_LAG + parts
    per_wave = LINE_PACE
    for wave in range(max(waves, len(events))):
        while events and wave * per_wave + ahead > total_done(events, blocks, parts, chunks):
            events.pop(0)()
        if wave < len(items):
            grads_job(wave)
            h_copy(wave, 0).start()
        for step in range(bits):
            number = wave - (step + 1) * REDUCE_LAG + 1
            if 0 <= number < len(items):
                fold(number, step)
                if step + 1 < bits:
                    h_copy(number, step + 1).start()
        for s in range(slab_count):
            phase = wave - ((s + 1) * parts + bits * REDUCE_LAG - 1)
            if 0 <= phase < parts - 1:
                z_pass(s, parts - 1 - phase, True)
                z_pass(s, parts - 1 - phase, False)
            elif phase == parts - 1:
                z_finish(s)
        if wave < small_bits:
            small_fold(wave)
    small_out[...] = small_sum[small_bits - 1]

    for copy in keeps:
        copy.wait()
    for b in range(blocks):
        for hop in range(parts - 1):
            for q in range(chunks):
                line_settle(b, hop, q)
    for step in range(small_bits):
        small_copy(step).wait_send()
    for number in range(len(items)):
        for step in range(bits):
            h_copy(number, step).wait_send()
    for s in range(slab_count):
        for hop in range(1, parts):
            @pl.when(t + hop < parts)
            def _():
                z_copy(s, t + hop, True, summed(s, t)).wait_send()

            @pl.when(t - hop >= 0)
            def _():
                z_copy(s, t - hop, False, summed(s, t)).wait_send()


def total_done(events, blocks, parts, chunks):
    return blocks * parts * chunks - len(events)


def finish(vectors, small, inputs, normed, second_low, hidden_low, act, grad_up, head_grads, token_grad, parts, dp_count):
    bits = dp_count.bit_length() - 1
    blocks = len(token_grad)
    micro_count, tokens, width = inputs.shape
    per_micro = blocks // micro_count
    slot_count, cols = act[0].shape[1:]
    rows = width // dp_count
    slab_count = 3
    count = slab_count * parts
    small_bits = bits + parts.bit_length() - 1
    dma = pltpu.SemaphoreType.DMA
    hbm, vmem = pl.BlockSpec(memory_space=pl.ANY), pl.BlockSpec(memory_space=pltpu.VMEM)
    block = (rows, cols)
    return pl.pallas_call(
        functools.partial(finish_kernel, parts, bits, micro_count, per_micro, slot_count, LINE_CHUNKS),
        out_shape=[
            jax.ShapeDtypeStruct((micro_count, tokens, width), LOW),
            jax.ShapeDtypeStruct((slab_count,) + block, WIDE),
            jax.ShapeDtypeStruct(small.shape, WIDE),
        ],
        in_specs=[vmem, vmem, hbm, hbm] + [hbm] * (6 * blocks),
        out_specs=[hbm, vmem, vmem],
        scratch_shapes=[
            pltpu.VMEM((slab_count, parts) + (2,) * bits + block, LOW),
            pltpu.VMEM((3, blocks * slot_count, cols), LOW),
            pltpu.VMEM((2, width, blocks * slot_count), LOW),
            pltpu.VMEM((3, blocks * slot_count, width), LOW),
            pltpu.VMEM((blocks * slot_count, width), WIDE),
            pltpu.VMEM((small_bits,) + small.shape, WIDE),
            pltpu.VMEM((small_bits,) + small.shape, WIDE),
            pltpu.VMEM((slab_count, parts) + block, LOW),
            pltpu.VMEM((slab_count, parts) + block, LOW),
        ]
        + [pltpu.VMEM((count,) + (2,) * (bits - 1 - step) + block, LOW) for step in range(bits)]
        + [dma((count, bits)), dma((count, bits))]
        + [dma((slab_count, parts))] * 4
        + [dma((small_bits,))] * 2
        + [dma((blocks, parts, LINE_CHUNKS, 2)), dma((blocks, parts, LINE_CHUNKS)), dma((blocks, LINE_CHUNKS))]
        + [dma((3, blocks)), dma((blocks,)), dma((3, blocks))],
        compiler_params=pltpu.CompilerParams(collective_id=3, has_side_effects=True, vmem_limit_bytes=VMEM_LIMIT),
        name="finish",
        cost_estimate=takes(100),
    )(vectors, small, inputs, normed, *second_low, *hidden_low, *act, *grad_up, *head_grads, *token_grad)


def place_kernel(parts, dp_count, place, shard, sums, grad_qkv, grad_out, grad_in, grad_down, grad_head, grad_ffn,
                 grad_gains, grad_shifts):
    groups = slab_parts(shard[0])
    for i in range(3):
        grad_qkv[i] = groups[i]
    grad_out[...] = groups[3].T
    grad_in[...] = shard[1]
    grad_down[...] = shard[2]
    grad_ffn[...] = sums[pl.ds(6 + place[0], 1), :]
    head = slab_parts(sums[pl.ds(6 + parts + place[0], 1), :])
    grad_head[...] = jnp.concatenate([head[0], head[2]], axis=0)
    rows = shard.shape[1]
    wide = sums[0:8, :]
    vectors = wide[:, :rows]
    for i in range(1, dp_count):
        vectors = jnp.where(place[1] == i, wide[:, i * rows : (i + 1) * rows], vectors)
    grad_gains[...] = vectors[0:2]
    grad_shifts[...] = vectors[2:6]


def place_results(shard, sums, rank, dp_rank, parts, dp_count):
    rows, cols = shard.shape[1:]
    head_cols = CHUNK_HEADS * HEAD_DIM
    smalls = [(3, rows, head_cols), (head_cols, rows), (rows, cols), (rows, cols), (2, head_cols), (1, cols), (2, rows), (4, rows)]
    vmem = pl.BlockSpec(memory_space=pltpu.VMEM)
    return pl.pallas_call(
        functools.partial(place_kernel, parts, dp_count),
        in_specs=[pl.BlockSpec(memory_space=pltpu.SMEM), vmem, vmem],
        out_specs=[vmem] * len(smalls),
        out_shape=[jax.ShapeDtypeStruct(dims, WIDE) for dims in smalls],
        compiler_params=pltpu.CompilerParams(vmem_limit_bytes=VMEM_LIMIT),
        name="place_results",
    )(jnp.stack([rank, dp_rank]).astype(jnp.int32), shard, sums)


def add_all(terms):
    total = terms[0]
    for term in terms[1:]:
        total = total + term
    return total


def after(values, *earlier):
    return lax.optimization_barrier((tuple(values), earlier))[0]


def body(
    inputs,
    cotangent,
    bucket,
    lengths,
    counts,
    w_qkv,
    w_out,
    w_in,
    w_down,
    head_bias,
    ffn_bias,
    norm_gains,
    row_biases,
):
    micro_count, _, width = inputs.shape
    blocks_all = bucket.shape[1]
    slot_count = inputs.shape[1] // blocks_all
    parts, dp_count = lax.axis_size("tensor"), lax.axis_size("dp")
    rank, dp_rank = lax.axis_index("tensor"), lax.axis_index("dp")
    per_micro = blocks_all // parts
    cols = w_in.shape[1]
    rows = w_in.shape[0]

    vector_count = norm_gains.shape[0] + row_biases.shape[0]
    blocks = [(m, k) for m in range(micro_count) for k in range(per_micro)]
    places = [jnp.full((1,), rank * per_micro + k, jnp.int32) for k in range(per_micro)]
    layout = (bucket, lengths, counts)
    kept = []
    if rows % 16 == 0:
        (weights, vectors, head_rows, ffn_rows, normed, inverse, proj, probs, context, *first_ffn) = forward(
            (w_qkv, w_out, w_in, w_down.T, head_bias, ffn_bias[None], norm_gains, row_biases),
            layout, inputs, cotangent, parts, dp_count, slot_count, micro_count, per_micro
        )
        attended = [tuple((array, b) for array in (normed, inverse, proj, probs, context)) for b in range(len(blocks))]
        ffns = [first_ffn]
    else:
        own = jnp.stack([slab_order(w_qkv[0], w_qkv[1], w_qkv[2], w_out.T), w_in, w_down.T])
        norm_rows = jnp.concatenate([norm_gains, row_biases], axis=0)
        no_bias = jnp.zeros_like(head_bias[:1])
        bias_rows = jnp.concatenate([slab_order(head_bias[:1], no_bias, head_bias[1:], no_bias), ffn_bias[None]], axis=0)
        small = jnp.stack([
            jnp.pad(norm_rows, ((0, 16 - vector_count), (0, cols - rows))),
            jnp.pad(bias_rows, ((0, 14), (0, 0))),
        ])
        weights, small_dp, small_t = gather_weights(own, small, parts, dp_count)
        vectors = small_dp[:, :8, :rows].transpose(1, 0, 2).reshape(8, width).astype(jnp.float32)
        head_rows = small_t[:, 0:1].astype(jnp.float32)
        ffn_rows = small_t[:, 1:2].astype(jnp.float32)
        attended = []
        for m, k in blocks:
            parts_of = attend(m, places[k], *layout, inputs, weights, head_rows, vectors, slot_count)
            attended.append(tuple((array[None], 0) for array in parts_of))
        ffns = []
    for m, k in blocks[len(ffns) :]:
        normed = attended[m * per_micro + k][0]
        ffns.append(ffn(m, places[k], *layout, normed, cotangent, weights, ffn_rows, vectors))
    outs = []
    for (normed, inverse, proj, probs, context), (act, slope, out, second, second_low, stat) in zip(attended, ffns):
        kept.append((normed, inverse, proj, probs, context, act, slope, second, second_low, stat))
        outs.append(out)
    results = [
        lax.all_gather(jnp.concatenate(outs[m * per_micro : (m + 1) * per_micro], axis=0), "tensor", axis=0, tiled=True)
        for m in range(micro_count)
    ]
    token_grads, saved = [], []
    kept[0] = kept[0][:7] + after(kept[0][7:], outs[-1])
    for (m, k), (normed, inverse, proj, probs, context, act, slope, second, second_low, stat) in zip(blocks, kept):
        grad_up, hidden, hidden_low, up_stat, first_stat = ffn_back(second, second_low, slope, weights, normed, inverse, vectors)
        if (m, k) == blocks[-1]:
            hidden, hidden_low = after((hidden, hidden_low), results[0])
        head_grads, token_grad, head_stat = attend_back(
            m, places[k], *layout, hidden, hidden_low, weights, proj, probs, context
        )
        token_grads.append(token_grad)
        saved.append((normed, second_low, hidden_low, act, grad_up, head_grads, stat, first_stat, up_stat, head_stat))
    columns = list(zip(*saved))
    stat, first_stat, up_stat, head_stat = [add_all(column) for column in columns[6:]]
    small_grads = jnp.concatenate(
        [
            jnp.stack([first_stat[0], stat[0], first_stat[2], first_stat[1], stat[2], stat[1]]),
            up_stat[:, 0],
            head_stat[:, 0],
        ],
        axis=0,
    )
    small_grads = jnp.pad(small_grads, ((0, -small_grads.shape[0] % 8), (0, 0)))
    if rows % 16 == 0:
        normed = columns[0][0][0]
        input_grad, shard, sums = finish(
            vectors, small_grads, inputs, normed, *columns[1:6], token_grads, parts, dp_count
        )
    else:
        input_grad = jnp.stack([
            lax.all_gather(jnp.concatenate(token_grads[m * per_micro : (m + 1) * per_micro], axis=0), "tensor", axis=0, tiled=True)
            for m in range(micro_count)
        ])
        grads = weight_grads(places[0], inputs, *columns[:6], vectors)
        shard, sums = reduce_grads(grads, small_grads, parts, dp_count)
    if rows % 16 == 0:
        grad_w_qkv, grad_w_out, grad_w_in, grad_w_down, grad_head, grad_ffn, grad_gains, grad_shifts = place_results(
            shard, sums, rank, dp_rank, parts, dp_count
        )
        grad_w_down, grad_ffn = grad_w_down.T, grad_ffn.reshape(-1)
    else:
        vector_sums = lax.dynamic_slice_in_dim(sums[:vector_count], dp_rank * rows, rows, 1)
        grad_gains, grad_shifts = vector_sums[:2], vector_sums[2:]
        grad_query, grad_key, grad_value, grad_out = slab_parts(shard[0])
        grad_w_qkv = jnp.stack([grad_query, grad_key, grad_value])
        grad_w_out, grad_w_in, grad_w_down = grad_out.T, shard[1], shard[2].T
        grad_ffn = lax.dynamic_slice_in_dim(sums, vector_count + rank, 1, 0)[0]
        head_sum = slab_parts(lax.dynamic_slice_in_dim(sums, vector_count + parts + rank, 1, 0))
        grad_head = jnp.concatenate([head_sum[0], head_sum[2]], axis=0)
    return (
        jnp.stack(results),
        input_grad,
        grad_w_qkv,
        grad_w_out,
        grad_w_in,
        grad_w_down,
        grad_head,
        grad_ffn,
        grad_gains,
        grad_shifts,
    )


def solution(mesh):
    in_specs = (
        P(None, "dp", None),
        P(None, "dp", None),
        P(None, "dp"),
        P(None, "dp", None),
        P(None, "dp"),
        P(None, "dp", "tensor"),
        P("tensor", "dp"),
        P("dp", "tensor"),
        P("tensor", "dp"),
        P(None, "tensor"),
        P("tensor"),
        P(None, "dp"),
        P(None, "dp"),
    )
    out_specs = (
        P(None, "dp", None),
        P(None, "dp", None),
        P(None, "dp", "tensor"),
        P("tensor", "dp"),
        P("dp", "tensor"),
        P("tensor", "dp"),
        P(None, "tensor"),
        P("tensor"),
        P(None, "dp"),
        P(None, "dp"),
    )
    return jax.shard_map(body, mesh=mesh, in_specs=in_specs, out_specs=out_specs, check_vma=False)
```

```python
import functools

import jax
import jax.numpy as jnp
from jax import lax
from jax.experimental import pallas as pl
from jax.experimental.pallas import tpu as pltpu
from jax.sharding import PartitionSpec as P

HEAD_DIM = 64
EPSILON = 1e-12
VMEM_LIMIT = 60 * 1024 * 1024
MESH = pl.DeviceIdType.MESH
GATHER_LAG = 2
Z_WAVES = (2, 3)
LINE_PACE = 1
LINE_START = ((0, 1, 7), (4, 9, 15))
LINE_CHUNKS = 4
REDUCE_LAG = 2
def takes(microseconds):
    return pl.CostEstimate(flops=int(microseconds * 1.15e8), bytes_accessed=0, transcendentals=0)


LOW = jnp.bfloat16
WIDE = jnp.float32
CHUNK_HEADS = 3
VALUE_AT = (6, 7, 10)
OUT_AT = (8, 9, 11)


def slab_order(query, key, value, out):
    columns = lambda group, head: group[..., head * HEAD_DIM : (head + 1) * HEAD_DIM]
    order = [(query, 0), (key, 0), (query, 1), (key, 1), (query, 2), (key, 2),
             (value, 0), (value, 1), (out, 0), (out, 1), (value, 2), (out, 2)]
    return jnp.concatenate([columns(group, head) for group, head in order], axis=-1)


def slab_parts(slab):
    columns = lambda at: slab[..., at * HEAD_DIM : (at + 1) * HEAD_DIM]
    groups = ((0, 2, 4), (1, 3, 5), VALUE_AT, OUT_AT)
    return [jnp.concatenate([columns(at) for at in group], axis=-1) for group in groups]


def dot_nn(left, right):
    return lax.dot_general(left, right, (((1,), (0,)), ((), ())), preferred_element_type=WIDE)


def dot_nt(left, right):
    return lax.dot_general(left, right, (((1,), (1,)), ((), ())), preferred_element_type=WIDE)


def dot_tn(left, right):
    return lax.dot_general(left, right, (((0,), (0,)), ((), ())), preferred_element_type=WIDE)


def piece(tile, at):
    return tile[:, at * HEAD_DIM : (at + 1) * HEAD_DIM]


def slot_codes(layout, micro, block, slot_count, shape, axis):
    bucket, lengths, counts = layout
    position = lax.broadcasted_iota(jnp.int32, shape, axis)
    quarter = slot_count // 4
    whole = bucket[micro, block] == 1
    item = jnp.where(whole, 0, position // quarter)
    place = position - item * quarter
    length = jnp.where(
        item == 0,
        lengths[micro, block, 0],
        jnp.where(
            item == 1,
            lengths[micro, block, 1],
            jnp.where(item == 2, lengths[micro, block, 2], lengths[micro, block, 3]),
        ),
    )
    return item, (item < counts[micro, block]) & (place < length)


def normalize(hidden):
    center = hidden - jnp.mean(hidden, axis=-1, keepdims=True)
    inverse = lax.rsqrt(jnp.mean(center * center, axis=-1, keepdims=True) + EPSILON)
    return center * inverse, inverse


def norm_pullback(grad_rows, normed, inverse, gain_row):
    grad_normed = grad_rows * gain_row
    return inverse * (
        grad_normed
        - jnp.mean(grad_normed, axis=-1, keepdims=True)
        - normed * jnp.mean(grad_normed * normed, axis=-1, keepdims=True)
    )


def row_sum(values):
    return jnp.sum(values, axis=0, keepdims=True)


def attend_unit(layout, micro, place, tokens, weights, bias_row, proj_ref, prob_ref, context_ref):
    slot_count = tokens.shape[0]
    proj = (dot_nn(tokens, weights) + bias_row).astype(LOW)
    proj_ref[...] = proj
    row_item, _ = slot_codes(layout, micro, place, slot_count, (slot_count, 1), 0)
    key_item, key_live = slot_codes(layout, micro, place, slot_count, (1, slot_count), 1)
    key_code = jnp.where(key_live, key_item, -1)
    outs = []
    for head in range(CHUNK_HEADS):
        query = piece(proj, 2 * head) * jnp.asarray(HEAD_DIM ** (-0.5), LOW)
        scores = dot_nt(query, piece(proj, 2 * head + 1))
        scores = jnp.where(row_item == key_code, scores, -10000.0)
        grown = jnp.exp(scores - jnp.max(scores, axis=-1, keepdims=True))
        probs = (grown * (1.0 / jnp.sum(grown, axis=-1, keepdims=True))).astype(LOW)
        prob_ref[head] = probs
        outs.append(dot_nn(probs, piece(proj, VALUE_AT[head])).astype(LOW))
    context = jnp.concatenate([outs[0], outs[1], jnp.zeros_like(outs[0]), outs[2]], axis=1)
    context_ref[...] = context
    return dot_nt(context, weights[:, 8 * HEAD_DIM :])


def ffn_unit(first_low, w_in, w_down, bias_row, act_ref, slope_ref):
    upward = dot_nn(first_low, w_in) + bias_row
    share = 0.5 + 0.5 * lax.erf(upward * (0.5**0.5))
    activated = (upward * share).astype(LOW)
    act_ref[...] = activated
    bell = jnp.exp(-0.5 * upward * upward) * 0.3989422804014327
    slope_ref[...] = (share + upward * bell).astype(LOW)
    return dot_nt(activated, w_down)


def second_norm(layout, micro, place, first_normed, down_total, cot_rows, vectors):
    slot_count = first_normed.shape[0]
    _, live = slot_codes(layout, micro, place, slot_count, (slot_count, 1), 0)
    first = first_normed * vectors[0:1] + vectors[3:4]
    normed, inverse = normalize(first + down_total + vectors[4:5])
    out = (normed * vectors[1:2] + vectors[5:6]).astype(LOW)
    grad_out = jnp.where(live, cot_rows.astype(WIDE), 0.0)
    second = norm_pullback(grad_out, normed, inverse, vectors[1:2])
    stat = jnp.concatenate(
        [row_sum(grad_out * normed), row_sum(grad_out), row_sum(second), jnp.zeros((5, second.shape[1]), WIDE)], axis=0
    )
    return out, second, stat


def attend_kernel(micro, place, bucket, lengths, counts, x_ref, w_ref, bias_ref, vec_ref,
                  normed_ref, inverse_ref, proj_ref, prob_ref, context_ref, total):
    step = pl.program_id(0)
    layout = (bucket, lengths, counts)
    tokens = x_ref[0]
    attention = attend_unit(layout, micro, place[0], tokens, w_ref[0, 0], bias_ref[0],
                            proj_ref.at[0], prob_ref, context_ref.at[0])

    @pl.when(step == 0)
    def _():
        total[...] = attention

    @pl.when(step > 0)
    def _():
        total[...] += attention

    @pl.when(step == pl.num_programs(0) - 1)
    def _():
        normed, inverse = normalize(tokens.astype(WIDE) + total[...] + vec_ref[2:3])
        normed_ref[...] = normed
        inverse_ref[...] = jnp.broadcast_to(inverse, inverse_ref.shape)


def ffn_kernel(micro, place, bucket, lengths, counts, normed_ref, cot_ref, w_in_ref, w_down_ref, bias_ref, vec_ref,
               act_ref, slope_ref, out_ref, second_ref, second_low_ref, stat_ref, first_low, total):
    step = pl.program_id(0)

    @pl.when(step == 0)
    def _():
        first_low[...] = (normed_ref[...] * vec_ref[0:1] + vec_ref[3:4]).astype(LOW)

    down = ffn_unit(first_low[...], w_in_ref[0, 0], w_down_ref[0, 0], bias_ref[0], act_ref.at[0], slope_ref.at[0])

    @pl.when(step == 0)
    def _():
        total[...] = down

    @pl.when(step > 0)
    def _():
        total[...] += down

    @pl.when(step == pl.num_programs(0) - 1)
    def _():
        out, second, stat = second_norm(
            (bucket, lengths, counts), micro, place[0], normed_ref[...], total[...], cot_ref[0], vec_ref
        )
        out_ref[...] = out
        second_ref[...] = second
        second_low_ref[...] = second.astype(LOW)
        stat_ref[...] = stat


def ffn_back_kernel(second_ref, second_low_ref, slope_ref, w_in_ref, w_down_ref, normed_ref, inverse_ref, vec_ref,
                    up_ref, hidden_ref, hidden_low_ref, up_stat_ref, stat_ref, total):
    step = pl.program_id(0)
    grad_act = dot_nn(second_low_ref[...], w_down_ref[0, 0])
    grad_up = (grad_act * slope_ref[0].astype(WIDE)).astype(LOW)
    up_ref[0] = grad_up
    up_stat_ref[0] = jnp.broadcast_to(row_sum(grad_up.astype(WIDE)), up_stat_ref.shape[1:])
    back = dot_nt(grad_up, w_in_ref[0, 0])

    @pl.when(step == 0)
    def _():
        total[...] = back + second_ref[...]

    @pl.when(step > 0)
    def _():
        total[...] += back

    @pl.when(step == pl.num_programs(0) - 1)
    def _():
        grad_first = total[...]
        normed = normed_ref[...]
        hidden = norm_pullback(grad_first, normed, inverse_ref[:, :1], vec_ref[0:1])
        hidden_ref[...] = hidden
        hidden_low_ref[...] = hidden.astype(LOW)
        stat_ref[...] = jnp.concatenate(
            [row_sum(grad_first * normed), row_sum(grad_first), row_sum(hidden), jnp.zeros((5, hidden.shape[1]), WIDE)],
            axis=0,
        )


def attend_back_unit(layout, micro, place, hidden_low, weights, proj, probs_of, context):
    slot_count = hidden_low.shape[0]
    row_item, _ = slot_codes(layout, micro, place, slot_count, (slot_count, 1), 0)
    key_item, key_live = slot_codes(layout, micro, place, slot_count, (1, slot_count), 1)
    key_code = jnp.where(key_live, key_item, -1)
    grad_context = dot_nn(hidden_low, weights[:, 8 * HEAD_DIM :]).astype(LOW)
    scale = HEAD_DIM ** (-0.5)
    grads = [None] * 12
    for head in range(CHUNK_HEADS):
        query, key = piece(proj, 2 * head), piece(proj, 2 * head + 1)
        probs = probs_of[head]
        grad_head = piece(grad_context, OUT_AT[head] - 8)
        grads[VALUE_AT[head]] = dot_tn(probs, grad_head).astype(LOW)
        grad_probs = dot_nt(grad_head, piece(proj, VALUE_AT[head]))
        wide = probs.astype(WIDE)
        inner = jnp.sum(wide * grad_probs, axis=-1, keepdims=True)
        grad_scores = jnp.where(row_item == key_code, wide * (grad_probs - inner), 0.0).astype(LOW)
        grads[2 * head] = (dot_nn(grad_scores, key) * scale).astype(LOW)
        grads[2 * head + 1] = (dot_tn(grad_scores, query) * scale).astype(LOW)
    zero = jnp.zeros_like(grads[0])
    for at in OUT_AT:
        grads[at] = zero
    slab = jnp.concatenate(grads, axis=1)
    back = dot_nt(slab, weights)
    sums = row_sum(slab.astype(WIDE))
    for at in OUT_AT:
        grads[at] = piece(context, at - 8)
    return jnp.concatenate(grads, axis=1), back, sums


def attend_back_kernel(micro, place, bucket, lengths, counts, hidden_ref, hidden_low_ref, w_ref, proj_ref, prob_ref,
                       context_ref, grad_ref, out_ref, stat_ref, total):
    step = pl.program_id(0)
    slab, back, sums = attend_back_unit((bucket, lengths, counts), micro, place[0], hidden_low_ref[...], w_ref[0, 0],
                                        proj_ref[0], prob_ref, context_ref[0])
    grad_ref[0] = slab
    stat_ref[0] = jnp.broadcast_to(sums, stat_ref.shape[1:])

    @pl.when(step == 0)
    def _():
        total[...] = back + hidden_ref[...]

    @pl.when(step > 0)
    def _():
        total[...] += back

    @pl.when(step == pl.num_programs(0) - 1)
    def _():
        out_ref[...] = total[...].astype(LOW)


def params(vmem=VMEM_LIMIT):
    return pltpu.CompilerParams(dimension_semantics=("arbitrary",), vmem_limit_bytes=vmem)


def attend(micro, place, bucket, lengths, counts, inputs, weights, bias, vectors, slot_count):
    parts, width = weights.shape[1], weights.shape[2]
    wide_slab = weights.shape[3]
    heads = parts * CHUNK_HEADS
    whole = lambda *shape: pl.BlockSpec(shape, lambda j, p, b, l, c: (0,) * len(shape))
    return pl.pallas_call(
        functools.partial(attend_kernel, micro),
        grid_spec=pltpu.PrefetchScalarGridSpec(
            num_scalar_prefetch=4,
            grid=(parts,),
            in_specs=[
                pl.BlockSpec((1, slot_count, width), lambda j, p, b, l, c: (micro, p[0], 0)),
                pl.BlockSpec((1, 1, width, wide_slab), lambda j, p, b, l, c: (0, j, 0, 0)),
                pl.BlockSpec((1, 1, wide_slab), lambda j, p, b, l, c: (j, 0, 0)),
                whole(*vectors.shape),
            ],
            out_specs=[
                whole(slot_count, width),
                whole(slot_count, 128),
                pl.BlockSpec((1, slot_count, wide_slab), lambda j, p, b, l, c: (j, 0, 0)),
                pl.BlockSpec((CHUNK_HEADS, slot_count, slot_count), lambda j, p, b, l, c: (j, 0, 0)),
                pl.BlockSpec((1, slot_count, 4 * HEAD_DIM), lambda j, p, b, l, c: (j, 0, 0)),
            ],
            scratch_shapes=[pltpu.VMEM((slot_count, width), WIDE)],
        ),
        out_shape=[
            jax.ShapeDtypeStruct((slot_count, width), WIDE),
            jax.ShapeDtypeStruct((slot_count, 128), WIDE),
            jax.ShapeDtypeStruct((parts, slot_count, wide_slab), LOW),
            jax.ShapeDtypeStruct((heads, slot_count, slot_count), LOW),
            jax.ShapeDtypeStruct((parts, slot_count, 4 * HEAD_DIM), LOW),
        ],
        compiler_params=params(),
        name="attend",
        cost_estimate=takes(16),
    )(place, bucket, lengths, counts, inputs, weights, bias, vectors)


def ffn(micro, place, bucket, lengths, counts, normed, cotangent, weights, bias, vectors):
    parts, width, cols = weights.shape[1:]
    normed, index = normed
    slot_count = normed.shape[1]
    whole = lambda *shape: pl.BlockSpec(shape, lambda j, p, b, l, c: (0,) * len(shape))
    each = pl.BlockSpec((1, slot_count, cols), lambda j, p, b, l, c: (j, 0, 0))
    return pl.pallas_call(
        functools.partial(ffn_kernel, micro),
        grid_spec=pltpu.PrefetchScalarGridSpec(
            num_scalar_prefetch=4,
            grid=(parts,),
            in_specs=[
                pl.BlockSpec((None, slot_count, width), lambda j, p, b, l, c: (index, 0, 0)),
                pl.BlockSpec((1, slot_count, width), lambda j, p, b, l, c: (micro, p[0], 0)),
                pl.BlockSpec((1, 1, width, cols), lambda j, p, b, l, c: (1, j, 0, 0)),
                pl.BlockSpec((1, 1, width, cols), lambda j, p, b, l, c: (2, j, 0, 0)),
                pl.BlockSpec((1, 1, cols), lambda j, p, b, l, c: (j, 0, 0)),
                whole(*vectors.shape),
            ],
            out_specs=[each, each, whole(slot_count, width), whole(slot_count, width), whole(slot_count, width), whole(8, width)],
            scratch_shapes=[pltpu.VMEM((slot_count, width), LOW), pltpu.VMEM((slot_count, width), WIDE)],
        ),
        out_shape=[
            jax.ShapeDtypeStruct((parts, slot_count, cols), LOW),
            jax.ShapeDtypeStruct((parts, slot_count, cols), LOW),
            jax.ShapeDtypeStruct((slot_count, width), LOW),
            jax.ShapeDtypeStruct((slot_count, width), WIDE),
            jax.ShapeDtypeStruct((slot_count, width), LOW),
            jax.ShapeDtypeStruct((8, width), WIDE),
        ],
        compiler_params=params(),
        name="ffn",
        cost_estimate=takes(16),
    )(place, bucket, lengths, counts, normed, cotangent, weights, weights, bias, vectors)


def ffn_back(second, second_low, slope, weights, normed, inverse, vectors):
    parts, width, cols = weights.shape[1:]
    (normed, index), (inverse, _) = normed, inverse
    slot_count = normed.shape[1]
    whole = lambda *shape: pl.BlockSpec(shape, lambda j: (0,) * len(shape))
    each = pl.BlockSpec((1, slot_count, cols), lambda j: (j, 0, 0))
    return pl.pallas_call(
        ffn_back_kernel,
        grid=(parts,),
        in_specs=[
            whole(slot_count, width),
            whole(slot_count, width),
            each,
            pl.BlockSpec((1, 1, width, cols), lambda j: (1, j, 0, 0)),
            pl.BlockSpec((1, 1, width, cols), lambda j: (2, j, 0, 0)),
            pl.BlockSpec((None, slot_count, width), lambda j: (index, 0, 0)),
            pl.BlockSpec((None, slot_count, 128), lambda j: (index, 0, 0)),
            whole(*vectors.shape),
        ],
        out_specs=[each, whole(slot_count, width), whole(slot_count, width),
                   pl.BlockSpec((1, 8, cols), lambda j: (j, 0, 0)), whole(8, width)],
        scratch_shapes=[pltpu.VMEM((slot_count, width), WIDE)],
        out_shape=[
            jax.ShapeDtypeStruct((parts, slot_count, cols), LOW),
            jax.ShapeDtypeStruct((slot_count, width), WIDE),
            jax.ShapeDtypeStruct((slot_count, width), LOW),
            jax.ShapeDtypeStruct((parts, 8, cols), WIDE),
            jax.ShapeDtypeStruct((8, width), WIDE),
        ],
        compiler_params=params(),
        name="ffn_back",
        cost_estimate=takes(14),
    )(second, second_low, slope, weights, weights, normed, inverse, vectors)


def attend_back(micro, place, bucket, lengths, counts, hidden, hidden_low, weights, proj, probs, context):
    parts, width = weights.shape[1], weights.shape[2]
    wide_slab = weights.shape[3]
    slot_count = hidden.shape[0]
    (proj, index), (probs, _), (context, _) = proj, probs, context
    whole = lambda *shape: pl.BlockSpec(shape, lambda j, p, b, l, c: (0,) * len(shape))
    each = pl.BlockSpec((1, slot_count, wide_slab), lambda j, p, b, l, c: (j, 0, 0))
    return pl.pallas_call(
        functools.partial(attend_back_kernel, micro),
        grid_spec=pltpu.PrefetchScalarGridSpec(
            num_scalar_prefetch=4,
            grid=(parts,),
            in_specs=[
                whole(slot_count, width),
                whole(slot_count, width),
                pl.BlockSpec((1, 1, width, wide_slab), lambda j, p, b, l, c: (0, j, 0, 0)),
                pl.BlockSpec((None, 1, slot_count, wide_slab), lambda j, p, b, l, c: (index, j, 0, 0)),
                pl.BlockSpec((None, CHUNK_HEADS, slot_count, slot_count), lambda j, p, b, l, c: (index, j, 0, 0)),
                pl.BlockSpec((None, 1, slot_count, 4 * HEAD_DIM), lambda j, p, b, l, c: (index, j, 0, 0)),
            ],
            out_specs=[each, whole(slot_count, width), pl.BlockSpec((1, 8, wide_slab), lambda j, p, b, l, c: (j, 0, 0))],
            scratch_shapes=[pltpu.VMEM((slot_count, width), WIDE)],
        ),
        out_shape=[
            jax.ShapeDtypeStruct((parts, slot_count, wide_slab), LOW),
            jax.ShapeDtypeStruct((slot_count, width), LOW),
            jax.ShapeDtypeStruct((parts, 8, wide_slab), WIDE),
        ],
        compiler_params=params(),
        name="attend_back",
        cost_estimate=takes(22),
    )(place, bucket, lengths, counts, hidden, hidden_low, weights, proj, probs, context)


def weight_grads_kernel(blocks, place, *refs):
    normed = refs[:blocks]
    second_low, hidden_low, act, grad_up, head_grads, tokens = [refs[(k + 1) * blocks : (k + 2) * blocks] for k in range(6)]
    vec_ref, out_ref = refs[7 * blocks], refs[7 * blocks + 1]
    turned = refs[7 * blocks + 2]
    step = pl.program_id(0)
    slot_count = second_low[0].shape[0]

    @pl.when(step == 0)
    def _():
        for b in range(blocks):
            span = slice(b * slot_count, (b + 1) * slot_count)
            first = (normed[b][...] * vec_ref[0:1] + vec_ref[3:4]).astype(LOW)
            turned[0, :, span] = tokens[b][0].T
            turned[1, :, span] = first.T
            turned[2, :, span] = second_low[b][...].T
            turned[3, :, span] = hidden_low[b][...].T

    grads = jnp.concatenate([ref[0] for ref in head_grads], axis=0)
    qkv = dot_nn(turned[0], grads)
    outs = dot_nn(turned[3], grads[:, 8 * HEAD_DIM :])
    lane = lax.broadcasted_iota(jnp.int32, (1, 2 * HEAD_DIM), 1)
    last = jnp.where(lane < HEAD_DIM, qkv[:, 10 * HEAD_DIM :], outs[:, 2 * HEAD_DIM :])
    out_ref[0, 0] = jnp.concatenate([qkv[:, : 8 * HEAD_DIM], outs[:, : 2 * HEAD_DIM], last], axis=1).astype(LOW)
    out_ref[1, 0] = dot_nn(turned[1], jnp.concatenate([ref[0] for ref in grad_up], axis=0)).astype(LOW)
    out_ref[2, 0] = dot_nn(turned[2], jnp.concatenate([ref[0] for ref in act], axis=0)).astype(LOW)


def weight_grads(place, inputs, normed, second_low, hidden_low, act, grad_up, head_grads, vectors):
    blocks = len(normed)
    normed_specs = [
        pl.BlockSpec((None,) + array.shape[1:], lambda j, p, index=index: (index, 0, 0)) for array, index in normed
    ]
    normed = [array for array, _ in normed]
    micro_count = inputs.shape[0]
    per_micro = blocks // micro_count
    parts, slot_count, cols = act[0].shape
    width = normed[0].shape[2]
    whole = lambda *shape: pl.BlockSpec(shape, lambda j, p: (0,) * len(shape))
    each = pl.BlockSpec((1, slot_count, cols), lambda j, p: (j, 0, 0))
    token_specs = [
        pl.BlockSpec((1, slot_count, width), lambda j, p, m=b // per_micro, k=b % per_micro: (m, p[0] + k, 0))
        for b in range(blocks)
    ]
    return pl.pallas_call(
        functools.partial(weight_grads_kernel, blocks),
        grid_spec=pltpu.PrefetchScalarGridSpec(
            num_scalar_prefetch=1,
            grid=(parts,),
            in_specs=normed_specs + [whole(slot_count, width)] * (2 * blocks) + [each] * (3 * blocks) + token_specs + [whole(*vectors.shape)],
            out_specs=pl.BlockSpec((3, 1, width, cols), lambda j, p: (0, j, 0, 0)),
            scratch_shapes=[pltpu.VMEM((4, width, blocks * slot_count), LOW)],
        ),
        out_shape=jax.ShapeDtypeStruct((3, parts, width, cols), LOW),
        compiler_params=params(),
        name="weight_grads",
        cost_estimate=takes(26),
    )(place, *normed, *second_low, *hidden_low, *act, *grad_up, *head_grads, *([inputs] * blocks), vectors)


def mesh_place(bits):
    d = lax.axis_index("dp")
    t = lax.axis_index("tensor")
    digits = [(d // (1 << k)) % 2 for k in range(bits)]
    mates = [d + (1 - 2 * digits[k]) * (1 << k) for k in range(bits)]
    return d, t, digits, mates


def digit_index(bits, digits, open_bits):
    return tuple(slice(None) if k in open_bits else digits[k] for k in reversed(range(bits)))


def greet(d, t, mates, parts):
    barrier = pltpu.get_barrier_semaphore()
    for mate in mates:
        pl.semaphore_signal(barrier, inc=1, device_id=(mate, t), device_id_type=MESH)
    for hop in range(1, parts):
        pl.semaphore_signal(barrier, inc=1, device_id=(d, (t + hop) % parts), device_id_type=MESH)
    pl.semaphore_wait(barrier, len(mates) + parts - 1)


def bit_order(bits, flip):
    far = list(range(1, bits))
    return (far[::-1] if flip else far) + [0]


def gather_kernel(parts, bits, own, small, full, small_dp, small_t, z_send, z_recv, h_send, h_recv, s_send, s_recv, keep):
    d, t, digits, mates = mesh_place(bits)
    slab_count = own.shape[0]
    mine = digit_index(bits, digits, ())
    greet(d, t, mates, parts)
    offsets = [0] + [sign * hop for hop in range(1, parts) for sign in (1, -1)]
    pending = []

    def remote(src, dst, send, recv, to):
        return pltpu.make_async_remote_copy(src, dst, send, recv, device_id=to, device_id_type=MESH)

    local = [pltpu.make_async_copy(own.at[s], full.at[(s, t) + mine], keep.at[s]) for s in range(slab_count)]
    local.append(pltpu.make_async_copy(small.at[0], small_dp.at[mine], keep.at[slab_count]))
    local.append(pltpu.make_async_copy(small.at[1], small_t.at[t], keep.at[slab_count + 1]))
    for copy in local:
        copy.start()

    def z_copy(s, at, src, up):
        to = (d, t + 1) if up else (d, t - 1)
        way = 0 if up else 1
        return remote(src, full.at[(s, at) + mine], z_send.at[s, at, way], z_recv.at[s, at], to)

    def h_copy(s, index, step):
        offset = offsets[index]
        order = bit_order(bits, (abs(offset) + s) % 2 == 1)
        blocks = (s, t + offset) + digit_index(bits, digits, order[:step])
        src = own.at[s] if offset == 0 and step == 0 else full.at[blocks]
        return remote(src, full.at[blocks], h_send.at[s, index, step], h_recv.at[s, index, step], (mates[order[step]], t))

    def exists(offset):
        return (t + offset >= 0) & (t + offset < parts)

    def begin(s, index):
        offset = offsets[index]
        if offset == 0:
            h_copy(s, index, 0).start()
            return

        @pl.when(exists(offset))
        def _():
            up = offset < 0
            z_copy(s, t + offset, own.at[s], up).wait_recv()

            @pl.when((t < parts - 1) if up else (t > 0))
            def _():
                z_copy(s, t + offset, full.at[(s, t + offset) + mine], up).start()

            h_copy(s, index, 0).start()

    def advance(s, index, step):
        @pl.when(exists(offsets[index]))
        def _():
            h_copy(s, index, step - 1).wait_recv()
            if step < bits:
                h_copy(s, index, step).start()

    def small_step(step):
        blocks = digit_index(bits, digits, range(step))
        src = small.at[0] if step == 0 else small_dp.at[blocks]
        return remote(src, small_dp.at[blocks], s_send.at[step], s_recv.at[step], (mates[step], t))

    def small_hop(hop):
        peer = (d, (t + hop) % parts)
        return remote(small.at[1], small_t.at[t], s_send.at[bits + hop - 1], s_recv.at[bits + hop - 1], peer)

    def send_own(s):
        @pl.when(t < parts - 1)
        def _():
            z_copy(s, t, own.at[s], True).start()

        @pl.when(t > 0)
        def _():
            z_copy(s, t, own.at[s], False).start()

    order = [(s, hop) for s in range(slab_count) for hop in range(parts)]
    groups = [(s, [index for index, offset in enumerate(offsets) if abs(offset) == hop]) for s, hop in order]
    send_own(0)
    begin(0, 0)
    for hop in range(1, parts):
        small_hop(hop).start()
    small_step(0).start()
    for copy in local:
        copy.wait()
    for wave in range(len(groups) + bits * GATHER_LAG):
        for step in range(bits + 1):
            if 0 <= wave - step * GATHER_LAG < len(groups):
                s, indices = groups[wave - step * GATHER_LAG]
                for index in indices:
                    if step:
                        advance(s, index, step)
                    elif (s, index) != (0, 0):
                        begin(s, index)
        if wave in Z_WAVES:
            send_own(1 + Z_WAVES.index(wave))
        if wave < bits:
            small_step(wave).wait_recv()
            if wave + 1 < bits:
                small_step(wave + 1).start()

    for hop in range(1, parts):
        small_hop(hop).wait()
    for step in range(bits):
        small_step(step).wait_send()
    for s, indices in groups:
        for index in indices:
            offset = offsets[index]

            @pl.when(exists(offset))
            def _():
                for step in range(bits):
                    h_copy(s, index, step).wait_send()
                if offset <= 0:
                    @pl.when(t < parts - 1)
                    def _():
                        z_copy(s, t + offset, own.at[s], True).wait_send()
                if offset >= 0:
                    @pl.when(t > 0)
                    def _():
                        z_copy(s, t + offset, own.at[s], False).wait_send()


def gather_weights(own, small, parts, dp_count):
    bits = dp_count.bit_length() - 1
    slab_count, rows, columns = own.shape
    places = 2 * parts - 1
    low = jnp.bfloat16
    full, small_dp, small_t = pl.pallas_call(
        functools.partial(gather_kernel, parts, bits),
        out_shape=[
            jax.ShapeDtypeStruct((slab_count, parts) + (2,) * bits + (rows, columns), low),
            jax.ShapeDtypeStruct((2,) * bits + small.shape[1:], low),
            jax.ShapeDtypeStruct((parts,) + small.shape[1:], low),
        ],
        in_specs=[pl.BlockSpec(memory_space=pl.ANY)] * 2,
        out_specs=[pl.BlockSpec(memory_space=pl.ANY)] * 3,
        scratch_shapes=[
            pltpu.SemaphoreType.DMA((slab_count, parts, 2)),
            pltpu.SemaphoreType.DMA((slab_count, parts)),
            pltpu.SemaphoreType.DMA((slab_count, places, bits)),
            pltpu.SemaphoreType.DMA((slab_count, places, bits)),
            pltpu.SemaphoreType.DMA((bits + parts - 1,)),
            pltpu.SemaphoreType.DMA((bits + parts - 1,)),
            pltpu.SemaphoreType.DMA((slab_count + 2,)),
        ],
        compiler_params=pltpu.CompilerParams(collective_id=0, has_side_effects=True, vmem_limit_bytes=VMEM_LIMIT),
        name="gather_weights",
        cost_estimate=takes(100),
    )(own, small)
    full = full.reshape(slab_count, parts, dp_count * rows, columns)
    return full, small_dp.reshape((dp_count,) + small.shape[1:]), small_t


def add_rows(target, first, second, rows):
    lead = target.shape[:-2]
    chunk = 16 if rows % 16 == 0 else rows
    steps = rows // chunk
    count = 1
    for extent in lead:
        count *= extent

    def one(i, carry):
        at, rest = [], i // steps
        for extent in reversed(lead):
            at.insert(0, rest % extent)
            rest = rest // extent
        where = tuple(at) + (pl.ds(pl.multiple_of((i % steps) * chunk, chunk), chunk),)
        total = first[where].astype(jnp.float32) + second[where].astype(jnp.float32)
        target[where] = total.astype(target.dtype)
        return carry

    lax.fori_loop(0, count * steps, one, 0)


def reduce_kernel(parts, bits, grads, small, out, small_out, *scratch):
    bufs = scratch[:bits]
    z_up, z_down, small_buf, small_sum = scratch[bits:bits + 4]
    h_send, h_recv, up_send, up_recv, down_send, down_recv, s_send, s_recv = scratch[bits + 4:]
    d, t, digits, mates = mesh_place(bits)
    slab_count = grads.shape[0]
    rows = grads.shape[-2]
    greet(d, t, mates, parts)
    items = [(s, at) for s in range(slab_count) for at in range(parts)]
    small_bits = bits + parts.bit_length() - 1

    def remote(src, dst, send, recv, to):
        return pltpu.make_async_remote_copy(src, dst, send, recv, device_id=to, device_id_type=MESH)

    def order_of(number):
        s, at = items[number]
        return bit_order(bits, (s + at) % 2 == 1)[::-1]

    def held(number, step):
        s, at = items[number]
        return grads.at[s, at] if step == 0 else bufs[step - 1].at[number]

    def part_of(number, step, side):
        order = order_of(number)
        left = [k for k in reversed(range(bits)) if k not in order[:step]]
        pick = tuple(side if k == order[step] else slice(None) for k in left)
        return held(number, step).at[pick]

    def h_copy(number, step):
        order = order_of(number)
        digit = digits[order[step]]
        return remote(part_of(number, step, 1 - digit), bufs[step].at[number],
                      h_send.at[number, step], h_recv.at[number, step], (mates[order[step]], t))

    def fold(number, step):
        h_copy(number, step).wait_recv()
        digit = digits[order_of(number)[step]]
        add_rows(bufs[step].at[number], bufs[step].at[number], part_of(number, step, digit), rows)

    def summed(s, at):
        return bufs[bits - 1].at[s * parts + at]

    def z_copy(s, at, up, src):
        buf, send, recv = (z_up, up_send, up_recv) if up else (z_down, down_send, down_recv)
        to = (d, t + 1) if up else (d, t - 1)
        return remote(src, buf.at[s, at], send.at[s, at], recv.at[s, at], to)

    def z_pass(s, hop, up):
        at = t + hop if up else t - hop
        edge = (t == 0) if up else (t == parts - 1)
        buf = z_up if up else z_down

        @pl.when((at < parts) if up else (at >= 0))
        def _():
            @pl.when(edge)
            def _():
                z_copy(s, at, up, summed(s, at)).start()

            @pl.when(jnp.logical_not(edge))
            def _():
                z_copy(s, at, up, summed(s, at)).wait_recv()
                add_rows(buf.at[s, at], buf.at[s, at], summed(s, at), rows)
                z_copy(s, at, up, buf.at[s, at]).start()

    def z_finish(s):
        add_rows(out.at[s], summed(s, t), summed(s, t), rows)

        def scaled(i, carry):
            out[s] = out[s] * 0.5
            return carry
        lax.fori_loop(0, 1, scaled, 0)
        for up, buf in ((True, z_up), (False, z_down)):
            @pl.when((t > 0) if up else (t < parts - 1))
            def _():
                z_copy(s, t, up, summed(s, t)).wait_recv()
                add_rows(out.at[s], out.at[s], buf.at[s, t], rows)

    def small_copy(step):
        if step < bits:
            to = (mates[step], t)
        else:
            gap = 1 << (step - bits)
            to = (d, t + (1 - 2 * ((t // gap) % 2)) * gap)
        src = small if step == 0 else small_sum.at[step - 1]
        return remote(src, small_buf.at[step], s_send.at[step], s_recv.at[step], to)

    def small_fold(step):
        small_copy(step).wait_recv()
        before = small[...] if step == 0 else small_sum[step - 1]
        small_sum[step] = before + small_buf[step]
        if step + 1 < small_bits:
            small_copy(step + 1).start()

    for number in range(len(items)):
        h_copy(number, 0).start()
        if number == 0:
            small_copy(0).start()
    for wave in range(len(items) + bits * REDUCE_LAG + parts + 1):
        for step in range(bits):
            number = wave - step * REDUCE_LAG
            if 0 <= number < len(items):
                fold(number, step)
                if step + 1 < bits:
                    h_copy(number, step + 1).start()
        for s in range(slab_count):
            phase = wave - ((s + 1) * parts - 1 + bits * REDUCE_LAG)
            if 0 <= phase < parts - 1:
                z_pass(s, parts - 1 - phase, True)
                z_pass(s, parts - 1 - phase, False)
            elif phase == parts - 1:
                z_finish(s)
        if wave < small_bits:
            small_fold(wave)
    small_out[...] = small_sum[small_bits - 1]

    for step in range(small_bits):
        small_copy(step).wait_send()
    for number in range(len(items)):
        for step in range(bits):
            h_copy(number, step).wait_send()
    for s in range(slab_count):
        for hop in range(1, parts):
            @pl.when(t + hop < parts)
            def _():
                z_copy(s, t + hop, True, summed(s, t)).wait_send()

            @pl.when(t - hop >= 0)
            def _():
                z_copy(s, t - hop, False, summed(s, t)).wait_send()


def reduce_grads(grads, small, parts, dp_count):
    bits = dp_count.bit_length() - 1
    slab_count, columns = grads.shape[0], grads.shape[-1]
    rows = grads.shape[2] // dp_count
    grads = grads.reshape((slab_count, parts) + (2,) * bits + (rows, columns))
    low = jnp.bfloat16
    count = slab_count * parts
    small_bits = bits + parts.bit_length() - 1
    dma = pltpu.SemaphoreType.DMA
    return pl.pallas_call(
        functools.partial(reduce_kernel, parts, bits),
        out_shape=[
            jax.ShapeDtypeStruct((slab_count, rows, columns), jnp.float32),
            jax.ShapeDtypeStruct(small.shape, jnp.float32),
        ],
        in_specs=[pl.BlockSpec(memory_space=pltpu.VMEM)] * 2,
        out_specs=[pl.BlockSpec(memory_space=pltpu.VMEM)] * 2,
        scratch_shapes=[pltpu.VMEM((count,) + (2,) * (bits - 1 - step) + (rows, columns), low) for step in range(bits)]
        + [pltpu.VMEM((slab_count, parts, rows, columns), low)] * 2
        + [pltpu.VMEM((small_bits,) + small.shape, jnp.float32)] * 2
        + [dma((count, bits)), dma((count, bits))]
        + [dma((slab_count, parts))] * 4
        + [dma((small_bits,))] * 2,
        compiler_params=pltpu.CompilerParams(collective_id=1, has_side_effects=True, vmem_limit_bytes=VMEM_LIMIT),
        name="reduce_grads",
        cost_estimate=takes(100),
    )(grads, small)


def forward_kernel(parts, bits, micro_count, per_micro, slot_count, w_qkv, w_out, w_in, w_down, head_bias, ffn_bias,
                   norm_gains, row_biases, bucket, lengths, counts, inputs, cotangent,
                   weights, vectors, head_rows, ffn_rows, normed_out, inverse_out, proj_out, prob_out, context_out,
                   act_out, slope_out, out_out, second_out, second_low_out, stat_out,
                   own, small, full, small_dp, small_t, tokens, cot, total, normed_buf, inverse_buf, proj_buf, prob_buf, context_buf,
                   act_buf, slope_buf, first_low, down_total, out_buf, second_buf, second_low_buf,
                   z_send, z_recv, h_send, h_recv, s_send, s_recv, keep, load, weight_done, unit_done, ffn_done, end_done):
    layout = (bucket, lengths, counts)
    d, t, digits, mates = mesh_place(bits)
    blocks = micro_count * per_micro
    slab_count = own.shape[0]
    width = own.shape[2]
    mine = digit_index(bits, digits, ())

    def block_place(b):
        return b // per_micro, t * per_micro + b % per_micro

    def block_rows(b):
        micro, place = block_place(b)
        return (micro, pl.ds(pl.multiple_of(place * slot_count, slot_count), slot_count))

    loads = [pltpu.make_async_copy(inputs.at[block_rows(b)], tokens.at[b], load.at[b]) for b in range(blocks)]
    loads.append(pltpu.make_async_copy(cotangent.at[block_rows(0)], cot, load.at[blocks]))
    own[0] = slab_order(w_qkv[0], w_qkv[1], w_qkv[2], w_out[...].T)
    own[1] = w_in[...]
    own[2] = w_down[...]
    small[...] = jnp.zeros_like(small)
    vector_count = norm_gains.shape[0] + row_biases.shape[0]
    small[0, :, : own.shape[1]] = jnp.concatenate(
        [norm_gains[...], row_biases[...], jnp.zeros((16 - vector_count, own.shape[1]), LOW)], axis=0
    )
    no_bias = jnp.zeros((1, head_bias.shape[1]), LOW)
    bias_row = slab_order(head_bias[0:1], no_bias, head_bias[1:2], no_bias)
    small[1] = jnp.concatenate([bias_row, ffn_bias[...].reshape(1, -1), jnp.zeros((14, own.shape[2]), LOW)], axis=0)
    greet(d, t, mates, parts)
    offsets = [0] + [sign * hop for hop in range(1, parts) for sign in (1, -1)]

    def remote(src, dst, send, recv, to):
        return pltpu.make_async_remote_copy(src, dst, send, recv, device_id=to, device_id_type=MESH)

    local = [pltpu.make_async_copy(own.at[s], full.at[(s, t) + mine], keep.at[s]) for s in range(slab_count)]
    local.append(pltpu.make_async_copy(small.at[0], small_dp.at[mine], keep.at[slab_count]))
    local.append(pltpu.make_async_copy(small.at[1], small_t.at[t], keep.at[slab_count + 1]))

    def z_copy(s, at, src, up):
        to = (d, t + 1) if up else (d, t - 1)
        return remote(src, full.at[(s, at) + mine], z_send.at[s, at, 0 if up else 1], z_recv.at[s, at], to)

    def h_copy(s, index, step):
        offset = offsets[index]
        order = bit_order(bits, (abs(offset) + s) % 2 == 1)
        where = (s, t + offset) + digit_index(bits, digits, order[:step])
        src = own.at[s] if offset == 0 and step == 0 else full.at[where]
        return remote(src, full.at[where], h_send.at[s, index, step], h_recv.at[s, index, step], (mates[order[step]], t))

    def exists(offset):
        return (t + offset >= 0) & (t + offset < parts)

    def weight_copy(s, at):
        return pltpu.make_async_copy(full.at[s, at], weights.at[s, at], weight_done.at[s, at])

    def begin(s, index):
        offset = offsets[index]
        if offset == 0:
            h_copy(s, index, 0).start()
            return

        @pl.when(exists(offset))
        def _():
            up = offset < 0
            z_copy(s, t + offset, own.at[s], up).wait_recv()

            @pl.when((t < parts - 1) if up else (t > 0))
            def _():
                z_copy(s, t + offset, full.at[(s, t + offset) + mine], up).start()

            h_copy(s, index, 0).start()

    def advance(s, index, step):
        @pl.when(exists(offsets[index]))
        def _():
            h_copy(s, index, step - 1).wait_recv()
            if step < bits:
                h_copy(s, index, step).start()
            else:
                weight_copy(s, t + offsets[index]).start()

    def small_step(step):
        where = digit_index(bits, digits, range(step))
        src = small.at[0] if step == 0 else small_dp.at[where]
        return remote(src, small_dp.at[where], s_send.at[step], s_recv.at[step], (mates[step], t))

    def small_hop(hop):
        peer = (d, (t + hop) % parts)
        return remote(small.at[1], small_t.at[t], s_send.at[bits + hop - 1], s_recv.at[bits + hop - 1], peer)

    def send_own(s):
        @pl.when(t < parts - 1)
        def _():
            z_copy(s, t, own.at[s], True).start()

        @pl.when(t > 0)
        def _():
            z_copy(s, t, own.at[s], False).start()

    toward = 1 - 2 * ((2 * t) // parts)

    def nearest(k):
        return (t + toward * k + parts) % parts

    def matrix(s, at):
        return full[s, at].reshape(width, full.shape[-1])

    def unit_copies(unit, at, b):
        slot = unit % 2
        heads = pl.ds(at * CHUNK_HEADS, CHUNK_HEADS)
        return [
            pltpu.make_async_copy(proj_buf.at[slot], proj_out.at[b, at], unit_done.at[slot, 0]),
            pltpu.make_async_copy(prob_buf.at[slot], prob_out.at[b, heads], unit_done.at[slot, 1]),
            pltpu.make_async_copy(context_buf.at[slot], context_out.at[b, at], unit_done.at[slot, 2]),
        ]

    def attend_part(b, k):
        unit = b * parts + k
        at = nearest(k)
        if unit >= 2:
            for copy in unit_copies(unit - 2, nearest((unit - 2) % parts), (unit - 2) // parts):
                copy.wait()
        slot = unit % 2
        micro, place = block_place(b)
        attention = attend_unit(layout, micro, place, tokens[b], matrix(0, at), head_rows[at],
                                proj_buf.at[slot], prob_buf.at[slot], context_buf.at[slot])
        if k == 0:
            total[...] = attention
        else:
            total[...] += attention
        for copy in unit_copies(unit, at, b):
            copy.start()
        if k == parts - 1:
            normed, inverse = normalize(tokens[b].astype(WIDE) + total[...] + vectors[2:3])
            normed_buf[b] = normed
            inverse_buf[b] = jnp.broadcast_to(inverse, inverse_buf.shape[1:])
            for copy in norm_copies(b):
                copy.start()

    def norm_copies(b):
        return [pltpu.make_async_copy(normed_buf.at[b], normed_out.at[b], end_done.at[b, 0]),
                pltpu.make_async_copy(inverse_buf.at[b], inverse_out.at[b], end_done.at[b, 1])]

    def ffn_copies(k):
        slot, at = k % 2, nearest(k)
        return [pltpu.make_async_copy(act_buf.at[slot], act_out.at[at], ffn_done.at[slot, 0]),
                pltpu.make_async_copy(slope_buf.at[slot], slope_out.at[at], ffn_done.at[slot, 1])]

    def final_copies():
        return [pltpu.make_async_copy(out_buf, out_out, end_done.at[blocks, 0]),
                pltpu.make_async_copy(second_buf, second_out, end_done.at[blocks, 1]),
                pltpu.make_async_copy(second_low_buf, second_low_out, end_done.at[blocks + 1, 0])]

    def ffn_part(k):
        at = nearest(k)
        if k == 0:
            first_low[...] = (normed_buf[0] * vectors[0:1] + vectors[3:4]).astype(LOW)
        if k >= 2:
            for copy in ffn_copies(k - 2):
                copy.wait()
        slot = k % 2
        down = ffn_unit(first_low[...], matrix(1, at), matrix(2, at), ffn_rows[at], act_buf.at[slot], slope_buf.at[slot])
        for copy in ffn_copies(k):
            copy.start()
        if k == 0:
            down_total[...] = down
        else:
            down_total[...] += down
        if k == parts - 1:
            micro, place = block_place(0)
            out, second, stat = second_norm(layout, micro, place, normed_buf[0], down_total[...], cot[...], vectors)
            out_buf[...] = out
            second_buf[...] = second
            second_low_buf[...] = second.astype(LOW)
            stat_out[...] = stat
            for copy in final_copies():
                copy.start()

    def finish_small():
        lanes = own.shape[1]
        pieces = [small_dp[digit_index(bits, [(i // (1 << k)) % 2 for k in range(bits)], ())][:8, :lanes].astype(WIDE)
                  for i in range(1 << bits)]
        vectors[...] = jnp.concatenate(pieces, axis=1)
        for at in range(parts):
            head_rows[at] = small_t[at, 0:1, :].astype(WIDE)
            ffn_rows[at] = small_t[at, 1:2, :].astype(WIDE)

    send_own(0)
    begin(0, 0)
    for hop in range(1, parts):
        small_hop(hop).start()
    small_step(0).start()
    for copy in local + loads:
        copy.start()
    for copy in local + loads:
        copy.wait()

    order = [(0, hop) for hop in range(parts)] + [(s, hop) for hop in range(parts) for s in range(1, slab_count)]
    groups = [(s, [index for index, offset in enumerate(offsets) if abs(offset) == hop]) for s, hop in order]
    done_at = {place: number + bits * GATHER_LAG for number, place in enumerate(order)}
    jobs = [(done_at[(0, k)], functools.partial(attend_part, b, k)) for b in range(blocks) for k in range(parts)]
    jobs += [(done_at[(slab_count - 1, k)], functools.partial(ffn_part, k)) for k in range(parts)]
    for wave in range(len(groups) + bits * GATHER_LAG):
        for step in range(bits + 1):
            if 0 <= wave - step * GATHER_LAG < len(groups):
                s, indices = groups[wave - step * GATHER_LAG]
                for index in indices:
                    if step:
                        advance(s, index, step)
                    elif (s, index) != (0, 0):
                        begin(s, index)
        if wave in Z_WAVES:
            send_own(1 + Z_WAVES.index(wave))
        if wave < bits:
            small_step(wave).wait_recv()
            if wave + 1 < bits:
                small_step(wave + 1).start()
            else:
                for hop in range(1, parts):
                    small_hop(hop).wait_recv()
                finish_small()
        if jobs and jobs[0][0] <= wave:
            jobs.pop(0)[1]()
    for _, job in jobs:
        job()

    for hop in range(1, parts):
        small_hop(hop).wait_send()
    for step in range(bits):
        small_step(step).wait_send()
    for s, indices in groups:
        for index in indices:
            offset = offsets[index]

            @pl.when(exists(offset))
            def _():
                for step in range(bits):
                    h_copy(s, index, step).wait_send()
                weight_copy(s, t + offset).wait()
                if offset <= 0:
                    @pl.when(t < parts - 1)
                    def _():
                        z_copy(s, t + offset, own.at[s], True).wait_send()
                if offset >= 0:
                    @pl.when(t > 0)
                    def _():
                        z_copy(s, t + offset, own.at[s], False).wait_send()
    last = blocks * parts
    for unit in range(max(0, last - 2), last):
        for copy in unit_copies(unit, nearest(unit % parts), unit // parts):
            copy.wait()
    for k in range(max(0, parts - 2), parts):
        for copy in ffn_copies(k):
            copy.wait()
    for b in range(blocks):
        for copy in norm_copies(b):
            copy.wait()
    for copy in final_copies():
        copy.wait()


def forward(arrays, layout, inputs, cotangent, parts, dp_count, slot_count, micro_count, per_micro):
    bits = dp_count.bit_length() - 1
    slab_count = 3
    rows, cols = arrays[2].shape
    width = rows * dp_count
    places = 2 * parts - 1
    blocks = micro_count * per_micro
    heads = parts * CHUNK_HEADS
    spread = (slab_count, parts) + (2,) * bits + (rows, cols)
    shape = jax.ShapeDtypeStruct
    dma = pltpu.SemaphoreType.DMA
    hbm, vmem, smem = [pl.BlockSpec(memory_space=space) for space in (pl.ANY, pltpu.VMEM, pltpu.SMEM)]
    slab = (slot_count, cols)
    rows_of = (slot_count, width)
    outs = [
        (spread, LOW, hbm),
        ((8, width), WIDE, vmem),
        ((parts, 1, cols), WIDE, vmem),
        ((parts, 1, cols), WIDE, vmem),
        ((blocks,) + rows_of, WIDE, hbm),
        ((blocks, slot_count, 128), WIDE, hbm),
        ((blocks, parts) + slab, LOW, hbm),
        ((blocks, heads, slot_count, slot_count), LOW, hbm),
        ((blocks, parts, slot_count, 4 * HEAD_DIM), LOW, hbm),
        ((parts,) + slab, LOW, hbm),
        ((parts,) + slab, LOW, hbm),
        (rows_of, LOW, hbm),
        (rows_of, WIDE, hbm),
        (rows_of, LOW, hbm),
        ((8, width), WIDE, vmem),
    ]
    result = pl.pallas_call(
        functools.partial(forward_kernel, parts, bits, micro_count, per_micro, slot_count),
        out_shape=[shape(dims, kind) for dims, kind, _ in outs],
        in_specs=[vmem] * len(arrays) + [smem, smem, smem, hbm, hbm],
        out_specs=[space for _, _, space in outs],
        scratch_shapes=[
            pltpu.VMEM((slab_count, rows, cols), LOW),
            pltpu.VMEM((2, 16, cols), LOW),
            pltpu.VMEM(spread, LOW),
            pltpu.VMEM((2,) * bits + (16, cols), LOW),
            pltpu.VMEM((parts, 16, cols), LOW),
            pltpu.VMEM((blocks,) + rows_of, LOW),
            pltpu.VMEM(rows_of, LOW),
            pltpu.VMEM(rows_of, WIDE),
            pltpu.VMEM((blocks,) + rows_of, WIDE),
            pltpu.VMEM((blocks, slot_count, 128), WIDE),
            pltpu.VMEM((2,) + slab, LOW),
            pltpu.VMEM((2, CHUNK_HEADS, slot_count, slot_count), LOW),
            pltpu.VMEM((2, slot_count, 4 * HEAD_DIM), LOW),
            pltpu.VMEM((2,) + slab, LOW),
            pltpu.VMEM((2,) + slab, LOW),
            pltpu.VMEM(rows_of, LOW),
            pltpu.VMEM(rows_of, WIDE),
            pltpu.VMEM(rows_of, LOW),
            pltpu.VMEM(rows_of, WIDE),
            pltpu.VMEM(rows_of, LOW),
            dma((slab_count, parts, 2)),
            dma((slab_count, parts)),
            dma((slab_count, places, bits)),
            dma((slab_count, places, bits)),
            dma((bits + parts - 1,)),
            dma((bits + parts - 1,)),
            dma((slab_count + 2,)),
            dma((blocks + 1,)),
            dma((slab_count, parts)),
            dma((2, 3)),
            dma((2, 2)),
            dma((blocks + 2, 2)),
        ],
        compiler_params=pltpu.CompilerParams(collective_id=2, has_side_effects=True, vmem_limit_bytes=VMEM_LIMIT),
        name="forward",
    )(*arrays, *layout, inputs, cotangent)
    return (result[0].reshape(slab_count, parts, width, cols),) + tuple(result[1:])


def phase_index(step, parts, uses):
    block = jnp.int32(uses[0][1])
    part = jnp.clip(step - uses[0][0] * parts, 0, parts - 1)
    for phase, b in uses[1:]:
        later = step >= phase * parts
        block = jnp.where(later, b, block)
        part = jnp.where(later, jnp.clip(step - phase * parts, 0, parts - 1), part)
    return block, part


def line_events(send, hand_on, blocks, parts, chunks, start):
    events = []
    for b in range(blocks):
        for q in range(chunks):
            events.append((start[b][0], functools.partial(send, b, q)))
            for hop in range(1, parts - 1):
                events.append((start[b][hop] + q, functools.partial(hand_on, b, hop, q)))
            events.append((start[b][parts - 2] + q + chunks, functools.partial(hand_on, b, parts - 1, q)))
    return events


def backward_kernel(parts, micro_count, per_micro, slot_count, chunks, phases, bucket, lengths, counts, stat_first, vectors,
                    ffn_rows, first_out, cotangent, w_head, w_in, w_down, normed, inverse, slope_first, second_first,
                    second_low_first, proj, probs, context,
                    line_out, act_out, second_low_out, up_out, hidden_low_out, head_out, token_out, small_out,
                    first_low, total, slope_buf, second_buf, second_low_buf, hidden_buf, hidden_low_buf, out_buf, cot,
                    g_send, g_recv, g_keep, load):
    layout = (bucket, lengths, counts)
    d = lax.axis_index("dp")
    t = lax.axis_index("tensor")
    step = pl.program_id(0)
    blocks = micro_count * per_micro
    chunk_rows = slot_count // chunks

    def block_place(b):
        return b // per_micro, t * per_micro + b % per_micro

    def line_rows(b, at, q):
        place = at * per_micro + b % per_micro
        start = pl.multiple_of(place * slot_count + q * chunk_rows, chunk_rows)
        return line_out.at[b // per_micro, pl.ds(start, chunk_rows)]

    def own_rows(b, q):
        source = first_out if b == 0 else out_buf.at[b - 1]
        return source.at[pl.ds(q * chunk_rows, chunk_rows)]

    def line_copy(b, at, q, src, up):
        to = (d, t + 1) if up else (d, t - 1)
        return pltpu.make_async_remote_copy(src, line_rows(b, at, q), g_send.at[b, at, q, 0 if up else 1], g_recv.at[b, at, q],
                                            device_id=to, device_id_type=MESH)

    def keep_copy(b, q):
        return pltpu.make_async_copy(own_rows(b, q), line_rows(b, t, q), g_keep.at[b, q])

    def line_send(b, q):
        for up in (True, False):
            @pl.when((t < parts - 1) if up else (t > 0))
            def _():
                line_copy(b, t, q, own_rows(b, q), up).start()
        keep_copy(b, q).start()

    def line_pass(b, hop, q):
        for up in (True, False):
            at = t - hop if up else t + hop

            @pl.when((at >= 0) if up else (at < parts))
            def _():
                line_copy(b, at, q, own_rows(b, q), up).wait_recv()

                @pl.when((t < parts - 1) if up else (t > 0))
                def _():
                    line_copy(b, at, q, line_rows(b, at, q), up).start()

    def line_settle(b, hop, q):
        for up in (True, False):
            at = t - hop if up else t + hop

            @pl.when(((at >= 0) if up else (at < parts)) & ((t < parts - 1) if up else (t > 0)))
            def _():
                line_copy(b, at, q, own_rows(b, q), up).wait_send()

    def cot_copy(b):
        micro, place = block_place(b)
        rows = pl.ds(pl.multiple_of(place * slot_count, slot_count), slot_count)
        return pltpu.make_async_copy(cotangent.at[micro, rows], cot.at[b - 1], load.at[b - 1])

    @pl.when(step == 0)
    def _():
        greet(d, t, [], parts)
        for b in range(1, blocks):
            cot_copy(b).start()
        small_out[...] = jnp.zeros_like(small_out)
        small_out[1:2] = stat_first[0:1]
        small_out[5:6] = stat_first[1:2]
        small_out[4:5] = stat_first[2:3]

    events = line_events(line_send, line_pass, blocks, parts, chunks, LINE_START)
    last_step = len(phases) * parts
    for when in sorted(set(at for at, _ in events)):
        if when < last_step:
            @pl.when(step == when)
            def _():
                for at, event in events:
                    if at == when:
                        event()

    def collect(part, value):
        @pl.when(part == 0)
        def _():
            total[...] = value

        @pl.when(part > 0)
        def _():
            total[...] += value

    def ffn_phase(b, part):
        @pl.when(part == 0)
        def _():
            first_low[...] = (normed[...] * vectors[0:1] + vectors[3:4]).astype(LOW)

        down = ffn_unit(first_low[...], w_in[0, 0], w_down[0, 0], ffn_rows[part], act_out.at[0, 0], slope_buf.at[b - 1, part])
        collect(part, down)

        @pl.when(part == parts - 1)
        def _():
            cot_copy(b).wait()
            micro, place = block_place(b)
            out, second, stat = second_norm(layout, micro, place, normed[...], total[...], cot[b - 1], vectors)
            out_buf[b - 1] = out
            second_buf[b - 1] = second
            second_low_buf[b - 1] = second.astype(LOW)
            second_low_out[0] = second.astype(LOW)
            small_out[1:2] += stat[0:1]
            small_out[5:6] += stat[1:2]
            small_out[4:5] += stat[2:3]

    def ffn_back_phase(b, part):
        second_low = second_low_first[...] if b == 0 else second_low_buf[b - 1]
        slope = slope_first[0] if b == 0 else slope_buf[b - 1, part]
        grad_act = dot_nn(second_low, w_down[0, 0])
        grad_up = (grad_act * slope.astype(WIDE)).astype(LOW)
        up_out[0, 0] = grad_up
        small_out[pl.ds(6 + part, 1)] += row_sum(grad_up.astype(WIDE))
        collect(part, dot_nt(grad_up, w_in[0, 0]))

        @pl.when(part == parts - 1)
        def _():
            grad_first = total[...] + (second_first[...] if b == 0 else second_buf[b - 1])
            unit = normed[...]
            hidden = norm_pullback(grad_first, unit, inverse[:, :1], vectors[0:1])
            hidden_buf[...] = hidden
            hidden_low_buf[...] = hidden.astype(LOW)
            hidden_low_out[0] = hidden.astype(LOW)
            small_out[0:1] += row_sum(grad_first * unit)
            small_out[3:4] += row_sum(grad_first)
            small_out[2:3] += row_sum(hidden)

    def attend_back_phase(b, part):
        micro, place = block_place(b)
        slab, back, sums = attend_back_unit(layout, micro, place, hidden_low_buf[...], w_head[0, 0], proj[0, 0], probs[0],
                                            context[0, 0])
        head_out[0, 0] = slab
        small_out[pl.ds(6 + parts + part, 1)] += sums
        collect(part, back)

        @pl.when(part == parts - 1)
        def _():
            token_out[0] = (total[...] + hidden_buf[...]).astype(LOW)

    kinds = {"ffn": ffn_phase, "ffn_back": ffn_back_phase, "attend_back": attend_back_phase}
    for number, (kind, b) in enumerate(phases):
        @pl.when((step >= number * parts) & (step < (number + 1) * parts))
        def _():
            kinds[kind](b, step - number * parts)

    @pl.when(step == last_step - 1)
    def _():
        for at, event in events:
            if at >= last_step:
                event()
        for b in range(blocks):
            for q in range(chunks):
                keep_copy(b, q).wait()
                for hop in range(parts - 1):
                    line_settle(b, hop, q)


def backward(layout, stat_first, vectors, ffn_rows, first_out, cotangent, weights, normed, inverse, slope_first, second_first,
             second_low_first, proj, probs, context, micro_count, per_micro):
    parts, width, cols = weights.shape[1:]
    blocks, slot_count = normed.shape[:2]
    tokens = cotangent.shape[1]
    phases = [("ffn", b) for b in range(1, blocks)]
    for b in range(blocks):
        phases += [("ffn_back", b), ("attend_back", b)]

    def uses(*kinds):
        return [(number, b) for number, (kind, b) in enumerate(phases) if kind in kinds]

    def whole(*dims):
        return pl.BlockSpec(dims, lambda i: (0,) * len(dims))

    def stacked(dims, kinds, shift=0):
        def place(i):
            block, part = phase_index(i, parts, uses(*kinds))
            return (block - shift, part) + (0,) * len(dims)
        return pl.BlockSpec((1, 1) + dims, place)

    def by_block(dims, kinds, shift=0, squeeze=False):
        def place(i):
            return (phase_index(i, parts, uses(*kinds))[0] - shift,) + (0,) * len(dims)
        return pl.BlockSpec((None if squeeze else 1,) + dims, place)

    def slab(index, kinds):
        def place(i):
            return (index, phase_index(i, parts, uses(*kinds))[1], 0, 0)
        return pl.BlockSpec((1, 1, width, cols), place)

    def first_parts(i):
        return (phase_index(i, parts, [use for use in uses("ffn_back") if use[1] == 0])[1], 0, 0)

    shape = jax.ShapeDtypeStruct
    dma = pltpu.SemaphoreType.DMA
    hbm, smem = pl.BlockSpec(memory_space=pl.ANY), pl.BlockSpec(memory_space=pltpu.SMEM)
    rows_of = (slot_count, width)
    square = (slot_count, cols)
    later = max(blocks - 1, 1)
    both = ("ffn", "ffn_back")
    return pl.pallas_call(
        functools.partial(backward_kernel, parts, micro_count, per_micro, slot_count, LINE_CHUNKS, phases),
        grid=(len(phases) * parts,),
        in_specs=[
            smem, smem, smem,
            whole(*stat_first.shape),
            whole(*vectors.shape),
            whole(*ffn_rows.shape),
            hbm,
            hbm,
            slab(0, ("attend_back",)),
            slab(1, both),
            slab(2, both),
            by_block(rows_of, both, squeeze=True),
            by_block((slot_count, 128), ("ffn_back",), squeeze=True),
            pl.BlockSpec((1,) + square, first_parts),
            whole(*rows_of),
            whole(*rows_of),
            stacked(square, ("attend_back",)),
            pl.BlockSpec((1, CHUNK_HEADS, slot_count, slot_count),
                         lambda i: phase_index(i, parts, uses("attend_back")) + (0, 0)),
            stacked((slot_count, 4 * HEAD_DIM), ("attend_back",)),
        ],
        out_specs=[
            hbm,
            stacked(square, ("ffn",), 1),
            by_block(rows_of, ("ffn",), 1),
            stacked(square, ("ffn_back",)),
            by_block(rows_of, ("ffn_back",)),
            stacked(square, ("attend_back",)),
            by_block(rows_of, ("attend_back",)),
            whole(16, width),
        ],
        out_shape=[
            shape((micro_count, tokens, width), LOW),
            shape((later, parts) + square, LOW),
            shape((later,) + rows_of, LOW),
            shape((blocks, parts) + square, LOW),
            shape((blocks,) + rows_of, LOW),
            shape((blocks, parts) + square, LOW),
            shape((blocks,) + rows_of, LOW),
            shape((16, width), WIDE),
        ],
        scratch_shapes=[
            pltpu.VMEM(rows_of, LOW),
            pltpu.VMEM(rows_of, WIDE),
            pltpu.VMEM((later, parts) + square, LOW),
            pltpu.VMEM((later,) + rows_of, WIDE),
            pltpu.VMEM((later,) + rows_of, LOW),
            pltpu.VMEM(rows_of, WIDE),
            pltpu.VMEM(rows_of, LOW),
            pltpu.VMEM((later,) + rows_of, LOW),
            pltpu.VMEM((later,) + rows_of, LOW),
            dma((blocks, parts, LINE_CHUNKS, 2)),
            dma((blocks, parts, LINE_CHUNKS)),
            dma((blocks, LINE_CHUNKS)),
            dma((later,)),
        ],
        compiler_params=pltpu.CompilerParams(
            dimension_semantics=("arbitrary",), collective_id=4, has_side_effects=True, vmem_limit_bytes=VMEM_LIMIT
        ),
        name="backward",
        cost_estimate=takes(100),
    )(*layout, stat_first, vectors, ffn_rows, first_out, cotangent, weights, weights, weights, normed, inverse, slope_first,
      second_first, second_low_first, proj, probs, context)


def finish_kernel(parts, bits, micro_count, per_micro, slot_count, chunks, vectors, small, inputs, normed, second_low_first,
                  second_low_later, hidden_low, act_first, act_later, grad_up, head_grads, token_grad, *rest):
    blocks = micro_count * per_micro
    second_low = [second_low_first] + [second_low_later.at[b - 1] for b in range(1, blocks)]
    act = [act_first] + [act_later.at[b - 1] for b in range(1, blocks)]
    hidden_low, grad_up, head_grads, token_grad = [
        [array.at[b] for b in range(blocks)] for array in (hidden_low, grad_up, head_grads, token_grad)
    ]
    gathered, out, small_out = rest[:3]
    (grads, operand, turned, staged, staged_wide, small_buf, small_sum, z_up, z_down) = rest[3:12]
    bufs = rest[12 : 12 + bits]
    (h_send, h_recv, up_send, up_recv, down_send, down_recv, s_send, s_recv, g_send, g_recv, g_keep, load, load_wide, fetch) = rest[
        12 + bits :
    ]
    d, t, digits, mates = mesh_place(bits)
    slab_count = grads.shape[0]
    rows = grads.shape[-2]
    width = inputs.shape[2]
    items = [(s, at) for s in range(slab_count) for at in range(parts)]
    small_bits = bits + parts.bit_length() - 1
    chunk_rows = slot_count // chunks

    def remote(src, dst, send, recv, to):
        return pltpu.make_async_remote_copy(src, dst, send, recv, device_id=to, device_id_type=MESH)

    def token_rows(b):
        place = t * per_micro + b % per_micro
        return inputs.at[b // per_micro, pl.ds(pl.multiple_of(place * slot_count, slot_count), slot_count)]

    def span(b):
        return pl.ds(b * slot_count, slot_count)

    def stage_loads(which):
        if which == 3:
            return [pltpu.make_async_copy(normed.at[b], staged_wide.at[span(b)], load_wide.at[b]) for b in range(blocks)]
        source = ([token_rows(b) for b in range(blocks)], hidden_low, second_low)[which]
        return [pltpu.make_async_copy(source[b], staged.at[which, span(b)], load.at[which, b]) for b in range(blocks)]

    def operand_loads(number):
        s, at = items[number]
        source = (head_grads, grad_up, act)[s]
        slot = number % 3
        return [pltpu.make_async_copy(source[b].at[at], operand.at[slot, span(b)], fetch.at[slot, b]) for b in range(blocks)]

    def grads_job(number):
        s, at = items[number]
        if number == 0:
            for copy in stage_loads(0) + stage_loads(1):
                copy.wait()
            turned[0] = staged[0].T
            turned[1] = staged[1].T
        elif at == 0 and s == 1:
            for copy in stage_loads(3):
                copy.wait()
            turned[0] = (staged_wide[...] * vectors[0:1] + vectors[3:4]).astype(LOW).T
        elif at == 0:
            for copy in stage_loads(2):
                copy.wait()
            turned[1] = staged[2].T
        for copy in operand_loads(number):
            copy.wait()
        right = operand[number % 3]
        if s == 0:
            qkv = dot_nn(turned[0], right)
            outs = dot_nn(turned[1], right[:, 8 * HEAD_DIM :])
            lane = lax.broadcasted_iota(jnp.int32, (1, 2 * HEAD_DIM), 1)
            last = jnp.where(lane < HEAD_DIM, qkv[:, 10 * HEAD_DIM :], outs[:, 2 * HEAD_DIM :])
            total = jnp.concatenate([qkv[:, : 8 * HEAD_DIM], outs[:, : 2 * HEAD_DIM], last], axis=1)
        else:
            total = dot_nn(turned[s - 1], right)
        grads[s, at] = total.astype(LOW).reshape(grads.shape[2:])
        if number + 3 < len(items):
            for copy in operand_loads(number + 3):
                copy.start()

    def order_of(number):
        s, at = items[number]
        return bit_order(bits, (s + at) % 2 == 1)[::-1]

    def held(number, step):
        s, at = items[number]
        return grads.at[s, at] if step == 0 else bufs[step - 1].at[number]

    def part_of(number, step, side):
        order = order_of(number)
        left = [k for k in reversed(range(bits)) if k not in order[:step]]
        pick = tuple(side if k == order[step] else slice(None) for k in left)
        return held(number, step).at[pick]

    def h_copy(number, step):
        order = order_of(number)
        digit = digits[order[step]]
        return remote(part_of(number, step, 1 - digit), bufs[step].at[number],
                      h_send.at[number, step], h_recv.at[number, step], (mates[order[step]], t))

    def fold(number, step):
        h_copy(number, step).wait_recv()
        digit = digits[order_of(number)[step]]
        add_rows(bufs[step].at[number], bufs[step].at[number], part_of(number, step, digit), rows)

    def summed(s, at):
        return bufs[bits - 1].at[s * parts + at]

    def z_copy(s, at, up, src):
        buf, send, recv = (z_up, up_send, up_recv) if up else (z_down, down_send, down_recv)
        to = (d, t + 1) if up else (d, t - 1)
        return remote(src, buf.at[s, at], send.at[s, at], recv.at[s, at], to)

    def z_pass(s, hop, up):
        at = t + hop if up else t - hop
        edge = (t == 0) if up else (t == parts - 1)
        buf = z_up if up else z_down

        @pl.when((at < parts) if up else (at >= 0))
        def _():
            @pl.when(edge)
            def _():
                z_copy(s, at, up, summed(s, at)).start()

            @pl.when(jnp.logical_not(edge))
            def _():
                z_copy(s, at, up, summed(s, at)).wait_recv()
                add_rows(buf.at[s, at], buf.at[s, at], summed(s, at), rows)
                z_copy(s, at, up, buf.at[s, at]).start()

    def z_finish(s):
        @pl.when(t > 0)
        def _():
            z_copy(s, t, True, summed(s, t)).wait_recv()
            add_rows(out.at[s], summed(s, t), z_up.at[s, t], rows)

        @pl.when(t < parts - 1)
        def _():
            z_copy(s, t, False, summed(s, t)).wait_recv()

            @pl.when(t > 0)
            def _():
                add_rows(out.at[s], out.at[s], z_down.at[s, t], rows)

            @pl.when(t == 0)
            def _():
                add_rows(out.at[s], summed(s, t), z_down.at[s, t], rows)

    def small_copy(step):
        if step < bits:
            to = (mates[step], t)
        else:
            gap = 1 << (step - bits)
            to = (d, t + (1 - 2 * ((t // gap) % 2)) * gap)
        src = small if step == 0 else small_sum.at[step - 1]
        return remote(src, small_buf.at[step], s_send.at[step], s_recv.at[step], to)

    def small_fold(step):
        small_copy(step).wait_recv()
        before = small[...] if step == 0 else small_sum[step - 1]
        small_sum[step] = before + small_buf[step]
        if step + 1 < small_bits:
            small_copy(step + 1).start()

    def line_rows(b, at, q):
        place = at * per_micro + b % per_micro
        start = pl.multiple_of(place * slot_count + q * chunk_rows, chunk_rows)
        return gathered.at[b // per_micro, pl.ds(start, chunk_rows)]

    def own_rows(b, q):
        return token_grad[b].at[pl.ds(q * chunk_rows, chunk_rows)]

    def line_copy(b, at, q, src, up):
        to = (d, t + 1) if up else (d, t - 1)
        return remote(src, line_rows(b, at, q), g_send.at[b, at, q, 0 if up else 1], g_recv.at[b, at, q], to)

    def line_send(b, q):
        for up in (True, False):
            @pl.when((t < parts - 1) if up else (t > 0))
            def _():
                line_copy(b, t, q, own_rows(b, q), up).start()

    def line_pass(b, hop, q):
        for up in (True, False):
            at = t - hop if up else t + hop

            @pl.when((at >= 0) if up else (at < parts))
            def _():
                line_copy(b, at, q, own_rows(b, q), up).wait_recv()

                @pl.when((t < parts - 1) if up else (t > 0))
                def _():
                    line_copy(b, at, q, line_rows(b, at, q), up).start()

    def line_settle(b, hop, q):
        for up in (True, False):
            at = t - hop if up else t + hop

            @pl.when(((at >= 0) if up else (at < parts)) & ((t < parts - 1) if up else (t > 0)))
            def _():
                line_copy(b, at, q, own_rows(b, q), up).wait_send()

    keeps = [pltpu.make_async_copy(own_rows(b, q), line_rows(b, t, q), g_keep.at[b, q])
             for b in range(blocks) for q in range(chunks)]
    events = []
    for turn in range(blocks + parts):
        for hop in range(parts + 1):
            b = turn - hop
            if 0 <= b < blocks and hop <= parts - 1:
                for q in range(chunks):
                    events.append(functools.partial(line_send, b, q) if hop == 0 else functools.partial(line_pass, b, hop, q))

    for copy in stage_loads(0) + stage_loads(1):
        copy.start()
    for number in range(min(3, len(items))):
        for copy in operand_loads(number):
            copy.start()
    for copy in stage_loads(3) + stage_loads(2):
        copy.start()
    greet(d, t, mates, parts)
    for copy in keeps:
        copy.start()
    small_copy(0).start()
    ahead = chunks

    waves = len(items) + bits * REDUCE_LAG + parts
    per_wave = LINE_PACE
    for wave in range(max(waves, len(events))):
        while events and wave * per_wave + ahead > total_done(events, blocks, parts, chunks):
            events.pop(0)()
        if wave < len(items):
            grads_job(wave)
            h_copy(wave, 0).start()
        for step in range(bits):
            number = wave - (step + 1) * REDUCE_LAG + 1
            if 0 <= number < len(items):
                fold(number, step)
                if step + 1 < bits:
                    h_copy(number, step + 1).start()
        for s in range(slab_count):
            phase = wave - ((s + 1) * parts + bits * REDUCE_LAG - 1)
            if 0 <= phase < parts - 1:
                z_pass(s, parts - 1 - phase, True)
                z_pass(s, parts - 1 - phase, False)
            elif phase == parts - 1:
                z_finish(s)
        if wave < small_bits:
            small_fold(wave)
    small_out[...] = small_sum[small_bits - 1]

    for copy in keeps:
        copy.wait()
    for b in range(blocks):
        for hop in range(parts - 1):
            for q in range(chunks):
                line_settle(b, hop, q)
    for step in range(small_bits):
        small_copy(step).wait_send()
    for number in range(len(items)):
        for step in range(bits):
            h_copy(number, step).wait_send()
    for s in range(slab_count):
        for hop in range(1, parts):
            @pl.when(t + hop < parts)
            def _():
                z_copy(s, t + hop, True, summed(s, t)).wait_send()

            @pl.when(t - hop >= 0)
            def _():
                z_copy(s, t - hop, False, summed(s, t)).wait_send()


def total_done(events, blocks, parts, chunks):
    return blocks * parts * chunks - len(events)


def finish(vectors, small, inputs, normed, second_low_first, second_low_later, hidden_low, act_first, act_later, grad_up,
           head_grads, token_grad, parts, dp_count):
    bits = dp_count.bit_length() - 1
    blocks = token_grad.shape[0]
    micro_count, tokens, width = inputs.shape
    per_micro = blocks // micro_count
    slot_count, cols = act_first.shape[1:]
    rows = width // dp_count
    slab_count = 3
    count = slab_count * parts
    small_bits = bits + parts.bit_length() - 1
    dma = pltpu.SemaphoreType.DMA
    hbm, vmem = pl.BlockSpec(memory_space=pl.ANY), pl.BlockSpec(memory_space=pltpu.VMEM)
    block = (rows, cols)
    return pl.pallas_call(
        functools.partial(finish_kernel, parts, bits, micro_count, per_micro, slot_count, LINE_CHUNKS),
        out_shape=[
            jax.ShapeDtypeStruct((micro_count, tokens, width), LOW),
            jax.ShapeDtypeStruct((slab_count,) + block, WIDE),
            jax.ShapeDtypeStruct(small.shape, WIDE),
        ],
        in_specs=[vmem, vmem] + [hbm] * 10,
        out_specs=[hbm, vmem, vmem],
        scratch_shapes=[
            pltpu.VMEM((slab_count, parts) + (2,) * bits + block, LOW),
            pltpu.VMEM((3, blocks * slot_count, cols), LOW),
            pltpu.VMEM((2, width, blocks * slot_count), LOW),
            pltpu.VMEM((3, blocks * slot_count, width), LOW),
            pltpu.VMEM((blocks * slot_count, width), WIDE),
            pltpu.VMEM((small_bits,) + small.shape, WIDE),
            pltpu.VMEM((small_bits,) + small.shape, WIDE),
            pltpu.VMEM((slab_count, parts) + block, LOW),
            pltpu.VMEM((slab_count, parts) + block, LOW),
        ]
        + [pltpu.VMEM((count,) + (2,) * (bits - 1 - step) + block, LOW) for step in range(bits)]
        + [dma((count, bits)), dma((count, bits))]
        + [dma((slab_count, parts))] * 4
        + [dma((small_bits,))] * 2
        + [dma((blocks, parts, LINE_CHUNKS, 2)), dma((blocks, parts, LINE_CHUNKS)), dma((blocks, LINE_CHUNKS))]
        + [dma((3, blocks)), dma((blocks,)), dma((3, blocks))],
        compiler_params=pltpu.CompilerParams(collective_id=3, has_side_effects=True, vmem_limit_bytes=VMEM_LIMIT),
        name="finish",
        cost_estimate=takes(100),
    )(vectors, small, inputs, normed, second_low_first, second_low_later, hidden_low, act_first, act_later, grad_up, head_grads,
      token_grad)


def place_kernel(parts, dp_count, shard, sums, grad_qkv, grad_out, grad_in, grad_down, grad_head, grad_ffn,
                 grad_gains, grad_shifts):
    dp_rank, rank = lax.axis_index("dp"), lax.axis_index("tensor")
    groups = slab_parts(shard[0])
    for i in range(3):
        grad_qkv[i] = groups[i]
    grad_out[...] = groups[3].T
    grad_in[...] = shard[1]
    grad_down[...] = shard[2]
    grad_ffn[...] = sums[pl.ds(6 + rank, 1), :].reshape(-1)
    head = slab_parts(sums[pl.ds(6 + parts + rank, 1), :])
    grad_head[...] = jnp.concatenate([head[0], head[2]], axis=0)
    rows = shard.shape[1]
    wide = sums[0:8, :]
    vectors = wide[:, :rows]
    for i in range(1, dp_count):
        vectors = jnp.where(dp_rank == i, wide[:, i * rows : (i + 1) * rows], vectors)
    grad_gains[...] = vectors[0:2]
    grad_shifts[...] = vectors[2:6]


def place_results(shard, sums, parts, dp_count):
    rows, cols = shard.shape[1:]
    head_cols = CHUNK_HEADS * HEAD_DIM
    smalls = [(3, rows, head_cols), (head_cols, rows), (rows, cols), (rows, cols), (2, head_cols), (cols,), (2, rows), (4, rows)]
    vmem = pl.BlockSpec(memory_space=pltpu.VMEM)
    return pl.pallas_call(
        functools.partial(place_kernel, parts, dp_count),
        in_specs=[vmem, vmem],
        out_specs=[vmem] * len(smalls),
        out_shape=[jax.ShapeDtypeStruct(dims, WIDE) for dims in smalls],
        compiler_params=pltpu.CompilerParams(vmem_limit_bytes=VMEM_LIMIT),
        name="place_results",
    )(shard, sums)


def add_all(terms):
    total = terms[0]
    for term in terms[1:]:
        total = total + term
    return total


def body(
    inputs,
    cotangent,
    bucket,
    lengths,
    counts,
    w_qkv,
    w_out,
    w_in,
    w_down,
    head_bias,
    ffn_bias,
    norm_gains,
    row_biases,
):
    micro_count, _, width = inputs.shape
    blocks_all = bucket.shape[1]
    slot_count = inputs.shape[1] // blocks_all
    parts, dp_count = lax.axis_size("tensor"), lax.axis_size("dp")
    rank, dp_rank = lax.axis_index("tensor"), lax.axis_index("dp")
    per_micro = blocks_all // parts
    cols = w_in.shape[1]
    rows = w_in.shape[0]

    vector_count = norm_gains.shape[0] + row_biases.shape[0]
    blocks = [(m, k) for m in range(micro_count) for k in range(per_micro)]
    places = [jnp.full((1,), rank * per_micro + k, jnp.int32) for k in range(per_micro)]
    layout = (bucket, lengths, counts)
    if rows % 16 == 0:
        (weights, vectors, _, ffn_rows, normed, inverse, proj, probs, context, act, slope, out, second, second_low, stat) = forward(
            (w_qkv, w_out, w_in, w_down.T, head_bias, ffn_bias, norm_gains, row_biases),
            layout, inputs, cotangent, parts, dp_count, slot_count, micro_count, per_micro
        )
        layer_output, act_later, second_low_later, grad_up, hidden_low, head_grads, token_grad, small_grads = backward(
            layout, stat, vectors, ffn_rows, out, cotangent, weights, normed, inverse, slope, second, second_low, proj, probs,
            context, micro_count, per_micro
        )
        input_grad, shard, sums = finish(
            vectors, small_grads, inputs, normed, second_low, second_low_later, hidden_low, act, act_later, grad_up, head_grads,
            token_grad, parts, dp_count
        )
        grad_w_qkv, grad_w_out, grad_w_in, grad_w_down, grad_head, grad_ffn, grad_gains, grad_shifts = place_results(
            shard, sums, parts, dp_count
        )
        grad_w_down = grad_w_down.T
    else:
        own = jnp.stack([slab_order(w_qkv[0], w_qkv[1], w_qkv[2], w_out.T), w_in, w_down.T])
        norm_rows = jnp.concatenate([norm_gains, row_biases], axis=0)
        no_bias = jnp.zeros_like(head_bias[:1])
        bias_rows = jnp.concatenate([slab_order(head_bias[:1], no_bias, head_bias[1:], no_bias), ffn_bias[None]], axis=0)
        small = jnp.stack([
            jnp.pad(norm_rows, ((0, 16 - vector_count), (0, cols - rows))),
            jnp.pad(bias_rows, ((0, 14), (0, 0))),
        ])
        weights, small_dp, small_t = gather_weights(own, small, parts, dp_count)
        vectors = small_dp[:, :8, :rows].transpose(1, 0, 2).reshape(8, width).astype(jnp.float32)
        head_rows = small_t[:, 0:1].astype(jnp.float32)
        ffn_rows = small_t[:, 1:2].astype(jnp.float32)
        outs, token_grads, saved = [], [], []
        for m, k in blocks:
            attended = attend(m, places[k], *layout, inputs, weights, head_rows, vectors, slot_count)
            normed, inverse, proj, probs, context = [(array[None], 0) for array in attended]
            act, slope, out, second, second_low, stat = ffn(m, places[k], *layout, normed, cotangent, weights, ffn_rows, vectors)
            grad_up, hidden, hidden_low, up_stat, first_stat = ffn_back(second, second_low, slope, weights, normed, inverse, vectors)
            head_grads, token_grad, head_stat = attend_back(
                m, places[k], *layout, hidden, hidden_low, weights, proj, probs, context
            )
            outs.append(out)
            token_grads.append(token_grad)
            saved.append((normed, second_low, hidden_low, act, grad_up, head_grads, stat, first_stat, up_stat, head_stat))

        def along_line(rows_of):
            return jnp.stack([
                lax.all_gather(jnp.concatenate(rows_of[m * per_micro : (m + 1) * per_micro], axis=0), "tensor", axis=0, tiled=True)
                for m in range(micro_count)
            ])

        layer_output, input_grad = along_line(outs), along_line(token_grads)
        columns = list(zip(*saved))
        stat, first_stat, up_stat, head_stat = [add_all(column) for column in columns[6:]]
        small_grads = jnp.concatenate(
            [
                jnp.stack([first_stat[0], stat[0], first_stat[2], first_stat[1], stat[2], stat[1]]),
                up_stat[:, 0],
                head_stat[:, 0],
            ],
            axis=0,
        )
        small_grads = jnp.pad(small_grads, ((0, -small_grads.shape[0] % 8), (0, 0)))
        grads = weight_grads(places[0], inputs, *columns[:6], vectors)
        shard, sums = reduce_grads(grads, small_grads, parts, dp_count)
        vector_sums = lax.dynamic_slice_in_dim(sums[:vector_count], dp_rank * rows, rows, 1)
        grad_gains, grad_shifts = vector_sums[:2], vector_sums[2:]
        grad_query, grad_key, grad_value, grad_out = slab_parts(shard[0])
        grad_w_qkv = jnp.stack([grad_query, grad_key, grad_value])
        grad_w_out, grad_w_in, grad_w_down = grad_out.T, shard[1], shard[2].T
        grad_ffn = lax.dynamic_slice_in_dim(sums, vector_count + rank, 1, 0)[0]
        head_sum = slab_parts(lax.dynamic_slice_in_dim(sums, vector_count + parts + rank, 1, 0))
        grad_head = jnp.concatenate([head_sum[0], head_sum[2]], axis=0)
    return (
        layer_output,
        input_grad,
        grad_w_qkv,
        grad_w_out,
        grad_w_in,
        grad_w_down,
        grad_head,
        grad_ffn,
        grad_gains,
        grad_shifts,
    )


def solution(mesh):
    in_specs = (
        P(None, "dp", None),
        P(None, "dp", None),
        P(None, "dp"),
        P(None, "dp", None),
        P(None, "dp"),
        P(None, "dp", "tensor"),
        P("tensor", "dp"),
        P("dp", "tensor"),
        P("tensor", "dp"),
        P(None, "tensor"),
        P("tensor"),
        P(None, "dp"),
        P(None, "dp"),
    )
    out_specs = (
        P(None, "dp", None),
        P(None, "dp", None),
        P(None, "dp", "tensor"),
        P("tensor", "dp"),
        P("dp", "tensor"),
        P("tensor", "dp"),
        P(None, "tensor"),
        P("tensor"),
        P(None, "dp"),
        P(None, "dp"),
    )
    return jax.shard_map(body, mesh=mesh, in_specs=in_specs, out_specs=out_specs, check_vma=False)
```

```python
import functools

import jax
import jax.numpy as jnp
from jax import lax
from jax.experimental import pallas as pl
from jax.experimental.pallas import tpu as pltpu
from jax.sharding import PartitionSpec as P

HEAD_DIM = 64
EPSILON = 1e-12
VMEM_LIMIT = 60 * 1024 * 1024
MESH = pl.DeviceIdType.MESH
GATHER_LAG = 2
Z_WAVES = (2, 3)
LINE_PACE = 1
LINE_START = ((0, 1, 7), (4, 9, 15))
LINE_CHUNKS = 4
REDUCE_LAG = 2
def takes(microseconds):
    return pl.CostEstimate(flops=int(microseconds * 1.15e8), bytes_accessed=0, transcendentals=0)


LOW = jnp.bfloat16
WIDE = jnp.float32
CHUNK_HEADS = 3
VALUE_AT = (6, 7, 10)
OUT_AT = (8, 9, 11)


def slab_order(query, key, value, out):
    columns = lambda group, head: group[..., head * HEAD_DIM : (head + 1) * HEAD_DIM]
    order = [(query, 0), (key, 0), (query, 1), (key, 1), (query, 2), (key, 2),
             (value, 0), (value, 1), (out, 0), (out, 1), (value, 2), (out, 2)]
    return jnp.concatenate([columns(group, head) for group, head in order], axis=-1)


def slab_parts(slab):
    columns = lambda at: slab[..., at * HEAD_DIM : (at + 1) * HEAD_DIM]
    groups = ((0, 2, 4), (1, 3, 5), VALUE_AT, OUT_AT)
    return [jnp.concatenate([columns(at) for at in group], axis=-1) for group in groups]


def dot_nn(left, right):
    return lax.dot_general(left, right, (((1,), (0,)), ((), ())), preferred_element_type=WIDE)


def dot_nt(left, right):
    return lax.dot_general(left, right, (((1,), (1,)), ((), ())), preferred_element_type=WIDE)


def dot_tn(left, right):
    return lax.dot_general(left, right, (((0,), (0,)), ((), ())), preferred_element_type=WIDE)


def piece(tile, at):
    return tile[:, at * HEAD_DIM : (at + 1) * HEAD_DIM]


def slot_codes(layout, micro, block, slot_count, shape, axis):
    bucket, lengths, counts = layout
    position = lax.broadcasted_iota(jnp.int32, shape, axis)
    quarter = slot_count // 4
    whole = bucket[micro, block] == 1
    item = jnp.where(whole, 0, position // quarter)
    place = position - item * quarter
    length = jnp.where(
        item == 0,
        lengths[micro, block, 0],
        jnp.where(
            item == 1,
            lengths[micro, block, 1],
            jnp.where(item == 2, lengths[micro, block, 2], lengths[micro, block, 3]),
        ),
    )
    return item, (item < counts[micro, block]) & (place < length)


def normalize(hidden):
    center = hidden - jnp.mean(hidden, axis=-1, keepdims=True)
    inverse = lax.rsqrt(jnp.mean(center * center, axis=-1, keepdims=True) + EPSILON)
    return center * inverse, inverse


def norm_pullback(grad_rows, normed, inverse, gain_row):
    grad_normed = grad_rows * gain_row
    return inverse * (
        grad_normed
        - jnp.mean(grad_normed, axis=-1, keepdims=True)
        - normed * jnp.mean(grad_normed * normed, axis=-1, keepdims=True)
    )


def row_sum(values):
    return jnp.sum(values, axis=0, keepdims=True)


def attend_unit(layout, micro, place, tokens, weights, bias_row, proj_ref, prob_ref, context_ref):
    slot_count = tokens.shape[0]
    proj = (dot_nn(tokens, weights) + bias_row).astype(LOW)
    proj_ref[...] = proj
    row_item, _ = slot_codes(layout, micro, place, slot_count, (slot_count, 1), 0)
    key_item, key_live = slot_codes(layout, micro, place, slot_count, (1, slot_count), 1)
    key_code = jnp.where(key_live, key_item, -1)
    outs = []
    for head in range(CHUNK_HEADS):
        query = piece(proj, 2 * head) * jnp.asarray(HEAD_DIM ** (-0.5), LOW)
        scores = dot_nt(query, piece(proj, 2 * head + 1))
        scores = jnp.where(row_item == key_code, scores, -10000.0)
        grown = jnp.exp(scores - jnp.max(scores, axis=-1, keepdims=True))
        probs = (grown * (1.0 / jnp.sum(grown, axis=-1, keepdims=True))).astype(LOW)
        prob_ref[head] = probs
        outs.append(dot_nn(probs, piece(proj, VALUE_AT[head])).astype(LOW))
    context = jnp.concatenate([outs[0], outs[1], jnp.zeros_like(outs[0]), outs[2]], axis=1)
    context_ref[...] = context
    return dot_nt(context, weights[:, 8 * HEAD_DIM :])


def ffn_unit(first_low, w_in, w_down, bias_row, act_ref, slope_ref):
    upward = dot_nn(first_low, w_in) + bias_row
    share = 0.5 + 0.5 * lax.erf(upward * (0.5**0.5))
    activated = (upward * share).astype(LOW)
    act_ref[...] = activated
    bell = jnp.exp(-0.5 * upward * upward) * 0.3989422804014327
    slope_ref[...] = (share + upward * bell).astype(LOW)
    return dot_nt(activated, w_down)


def second_norm(layout, micro, place, first_normed, down_total, cot_rows, vectors):
    slot_count = first_normed.shape[0]
    _, live = slot_codes(layout, micro, place, slot_count, (slot_count, 1), 0)
    first = first_normed * vectors[0:1] + vectors[3:4]
    normed, inverse = normalize(first + down_total + vectors[4:5])
    out = (normed * vectors[1:2] + vectors[5:6]).astype(LOW)
    grad_out = jnp.where(live, cot_rows.astype(WIDE), 0.0)
    second = norm_pullback(grad_out, normed, inverse, vectors[1:2])
    stat = jnp.concatenate(
        [row_sum(grad_out * normed), row_sum(grad_out), row_sum(second), jnp.zeros((5, second.shape[1]), WIDE)], axis=0
    )
    return out, second, stat


def attend_kernel(micro, place, bucket, lengths, counts, x_ref, w_ref, bias_ref, vec_ref,
                  normed_ref, inverse_ref, proj_ref, prob_ref, context_ref, total):
    step = pl.program_id(0)
    layout = (bucket, lengths, counts)
    tokens = x_ref[0]
    attention = attend_unit(layout, micro, place[0], tokens, w_ref[0, 0], bias_ref[0],
                            proj_ref.at[0], prob_ref, context_ref.at[0])

    @pl.when(step == 0)
    def _():
        total[...] = attention

    @pl.when(step > 0)
    def _():
        total[...] += attention

    @pl.when(step == pl.num_programs(0) - 1)
    def _():
        normed, inverse = normalize(tokens.astype(WIDE) + total[...] + vec_ref[2:3])
        normed_ref[...] = normed
        inverse_ref[...] = jnp.broadcast_to(inverse, inverse_ref.shape)


def ffn_kernel(micro, place, bucket, lengths, counts, normed_ref, cot_ref, w_in_ref, w_down_ref, bias_ref, vec_ref,
               act_ref, slope_ref, out_ref, second_ref, second_low_ref, stat_ref, first_low, total):
    step = pl.program_id(0)

    @pl.when(step == 0)
    def _():
        first_low[...] = (normed_ref[...] * vec_ref[0:1] + vec_ref[3:4]).astype(LOW)

    down = ffn_unit(first_low[...], w_in_ref[0, 0], w_down_ref[0, 0], bias_ref[0], act_ref.at[0], slope_ref.at[0])

    @pl.when(step == 0)
    def _():
        total[...] = down

    @pl.when(step > 0)
    def _():
        total[...] += down

    @pl.when(step == pl.num_programs(0) - 1)
    def _():
        out, second, stat = second_norm(
            (bucket, lengths, counts), micro, place[0], normed_ref[...], total[...], cot_ref[0], vec_ref
        )
        out_ref[...] = out
        second_ref[...] = second
        second_low_ref[...] = second.astype(LOW)
        stat_ref[...] = stat


def ffn_back_kernel(second_ref, second_low_ref, slope_ref, w_in_ref, w_down_ref, normed_ref, inverse_ref, vec_ref,
                    up_ref, hidden_ref, hidden_low_ref, up_stat_ref, stat_ref, total):
    step = pl.program_id(0)
    grad_act = dot_nn(second_low_ref[...], w_down_ref[0, 0])
    grad_up = (grad_act * slope_ref[0].astype(WIDE)).astype(LOW)
    up_ref[0] = grad_up
    up_stat_ref[0] = jnp.broadcast_to(row_sum(grad_up.astype(WIDE)), up_stat_ref.shape[1:])
    back = dot_nt(grad_up, w_in_ref[0, 0])

    @pl.when(step == 0)
    def _():
        total[...] = back + second_ref[...]

    @pl.when(step > 0)
    def _():
        total[...] += back

    @pl.when(step == pl.num_programs(0) - 1)
    def _():
        grad_first = total[...]
        normed = normed_ref[...]
        hidden = norm_pullback(grad_first, normed, inverse_ref[:, :1], vec_ref[0:1])
        hidden_ref[...] = hidden
        hidden_low_ref[...] = hidden.astype(LOW)
        stat_ref[...] = jnp.concatenate(
            [row_sum(grad_first * normed), row_sum(grad_first), row_sum(hidden), jnp.zeros((5, hidden.shape[1]), WIDE)],
            axis=0,
        )


def attend_back_unit(layout, micro, place, hidden_low, weights, proj, probs_of, context):
    slot_count = hidden_low.shape[0]
    row_item, _ = slot_codes(layout, micro, place, slot_count, (slot_count, 1), 0)
    key_item, key_live = slot_codes(layout, micro, place, slot_count, (1, slot_count), 1)
    key_code = jnp.where(key_live, key_item, -1)
    grad_context = dot_nn(hidden_low, weights[:, 8 * HEAD_DIM :]).astype(LOW)
    scale = HEAD_DIM ** (-0.5)
    grads = [None] * 12
    for head in range(CHUNK_HEADS):
        query, key = piece(proj, 2 * head), piece(proj, 2 * head + 1)
        probs = probs_of[head]
        grad_head = piece(grad_context, OUT_AT[head] - 8)
        grads[VALUE_AT[head]] = dot_tn(probs, grad_head).astype(LOW)
        grad_probs = dot_nt(grad_head, piece(proj, VALUE_AT[head]))
        wide = probs.astype(WIDE)
        inner = jnp.sum(wide * grad_probs, axis=-1, keepdims=True)
        grad_scores = jnp.where(row_item == key_code, wide * (grad_probs - inner), 0.0).astype(LOW)
        grads[2 * head] = (dot_nn(grad_scores, key) * scale).astype(LOW)
        grads[2 * head + 1] = (dot_tn(grad_scores, query) * scale).astype(LOW)
    zero = jnp.zeros_like(grads[0])
    for at in OUT_AT:
        grads[at] = zero
    slab = jnp.concatenate(grads, axis=1)
    back = dot_nt(slab, weights)
    sums = row_sum(slab.astype(WIDE))
    for at in OUT_AT:
        grads[at] = piece(context, at - 8)
    return jnp.concatenate(grads, axis=1), back, sums


def attend_back_kernel(micro, place, bucket, lengths, counts, hidden_ref, hidden_low_ref, w_ref, proj_ref, prob_ref,
                       context_ref, grad_ref, out_ref, stat_ref, total):
    step = pl.program_id(0)
    slab, back, sums = attend_back_unit((bucket, lengths, counts), micro, place[0], hidden_low_ref[...], w_ref[0, 0],
                                        proj_ref[0], prob_ref, context_ref[0])
    grad_ref[0] = slab
    stat_ref[0] = jnp.broadcast_to(sums, stat_ref.shape[1:])

    @pl.when(step == 0)
    def _():
        total[...] = back + hidden_ref[...]

    @pl.when(step > 0)
    def _():
        total[...] += back

    @pl.when(step == pl.num_programs(0) - 1)
    def _():
        out_ref[...] = total[...].astype(LOW)


def params(vmem=VMEM_LIMIT):
    return pltpu.CompilerParams(dimension_semantics=("arbitrary",), vmem_limit_bytes=vmem)


def attend(micro, place, bucket, lengths, counts, inputs, weights, bias, vectors, slot_count):
    parts, width = weights.shape[1], weights.shape[2]
    wide_slab = weights.shape[3]
    heads = parts * CHUNK_HEADS
    whole = lambda *shape: pl.BlockSpec(shape, lambda j, p, b, l, c: (0,) * len(shape))
    return pl.pallas_call(
        functools.partial(attend_kernel, micro),
        grid_spec=pltpu.PrefetchScalarGridSpec(
            num_scalar_prefetch=4,
            grid=(parts,),
            in_specs=[
                pl.BlockSpec((1, slot_count, width), lambda j, p, b, l, c: (micro, p[0], 0)),
                pl.BlockSpec((1, 1, width, wide_slab), lambda j, p, b, l, c: (0, j, 0, 0)),
                pl.BlockSpec((1, 1, wide_slab), lambda j, p, b, l, c: (j, 0, 0)),
                whole(*vectors.shape),
            ],
            out_specs=[
                whole(slot_count, width),
                whole(slot_count, 128),
                pl.BlockSpec((1, slot_count, wide_slab), lambda j, p, b, l, c: (j, 0, 0)),
                pl.BlockSpec((CHUNK_HEADS, slot_count, slot_count), lambda j, p, b, l, c: (j, 0, 0)),
                pl.BlockSpec((1, slot_count, 4 * HEAD_DIM), lambda j, p, b, l, c: (j, 0, 0)),
            ],
            scratch_shapes=[pltpu.VMEM((slot_count, width), WIDE)],
        ),
        out_shape=[
            jax.ShapeDtypeStruct((slot_count, width), WIDE),
            jax.ShapeDtypeStruct((slot_count, 128), WIDE),
            jax.ShapeDtypeStruct((parts, slot_count, wide_slab), LOW),
            jax.ShapeDtypeStruct((heads, slot_count, slot_count), LOW),
            jax.ShapeDtypeStruct((parts, slot_count, 4 * HEAD_DIM), LOW),
        ],
        compiler_params=params(),
        name="attend",
        cost_estimate=takes(16),
    )(place, bucket, lengths, counts, inputs, weights, bias, vectors)


def ffn(micro, place, bucket, lengths, counts, normed, cotangent, weights, bias, vectors):
    parts, width, cols = weights.shape[1:]
    normed, index = normed
    slot_count = normed.shape[1]
    whole = lambda *shape: pl.BlockSpec(shape, lambda j, p, b, l, c: (0,) * len(shape))
    each = pl.BlockSpec((1, slot_count, cols), lambda j, p, b, l, c: (j, 0, 0))
    return pl.pallas_call(
        functools.partial(ffn_kernel, micro),
        grid_spec=pltpu.PrefetchScalarGridSpec(
            num_scalar_prefetch=4,
            grid=(parts,),
            in_specs=[
                pl.BlockSpec((None, slot_count, width), lambda j, p, b, l, c: (index, 0, 0)),
                pl.BlockSpec((1, slot_count, width), lambda j, p, b, l, c: (micro, p[0], 0)),
                pl.BlockSpec((1, 1, width, cols), lambda j, p, b, l, c: (1, j, 0, 0)),
                pl.BlockSpec((1, 1, width, cols), lambda j, p, b, l, c: (2, j, 0, 0)),
                pl.BlockSpec((1, 1, cols), lambda j, p, b, l, c: (j, 0, 0)),
                whole(*vectors.shape),
            ],
            out_specs=[each, each, whole(slot_count, width), whole(slot_count, width), whole(slot_count, width), whole(8, width)],
            scratch_shapes=[pltpu.VMEM((slot_count, width), LOW), pltpu.VMEM((slot_count, width), WIDE)],
        ),
        out_shape=[
            jax.ShapeDtypeStruct((parts, slot_count, cols), LOW),
            jax.ShapeDtypeStruct((parts, slot_count, cols), LOW),
            jax.ShapeDtypeStruct((slot_count, width), LOW),
            jax.ShapeDtypeStruct((slot_count, width), WIDE),
            jax.ShapeDtypeStruct((slot_count, width), LOW),
            jax.ShapeDtypeStruct((8, width), WIDE),
        ],
        compiler_params=params(),
        name="ffn",
        cost_estimate=takes(16),
    )(place, bucket, lengths, counts, normed, cotangent, weights, weights, bias, vectors)


def ffn_back(second, second_low, slope, weights, normed, inverse, vectors):
    parts, width, cols = weights.shape[1:]
    (normed, index), (inverse, _) = normed, inverse
    slot_count = normed.shape[1]
    whole = lambda *shape: pl.BlockSpec(shape, lambda j: (0,) * len(shape))
    each = pl.BlockSpec((1, slot_count, cols), lambda j: (j, 0, 0))
    return pl.pallas_call(
        ffn_back_kernel,
        grid=(parts,),
        in_specs=[
            whole(slot_count, width),
            whole(slot_count, width),
            each,
            pl.BlockSpec((1, 1, width, cols), lambda j: (1, j, 0, 0)),
            pl.BlockSpec((1, 1, width, cols), lambda j: (2, j, 0, 0)),
            pl.BlockSpec((None, slot_count, width), lambda j: (index, 0, 0)),
            pl.BlockSpec((None, slot_count, 128), lambda j: (index, 0, 0)),
            whole(*vectors.shape),
        ],
        out_specs=[each, whole(slot_count, width), whole(slot_count, width),
                   pl.BlockSpec((1, 8, cols), lambda j: (j, 0, 0)), whole(8, width)],
        scratch_shapes=[pltpu.VMEM((slot_count, width), WIDE)],
        out_shape=[
            jax.ShapeDtypeStruct((parts, slot_count, cols), LOW),
            jax.ShapeDtypeStruct((slot_count, width), WIDE),
            jax.ShapeDtypeStruct((slot_count, width), LOW),
            jax.ShapeDtypeStruct((parts, 8, cols), WIDE),
            jax.ShapeDtypeStruct((8, width), WIDE),
        ],
        compiler_params=params(),
        name="ffn_back",
        cost_estimate=takes(14),
    )(second, second_low, slope, weights, weights, normed, inverse, vectors)


def attend_back(micro, place, bucket, lengths, counts, hidden, hidden_low, weights, proj, probs, context):
    parts, width = weights.shape[1], weights.shape[2]
    wide_slab = weights.shape[3]
    slot_count = hidden.shape[0]
    (proj, index), (probs, _), (context, _) = proj, probs, context
    whole = lambda *shape: pl.BlockSpec(shape, lambda j, p, b, l, c: (0,) * len(shape))
    each = pl.BlockSpec((1, slot_count, wide_slab), lambda j, p, b, l, c: (j, 0, 0))
    return pl.pallas_call(
        functools.partial(attend_back_kernel, micro),
        grid_spec=pltpu.PrefetchScalarGridSpec(
            num_scalar_prefetch=4,
            grid=(parts,),
            in_specs=[
                whole(slot_count, width),
                whole(slot_count, width),
                pl.BlockSpec((1, 1, width, wide_slab), lambda j, p, b, l, c: (0, j, 0, 0)),
                pl.BlockSpec((None, 1, slot_count, wide_slab), lambda j, p, b, l, c: (index, j, 0, 0)),
                pl.BlockSpec((None, CHUNK_HEADS, slot_count, slot_count), lambda j, p, b, l, c: (index, j, 0, 0)),
                pl.BlockSpec((None, 1, slot_count, 4 * HEAD_DIM), lambda j, p, b, l, c: (index, j, 0, 0)),
            ],
            out_specs=[each, whole(slot_count, width), pl.BlockSpec((1, 8, wide_slab), lambda j, p, b, l, c: (j, 0, 0))],
            scratch_shapes=[pltpu.VMEM((slot_count, width), WIDE)],
        ),
        out_shape=[
            jax.ShapeDtypeStruct((parts, slot_count, wide_slab), LOW),
            jax.ShapeDtypeStruct((slot_count, width), LOW),
            jax.ShapeDtypeStruct((parts, 8, wide_slab), WIDE),
        ],
        compiler_params=params(),
        name="attend_back",
        cost_estimate=takes(22),
    )(place, bucket, lengths, counts, hidden, hidden_low, weights, proj, probs, context)


def weight_grads_kernel(blocks, place, *refs):
    normed = refs[:blocks]
    second_low, hidden_low, act, grad_up, head_grads, tokens = [refs[(k + 1) * blocks : (k + 2) * blocks] for k in range(6)]
    vec_ref, out_ref = refs[7 * blocks], refs[7 * blocks + 1]
    turned = refs[7 * blocks + 2]
    step = pl.program_id(0)
    slot_count = second_low[0].shape[0]

    @pl.when(step == 0)
    def _():
        for b in range(blocks):
            span = slice(b * slot_count, (b + 1) * slot_count)
            first = (normed[b][...] * vec_ref[0:1] + vec_ref[3:4]).astype(LOW)
            turned[0, :, span] = tokens[b][0].T
            turned[1, :, span] = first.T
            turned[2, :, span] = second_low[b][...].T
            turned[3, :, span] = hidden_low[b][...].T

    grads = jnp.concatenate([ref[0] for ref in head_grads], axis=0)
    qkv = dot_nn(turned[0], grads)
    outs = dot_nn(turned[3], grads[:, 8 * HEAD_DIM :])
    lane = lax.broadcasted_iota(jnp.int32, (1, 2 * HEAD_DIM), 1)
    last = jnp.where(lane < HEAD_DIM, qkv[:, 10 * HEAD_DIM :], outs[:, 2 * HEAD_DIM :])
    out_ref[0, 0] = jnp.concatenate([qkv[:, : 8 * HEAD_DIM], outs[:, : 2 * HEAD_DIM], last], axis=1).astype(LOW)
    out_ref[1, 0] = dot_nn(turned[1], jnp.concatenate([ref[0] for ref in grad_up], axis=0)).astype(LOW)
    out_ref[2, 0] = dot_nn(turned[2], jnp.concatenate([ref[0] for ref in act], axis=0)).astype(LOW)


def weight_grads(place, inputs, normed, second_low, hidden_low, act, grad_up, head_grads, vectors):
    blocks = len(normed)
    normed_specs = [
        pl.BlockSpec((None,) + array.shape[1:], lambda j, p, index=index: (index, 0, 0)) for array, index in normed
    ]
    normed = [array for array, _ in normed]
    micro_count = inputs.shape[0]
    per_micro = blocks // micro_count
    parts, slot_count, cols = act[0].shape
    width = normed[0].shape[2]
    whole = lambda *shape: pl.BlockSpec(shape, lambda j, p: (0,) * len(shape))
    each = pl.BlockSpec((1, slot_count, cols), lambda j, p: (j, 0, 0))
    token_specs = [
        pl.BlockSpec((1, slot_count, width), lambda j, p, m=b // per_micro, k=b % per_micro: (m, p[0] + k, 0))
        for b in range(blocks)
    ]
    return pl.pallas_call(
        functools.partial(weight_grads_kernel, blocks),
        grid_spec=pltpu.PrefetchScalarGridSpec(
            num_scalar_prefetch=1,
            grid=(parts,),
            in_specs=normed_specs + [whole(slot_count, width)] * (2 * blocks) + [each] * (3 * blocks) + token_specs + [whole(*vectors.shape)],
            out_specs=pl.BlockSpec((3, 1, width, cols), lambda j, p: (0, j, 0, 0)),
            scratch_shapes=[pltpu.VMEM((4, width, blocks * slot_count), LOW)],
        ),
        out_shape=jax.ShapeDtypeStruct((3, parts, width, cols), LOW),
        compiler_params=params(),
        name="weight_grads",
        cost_estimate=takes(26),
    )(place, *normed, *second_low, *hidden_low, *act, *grad_up, *head_grads, *([inputs] * blocks), vectors)


def mesh_place(bits):
    d = lax.axis_index("dp")
    t = lax.axis_index("tensor")
    digits = [(d // (1 << k)) % 2 for k in range(bits)]
    mates = [d + (1 - 2 * digits[k]) * (1 << k) for k in range(bits)]
    return d, t, digits, mates


def digit_index(bits, digits, open_bits):
    return tuple(slice(None) if k in open_bits else digits[k] for k in reversed(range(bits)))


def greet(d, t, mates, parts):
    barrier = pltpu.get_barrier_semaphore()
    for mate in mates:
        pl.semaphore_signal(barrier, inc=1, device_id=(mate, t), device_id_type=MESH)
    for hop in range(1, parts):
        pl.semaphore_signal(barrier, inc=1, device_id=(d, (t + hop) % parts), device_id_type=MESH)
    pl.semaphore_wait(barrier, len(mates) + parts - 1)


def bit_order(bits, flip):
    far = list(range(1, bits))
    return (far[::-1] if flip else far) + [0]


def gather_kernel(parts, bits, own, small, full, small_dp, small_t, z_send, z_recv, h_send, h_recv, s_send, s_recv, keep):
    d, t, digits, mates = mesh_place(bits)
    slab_count = own.shape[0]
    mine = digit_index(bits, digits, ())
    greet(d, t, mates, parts)
    offsets = [0] + [sign * hop for hop in range(1, parts) for sign in (1, -1)]
    pending = []

    def remote(src, dst, send, recv, to):
        return pltpu.make_async_remote_copy(src, dst, send, recv, device_id=to, device_id_type=MESH)

    local = [pltpu.make_async_copy(own.at[s], full.at[(s, t) + mine], keep.at[s]) for s in range(slab_count)]
    local.append(pltpu.make_async_copy(small.at[0], small_dp.at[mine], keep.at[slab_count]))
    local.append(pltpu.make_async_copy(small.at[1], small_t.at[t], keep.at[slab_count + 1]))
    for copy in local:
        copy.start()

    def z_copy(s, at, src, up):
        to = (d, t + 1) if up else (d, t - 1)
        way = 0 if up else 1
        return remote(src, full.at[(s, at) + mine], z_send.at[s, at, way], z_recv.at[s, at], to)

    def h_copy(s, index, step):
        offset = offsets[index]
        order = bit_order(bits, (abs(offset) + s) % 2 == 1)
        blocks = (s, t + offset) + digit_index(bits, digits, order[:step])
        src = own.at[s] if offset == 0 and step == 0 else full.at[blocks]
        return remote(src, full.at[blocks], h_send.at[s, index, step], h_recv.at[s, index, step], (mates[order[step]], t))

    def exists(offset):
        return (t + offset >= 0) & (t + offset < parts)

    def begin(s, index):
        offset = offsets[index]
        if offset == 0:
            h_copy(s, index, 0).start()
            return

        @pl.when(exists(offset))
        def _():
            up = offset < 0
            z_copy(s, t + offset, own.at[s], up).wait_recv()

            @pl.when((t < parts - 1) if up else (t > 0))
            def _():
                z_copy(s, t + offset, full.at[(s, t + offset) + mine], up).start()

            h_copy(s, index, 0).start()

    def advance(s, index, step):
        @pl.when(exists(offsets[index]))
        def _():
            h_copy(s, index, step - 1).wait_recv()
            if step < bits:
                h_copy(s, index, step).start()

    def small_step(step):
        blocks = digit_index(bits, digits, range(step))
        src = small.at[0] if step == 0 else small_dp.at[blocks]
        return remote(src, small_dp.at[blocks], s_send.at[step], s_recv.at[step], (mates[step], t))

    def small_hop(hop):
        peer = (d, (t + hop) % parts)
        return remote(small.at[1], small_t.at[t], s_send.at[bits + hop - 1], s_recv.at[bits + hop - 1], peer)

    def send_own(s):
        @pl.when(t < parts - 1)
        def _():
            z_copy(s, t, own.at[s], True).start()

        @pl.when(t > 0)
        def _():
            z_copy(s, t, own.at[s], False).start()

    order = [(s, hop) for s in range(slab_count) for hop in range(parts)]
    groups = [(s, [index for index, offset in enumerate(offsets) if abs(offset) == hop]) for s, hop in order]
    send_own(0)
    begin(0, 0)
    for hop in range(1, parts):
        small_hop(hop).start()
    small_step(0).start()
    for copy in local:
        copy.wait()
    for wave in range(len(groups) + bits * GATHER_LAG):
        for step in range(bits + 1):
            if 0 <= wave - step * GATHER_LAG < len(groups):
                s, indices = groups[wave - step * GATHER_LAG]
                for index in indices:
                    if step:
                        advance(s, index, step)
                    elif (s, index) != (0, 0):
                        begin(s, index)
        if wave in Z_WAVES:
            send_own(1 + Z_WAVES.index(wave))
        if wave < bits:
            small_step(wave).wait_recv()
            if wave + 1 < bits:
                small_step(wave + 1).start()

    for hop in range(1, parts):
        small_hop(hop).wait()
    for step in range(bits):
        small_step(step).wait_send()
    for s, indices in groups:
        for index in indices:
            offset = offsets[index]

            @pl.when(exists(offset))
            def _():
                for step in range(bits):
                    h_copy(s, index, step).wait_send()
                if offset <= 0:
                    @pl.when(t < parts - 1)
                    def _():
                        z_copy(s, t + offset, own.at[s], True).wait_send()
                if offset >= 0:
                    @pl.when(t > 0)
                    def _():
                        z_copy(s, t + offset, own.at[s], False).wait_send()


def gather_weights(own, small, parts, dp_count):
    bits = dp_count.bit_length() - 1
    slab_count, rows, columns = own.shape
    places = 2 * parts - 1
    low = jnp.bfloat16
    full, small_dp, small_t = pl.pallas_call(
        functools.partial(gather_kernel, parts, bits),
        out_shape=[
            jax.ShapeDtypeStruct((slab_count, parts) + (2,) * bits + (rows, columns), low),
            jax.ShapeDtypeStruct((2,) * bits + small.shape[1:], low),
            jax.ShapeDtypeStruct((parts,) + small.shape[1:], low),
        ],
        in_specs=[pl.BlockSpec(memory_space=pl.ANY)] * 2,
        out_specs=[pl.BlockSpec(memory_space=pl.ANY)] * 3,
        scratch_shapes=[
            pltpu.SemaphoreType.DMA((slab_count, parts, 2)),
            pltpu.SemaphoreType.DMA((slab_count, parts)),
            pltpu.SemaphoreType.DMA((slab_count, places, bits)),
            pltpu.SemaphoreType.DMA((slab_count, places, bits)),
            pltpu.SemaphoreType.DMA((bits + parts - 1,)),
            pltpu.SemaphoreType.DMA((bits + parts - 1,)),
            pltpu.SemaphoreType.DMA((slab_count + 2,)),
        ],
        compiler_params=pltpu.CompilerParams(collective_id=0, has_side_effects=True, vmem_limit_bytes=VMEM_LIMIT),
        name="gather_weights",
        cost_estimate=takes(100),
    )(own, small)
    full = full.reshape(slab_count, parts, dp_count * rows, columns)
    return full, small_dp.reshape((dp_count,) + small.shape[1:]), small_t


def add_rows(target, first, second, rows):
    lead = target.shape[:-2]
    chunk = 16 if rows % 16 == 0 else rows
    steps = rows // chunk
    count = 1
    for extent in lead:
        count *= extent

    def one(i, carry):
        at, rest = [], i // steps
        for extent in reversed(lead):
            at.insert(0, rest % extent)
            rest = rest // extent
        where = tuple(at) + (pl.ds(pl.multiple_of((i % steps) * chunk, chunk), chunk),)
        total = first[where].astype(jnp.float32) + second[where].astype(jnp.float32)
        target[where] = total.astype(target.dtype)
        return carry

    lax.fori_loop(0, count * steps, one, 0)


def reduce_kernel(parts, bits, grads, small, out, small_out, *scratch):
    bufs = scratch[:bits]
    z_up, z_down, small_buf, small_sum = scratch[bits:bits + 4]
    h_send, h_recv, up_send, up_recv, down_send, down_recv, s_send, s_recv = scratch[bits + 4:]
    d, t, digits, mates = mesh_place(bits)
    slab_count = grads.shape[0]
    rows = grads.shape[-2]
    greet(d, t, mates, parts)
    items = [(s, at) for s in range(slab_count) for at in range(parts)]
    small_bits = bits + parts.bit_length() - 1

    def remote(src, dst, send, recv, to):
        return pltpu.make_async_remote_copy(src, dst, send, recv, device_id=to, device_id_type=MESH)

    def order_of(number):
        s, at = items[number]
        return bit_order(bits, (s + at) % 2 == 1)[::-1]

    def held(number, step):
        s, at = items[number]
        return grads.at[s, at] if step == 0 else bufs[step - 1].at[number]

    def part_of(number, step, side):
        order = order_of(number)
        left = [k for k in reversed(range(bits)) if k not in order[:step]]
        pick = tuple(side if k == order[step] else slice(None) for k in left)
        return held(number, step).at[pick]

    def h_copy(number, step):
        order = order_of(number)
        digit = digits[order[step]]
        return remote(part_of(number, step, 1 - digit), bufs[step].at[number],
                      h_send.at[number, step], h_recv.at[number, step], (mates[order[step]], t))

    def fold(number, step):
        h_copy(number, step).wait_recv()
        digit = digits[order_of(number)[step]]
        add_rows(bufs[step].at[number], bufs[step].at[number], part_of(number, step, digit), rows)

    def summed(s, at):
        return bufs[bits - 1].at[s * parts + at]

    def z_copy(s, at, up, src):
        buf, send, recv = (z_up, up_send, up_recv) if up else (z_down, down_send, down_recv)
        to = (d, t + 1) if up else (d, t - 1)
        return remote(src, buf.at[s, at], send.at[s, at], recv.at[s, at], to)

    def z_pass(s, hop, up):
        at = t + hop if up else t - hop
        edge = (t == 0) if up else (t == parts - 1)
        buf = z_up if up else z_down

        @pl.when((at < parts) if up else (at >= 0))
        def _():
            @pl.when(edge)
            def _():
                z_copy(s, at, up, summed(s, at)).start()

            @pl.when(jnp.logical_not(edge))
            def _():
                z_copy(s, at, up, summed(s, at)).wait_recv()
                add_rows(buf.at[s, at], buf.at[s, at], summed(s, at), rows)
                z_copy(s, at, up, buf.at[s, at]).start()

    def z_finish(s):
        add_rows(out.at[s], summed(s, t), summed(s, t), rows)

        def scaled(i, carry):
            out[s] = out[s] * 0.5
            return carry
        lax.fori_loop(0, 1, scaled, 0)
        for up, buf in ((True, z_up), (False, z_down)):
            @pl.when((t > 0) if up else (t < parts - 1))
            def _():
                z_copy(s, t, up, summed(s, t)).wait_recv()
                add_rows(out.at[s], out.at[s], buf.at[s, t], rows)

    def small_copy(step):
        if step < bits:
            to = (mates[step], t)
        else:
            gap = 1 << (step - bits)
            to = (d, t + (1 - 2 * ((t // gap) % 2)) * gap)
        src = small if step == 0 else small_sum.at[step - 1]
        return remote(src, small_buf.at[step], s_send.at[step], s_recv.at[step], to)

    def small_fold(step):
        small_copy(step).wait_recv()
        before = small[...] if step == 0 else small_sum[step - 1]
        small_sum[step] = before + small_buf[step]
        if step + 1 < small_bits:
            small_copy(step + 1).start()

    for number in range(len(items)):
        h_copy(number, 0).start()
        if number == 0:
            small_copy(0).start()
    for wave in range(len(items) + bits * REDUCE_LAG + parts + 1):
        for step in range(bits):
            number = wave - step * REDUCE_LAG
            if 0 <= number < len(items):
                fold(number, step)
                if step + 1 < bits:
                    h_copy(number, step + 1).start()
        for s in range(slab_count):
            phase = wave - ((s + 1) * parts - 1 + bits * REDUCE_LAG)
            if 0 <= phase < parts - 1:
                z_pass(s, parts - 1 - phase, True)
                z_pass(s, parts - 1 - phase, False)
            elif phase == parts - 1:
                z_finish(s)
        if wave < small_bits:
            small_fold(wave)
    small_out[...] = small_sum[small_bits - 1]

    for step in range(small_bits):
        small_copy(step).wait_send()
    for number in range(len(items)):
        for step in range(bits):
            h_copy(number, step).wait_send()
    for s in range(slab_count):
        for hop in range(1, parts):
            @pl.when(t + hop < parts)
            def _():
                z_copy(s, t + hop, True, summed(s, t)).wait_send()

            @pl.when(t - hop >= 0)
            def _():
                z_copy(s, t - hop, False, summed(s, t)).wait_send()


def reduce_grads(grads, small, parts, dp_count):
    bits = dp_count.bit_length() - 1
    slab_count, columns = grads.shape[0], grads.shape[-1]
    rows = grads.shape[2] // dp_count
    grads = grads.reshape((slab_count, parts) + (2,) * bits + (rows, columns))
    low = jnp.bfloat16
    count = slab_count * parts
    small_bits = bits + parts.bit_length() - 1
    dma = pltpu.SemaphoreType.DMA
    return pl.pallas_call(
        functools.partial(reduce_kernel, parts, bits),
        out_shape=[
            jax.ShapeDtypeStruct((slab_count, rows, columns), jnp.float32),
            jax.ShapeDtypeStruct(small.shape, jnp.float32),
        ],
        in_specs=[pl.BlockSpec(memory_space=pltpu.VMEM)] * 2,
        out_specs=[pl.BlockSpec(memory_space=pltpu.VMEM)] * 2,
        scratch_shapes=[pltpu.VMEM((count,) + (2,) * (bits - 1 - step) + (rows, columns), low) for step in range(bits)]
        + [pltpu.VMEM((slab_count, parts, rows, columns), low)] * 2
        + [pltpu.VMEM((small_bits,) + small.shape, jnp.float32)] * 2
        + [dma((count, bits)), dma((count, bits))]
        + [dma((slab_count, parts))] * 4
        + [dma((small_bits,))] * 2,
        compiler_params=pltpu.CompilerParams(collective_id=1, has_side_effects=True, vmem_limit_bytes=VMEM_LIMIT),
        name="reduce_grads",
        cost_estimate=takes(100),
    )(grads, small)


def forward_kernel(parts, bits, micro_count, per_micro, slot_count, w_qkv, w_out, w_in, w_down, head_bias, ffn_bias,
                   norm_gains, row_biases, bucket, lengths, counts, inputs, cotangent,
                   weights, vectors, head_rows, ffn_rows, normed_out, inverse_out, proj_out, prob_out, context_out,
                   act_out, slope_out, out_out, second_out, second_low_out, stat_out,
                   own, small, full, small_dp, small_t, tokens, cot, total, normed_buf, inverse_buf, proj_buf, prob_buf, context_buf,
                   act_buf, slope_buf, first_low, down_total, out_buf, second_buf, second_low_buf,
                   z_send, z_recv, h_send, h_recv, s_send, s_recv, keep, load, weight_done, unit_done, ffn_done, end_done):
    layout = (bucket, lengths, counts)
    d, t, digits, mates = mesh_place(bits)
    blocks = micro_count * per_micro
    slab_count = own.shape[0]
    width = own.shape[2]
    mine = digit_index(bits, digits, ())

    def block_place(b):
        return b // per_micro, t * per_micro + b % per_micro

    def block_rows(b):
        micro, place = block_place(b)
        return (micro, pl.ds(pl.multiple_of(place * slot_count, slot_count), slot_count))

    loads = [pltpu.make_async_copy(inputs.at[block_rows(b)], tokens.at[b], load.at[b]) for b in range(blocks)]
    loads.append(pltpu.make_async_copy(cotangent.at[block_rows(0)], cot, load.at[blocks]))
    own[0] = slab_order(w_qkv[0], w_qkv[1], w_qkv[2], w_out[...].T)
    own[1] = w_in[...]
    own[2] = w_down[...]
    small[...] = jnp.zeros_like(small)
    vector_count = norm_gains.shape[0] + row_biases.shape[0]
    small[0, :, : own.shape[1]] = jnp.concatenate(
        [norm_gains[...], row_biases[...], jnp.zeros((16 - vector_count, own.shape[1]), LOW)], axis=0
    )
    no_bias = jnp.zeros((1, head_bias.shape[1]), LOW)
    bias_row = slab_order(head_bias[0:1], no_bias, head_bias[1:2], no_bias)
    small[1] = jnp.concatenate([bias_row, ffn_bias[...].reshape(1, -1), jnp.zeros((14, own.shape[2]), LOW)], axis=0)
    greet(d, t, mates, parts)
    offsets = [0] + [sign * hop for hop in range(1, parts) for sign in (1, -1)]

    def remote(src, dst, send, recv, to):
        return pltpu.make_async_remote_copy(src, dst, send, recv, device_id=to, device_id_type=MESH)

    local = [pltpu.make_async_copy(own.at[s], full.at[(s, t) + mine], keep.at[s]) for s in range(slab_count)]
    local.append(pltpu.make_async_copy(small.at[0], small_dp.at[mine], keep.at[slab_count]))
    local.append(pltpu.make_async_copy(small.at[1], small_t.at[t], keep.at[slab_count + 1]))

    def z_copy(s, at, src, up):
        to = (d, t + 1) if up else (d, t - 1)
        return remote(src, full.at[(s, at) + mine], z_send.at[s, at, 0 if up else 1], z_recv.at[s, at], to)

    def h_copy(s, index, step):
        offset = offsets[index]
        order = bit_order(bits, (abs(offset) + s) % 2 == 1)
        where = (s, t + offset) + digit_index(bits, digits, order[:step])
        src = own.at[s] if offset == 0 and step == 0 else full.at[where]
        return remote(src, full.at[where], h_send.at[s, index, step], h_recv.at[s, index, step], (mates[order[step]], t))

    def exists(offset):
        return (t + offset >= 0) & (t + offset < parts)

    def weight_copy(s, at):
        return pltpu.make_async_copy(full.at[s, at], weights.at[s, at], weight_done.at[s, at])

    def begin(s, index):
        offset = offsets[index]
        if offset == 0:
            h_copy(s, index, 0).start()
            return

        @pl.when(exists(offset))
        def _():
            up = offset < 0
            z_copy(s, t + offset, own.at[s], up).wait_recv()

            @pl.when((t < parts - 1) if up else (t > 0))
            def _():
                z_copy(s, t + offset, full.at[(s, t + offset) + mine], up).start()

            h_copy(s, index, 0).start()

    def advance(s, index, step):
        @pl.when(exists(offsets[index]))
        def _():
            h_copy(s, index, step - 1).wait_recv()
            if step < bits:
                h_copy(s, index, step).start()
            else:
                weight_copy(s, t + offsets[index]).start()

    def small_step(step):
        where = digit_index(bits, digits, range(step))
        src = small.at[0] if step == 0 else small_dp.at[where]
        return remote(src, small_dp.at[where], s_send.at[step], s_recv.at[step], (mates[step], t))

    def small_hop(hop):
        peer = (d, (t + hop) % parts)
        return remote(small.at[1], small_t.at[t], s_send.at[bits + hop - 1], s_recv.at[bits + hop - 1], peer)

    def send_own(s):
        @pl.when(t < parts - 1)
        def _():
            z_copy(s, t, own.at[s], True).start()

        @pl.when(t > 0)
        def _():
            z_copy(s, t, own.at[s], False).start()

    toward = 1 - 2 * ((2 * t) // parts)

    def nearest(k):
        return (t + toward * k + parts) % parts

    def matrix(s, at):
        return full[s, at].reshape(width, full.shape[-1])

    def unit_copies(unit, at, b):
        slot = unit % 2
        heads = pl.ds(at * CHUNK_HEADS, CHUNK_HEADS)
        return [
            pltpu.make_async_copy(proj_buf.at[slot], proj_out.at[b, at], unit_done.at[slot, 0]),
            pltpu.make_async_copy(prob_buf.at[slot], prob_out.at[b, heads], unit_done.at[slot, 1]),
            pltpu.make_async_copy(context_buf.at[slot], context_out.at[b, at], unit_done.at[slot, 2]),
        ]

    def attend_part(b, k):
        unit = b * parts + k
        at = nearest(k)
        if unit >= 2:
            for copy in unit_copies(unit - 2, nearest((unit - 2) % parts), (unit - 2) // parts):
                copy.wait()
        slot = unit % 2
        micro, place = block_place(b)
        attention = attend_unit(layout, micro, place, tokens[b], matrix(0, at), head_rows[at],
                                proj_buf.at[slot], prob_buf.at[slot], context_buf.at[slot])
        if k == 0:
            total[...] = attention
        else:
            total[...] += attention
        for copy in unit_copies(unit, at, b):
            copy.start()
        if k == parts - 1:
            normed, inverse = normalize(tokens[b].astype(WIDE) + total[...] + vectors[2:3])
            normed_buf[b] = normed
            inverse_buf[b] = jnp.broadcast_to(inverse, inverse_buf.shape[1:])
            for copy in norm_copies(b):
                copy.start()

    def norm_copies(b):
        return [pltpu.make_async_copy(normed_buf.at[b], normed_out.at[b], end_done.at[b, 0]),
                pltpu.make_async_copy(inverse_buf.at[b], inverse_out.at[b], end_done.at[b, 1])]

    def ffn_copies(k):
        slot, at = k % 2, nearest(k)
        return [pltpu.make_async_copy(act_buf.at[slot], act_out.at[at], ffn_done.at[slot, 0]),
                pltpu.make_async_copy(slope_buf.at[slot], slope_out.at[at], ffn_done.at[slot, 1])]

    def final_copies():
        return [pltpu.make_async_copy(out_buf, out_out, end_done.at[blocks, 0]),
                pltpu.make_async_copy(second_buf, second_out, end_done.at[blocks, 1]),
                pltpu.make_async_copy(second_low_buf, second_low_out, end_done.at[blocks + 1, 0])]

    def ffn_part(k):
        at = nearest(k)
        if k == 0:
            first_low[...] = (normed_buf[0] * vectors[0:1] + vectors[3:4]).astype(LOW)
        if k >= 2:
            for copy in ffn_copies(k - 2):
                copy.wait()
        slot = k % 2
        down = ffn_unit(first_low[...], matrix(1, at), matrix(2, at), ffn_rows[at], act_buf.at[slot], slope_buf.at[slot])
        for copy in ffn_copies(k):
            copy.start()
        if k == 0:
            down_total[...] = down
        else:
            down_total[...] += down
        if k == parts - 1:
            micro, place = block_place(0)
            out, second, stat = second_norm(layout, micro, place, normed_buf[0], down_total[...], cot[...], vectors)
            out_buf[...] = out
            second_buf[...] = second
            second_low_buf[...] = second.astype(LOW)
            stat_out[...] = stat
            for copy in final_copies():
                copy.start()

    def finish_small():
        lanes = own.shape[1]
        pieces = [small_dp[digit_index(bits, [(i // (1 << k)) % 2 for k in range(bits)], ())][:8, :lanes].astype(WIDE)
                  for i in range(1 << bits)]
        vectors[...] = jnp.concatenate(pieces, axis=1)
        for at in range(parts):
            head_rows[at] = small_t[at, 0:1, :].astype(WIDE)
            ffn_rows[at] = small_t[at, 1:2, :].astype(WIDE)

    send_own(0)
    begin(0, 0)
    for hop in range(1, parts):
        small_hop(hop).start()
    small_step(0).start()
    for copy in local + loads:
        copy.start()
    for copy in local + loads:
        copy.wait()

    order = [(s, hop) for s in range(slab_count) for hop in range(parts)]
    groups = [(s, [index for index, offset in enumerate(offsets) if abs(offset) == hop]) for s, hop in order]
    done_at = {place: number + bits * GATHER_LAG for number, place in enumerate(order)}
    jobs = [(done_at[(0, k)], functools.partial(attend_part, b, k)) for b in range(blocks) for k in range(parts)]
    jobs += [(done_at[(slab_count - 1, k)], functools.partial(ffn_part, k)) for k in range(parts)]
    for wave in range(len(groups) + bits * GATHER_LAG):
        for step in range(bits + 1):
            if 0 <= wave - step * GATHER_LAG < len(groups):
                s, indices = groups[wave - step * GATHER_LAG]
                for index in indices:
                    if step:
                        advance(s, index, step)
                    elif (s, index) != (0, 0):
                        begin(s, index)
        if wave in Z_WAVES:
            send_own(1 + Z_WAVES.index(wave))
        if wave < bits:
            small_step(wave).wait_recv()
            if wave + 1 < bits:
                small_step(wave + 1).start()
            else:
                for hop in range(1, parts):
                    small_hop(hop).wait_recv()
                finish_small()
        if jobs and jobs[0][0] <= wave:
            jobs.pop(0)[1]()
    for _, job in jobs:
        job()

    for hop in range(1, parts):
        small_hop(hop).wait_send()
    for step in range(bits):
        small_step(step).wait_send()
    for s, indices in groups:
        for index in indices:
            offset = offsets[index]

            @pl.when(exists(offset))
            def _():
                for step in range(bits):
                    h_copy(s, index, step).wait_send()
                weight_copy(s, t + offset).wait()
                if offset <= 0:
                    @pl.when(t < parts - 1)
                    def _():
                        z_copy(s, t + offset, own.at[s], True).wait_send()
                if offset >= 0:
                    @pl.when(t > 0)
                    def _():
                        z_copy(s, t + offset, own.at[s], False).wait_send()
    last = blocks * parts
    for unit in range(max(0, last - 2), last):
        for copy in unit_copies(unit, nearest(unit % parts), unit // parts):
            copy.wait()
    for k in range(max(0, parts - 2), parts):
        for copy in ffn_copies(k):
            copy.wait()
    for b in range(blocks):
        for copy in norm_copies(b):
            copy.wait()
    for copy in final_copies():
        copy.wait()


def forward(arrays, layout, inputs, cotangent, parts, dp_count, slot_count, micro_count, per_micro):
    bits = dp_count.bit_length() - 1
    slab_count = 3
    rows, cols = arrays[2].shape
    width = rows * dp_count
    places = 2 * parts - 1
    blocks = micro_count * per_micro
    heads = parts * CHUNK_HEADS
    spread = (slab_count, parts) + (2,) * bits + (rows, cols)
    shape = jax.ShapeDtypeStruct
    dma = pltpu.SemaphoreType.DMA
    hbm, vmem, smem = [pl.BlockSpec(memory_space=space) for space in (pl.ANY, pltpu.VMEM, pltpu.SMEM)]
    slab = (slot_count, cols)
    rows_of = (slot_count, width)
    outs = [
        (spread, LOW, hbm),
        ((8, width), WIDE, vmem),
        ((parts, 1, cols), WIDE, vmem),
        ((parts, 1, cols), WIDE, vmem),
        ((blocks,) + rows_of, WIDE, hbm),
        ((blocks, slot_count, 128), WIDE, hbm),
        ((blocks, parts) + slab, LOW, hbm),
        ((blocks, heads, slot_count, slot_count), LOW, hbm),
        ((blocks, parts, slot_count, 4 * HEAD_DIM), LOW, hbm),
        ((parts,) + slab, LOW, hbm),
        ((parts,) + slab, LOW, hbm),
        (rows_of, LOW, hbm),
        (rows_of, WIDE, hbm),
        (rows_of, LOW, hbm),
        ((8, width), WIDE, vmem),
    ]
    result = pl.pallas_call(
        functools.partial(forward_kernel, parts, bits, micro_count, per_micro, slot_count),
        out_shape=[shape(dims, kind) for dims, kind, _ in outs],
        in_specs=[vmem] * len(arrays) + [smem, smem, smem, hbm, hbm],
        out_specs=[space for _, _, space in outs],
        scratch_shapes=[
            pltpu.VMEM((slab_count, rows, cols), LOW),
            pltpu.VMEM((2, 16, cols), LOW),
            pltpu.VMEM(spread, LOW),
            pltpu.VMEM((2,) * bits + (16, cols), LOW),
            pltpu.VMEM((parts, 16, cols), LOW),
            pltpu.VMEM((blocks,) + rows_of, LOW),
            pltpu.VMEM(rows_of, LOW),
            pltpu.VMEM(rows_of, WIDE),
            pltpu.VMEM((blocks,) + rows_of, WIDE),
            pltpu.VMEM((blocks, slot_count, 128), WIDE),
            pltpu.VMEM((2,) + slab, LOW),
            pltpu.VMEM((2, CHUNK_HEADS, slot_count, slot_count), LOW),
            pltpu.VMEM((2, slot_count, 4 * HEAD_DIM), LOW),
            pltpu.VMEM((2,) + slab, LOW),
            pltpu.VMEM((2,) + slab, LOW),
            pltpu.VMEM(rows_of, LOW),
            pltpu.VMEM(rows_of, WIDE),
            pltpu.VMEM(rows_of, LOW),
            pltpu.VMEM(rows_of, WIDE),
            pltpu.VMEM(rows_of, LOW),
            dma((slab_count, parts, 2)),
            dma((slab_count, parts)),
            dma((slab_count, places, bits)),
            dma((slab_count, places, bits)),
            dma((bits + parts - 1,)),
            dma((bits + parts - 1,)),
            dma((slab_count + 2,)),
            dma((blocks + 1,)),
            dma((slab_count, parts)),
            dma((2, 3)),
            dma((2, 2)),
            dma((blocks + 2, 2)),
        ],
        compiler_params=pltpu.CompilerParams(collective_id=2, has_side_effects=True, vmem_limit_bytes=VMEM_LIMIT),
        name="forward",
    )(*arrays, *layout, inputs, cotangent)
    return (result[0].reshape(slab_count, parts, width, cols),) + tuple(result[1:])


def phase_index(step, parts, uses):
    block = jnp.int32(uses[0][1])
    part = jnp.clip(step - uses[0][0] * parts, 0, parts - 1)
    for phase, b in uses[1:]:
        later = step >= phase * parts
        block = jnp.where(later, b, block)
        part = jnp.where(later, jnp.clip(step - phase * parts, 0, parts - 1), part)
    return block, part


def line_events(send, hand_on, blocks, parts, chunks, start):
    events = []
    for b in range(blocks):
        for q in range(chunks):
            events.append((start[b][0], functools.partial(send, b, q)))
            for hop in range(1, parts - 1):
                events.append((start[b][hop] + q, functools.partial(hand_on, b, hop, q)))
            events.append((start[b][parts - 2] + q + chunks, functools.partial(hand_on, b, parts - 1, q)))
    return events


def backward_kernel(parts, micro_count, per_micro, slot_count, chunks, phases, bucket, lengths, counts, stat_first, vectors,
                    ffn_rows, first_out, cotangent, w_head, w_in, w_down, normed, inverse, slope_first, second_first,
                    second_low_first, proj, probs, context,
                    line_out, act_out, second_low_out, up_out, hidden_low_out, head_out, token_out, small_out,
                    first_low, total, slope_buf, second_buf, second_low_buf, hidden_buf, hidden_low_buf, out_buf, cot,
                    g_send, g_recv, g_keep, load):
    layout = (bucket, lengths, counts)
    d = lax.axis_index("dp")
    t = lax.axis_index("tensor")
    step = pl.program_id(0)
    blocks = micro_count * per_micro
    chunk_rows = slot_count // chunks

    def block_place(b):
        return b // per_micro, t * per_micro + b % per_micro

    def line_rows(b, at, q):
        place = at * per_micro + b % per_micro
        start = pl.multiple_of(place * slot_count + q * chunk_rows, chunk_rows)
        return line_out.at[b // per_micro, pl.ds(start, chunk_rows)]

    def own_rows(b, q):
        source = first_out if b == 0 else out_buf.at[b - 1]
        return source.at[pl.ds(q * chunk_rows, chunk_rows)]

    def line_copy(b, at, q, src, up):
        to = (d, t + 1) if up else (d, t - 1)
        return pltpu.make_async_remote_copy(src, line_rows(b, at, q), g_send.at[b, at, q, 0 if up else 1], g_recv.at[b, at, q],
                                            device_id=to, device_id_type=MESH)

    def keep_copy(b, q):
        return pltpu.make_async_copy(own_rows(b, q), line_rows(b, t, q), g_keep.at[b, q])

    def line_send(b, q):
        for up in (True, False):
            @pl.when((t < parts - 1) if up else (t > 0))
            def _():
                line_copy(b, t, q, own_rows(b, q), up).start()
        keep_copy(b, q).start()

    def line_pass(b, hop, q):
        for up in (True, False):
            at = t - hop if up else t + hop

            @pl.when((at >= 0) if up else (at < parts))
            def _():
                line_copy(b, at, q, own_rows(b, q), up).wait_recv()

                @pl.when((t < parts - 1) if up else (t > 0))
                def _():
                    line_copy(b, at, q, line_rows(b, at, q), up).start()

    def line_settle(b, hop, q):
        for up in (True, False):
            at = t - hop if up else t + hop

            @pl.when(((at >= 0) if up else (at < parts)) & ((t < parts - 1) if up else (t > 0)))
            def _():
                line_copy(b, at, q, own_rows(b, q), up).wait_send()

    def cot_copy(b):
        micro, place = block_place(b)
        rows = pl.ds(pl.multiple_of(place * slot_count, slot_count), slot_count)
        return pltpu.make_async_copy(cotangent.at[micro, rows], cot.at[b - 1], load.at[b - 1])

    @pl.when(step == 0)
    def _():
        greet(d, t, [], parts)
        for b in range(1, blocks):
            cot_copy(b).start()
        small_out[...] = jnp.zeros_like(small_out)
        small_out[1:2] = stat_first[0:1]
        small_out[5:6] = stat_first[1:2]
        small_out[4:5] = stat_first[2:3]

    events = line_events(line_send, line_pass, blocks, parts, chunks, LINE_START)
    last_step = len(phases) * parts
    for when in sorted(set(at for at, _ in events)):
        if when < last_step:
            @pl.when(step == when)
            def _():
                for at, event in events:
                    if at == when:
                        event()

    def collect(part, value):
        @pl.when(part == 0)
        def _():
            total[...] = value

        @pl.when(part > 0)
        def _():
            total[...] += value

    def ffn_phase(b, part):
        @pl.when(part == 0)
        def _():
            first_low[...] = (normed[...] * vectors[0:1] + vectors[3:4]).astype(LOW)

        down = ffn_unit(first_low[...], w_in[0, 0], w_down[0, 0], ffn_rows[part], act_out.at[0, 0], slope_buf.at[b - 1, part])
        collect(part, down)

        @pl.when(part == parts - 1)
        def _():
            cot_copy(b).wait()
            micro, place = block_place(b)
            out, second, stat = second_norm(layout, micro, place, normed[...], total[...], cot[b - 1], vectors)
            out_buf[b - 1] = out
            second_buf[b - 1] = second
            second_low_buf[b - 1] = second.astype(LOW)
            second_low_out[0] = second.astype(LOW)
            small_out[1:2] += stat[0:1]
            small_out[5:6] += stat[1:2]
            small_out[4:5] += stat[2:3]

    def ffn_back_phase(b, part):
        second_low = second_low_first[...] if b == 0 else second_low_buf[b - 1]
        slope = slope_first[0] if b == 0 else slope_buf[b - 1, part]
        grad_act = dot_nn(second_low, w_down[0, 0])
        grad_up = (grad_act * slope.astype(WIDE)).astype(LOW)
        up_out[0, 0] = grad_up
        small_out[pl.ds(6 + part, 1)] += row_sum(grad_up.astype(WIDE))
        collect(part, dot_nt(grad_up, w_in[0, 0]))

        @pl.when(part == parts - 1)
        def _():
            grad_first = total[...] + (second_first[...] if b == 0 else second_buf[b - 1])
            unit = normed[...]
            hidden = norm_pullback(grad_first, unit, inverse[:, :1], vectors[0:1])
            hidden_buf[...] = hidden
            hidden_low_buf[...] = hidden.astype(LOW)
            hidden_low_out[0] = hidden.astype(LOW)
            small_out[0:1] += row_sum(grad_first * unit)
            small_out[3:4] += row_sum(grad_first)
            small_out[2:3] += row_sum(hidden)

    def attend_back_phase(b, part):
        micro, place = block_place(b)
        slab, back, sums = attend_back_unit(layout, micro, place, hidden_low_buf[...], w_head[0, 0], proj[0, 0], probs[0],
                                            context[0, 0])
        head_out[0, 0] = slab
        small_out[pl.ds(6 + parts + part, 1)] += sums
        collect(part, back)

        @pl.when(part == parts - 1)
        def _():
            token_out[0] = (total[...] + hidden_buf[...]).astype(LOW)

    kinds = {"ffn": ffn_phase, "ffn_back": ffn_back_phase, "attend_back": attend_back_phase}
    for number, (kind, b) in enumerate(phases):
        @pl.when((step >= number * parts) & (step < (number + 1) * parts))
        def _():
            kinds[kind](b, step - number * parts)

    @pl.when(step == last_step - 1)
    def _():
        for at, event in events:
            if at >= last_step:
                event()
        for b in range(blocks):
            for q in range(chunks):
                keep_copy(b, q).wait()
                for hop in range(parts - 1):
                    line_settle(b, hop, q)


def backward(layout, stat_first, vectors, ffn_rows, first_out, cotangent, weights, normed, inverse, slope_first, second_first,
             second_low_first, proj, probs, context, micro_count, per_micro):
    parts, width, cols = weights.shape[1:]
    blocks, slot_count = normed.shape[:2]
    tokens = cotangent.shape[1]
    phases = [("ffn", b) for b in range(1, blocks)]
    for b in range(blocks):
        phases += [("ffn_back", b), ("attend_back", b)]

    def uses(*kinds):
        return [(number, b) for number, (kind, b) in enumerate(phases) if kind in kinds]

    def whole(*dims):
        return pl.BlockSpec(dims, lambda i: (0,) * len(dims))

    def stacked(dims, kinds, shift=0):
        def place(i):
            block, part = phase_index(i, parts, uses(*kinds))
            return (block - shift, part) + (0,) * len(dims)
        return pl.BlockSpec((1, 1) + dims, place)

    def by_block(dims, kinds, shift=0, squeeze=False):
        def place(i):
            return (phase_index(i, parts, uses(*kinds))[0] - shift,) + (0,) * len(dims)
        return pl.BlockSpec((None if squeeze else 1,) + dims, place)

    def slab(index, kinds):
        def place(i):
            return (index, phase_index(i, parts, uses(*kinds))[1], 0, 0)
        return pl.BlockSpec((1, 1, width, cols), place)

    def first_parts(i):
        return (phase_index(i, parts, [use for use in uses("ffn_back") if use[1] == 0])[1], 0, 0)

    shape = jax.ShapeDtypeStruct
    dma = pltpu.SemaphoreType.DMA
    hbm, smem = pl.BlockSpec(memory_space=pl.ANY), pl.BlockSpec(memory_space=pltpu.SMEM)
    rows_of = (slot_count, width)
    square = (slot_count, cols)
    later = max(blocks - 1, 1)
    both = ("ffn", "ffn_back")
    return pl.pallas_call(
        functools.partial(backward_kernel, parts, micro_count, per_micro, slot_count, LINE_CHUNKS, phases),
        grid=(len(phases) * parts,),
        in_specs=[
            smem, smem, smem,
            whole(*stat_first.shape),
            whole(*vectors.shape),
            whole(*ffn_rows.shape),
            hbm,
            hbm,
            slab(0, ("attend_back",)),
            slab(1, both),
            slab(2, both),
            by_block(rows_of, both, squeeze=True),
            by_block((slot_count, 128), ("ffn_back",), squeeze=True),
            pl.BlockSpec((1,) + square, first_parts),
            whole(*rows_of),
            whole(*rows_of),
            stacked(square, ("attend_back",)),
            pl.BlockSpec((1, CHUNK_HEADS, slot_count, slot_count),
                         lambda i: phase_index(i, parts, uses("attend_back")) + (0, 0)),
            stacked((slot_count, 4 * HEAD_DIM), ("attend_back",)),
        ],
        out_specs=[
            hbm,
            stacked(square, ("ffn",), 1),
            by_block(rows_of, ("ffn",), 1),
            stacked(square, ("ffn_back",)),
            by_block(rows_of, ("ffn_back",)),
            stacked(square, ("attend_back",)),
            by_block(rows_of, ("attend_back",)),
            whole(16, width),
        ],
        out_shape=[
            shape((micro_count, tokens, width), LOW),
            shape((later, parts) + square, LOW),
            shape((later,) + rows_of, LOW),
            shape((blocks, parts) + square, LOW),
            shape((blocks,) + rows_of, LOW),
            shape((blocks, parts) + square, LOW),
            shape((blocks,) + rows_of, LOW),
            shape((16, width), WIDE),
        ],
        scratch_shapes=[
            pltpu.VMEM(rows_of, LOW),
            pltpu.VMEM(rows_of, WIDE),
            pltpu.VMEM((later, parts) + square, LOW),
            pltpu.VMEM((later,) + rows_of, WIDE),
            pltpu.VMEM((later,) + rows_of, LOW),
            pltpu.VMEM(rows_of, WIDE),
            pltpu.VMEM(rows_of, LOW),
            pltpu.VMEM((later,) + rows_of, LOW),
            pltpu.VMEM((later,) + rows_of, LOW),
            dma((blocks, parts, LINE_CHUNKS, 2)),
            dma((blocks, parts, LINE_CHUNKS)),
            dma((blocks, LINE_CHUNKS)),
            dma((later,)),
        ],
        compiler_params=pltpu.CompilerParams(
            dimension_semantics=("arbitrary",), collective_id=4, has_side_effects=True, vmem_limit_bytes=VMEM_LIMIT
        ),
        name="backward",
        cost_estimate=takes(100),
    )(*layout, stat_first, vectors, ffn_rows, first_out, cotangent, weights, weights, weights, normed, inverse, slope_first,
      second_first, second_low_first, proj, probs, context)


def finish_kernel(parts, bits, micro_count, per_micro, slot_count, chunks, vectors, small, inputs, normed, second_low_first,
                  second_low_later, hidden_low, act_first, act_later, grad_up, head_grads, token_grad, *rest):
    blocks = micro_count * per_micro
    second_low = [second_low_first] + [second_low_later.at[b - 1] for b in range(1, blocks)]
    act = [act_first] + [act_later.at[b - 1] for b in range(1, blocks)]
    hidden_low, grad_up, head_grads, token_grad = [
        [array.at[b] for b in range(blocks)] for array in (hidden_low, grad_up, head_grads, token_grad)
    ]
    gathered, out, small_out = rest[:3]
    (grads, operand, turned, staged, staged_wide, small_buf, small_sum, z_up, z_down) = rest[3:12]
    bufs = rest[12 : 12 + bits]
    (h_send, h_recv, up_send, up_recv, down_send, down_recv, s_send, s_recv, g_send, g_recv, g_keep, load, load_wide, fetch) = rest[
        12 + bits :
    ]
    d, t, digits, mates = mesh_place(bits)
    slab_count = grads.shape[0]
    rows = grads.shape[-2]
    width = inputs.shape[2]
    items = [(s, at) for s in range(slab_count) for at in range(parts)]
    small_bits = bits + parts.bit_length() - 1
    chunk_rows = slot_count // chunks

    def remote(src, dst, send, recv, to):
        return pltpu.make_async_remote_copy(src, dst, send, recv, device_id=to, device_id_type=MESH)

    def token_rows(b):
        place = t * per_micro + b % per_micro
        return inputs.at[b // per_micro, pl.ds(pl.multiple_of(place * slot_count, slot_count), slot_count)]

    def span(b):
        return pl.ds(b * slot_count, slot_count)

    def stage_loads(which):
        if which == 3:
            return [pltpu.make_async_copy(normed.at[b], staged_wide.at[span(b)], load_wide.at[b]) for b in range(blocks)]
        source = ([token_rows(b) for b in range(blocks)], hidden_low, second_low)[which]
        return [pltpu.make_async_copy(source[b], staged.at[which, span(b)], load.at[which, b]) for b in range(blocks)]

    def operand_loads(number):
        s, at = items[number]
        source = (head_grads, grad_up, act)[s]
        slot = number % 3
        return [pltpu.make_async_copy(source[b].at[at], operand.at[slot, span(b)], fetch.at[slot, b]) for b in range(blocks)]

    def grads_job(number):
        s, at = items[number]
        if number == 0:
            for copy in stage_loads(0) + stage_loads(1):
                copy.wait()
            turned[0] = staged[0].T
            turned[1] = staged[1].T
        elif at == 0 and s == 1:
            for copy in stage_loads(3):
                copy.wait()
            turned[0] = (staged_wide[...] * vectors[0:1] + vectors[3:4]).astype(LOW).T
        elif at == 0:
            for copy in stage_loads(2):
                copy.wait()
            turned[1] = staged[2].T
        for copy in operand_loads(number):
            copy.wait()
        right = operand[number % 3]
        if s == 0:
            qkv = dot_nn(turned[0], right)
            outs = dot_nn(turned[1], right[:, 8 * HEAD_DIM :])
            lane = lax.broadcasted_iota(jnp.int32, (1, 2 * HEAD_DIM), 1)
            last = jnp.where(lane < HEAD_DIM, qkv[:, 10 * HEAD_DIM :], outs[:, 2 * HEAD_DIM :])
            total = jnp.concatenate([qkv[:, : 8 * HEAD_DIM], outs[:, : 2 * HEAD_DIM], last], axis=1)
        else:
            total = dot_nn(turned[s - 1], right)
        grads[s, at] = total.astype(LOW).reshape(grads.shape[2:])
        if number + 3 < len(items):
            for copy in operand_loads(number + 3):
                copy.start()

    def order_of(number):
        s, at = items[number]
        return bit_order(bits, (s + at) % 2 == 1)[::-1]

    def held(number, step):
        s, at = items[number]
        return grads.at[s, at] if step == 0 else bufs[step - 1].at[number]

    def part_of(number, step, side):
        order = order_of(number)
        left = [k for k in reversed(range(bits)) if k not in order[:step]]
        pick = tuple(side if k == order[step] else slice(None) for k in left)
        return held(number, step).at[pick]

    def h_copy(number, step):
        order = order_of(number)
        digit = digits[order[step]]
        return remote(part_of(number, step, 1 - digit), bufs[step].at[number],
                      h_send.at[number, step], h_recv.at[number, step], (mates[order[step]], t))

    def fold(number, step):
        h_copy(number, step).wait_recv()
        digit = digits[order_of(number)[step]]
        add_rows(bufs[step].at[number], bufs[step].at[number], part_of(number, step, digit), rows)

    def summed(s, at):
        return bufs[bits - 1].at[s * parts + at]

    def z_copy(s, at, up, src):
        buf, send, recv = (z_up, up_send, up_recv) if up else (z_down, down_send, down_recv)
        to = (d, t + 1) if up else (d, t - 1)
        return remote(src, buf.at[s, at], send.at[s, at], recv.at[s, at], to)

    def z_pass(s, hop, up):
        at = t + hop if up else t - hop
        edge = (t == 0) if up else (t == parts - 1)
        buf = z_up if up else z_down

        @pl.when((at < parts) if up else (at >= 0))
        def _():
            @pl.when(edge)
            def _():
                z_copy(s, at, up, summed(s, at)).start()

            @pl.when(jnp.logical_not(edge))
            def _():
                z_copy(s, at, up, summed(s, at)).wait_recv()
                add_rows(buf.at[s, at], buf.at[s, at], summed(s, at), rows)
                z_copy(s, at, up, buf.at[s, at]).start()

    def z_finish(s):
        @pl.when(t > 0)
        def _():
            z_copy(s, t, True, summed(s, t)).wait_recv()
            add_rows(out.at[s], summed(s, t), z_up.at[s, t], rows)

        @pl.when(t < parts - 1)
        def _():
            z_copy(s, t, False, summed(s, t)).wait_recv()

            @pl.when(t > 0)
            def _():
                add_rows(out.at[s], out.at[s], z_down.at[s, t], rows)

            @pl.when(t == 0)
            def _():
                add_rows(out.at[s], summed(s, t), z_down.at[s, t], rows)

    def small_copy(step):
        if step < bits:
            to = (mates[step], t)
        else:
            gap = 1 << (step - bits)
            to = (d, t + (1 - 2 * ((t // gap) % 2)) * gap)
        src = small if step == 0 else small_sum.at[step - 1]
        return remote(src, small_buf.at[step], s_send.at[step], s_recv.at[step], to)

    def small_fold(step):
        small_copy(step).wait_recv()
        before = small[...] if step == 0 else small_sum[step - 1]
        small_sum[step] = before + small_buf[step]
        if step + 1 < small_bits:
            small_copy(step + 1).start()

    def line_rows(b, at, q):
        place = at * per_micro + b % per_micro
        start = pl.multiple_of(place * slot_count + q * chunk_rows, chunk_rows)
        return gathered.at[b // per_micro, pl.ds(start, chunk_rows)]

    def own_rows(b, q):
        return token_grad[b].at[pl.ds(q * chunk_rows, chunk_rows)]

    def line_copy(b, at, q, src, up):
        to = (d, t + 1) if up else (d, t - 1)
        return remote(src, line_rows(b, at, q), g_send.at[b, at, q, 0 if up else 1], g_recv.at[b, at, q], to)

    def line_send(b, q):
        for up in (True, False):
            @pl.when((t < parts - 1) if up else (t > 0))
            def _():
                line_copy(b, t, q, own_rows(b, q), up).start()

    def line_pass(b, hop, q):
        for up in (True, False):
            at = t - hop if up else t + hop

            @pl.when((at >= 0) if up else (at < parts))
            def _():
                line_copy(b, at, q, own_rows(b, q), up).wait_recv()

                @pl.when((t < parts - 1) if up else (t > 0))
                def _():
                    line_copy(b, at, q, line_rows(b, at, q), up).start()

    def line_settle(b, hop, q):
        for up in (True, False):
            at = t - hop if up else t + hop

            @pl.when(((at >= 0) if up else (at < parts)) & ((t < parts - 1) if up else (t > 0)))
            def _():
                line_copy(b, at, q, own_rows(b, q), up).wait_send()

    keeps = [pltpu.make_async_copy(own_rows(b, q), line_rows(b, t, q), g_keep.at[b, q])
             for b in range(blocks) for q in range(chunks)]
    events = []
    for turn in range(blocks + parts):
        for hop in range(parts + 1):
            b = turn - hop
            if 0 <= b < blocks and hop <= parts - 1:
                for q in range(chunks):
                    events.append(functools.partial(line_send, b, q) if hop == 0 else functools.partial(line_pass, b, hop, q))

    for copy in stage_loads(0) + stage_loads(1):
        copy.start()
    for number in range(min(3, len(items))):
        for copy in operand_loads(number):
            copy.start()
    for copy in stage_loads(3) + stage_loads(2):
        copy.start()
    greet(d, t, mates, parts)
    for copy in keeps:
        copy.start()
    small_copy(0).start()
    ahead = chunks

    waves = len(items) + bits * REDUCE_LAG + parts
    per_wave = LINE_PACE
    for wave in range(max(waves, len(events))):
        while events and wave * per_wave + ahead > total_done(events, blocks, parts, chunks):
            events.pop(0)()
        if wave < len(items):
            grads_job(wave)
            h_copy(wave, 0).start()
        for step in range(bits):
            number = wave - (step + 1) * REDUCE_LAG + 1
            if 0 <= number < len(items):
                fold(number, step)
                if step + 1 < bits:
                    h_copy(number, step + 1).start()
        for s in range(slab_count):
            phase = wave - ((s + 1) * parts + bits * REDUCE_LAG - 1)
            if 0 <= phase < parts - 1:
                z_pass(s, parts - 1 - phase, True)
                z_pass(s, parts - 1 - phase, False)
            elif phase == parts - 1:
                z_finish(s)
        if wave < small_bits:
            small_fold(wave)
    small_out[...] = small_sum[small_bits - 1]

    for copy in keeps:
        copy.wait()
    for b in range(blocks):
        for hop in range(parts - 1):
            for q in range(chunks):
                line_settle(b, hop, q)
    for step in range(small_bits):
        small_copy(step).wait_send()
    for number in range(len(items)):
        for step in range(bits):
            h_copy(number, step).wait_send()
    for s in range(slab_count):
        for hop in range(1, parts):
            @pl.when(t + hop < parts)
            def _():
                z_copy(s, t + hop, True, summed(s, t)).wait_send()

            @pl.when(t - hop >= 0)
            def _():
                z_copy(s, t - hop, False, summed(s, t)).wait_send()


def total_done(events, blocks, parts, chunks):
    return blocks * parts * chunks - len(events)


def finish(vectors, small, inputs, normed, second_low_first, second_low_later, hidden_low, act_first, act_later, grad_up,
           head_grads, token_grad, parts, dp_count):
    bits = dp_count.bit_length() - 1
    blocks = token_grad.shape[0]
    micro_count, tokens, width = inputs.shape
    per_micro = blocks // micro_count
    slot_count, cols = act_first.shape[1:]
    rows = width // dp_count
    slab_count = 3
    count = slab_count * parts
    small_bits = bits + parts.bit_length() - 1
    dma = pltpu.SemaphoreType.DMA
    hbm, vmem = pl.BlockSpec(memory_space=pl.ANY), pl.BlockSpec(memory_space=pltpu.VMEM)
    block = (rows, cols)
    return pl.pallas_call(
        functools.partial(finish_kernel, parts, bits, micro_count, per_micro, slot_count, LINE_CHUNKS),
        out_shape=[
            jax.ShapeDtypeStruct((micro_count, tokens, width), LOW),
            jax.ShapeDtypeStruct((slab_count,) + block, WIDE),
            jax.ShapeDtypeStruct(small.shape, WIDE),
        ],
        in_specs=[vmem, vmem] + [hbm] * 10,
        out_specs=[hbm, vmem, vmem],
        scratch_shapes=[
            pltpu.VMEM((slab_count, parts) + (2,) * bits + block, LOW),
            pltpu.VMEM((3, blocks * slot_count, cols), LOW),
            pltpu.VMEM((2, width, blocks * slot_count), LOW),
            pltpu.VMEM((3, blocks * slot_count, width), LOW),
            pltpu.VMEM((blocks * slot_count, width), WIDE),
            pltpu.VMEM((small_bits,) + small.shape, WIDE),
            pltpu.VMEM((small_bits,) + small.shape, WIDE),
            pltpu.VMEM((slab_count, parts) + block, LOW),
            pltpu.VMEM((slab_count, parts) + block, LOW),
        ]
        + [pltpu.VMEM((count,) + (2,) * (bits - 1 - step) + block, LOW) for step in range(bits)]
        + [dma((count, bits)), dma((count, bits))]
        + [dma((slab_count, parts))] * 4
        + [dma((small_bits,))] * 2
        + [dma((blocks, parts, LINE_CHUNKS, 2)), dma((blocks, parts, LINE_CHUNKS)), dma((blocks, LINE_CHUNKS))]
        + [dma((3, blocks)), dma((blocks,)), dma((3, blocks))],
        compiler_params=pltpu.CompilerParams(collective_id=3, has_side_effects=True, vmem_limit_bytes=VMEM_LIMIT),
        name="finish",
        cost_estimate=takes(100),
    )(vectors, small, inputs, normed, second_low_first, second_low_later, hidden_low, act_first, act_later, grad_up, head_grads,
      token_grad)


def place_kernel(parts, dp_count, shard, sums, grad_qkv, grad_out, grad_in, grad_down, grad_head, grad_ffn,
                 grad_gains, grad_shifts):
    dp_rank, rank = lax.axis_index("dp"), lax.axis_index("tensor")
    groups = slab_parts(shard[0])
    for i in range(3):
        grad_qkv[i] = groups[i]
    grad_out[...] = groups[3].T
    grad_in[...] = shard[1]
    grad_down[...] = shard[2]
    grad_ffn[...] = sums[pl.ds(6 + rank, 1), :].reshape(-1)
    head = slab_parts(sums[pl.ds(6 + parts + rank, 1), :])
    grad_head[...] = jnp.concatenate([head[0], head[2]], axis=0)
    rows = shard.shape[1]
    wide = sums[0:8, :]
    vectors = wide[:, :rows]
    for i in range(1, dp_count):
        vectors = jnp.where(dp_rank == i, wide[:, i * rows : (i + 1) * rows], vectors)
    grad_gains[...] = vectors[0:2]
    grad_shifts[...] = vectors[2:6]


def place_results(shard, sums, parts, dp_count):
    rows, cols = shard.shape[1:]
    head_cols = CHUNK_HEADS * HEAD_DIM
    smalls = [(3, rows, head_cols), (head_cols, rows), (rows, cols), (rows, cols), (2, head_cols), (cols,), (2, rows), (4, rows)]
    vmem = pl.BlockSpec(memory_space=pltpu.VMEM)
    return pl.pallas_call(
        functools.partial(place_kernel, parts, dp_count),
        in_specs=[vmem, vmem],
        out_specs=[vmem] * len(smalls),
        out_shape=[jax.ShapeDtypeStruct(dims, WIDE) for dims in smalls],
        compiler_params=pltpu.CompilerParams(vmem_limit_bytes=VMEM_LIMIT),
        name="place_results",
    )(shard, sums)


def add_all(terms):
    total = terms[0]
    for term in terms[1:]:
        total = total + term
    return total


def body(
    inputs,
    cotangent,
    bucket,
    lengths,
    counts,
    w_qkv,
    w_out,
    w_in,
    w_down,
    head_bias,
    ffn_bias,
    norm_gains,
    row_biases,
):
    micro_count, _, width = inputs.shape
    blocks_all = bucket.shape[1]
    slot_count = inputs.shape[1] // blocks_all
    parts, dp_count = lax.axis_size("tensor"), lax.axis_size("dp")
    rank, dp_rank = lax.axis_index("tensor"), lax.axis_index("dp")
    per_micro = blocks_all // parts
    cols = w_in.shape[1]
    rows = w_in.shape[0]

    vector_count = norm_gains.shape[0] + row_biases.shape[0]
    blocks = [(m, k) for m in range(micro_count) for k in range(per_micro)]
    places = [jnp.full((1,), rank * per_micro + k, jnp.int32) for k in range(per_micro)]
    layout = (bucket, lengths, counts)
    if rows % 16 == 0:
        (weights, vectors, _, ffn_rows, normed, inverse, proj, probs, context, act, slope, out, second, second_low, stat) = forward(
            (w_qkv, w_out, w_in, w_down.T, head_bias, ffn_bias, norm_gains, row_biases),
            layout, inputs, cotangent, parts, dp_count, slot_count, micro_count, per_micro
        )
        layer_output, act_later, second_low_later, grad_up, hidden_low, head_grads, token_grad, small_grads = backward(
            layout, stat, vectors, ffn_rows, out, cotangent, weights, normed, inverse, slope, second, second_low, proj, probs,
            context, micro_count, per_micro
        )
        input_grad, shard, sums = finish(
            vectors, small_grads, inputs, normed, second_low, second_low_later, hidden_low, act, act_later, grad_up, head_grads,
            token_grad, parts, dp_count
        )
        grad_w_qkv, grad_w_out, grad_w_in, grad_w_down, grad_head, grad_ffn, grad_gains, grad_shifts = place_results(
            shard, sums, parts, dp_count
        )
        grad_w_down = grad_w_down.T
    else:
        own = jnp.stack([slab_order(w_qkv[0], w_qkv[1], w_qkv[2], w_out.T), w_in, w_down.T])
        norm_rows = jnp.concatenate([norm_gains, row_biases], axis=0)
        no_bias = jnp.zeros_like(head_bias[:1])
        bias_rows = jnp.concatenate([slab_order(head_bias[:1], no_bias, head_bias[1:], no_bias), ffn_bias[None]], axis=0)
        small = jnp.stack([
            jnp.pad(norm_rows, ((0, 16 - vector_count), (0, cols - rows))),
            jnp.pad(bias_rows, ((0, 14), (0, 0))),
        ])
        weights, small_dp, small_t = gather_weights(own, small, parts, dp_count)
        vectors = small_dp[:, :8, :rows].transpose(1, 0, 2).reshape(8, width).astype(jnp.float32)
        head_rows = small_t[:, 0:1].astype(jnp.float32)
        ffn_rows = small_t[:, 1:2].astype(jnp.float32)
        outs, token_grads, saved = [], [], []
        for m, k in blocks:
            attended = attend(m, places[k], *layout, inputs, weights, head_rows, vectors, slot_count)
            normed, inverse, proj, probs, context = [(array[None], 0) for array in attended]
            act, slope, out, second, second_low, stat = ffn(m, places[k], *layout, normed, cotangent, weights, ffn_rows, vectors)
            grad_up, hidden, hidden_low, up_stat, first_stat = ffn_back(second, second_low, slope, weights, normed, inverse, vectors)
            head_grads, token_grad, head_stat = attend_back(
                m, places[k], *layout, hidden, hidden_low, weights, proj, probs, context
            )
            outs.append(out)
            token_grads.append(token_grad)
            saved.append((normed, second_low, hidden_low, act, grad_up, head_grads, stat, first_stat, up_stat, head_stat))

        def along_line(rows_of):
            return jnp.stack([
                lax.all_gather(jnp.concatenate(rows_of[m * per_micro : (m + 1) * per_micro], axis=0), "tensor", axis=0, tiled=True)
                for m in range(micro_count)
            ])

        layer_output, input_grad = along_line(outs), along_line(token_grads)
        columns = list(zip(*saved))
        stat, first_stat, up_stat, head_stat = [add_all(column) for column in columns[6:]]
        small_grads = jnp.concatenate(
            [
                jnp.stack([first_stat[0], stat[0], first_stat[2], first_stat[1], stat[2], stat[1]]),
                up_stat[:, 0],
                head_stat[:, 0],
            ],
            axis=0,
        )
        small_grads = jnp.pad(small_grads, ((0, -small_grads.shape[0] % 8), (0, 0)))
        grads = weight_grads(places[0], inputs, *columns[:6], vectors)
        shard, sums = reduce_grads(grads, small_grads, parts, dp_count)
        vector_sums = lax.dynamic_slice_in_dim(sums[:vector_count], dp_rank * rows, rows, 1)
        grad_gains, grad_shifts = vector_sums[:2], vector_sums[2:]
        grad_query, grad_key, grad_value, grad_out = slab_parts(shard[0])
        grad_w_qkv = jnp.stack([grad_query, grad_key, grad_value])
        grad_w_out, grad_w_in, grad_w_down = grad_out.T, shard[1], shard[2].T
        grad_ffn = lax.dynamic_slice_in_dim(sums, vector_count + rank, 1, 0)[0]
        head_sum = slab_parts(lax.dynamic_slice_in_dim(sums, vector_count + parts + rank, 1, 0))
        grad_head = jnp.concatenate([head_sum[0], head_sum[2]], axis=0)
    return (
        layer_output,
        input_grad,
        grad_w_qkv,
        grad_w_out,
        grad_w_in,
        grad_w_down,
        grad_head,
        grad_ffn,
        grad_gains,
        grad_shifts,
    )


def solution(mesh):
    in_specs = (
        P(None, "dp", None),
        P(None, "dp", None),
        P(None, "dp"),
        P(None, "dp", None),
        P(None, "dp"),
        P(None, "dp", "tensor"),
        P("tensor", "dp"),
        P("dp", "tensor"),
        P("tensor", "dp"),
        P(None, "tensor"),
        P("tensor"),
        P(None, "dp"),
        P(None, "dp"),
    )
    out_specs = (
        P(None, "dp", None),
        P(None, "dp", None),
        P(None, "dp", "tensor"),
        P("tensor", "dp"),
        P("dp", "tensor"),
        P("tensor", "dp"),
        P(None, "tensor"),
        P("tensor"),
        P(None, "dp"),
        P(None, "dp"),
    )
    return jax.shard_map(body, mesh=mesh, in_specs=in_specs, out_specs=out_specs, check_vma=False)
```

```python
import functools

import jax
import jax.numpy as jnp
from jax import lax
from jax.experimental import pallas as pl
from jax.experimental.pallas import tpu as pltpu
from jax.sharding import PartitionSpec as P

HEAD_DIM = 64
EPSILON = 1e-12
VMEM_LIMIT = 60 * 1024 * 1024
MESH = pl.DeviceIdType.MESH
GATHER_LAG = 2
Z_WAVES = (2, 3)
LINE_PACE = 1
LINE_START = ((0, 1, 7), (4, 9, 15))
LINE_CHUNKS = 4
REDUCE_LAG = 2
def takes(microseconds):
    return pl.CostEstimate(flops=int(microseconds * 1.15e8), bytes_accessed=0, transcendentals=0)


LOW = jnp.bfloat16
WIDE = jnp.float32
CHUNK_HEADS = 3
VALUE_AT = (6, 7, 10)
OUT_AT = (8, 9, 11)


def slab_order(query, key, value, out):
    columns = lambda group, head: group[..., head * HEAD_DIM : (head + 1) * HEAD_DIM]
    order = [(query, 0), (key, 0), (query, 1), (key, 1), (query, 2), (key, 2),
             (value, 0), (value, 1), (out, 0), (out, 1), (value, 2), (out, 2)]
    return jnp.concatenate([columns(group, head) for group, head in order], axis=-1)


def slab_parts(slab):
    columns = lambda at: slab[..., at * HEAD_DIM : (at + 1) * HEAD_DIM]
    groups = ((0, 2, 4), (1, 3, 5), VALUE_AT, OUT_AT)
    return [jnp.concatenate([columns(at) for at in group], axis=-1) for group in groups]


def dot_nn(left, right):
    return lax.dot_general(left, right, (((1,), (0,)), ((), ())), preferred_element_type=WIDE)


def dot_nt(left, right):
    return lax.dot_general(left, right, (((1,), (1,)), ((), ())), preferred_element_type=WIDE)


def dot_tn(left, right):
    return dot_nn(right.T, left).T


def piece(tile, at):
    return tile[:, at * HEAD_DIM : (at + 1) * HEAD_DIM]


def slot_codes(layout, micro, block, slot_count, shape, axis):
    bucket, lengths, counts = layout
    position = lax.broadcasted_iota(jnp.int32, shape, axis)
    quarter = slot_count // 4
    whole = bucket[micro, block] == 1
    item = jnp.where(whole, 0, position // quarter)
    place = position - item * quarter
    length = jnp.where(
        item == 0,
        lengths[micro, block, 0],
        jnp.where(
            item == 1,
            lengths[micro, block, 1],
            jnp.where(item == 2, lengths[micro, block, 2], lengths[micro, block, 3]),
        ),
    )
    return item, (item < counts[micro, block]) & (place < length)


def normalize(hidden):
    center = hidden - jnp.mean(hidden, axis=-1, keepdims=True)
    inverse = lax.rsqrt(jnp.mean(center * center, axis=-1, keepdims=True) + EPSILON)
    return center * inverse, inverse


def norm_pullback(grad_rows, normed, inverse, gain_row):
    grad_normed = grad_rows * gain_row
    return inverse * (
        grad_normed
        - jnp.mean(grad_normed, axis=-1, keepdims=True)
        - normed * jnp.mean(grad_normed * normed, axis=-1, keepdims=True)
    )


def row_sum(values):
    return jnp.sum(values, axis=0, keepdims=True)


def attend_unit(layout, micro, place, tokens, weights, bias_row, proj_ref, prob_ref, context_ref):
    slot_count = tokens.shape[0]
    proj = (dot_nn(tokens, weights) + bias_row).astype(LOW)
    proj_ref[...] = proj
    row_item, _ = slot_codes(layout, micro, place, slot_count, (slot_count, 1), 0)
    key_item, key_live = slot_codes(layout, micro, place, slot_count, (1, slot_count), 1)
    key_code = jnp.where(key_live, key_item, -1)
    outs = []
    for head in range(CHUNK_HEADS):
        query = piece(proj, 2 * head) * jnp.asarray(HEAD_DIM ** (-0.5), LOW)
        scores = dot_nt(query, piece(proj, 2 * head + 1))
        scores = jnp.where(row_item == key_code, scores, -10000.0)
        grown = jnp.exp(scores - jnp.max(scores, axis=-1, keepdims=True))
        probs = (grown * (1.0 / jnp.sum(grown, axis=-1, keepdims=True))).astype(LOW)
        prob_ref[head] = probs
        outs.append(dot_nn(probs, piece(proj, VALUE_AT[head])).astype(LOW))
    context = jnp.concatenate([outs[0], outs[1], jnp.zeros_like(outs[0]), outs[2]], axis=1)
    context_ref[...] = context
    return dot_nt(context, weights[:, 8 * HEAD_DIM :])


def ffn_unit(first_low, w_in, w_down, bias_row, act_ref, slope_ref):
    upward = dot_nn(first_low, w_in) + bias_row
    share = 0.5 + 0.5 * lax.erf(upward * (0.5**0.5))
    activated = (upward * share).astype(LOW)
    act_ref[...] = activated
    bell = jnp.exp(-0.5 * upward * upward) * 0.3989422804014327
    slope_ref[...] = (share + upward * bell).astype(LOW)
    return dot_nt(activated, w_down)


def second_norm(layout, micro, place, first_normed, down_total, cot_rows, vectors):
    slot_count = first_normed.shape[0]
    _, live = slot_codes(layout, micro, place, slot_count, (slot_count, 1), 0)
    first = first_normed * vectors[0:1] + vectors[3:4]
    normed, inverse = normalize(first + down_total + vectors[4:5])
    out = (normed * vectors[1:2] + vectors[5:6]).astype(LOW)
    grad_out = jnp.where(live, cot_rows.astype(WIDE), 0.0)
    second = norm_pullback(grad_out, normed, inverse, vectors[1:2])
    stat = jnp.concatenate(
        [row_sum(grad_out * normed), row_sum(grad_out), row_sum(second), jnp.zeros((5, second.shape[1]), WIDE)], axis=0
    )
    return out, second, stat


def attend_kernel(micro, place, bucket, lengths, counts, x_ref, w_ref, bias_ref, vec_ref,
                  normed_ref, inverse_ref, proj_ref, prob_ref, context_ref, total):
    step = pl.program_id(0)
    layout = (bucket, lengths, counts)
    tokens = x_ref[0]
    attention = attend_unit(layout, micro, place[0], tokens, w_ref[0, 0], bias_ref[0],
                            proj_ref.at[0], prob_ref, context_ref.at[0])

    @pl.when(step == 0)
    def _():
        total[...] = attention

    @pl.when(step > 0)
    def _():
        total[...] += attention

    @pl.when(step == pl.num_programs(0) - 1)
    def _():
        normed, inverse = normalize(tokens.astype(WIDE) + total[...] + vec_ref[2:3])
        normed_ref[...] = normed
        inverse_ref[...] = jnp.broadcast_to(inverse, inverse_ref.shape)


def ffn_kernel(micro, place, bucket, lengths, counts, normed_ref, cot_ref, w_in_ref, w_down_ref, bias_ref, vec_ref,
               act_ref, slope_ref, out_ref, second_ref, second_low_ref, stat_ref, first_low, total):
    step = pl.program_id(0)

    @pl.when(step == 0)
    def _():
        first_low[...] = (normed_ref[...] * vec_ref[0:1] + vec_ref[3:4]).astype(LOW)

    down = ffn_unit(first_low[...], w_in_ref[0, 0], w_down_ref[0, 0], bias_ref[0], act_ref.at[0], slope_ref.at[0])

    @pl.when(step == 0)
    def _():
        total[...] = down

    @pl.when(step > 0)
    def _():
        total[...] += down

    @pl.when(step == pl.num_programs(0) - 1)
    def _():
        out, second, stat = second_norm(
            (bucket, lengths, counts), micro, place[0], normed_ref[...], total[...], cot_ref[0], vec_ref
        )
        out_ref[...] = out
        second_ref[...] = second
        second_low_ref[...] = second.astype(LOW)
        stat_ref[...] = stat


def ffn_back_kernel(second_ref, second_low_ref, slope_ref, w_in_ref, w_down_ref, normed_ref, inverse_ref, vec_ref,
                    up_ref, hidden_ref, hidden_low_ref, up_stat_ref, stat_ref, total):
    step = pl.program_id(0)
    grad_act = dot_nn(second_low_ref[...], w_down_ref[0, 0])
    grad_up = (grad_act * slope_ref[0].astype(WIDE)).astype(LOW)
    up_ref[0] = grad_up
    up_stat_ref[0] = jnp.broadcast_to(row_sum(grad_up.astype(WIDE)), up_stat_ref.shape[1:])
    back = dot_nt(grad_up, w_in_ref[0, 0])

    @pl.when(step == 0)
    def _():
        total[...] = back + second_ref[...]

    @pl.when(step > 0)
    def _():
        total[...] += back

    @pl.when(step == pl.num_programs(0) - 1)
    def _():
        grad_first = total[...]
        normed = normed_ref[...]
        hidden = norm_pullback(grad_first, normed, inverse_ref[:, :1], vec_ref[0:1])
        hidden_ref[...] = hidden
        hidden_low_ref[...] = hidden.astype(LOW)
        stat_ref[...] = jnp.concatenate(
            [row_sum(grad_first * normed), row_sum(grad_first), row_sum(hidden), jnp.zeros((5, hidden.shape[1]), WIDE)],
            axis=0,
        )


def attend_back_unit(layout, micro, place, hidden_low, weights, proj, probs_of, context):
    slot_count = hidden_low.shape[0]
    row_item, _ = slot_codes(layout, micro, place, slot_count, (slot_count, 1), 0)
    key_item, key_live = slot_codes(layout, micro, place, slot_count, (1, slot_count), 1)
    key_code = jnp.where(key_live, key_item, -1)
    grad_context = dot_nn(hidden_low, weights[:, 8 * HEAD_DIM :]).astype(LOW)
    scale = HEAD_DIM ** (-0.5)
    grads = [None] * 12
    for head in range(CHUNK_HEADS):
        query, key = piece(proj, 2 * head), piece(proj, 2 * head + 1)
        probs = probs_of[head]
        grad_head = piece(grad_context, OUT_AT[head] - 8)
        grads[VALUE_AT[head]] = dot_tn(probs, grad_head).astype(LOW)
        grad_probs = dot_nt(grad_head, piece(proj, VALUE_AT[head]))
        wide = probs.astype(WIDE)
        inner = jnp.sum(wide * grad_probs, axis=-1, keepdims=True)
        grad_scores = jnp.where(row_item == key_code, wide * (grad_probs - inner), 0.0).astype(LOW)
        grads[2 * head] = (dot_nn(grad_scores, key) * scale).astype(LOW)
        grads[2 * head + 1] = (dot_tn(grad_scores, query) * scale).astype(LOW)
    zero = jnp.zeros_like(grads[0])
    for at in OUT_AT:
        grads[at] = zero
    slab = jnp.concatenate(grads, axis=1)
    back = dot_nt(slab, weights)
    sums = row_sum(slab.astype(WIDE))
    for at in OUT_AT:
        grads[at] = piece(context, at - 8)
    return jnp.concatenate(grads, axis=1), back, sums


def attend_back_kernel(micro, place, bucket, lengths, counts, hidden_ref, hidden_low_ref, w_ref, proj_ref, prob_ref,
                       context_ref, grad_ref, out_ref, stat_ref, total):
    step = pl.program_id(0)
    slab, back, sums = attend_back_unit((bucket, lengths, counts), micro, place[0], hidden_low_ref[...], w_ref[0, 0],
                                        proj_ref[0], prob_ref, context_ref[0])
    grad_ref[0] = slab
    stat_ref[0] = jnp.broadcast_to(sums, stat_ref.shape[1:])

    @pl.when(step == 0)
    def _():
        total[...] = back + hidden_ref[...]

    @pl.when(step > 0)
    def _():
        total[...] += back

    @pl.when(step == pl.num_programs(0) - 1)
    def _():
        out_ref[...] = total[...].astype(LOW)


def params(vmem=VMEM_LIMIT):
    return pltpu.CompilerParams(dimension_semantics=("arbitrary",), vmem_limit_bytes=vmem)


def attend(micro, place, bucket, lengths, counts, inputs, weights, bias, vectors, slot_count):
    parts, width = weights.shape[1], weights.shape[2]
    wide_slab = weights.shape[3]
    heads = parts * CHUNK_HEADS
    whole = lambda *shape: pl.BlockSpec(shape, lambda j, p, b, l, c: (0,) * len(shape))
    return pl.pallas_call(
        functools.partial(attend_kernel, micro),
        grid_spec=pltpu.PrefetchScalarGridSpec(
            num_scalar_prefetch=4,
            grid=(parts,),
            in_specs=[
                pl.BlockSpec((1, slot_count, width), lambda j, p, b, l, c: (micro, p[0], 0)),
                pl.BlockSpec((1, 1, width, wide_slab), lambda j, p, b, l, c: (0, j, 0, 0)),
                pl.BlockSpec((1, 1, wide_slab), lambda j, p, b, l, c: (j, 0, 0)),
                whole(*vectors.shape),
            ],
            out_specs=[
                whole(slot_count, width),
                whole(slot_count, 128),
                pl.BlockSpec((1, slot_count, wide_slab), lambda j, p, b, l, c: (j, 0, 0)),
                pl.BlockSpec((CHUNK_HEADS, slot_count, slot_count), lambda j, p, b, l, c: (j, 0, 0)),
                pl.BlockSpec((1, slot_count, 4 * HEAD_DIM), lambda j, p, b, l, c: (j, 0, 0)),
            ],
            scratch_shapes=[pltpu.VMEM((slot_count, width), WIDE)],
        ),
        out_shape=[
            jax.ShapeDtypeStruct((slot_count, width), WIDE),
            jax.ShapeDtypeStruct((slot_count, 128), WIDE),
            jax.ShapeDtypeStruct((parts, slot_count, wide_slab), LOW),
            jax.ShapeDtypeStruct((heads, slot_count, slot_count), LOW),
            jax.ShapeDtypeStruct((parts, slot_count, 4 * HEAD_DIM), LOW),
        ],
        compiler_params=params(),
        name="attend",
        cost_estimate=takes(16),
    )(place, bucket, lengths, counts, inputs, weights, bias, vectors)


def ffn(micro, place, bucket, lengths, counts, normed, cotangent, weights, bias, vectors):
    parts, width, cols = weights.shape[1:]
    normed, index = normed
    slot_count = normed.shape[1]
    whole = lambda *shape: pl.BlockSpec(shape, lambda j, p, b, l, c: (0,) * len(shape))
    each = pl.BlockSpec((1, slot_count, cols), lambda j, p, b, l, c: (j, 0, 0))
    return pl.pallas_call(
        functools.partial(ffn_kernel, micro),
        grid_spec=pltpu.PrefetchScalarGridSpec(
            num_scalar_prefetch=4,
            grid=(parts,),
            in_specs=[
                pl.BlockSpec((None, slot_count, width), lambda j, p, b, l, c: (index, 0, 0)),
                pl.BlockSpec((1, slot_count, width), lambda j, p, b, l, c: (micro, p[0], 0)),
                pl.BlockSpec((1, 1, width, cols), lambda j, p, b, l, c: (1, j, 0, 0)),
                pl.BlockSpec((1, 1, width, cols), lambda j, p, b, l, c: (2, j, 0, 0)),
                pl.BlockSpec((1, 1, cols), lambda j, p, b, l, c: (j, 0, 0)),
                whole(*vectors.shape),
            ],
            out_specs=[each, each, whole(slot_count, width), whole(slot_count, width), whole(slot_count, width), whole(8, width)],
            scratch_shapes=[pltpu.VMEM((slot_count, width), LOW), pltpu.VMEM((slot_count, width), WIDE)],
        ),
        out_shape=[
            jax.ShapeDtypeStruct((parts, slot_count, cols), LOW),
            jax.ShapeDtypeStruct((parts, slot_count, cols), LOW),
            jax.ShapeDtypeStruct((slot_count, width), LOW),
            jax.ShapeDtypeStruct((slot_count, width), WIDE),
            jax.ShapeDtypeStruct((slot_count, width), LOW),
            jax.ShapeDtypeStruct((8, width), WIDE),
        ],
        compiler_params=params(),
        name="ffn",
        cost_estimate=takes(16),
    )(place, bucket, lengths, counts, normed, cotangent, weights, weights, bias, vectors)


def ffn_back(second, second_low, slope, weights, normed, inverse, vectors):
    parts, width, cols = weights.shape[1:]
    (normed, index), (inverse, _) = normed, inverse
    slot_count = normed.shape[1]
    whole = lambda *shape: pl.BlockSpec(shape, lambda j: (0,) * len(shape))
    each = pl.BlockSpec((1, slot_count, cols), lambda j: (j, 0, 0))
    return pl.pallas_call(
        ffn_back_kernel,
        grid=(parts,),
        in_specs=[
            whole(slot_count, width),
            whole(slot_count, width),
            each,
            pl.BlockSpec((1, 1, width, cols), lambda j: (1, j, 0, 0)),
            pl.BlockSpec((1, 1, width, cols), lambda j: (2, j, 0, 0)),
            pl.BlockSpec((None, slot_count, width), lambda j: (index, 0, 0)),
            pl.BlockSpec((None, slot_count, 128), lambda j: (index, 0, 0)),
            whole(*vectors.shape),
        ],
        out_specs=[each, whole(slot_count, width), whole(slot_count, width),
                   pl.BlockSpec((1, 8, cols), lambda j: (j, 0, 0)), whole(8, width)],
        scratch_shapes=[pltpu.VMEM((slot_count, width), WIDE)],
        out_shape=[
            jax.ShapeDtypeStruct((parts, slot_count, cols), LOW),
            jax.ShapeDtypeStruct((slot_count, width), WIDE),
            jax.ShapeDtypeStruct((slot_count, width), LOW),
            jax.ShapeDtypeStruct((parts, 8, cols), WIDE),
            jax.ShapeDtypeStruct((8, width), WIDE),
        ],
        compiler_params=params(),
        name="ffn_back",
        cost_estimate=takes(14),
    )(second, second_low, slope, weights, weights, normed, inverse, vectors)


def attend_back(micro, place, bucket, lengths, counts, hidden, hidden_low, weights, proj, probs, context):
    parts, width = weights.shape[1], weights.shape[2]
    wide_slab = weights.shape[3]
    slot_count = hidden.shape[0]
    (proj, index), (probs, _), (context, _) = proj, probs, context
    whole = lambda *shape: pl.BlockSpec(shape, lambda j, p, b, l, c: (0,) * len(shape))
    each = pl.BlockSpec((1, slot_count, wide_slab), lambda j, p, b, l, c: (j, 0, 0))
    return pl.pallas_call(
        functools.partial(attend_back_kernel, micro),
        grid_spec=pltpu.PrefetchScalarGridSpec(
            num_scalar_prefetch=4,
            grid=(parts,),
            in_specs=[
                whole(slot_count, width),
                whole(slot_count, width),
                pl.BlockSpec((1, 1, width, wide_slab), lambda j, p, b, l, c: (0, j, 0, 0)),
                pl.BlockSpec((None, 1, slot_count, wide_slab), lambda j, p, b, l, c: (index, j, 0, 0)),
                pl.BlockSpec((None, CHUNK_HEADS, slot_count, slot_count), lambda j, p, b, l, c: (index, j, 0, 0)),
                pl.BlockSpec((None, 1, slot_count, 4 * HEAD_DIM), lambda j, p, b, l, c: (index, j, 0, 0)),
            ],
            out_specs=[each, whole(slot_count, width), pl.BlockSpec((1, 8, wide_slab), lambda j, p, b, l, c: (j, 0, 0))],
            scratch_shapes=[pltpu.VMEM((slot_count, width), WIDE)],
        ),
        out_shape=[
            jax.ShapeDtypeStruct((parts, slot_count, wide_slab), LOW),
            jax.ShapeDtypeStruct((slot_count, width), LOW),
            jax.ShapeDtypeStruct((parts, 8, wide_slab), WIDE),
        ],
        compiler_params=params(),
        name="attend_back",
        cost_estimate=takes(22),
    )(place, bucket, lengths, counts, hidden, hidden_low, weights, proj, probs, context)


def weight_grads_kernel(blocks, place, *refs):
    normed = refs[:blocks]
    second_low, hidden_low, act, grad_up, head_grads, tokens = [refs[(k + 1) * blocks : (k + 2) * blocks] for k in range(6)]
    vec_ref, out_ref = refs[7 * blocks], refs[7 * blocks + 1]
    turned = refs[7 * blocks + 2]
    step = pl.program_id(0)
    slot_count = second_low[0].shape[0]

    @pl.when(step == 0)
    def _():
        for b in range(blocks):
            span = slice(b * slot_count, (b + 1) * slot_count)
            first = (normed[b][...] * vec_ref[0:1] + vec_ref[3:4]).astype(LOW)
            turned[0, :, span] = tokens[b][0].T
            turned[1, :, span] = first.T
            turned[2, :, span] = second_low[b][...].T
            turned[3, :, span] = hidden_low[b][...].T

    grads = jnp.concatenate([ref[0] for ref in head_grads], axis=0)
    qkv = dot_nn(turned[0], grads)
    outs = dot_nn(turned[3], grads[:, 8 * HEAD_DIM :])
    lane = lax.broadcasted_iota(jnp.int32, (1, 2 * HEAD_DIM), 1)
    last = jnp.where(lane < HEAD_DIM, qkv[:, 10 * HEAD_DIM :], outs[:, 2 * HEAD_DIM :])
    out_ref[0, 0] = jnp.concatenate([qkv[:, : 8 * HEAD_DIM], outs[:, : 2 * HEAD_DIM], last], axis=1).astype(LOW)
    out_ref[1, 0] = dot_nn(turned[1], jnp.concatenate([ref[0] for ref in grad_up], axis=0)).astype(LOW)
    out_ref[2, 0] = dot_nn(turned[2], jnp.concatenate([ref[0] for ref in act], axis=0)).astype(LOW)


def weight_grads(place, inputs, normed, second_low, hidden_low, act, grad_up, head_grads, vectors):
    blocks = len(normed)
    normed_specs = [
        pl.BlockSpec((None,) + array.shape[1:], lambda j, p, index=index: (index, 0, 0)) for array, index in normed
    ]
    normed = [array for array, _ in normed]
    micro_count = inputs.shape[0]
    per_micro = blocks // micro_count
    parts, slot_count, cols = act[0].shape
    width = normed[0].shape[2]
    whole = lambda *shape: pl.BlockSpec(shape, lambda j, p: (0,) * len(shape))
    each = pl.BlockSpec((1, slot_count, cols), lambda j, p: (j, 0, 0))
    token_specs = [
        pl.BlockSpec((1, slot_count, width), lambda j, p, m=b // per_micro, k=b % per_micro: (m, p[0] + k, 0))
        for b in range(blocks)
    ]
    return pl.pallas_call(
        functools.partial(weight_grads_kernel, blocks),
        grid_spec=pltpu.PrefetchScalarGridSpec(
            num_scalar_prefetch=1,
            grid=(parts,),
            in_specs=normed_specs + [whole(slot_count, width)] * (2 * blocks) + [each] * (3 * blocks) + token_specs + [whole(*vectors.shape)],
            out_specs=pl.BlockSpec((3, 1, width, cols), lambda j, p: (0, j, 0, 0)),
            scratch_shapes=[pltpu.VMEM((4, width, blocks * slot_count), LOW)],
        ),
        out_shape=jax.ShapeDtypeStruct((3, parts, width, cols), LOW),
        compiler_params=params(),
        name="weight_grads",
        cost_estimate=takes(26),
    )(place, *normed, *second_low, *hidden_low, *act, *grad_up, *head_grads, *([inputs] * blocks), vectors)


def mesh_place(bits):
    d = lax.axis_index("dp")
    t = lax.axis_index("tensor")
    digits = [(d // (1 << k)) % 2 for k in range(bits)]
    mates = [d + (1 - 2 * digits[k]) * (1 << k) for k in range(bits)]
    return d, t, digits, mates


def digit_index(bits, digits, open_bits):
    return tuple(slice(None) if k in open_bits else digits[k] for k in reversed(range(bits)))


def greet(d, t, mates, parts):
    barrier = pltpu.get_barrier_semaphore()
    for mate in mates:
        pl.semaphore_signal(barrier, inc=1, device_id=(mate, t), device_id_type=MESH)
    for hop in range(1, parts):
        pl.semaphore_signal(barrier, inc=1, device_id=(d, (t + hop) % parts), device_id_type=MESH)
    pl.semaphore_wait(barrier, len(mates) + parts - 1)


def bit_order(bits, flip):
    far = list(range(1, bits))
    return (far[::-1] if flip else far) + [0]


def gather_kernel(parts, bits, own, small, full, small_dp, small_t, z_send, z_recv, h_send, h_recv, s_send, s_recv, keep):
    d, t, digits, mates = mesh_place(bits)
    slab_count = own.shape[0]
    mine = digit_index(bits, digits, ())
    greet(d, t, mates, parts)
    offsets = [0] + [sign * hop for hop in range(1, parts) for sign in (1, -1)]
    pending = []

    def remote(src, dst, send, recv, to):
        return pltpu.make_async_remote_copy(src, dst, send, recv, device_id=to, device_id_type=MESH)

    local = [pltpu.make_async_copy(own.at[s], full.at[(s, t) + mine], keep.at[s]) for s in range(slab_count)]
    local.append(pltpu.make_async_copy(small.at[0], small_dp.at[mine], keep.at[slab_count]))
    local.append(pltpu.make_async_copy(small.at[1], small_t.at[t], keep.at[slab_count + 1]))
    for copy in local:
        copy.start()

    def z_copy(s, at, src, up):
        to = (d, t + 1) if up else (d, t - 1)
        way = 0 if up else 1
        return remote(src, full.at[(s, at) + mine], z_send.at[s, at, way], z_recv.at[s, at], to)

    def h_copy(s, index, step):
        offset = offsets[index]
        order = bit_order(bits, (abs(offset) + s) % 2 == 1)
        blocks = (s, t + offset) + digit_index(bits, digits, order[:step])
        src = own.at[s] if offset == 0 and step == 0 else full.at[blocks]
        return remote(src, full.at[blocks], h_send.at[s, index, step], h_recv.at[s, index, step], (mates[order[step]], t))

    def exists(offset):
        return (t + offset >= 0) & (t + offset < parts)

    def begin(s, index):
        offset = offsets[index]
        if offset == 0:
            h_copy(s, index, 0).start()
            return

        @pl.when(exists(offset))
        def _():
            up = offset < 0
            z_copy(s, t + offset, own.at[s], up).wait_recv()

            @pl.when((t < parts - 1) if up else (t > 0))
            def _():
                z_copy(s, t + offset, full.at[(s, t + offset) + mine], up).start()

            h_copy(s, index, 0).start()

    def advance(s, index, step):
        @pl.when(exists(offsets[index]))
        def _():
            h_copy(s, index, step - 1).wait_recv()
            if step < bits:
                h_copy(s, index, step).start()

    def small_step(step):
        blocks = digit_index(bits, digits, range(step))
        src = small.at[0] if step == 0 else small_dp.at[blocks]
        return remote(src, small_dp.at[blocks], s_send.at[step], s_recv.at[step], (mates[step], t))

    def small_hop(hop):
        peer = (d, (t + hop) % parts)
        return remote(small.at[1], small_t.at[t], s_send.at[bits + hop - 1], s_recv.at[bits + hop - 1], peer)

    def send_own(s):
        @pl.when(t < parts - 1)
        def _():
            z_copy(s, t, own.at[s], True).start()

        @pl.when(t > 0)
        def _():
            z_copy(s, t, own.at[s], False).start()

    order = [(s, hop) for s in range(slab_count) for hop in range(parts)]
    groups = [(s, [index for index, offset in enumerate(offsets) if abs(offset) == hop]) for s, hop in order]
    send_own(0)
    begin(0, 0)
    for hop in range(1, parts):
        small_hop(hop).start()
    small_step(0).start()
    for copy in local:
        copy.wait()
    for wave in range(len(groups) + bits * GATHER_LAG):
        for step in range(bits + 1):
            if 0 <= wave - step * GATHER_LAG < len(groups):
                s, indices = groups[wave - step * GATHER_LAG]
                for index in indices:
                    if step:
                        advance(s, index, step)
                    elif (s, index) != (0, 0):
                        begin(s, index)
        if wave in Z_WAVES:
            send_own(1 + Z_WAVES.index(wave))
        if wave < bits:
            small_step(wave).wait_recv()
            if wave + 1 < bits:
                small_step(wave + 1).start()

    for hop in range(1, parts):
        small_hop(hop).wait()
    for step in range(bits):
        small_step(step).wait_send()
    for s, indices in groups:
        for index in indices:
            offset = offsets[index]

            @pl.when(exists(offset))
            def _():
                for step in range(bits):
                    h_copy(s, index, step).wait_send()
                if offset <= 0:
                    @pl.when(t < parts - 1)
                    def _():
                        z_copy(s, t + offset, own.at[s], True).wait_send()
                if offset >= 0:
                    @pl.when(t > 0)
                    def _():
                        z_copy(s, t + offset, own.at[s], False).wait_send()


def gather_weights(own, small, parts, dp_count):
    bits = dp_count.bit_length() - 1
    slab_count, rows, columns = own.shape
    places = 2 * parts - 1
    low = jnp.bfloat16
    full, small_dp, small_t = pl.pallas_call(
        functools.partial(gather_kernel, parts, bits),
        out_shape=[
            jax.ShapeDtypeStruct((slab_count, parts) + (2,) * bits + (rows, columns), low),
            jax.ShapeDtypeStruct((2,) * bits + small.shape[1:], low),
            jax.ShapeDtypeStruct((parts,) + small.shape[1:], low),
        ],
        in_specs=[pl.BlockSpec(memory_space=pl.ANY)] * 2,
        out_specs=[pl.BlockSpec(memory_space=pl.ANY)] * 3,
        scratch_shapes=[
            pltpu.SemaphoreType.DMA((slab_count, parts, 2)),
            pltpu.SemaphoreType.DMA((slab_count, parts)),
            pltpu.SemaphoreType.DMA((slab_count, places, bits)),
            pltpu.SemaphoreType.DMA((slab_count, places, bits)),
            pltpu.SemaphoreType.DMA((bits + parts - 1,)),
            pltpu.SemaphoreType.DMA((bits + parts - 1,)),
            pltpu.SemaphoreType.DMA((slab_count + 2,)),
        ],
        compiler_params=pltpu.CompilerParams(collective_id=0, has_side_effects=True, vmem_limit_bytes=VMEM_LIMIT),
        name="gather_weights",
        cost_estimate=takes(100),
    )(own, small)
    full = full.reshape(slab_count, parts, dp_count * rows, columns)
    return full, small_dp.reshape((dp_count,) + small.shape[1:]), small_t


def add_rows(target, first, second, rows):
    lead = target.shape[:-2]
    chunk = 16 if rows % 16 == 0 else rows
    steps = rows // chunk
    count = 1
    for extent in lead:
        count *= extent

    def one(i, carry):
        at, rest = [], i // steps
        for extent in reversed(lead):
            at.insert(0, rest % extent)
            rest = rest // extent
        where = tuple(at) + (pl.ds(pl.multiple_of((i % steps) * chunk, chunk), chunk),)
        total = first[where].astype(jnp.float32) + second[where].astype(jnp.float32)
        target[where] = total.astype(target.dtype)
        return carry

    lax.fori_loop(0, count * steps, one, 0)


def reduce_kernel(parts, bits, grads, small, out, small_out, *scratch):
    bufs = scratch[:bits]
    z_up, z_down, small_buf, small_sum = scratch[bits:bits + 4]
    h_send, h_recv, up_send, up_recv, down_send, down_recv, s_send, s_recv = scratch[bits + 4:]
    d, t, digits, mates = mesh_place(bits)
    slab_count = grads.shape[0]
    rows = grads.shape[-2]
    greet(d, t, mates, parts)
    items = [(s, at) for s in range(slab_count) for at in range(parts)]
    small_bits = bits + parts.bit_length() - 1

    def remote(src, dst, send, recv, to):
        return pltpu.make_async_remote_copy(src, dst, send, recv, device_id=to, device_id_type=MESH)

    def order_of(number):
        s, at = items[number]
        return bit_order(bits, (s + at) % 2 == 1)[::-1]

    def held(number, step):
        s, at = items[number]
        return grads.at[s, at] if step == 0 else bufs[step - 1].at[number]

    def part_of(number, step, side):
        order = order_of(number)
        left = [k for k in reversed(range(bits)) if k not in order[:step]]
        pick = tuple(side if k == order[step] else slice(None) for k in left)
        return held(number, step).at[pick]

    def h_copy(number, step):
        order = order_of(number)
        digit = digits[order[step]]
        return remote(part_of(number, step, 1 - digit), bufs[step].at[number],
                      h_send.at[number, step], h_recv.at[number, step], (mates[order[step]], t))

    def fold(number, step):
        h_copy(number, step).wait_recv()
        digit = digits[order_of(number)[step]]
        add_rows(bufs[step].at[number], bufs[step].at[number], part_of(number, step, digit), rows)

    def summed(s, at):
        return bufs[bits - 1].at[s * parts + at]

    def z_copy(s, at, up, src):
        buf, send, recv = (z_up, up_send, up_recv) if up else (z_down, down_send, down_recv)
        to = (d, t + 1) if up else (d, t - 1)
        return remote(src, buf.at[s, at], send.at[s, at], recv.at[s, at], to)

    def z_pass(s, hop, up):
        at = t + hop if up else t - hop
        edge = (t == 0) if up else (t == parts - 1)
        buf = z_up if up else z_down

        @pl.when((at < parts) if up else (at >= 0))
        def _():
            @pl.when(edge)
            def _():
                z_copy(s, at, up, summed(s, at)).start()

            @pl.when(jnp.logical_not(edge))
            def _():
                z_copy(s, at, up, summed(s, at)).wait_recv()
                add_rows(buf.at[s, at], buf.at[s, at], summed(s, at), rows)
                z_copy(s, at, up, buf.at[s, at]).start()

    def z_finish(s):
        add_rows(out.at[s], summed(s, t), summed(s, t), rows)

        def scaled(i, carry):
            out[s] = out[s] * 0.5
            return carry
        lax.fori_loop(0, 1, scaled, 0)
        for up, buf in ((True, z_up), (False, z_down)):
            @pl.when((t > 0) if up else (t < parts - 1))
            def _():
                z_copy(s, t, up, summed(s, t)).wait_recv()
                add_rows(out.at[s], out.at[s], buf.at[s, t], rows)

    def small_copy(step):
        if step < bits:
            to = (mates[step], t)
        else:
            gap = 1 << (step - bits)
            to = (d, t + (1 - 2 * ((t // gap) % 2)) * gap)
        src = small if step == 0 else small_sum.at[step - 1]
        return remote(src, small_buf.at[step], s_send.at[step], s_recv.at[step], to)

    def small_fold(step):
        small_copy(step).wait_recv()
        before = small[...] if step == 0 else small_sum[step - 1]
        small_sum[step] = before + small_buf[step]
        if step + 1 < small_bits:
            small_copy(step + 1).start()

    for number in range(len(items)):
        h_copy(number, 0).start()
        if number == 0:
            small_copy(0).start()
    for wave in range(len(items) + bits * REDUCE_LAG + parts + 1):
        for step in range(bits):
            number = wave - step * REDUCE_LAG
            if 0 <= number < len(items):
                fold(number, step)
                if step + 1 < bits:
                    h_copy(number, step + 1).start()
        for s in range(slab_count):
            phase = wave - ((s + 1) * parts - 1 + bits * REDUCE_LAG)
            if 0 <= phase < parts - 1:
                z_pass(s, parts - 1 - phase, True)
                z_pass(s, parts - 1 - phase, False)
            elif phase == parts - 1:
                z_finish(s)
        if wave < small_bits:
            small_fold(wave)
    small_out[...] = small_sum[small_bits - 1]

    for step in range(small_bits):
        small_copy(step).wait_send()
    for number in range(len(items)):
        for step in range(bits):
            h_copy(number, step).wait_send()
    for s in range(slab_count):
        for hop in range(1, parts):
            @pl.when(t + hop < parts)
            def _():
                z_copy(s, t + hop, True, summed(s, t)).wait_send()

            @pl.when(t - hop >= 0)
            def _():
                z_copy(s, t - hop, False, summed(s, t)).wait_send()


def reduce_grads(grads, small, parts, dp_count):
    bits = dp_count.bit_length() - 1
    slab_count, columns = grads.shape[0], grads.shape[-1]
    rows = grads.shape[2] // dp_count
    grads = grads.reshape((slab_count, parts) + (2,) * bits + (rows, columns))
    low = jnp.bfloat16
    count = slab_count * parts
    small_bits = bits + parts.bit_length() - 1
    dma = pltpu.SemaphoreType.DMA
    return pl.pallas_call(
        functools.partial(reduce_kernel, parts, bits),
        out_shape=[
            jax.ShapeDtypeStruct((slab_count, rows, columns), jnp.float32),
            jax.ShapeDtypeStruct(small.shape, jnp.float32),
        ],
        in_specs=[pl.BlockSpec(memory_space=pltpu.VMEM)] * 2,
        out_specs=[pl.BlockSpec(memory_space=pltpu.VMEM)] * 2,
        scratch_shapes=[pltpu.VMEM((count,) + (2,) * (bits - 1 - step) + (rows, columns), low) for step in range(bits)]
        + [pltpu.VMEM((slab_count, parts, rows, columns), low)] * 2
        + [pltpu.VMEM((small_bits,) + small.shape, jnp.float32)] * 2
        + [dma((count, bits)), dma((count, bits))]
        + [dma((slab_count, parts))] * 4
        + [dma((small_bits,))] * 2,
        compiler_params=pltpu.CompilerParams(collective_id=1, has_side_effects=True, vmem_limit_bytes=VMEM_LIMIT),
        name="reduce_grads",
        cost_estimate=takes(100),
    )(grads, small)


def forward_kernel(parts, bits, micro_count, per_micro, slot_count, w_qkv, w_out, w_in, w_down, head_bias, ffn_bias,
                   norm_gains, row_biases, bucket, lengths, counts, inputs, cotangent,
                   weights, vectors, head_rows, ffn_rows, normed_out, inverse_out, proj_out, prob_out, context_out,
                   act_out, slope_out, out_out, second_out, second_low_out, stat_out,
                   own, small, full, small_dp, small_t, tokens, cot, total, normed_buf, inverse_buf, proj_buf, prob_buf, context_buf,
                   act_buf, slope_buf, first_low, down_total, out_buf, second_buf, second_low_buf,
                   z_send, z_recv, h_send, h_recv, s_send, s_recv, keep, load, weight_done, unit_done, ffn_done, end_done):
    layout = (bucket, lengths, counts)
    d, t, digits, mates = mesh_place(bits)
    blocks = micro_count * per_micro
    slab_count = own.shape[0]
    width = own.shape[2]
    mine = digit_index(bits, digits, ())

    def block_place(b):
        return b // per_micro, t * per_micro + b % per_micro

    def block_rows(b):
        micro, place = block_place(b)
        return (micro, pl.ds(pl.multiple_of(place * slot_count, slot_count), slot_count))

    loads = [pltpu.make_async_copy(inputs.at[block_rows(b)], tokens.at[b], load.at[b]) for b in range(blocks)]
    loads.append(pltpu.make_async_copy(cotangent.at[block_rows(0)], cot, load.at[blocks]))
    own[0] = slab_order(w_qkv[0], w_qkv[1], w_qkv[2], w_out[...].T)
    own[1] = w_in[...]
    own[2] = w_down[...]
    small[...] = jnp.zeros_like(small)
    vector_count = norm_gains.shape[0] + row_biases.shape[0]
    small[0, :, : own.shape[1]] = jnp.concatenate(
        [norm_gains[...], row_biases[...], jnp.zeros((16 - vector_count, own.shape[1]), LOW)], axis=0
    )
    no_bias = jnp.zeros((1, head_bias.shape[1]), LOW)
    bias_row = slab_order(head_bias[0:1], no_bias, head_bias[1:2], no_bias)
    small[1] = jnp.concatenate([bias_row, ffn_bias[...].reshape(1, -1), jnp.zeros((14, own.shape[2]), LOW)], axis=0)
    greet(d, t, mates, parts)
    offsets = [0] + [sign * hop for hop in range(1, parts) for sign in (1, -1)]

    def remote(src, dst, send, recv, to):
        return pltpu.make_async_remote_copy(src, dst, send, recv, device_id=to, device_id_type=MESH)

    local = [pltpu.make_async_copy(own.at[s], full.at[(s, t) + mine], keep.at[s]) for s in range(slab_count)]
    local.append(pltpu.make_async_copy(small.at[0], small_dp.at[mine], keep.at[slab_count]))
    local.append(pltpu.make_async_copy(small.at[1], small_t.at[t], keep.at[slab_count + 1]))

    def z_copy(s, at, src, up):
        to = (d, t + 1) if up else (d, t - 1)
        return remote(src, full.at[(s, at) + mine], z_send.at[s, at, 0 if up else 1], z_recv.at[s, at], to)

    def h_copy(s, index, step):
        offset = offsets[index]
        order = bit_order(bits, (abs(offset) + s) % 2 == 1)
        where = (s, t + offset) + digit_index(bits, digits, order[:step])
        src = own.at[s] if offset == 0 and step == 0 else full.at[where]
        return remote(src, full.at[where], h_send.at[s, index, step], h_recv.at[s, index, step], (mates[order[step]], t))

    def exists(offset):
        return (t + offset >= 0) & (t + offset < parts)

    def weight_copy(s, at):
        return pltpu.make_async_copy(full.at[s, at], weights.at[s, at], weight_done.at[s, at])

    def begin(s, index):
        offset = offsets[index]
        if offset == 0:
            h_copy(s, index, 0).start()
            return

        @pl.when(exists(offset))
        def _():
            up = offset < 0
            z_copy(s, t + offset, own.at[s], up).wait_recv()

            @pl.when((t < parts - 1) if up else (t > 0))
            def _():
                z_copy(s, t + offset, full.at[(s, t + offset) + mine], up).start()

            h_copy(s, index, 0).start()

    def advance(s, index, step):
        @pl.when(exists(offsets[index]))
        def _():
            h_copy(s, index, step - 1).wait_recv()
            if step < bits:
                h_copy(s, index, step).start()
            else:
                weight_copy(s, t + offsets[index]).start()

    def small_step(step):
        where = digit_index(bits, digits, range(step))
        src = small.at[0] if step == 0 else small_dp.at[where]
        return remote(src, small_dp.at[where], s_send.at[step], s_recv.at[step], (mates[step], t))

    def small_hop(hop):
        peer = (d, (t + hop) % parts)
        return remote(small.at[1], small_t.at[t], s_send.at[bits + hop - 1], s_recv.at[bits + hop - 1], peer)

    def send_own(s):
        @pl.when(t < parts - 1)
        def _():
            z_copy(s, t, own.at[s], True).start()

        @pl.when(t > 0)
        def _():
            z_copy(s, t, own.at[s], False).start()

    toward = 1 - 2 * ((2 * t) // parts)

    def nearest(k):
        return (t + toward * k + parts) % parts

    def matrix(s, at):
        return full[s, at].reshape(width, full.shape[-1])

    def unit_copies(unit, at, b):
        slot = unit % 2
        heads = pl.ds(at * CHUNK_HEADS, CHUNK_HEADS)
        return [
            pltpu.make_async_copy(proj_buf.at[slot], proj_out.at[b, at], unit_done.at[slot, 0]),
            pltpu.make_async_copy(prob_buf.at[slot], prob_out.at[b, heads], unit_done.at[slot, 1]),
            pltpu.make_async_copy(context_buf.at[slot], context_out.at[b, at], unit_done.at[slot, 2]),
        ]

    def attend_part(b, k):
        unit = b * parts + k
        at = nearest(k)
        if unit >= 2:
            for copy in unit_copies(unit - 2, nearest((unit - 2) % parts), (unit - 2) // parts):
                copy.wait()
        slot = unit % 2
        micro, place = block_place(b)
        attention = attend_unit(layout, micro, place, tokens[b], matrix(0, at), head_rows[at],
                                proj_buf.at[slot], prob_buf.at[slot], context_buf.at[slot])
        if k == 0:
            total[...] = attention
        else:
            total[...] += attention
        for copy in unit_copies(unit, at, b):
            copy.start()
        if k == parts - 1:
            normed, inverse = normalize(tokens[b].astype(WIDE) + total[...] + vectors[2:3])
            normed_buf[b] = normed
            inverse_buf[b] = jnp.broadcast_to(inverse, inverse_buf.shape[1:])
            for copy in norm_copies(b):
                copy.start()

    def norm_copies(b):
        return [pltpu.make_async_copy(normed_buf.at[b], normed_out.at[b], end_done.at[b, 0]),
                pltpu.make_async_copy(inverse_buf.at[b], inverse_out.at[b], end_done.at[b, 1])]

    def ffn_copies(k):
        slot, at = k % 2, nearest(k)
        return [pltpu.make_async_copy(act_buf.at[slot], act_out.at[at], ffn_done.at[slot, 0]),
                pltpu.make_async_copy(slope_buf.at[slot], slope_out.at[at], ffn_done.at[slot, 1])]

    def final_copies():
        return [pltpu.make_async_copy(out_buf, out_out, end_done.at[blocks, 0]),
                pltpu.make_async_copy(second_buf, second_out, end_done.at[blocks, 1]),
                pltpu.make_async_copy(second_low_buf, second_low_out, end_done.at[blocks + 1, 0])]

    def ffn_part(k):
        at = nearest(k)
        if k == 0:
            first_low[...] = (normed_buf[0] * vectors[0:1] + vectors[3:4]).astype(LOW)
        if k >= 2:
            for copy in ffn_copies(k - 2):
                copy.wait()
        slot = k % 2
        down = ffn_unit(first_low[...], matrix(1, at), matrix(2, at), ffn_rows[at], act_buf.at[slot], slope_buf.at[slot])
        for copy in ffn_copies(k):
            copy.start()
        if k == 0:
            down_total[...] = down
        else:
            down_total[...] += down
        if k == parts - 1:
            micro, place = block_place(0)
            out, second, stat = second_norm(layout, micro, place, normed_buf[0], down_total[...], cot[...], vectors)
            out_buf[...] = out
            second_buf[...] = second
            second_low_buf[...] = second.astype(LOW)
            stat_out[...] = stat
            for copy in final_copies():
                copy.start()

    def finish_small():
        lanes = own.shape[1]
        pieces = [small_dp[digit_index(bits, [(i // (1 << k)) % 2 for k in range(bits)], ())][:8, :lanes].astype(WIDE)
                  for i in range(1 << bits)]
        vectors[...] = jnp.concatenate(pieces, axis=1)
        for at in range(parts):
            head_rows[at] = small_t[at, 0:1, :].astype(WIDE)
            ffn_rows[at] = small_t[at, 1:2, :].astype(WIDE)

    send_own(0)
    begin(0, 0)
    for hop in range(1, parts):
        small_hop(hop).start()
    small_step(0).start()
    for copy in local + loads:
        copy.start()
    for copy in local + loads:
        copy.wait()

    order = [(s, hop) for s in range(slab_count) for hop in range(parts)]
    groups = [(s, [index for index, offset in enumerate(offsets) if abs(offset) == hop]) for s, hop in order]
    done_at = {place: number + bits * GATHER_LAG for number, place in enumerate(order)}
    jobs = [(done_at[(0, k)], functools.partial(attend_part, b, k)) for b in range(blocks) for k in range(parts)]
    jobs += [(done_at[(slab_count - 1, k)], functools.partial(ffn_part, k)) for k in range(parts)]
    for wave in range(len(groups) + bits * GATHER_LAG):
        for step in range(bits + 1):
            if 0 <= wave - step * GATHER_LAG < len(groups):
                s, indices = groups[wave - step * GATHER_LAG]
                for index in indices:
                    if step:
                        advance(s, index, step)
                    elif (s, index) != (0, 0):
                        begin(s, index)
        if wave in Z_WAVES:
            send_own(1 + Z_WAVES.index(wave))
        if wave < bits:
            small_step(wave).wait_recv()
            if wave + 1 < bits:
                small_step(wave + 1).start()
            else:
                for hop in range(1, parts):
                    small_hop(hop).wait_recv()
                finish_small()
        if jobs and jobs[0][0] <= wave:
            jobs.pop(0)[1]()
    for _, job in jobs:
        job()

    for hop in range(1, parts):
        small_hop(hop).wait_send()
    for step in range(bits):
        small_step(step).wait_send()
    for s, indices in groups:
        for index in indices:
            offset = offsets[index]

            @pl.when(exists(offset))
            def _():
                for step in range(bits):
                    h_copy(s, index, step).wait_send()
                weight_copy(s, t + offset).wait()
                if offset <= 0:
                    @pl.when(t < parts - 1)
                    def _():
                        z_copy(s, t + offset, own.at[s], True).wait_send()
                if offset >= 0:
                    @pl.when(t > 0)
                    def _():
                        z_copy(s, t + offset, own.at[s], False).wait_send()
    last = blocks * parts
    for unit in range(max(0, last - 2), last):
        for copy in unit_copies(unit, nearest(unit % parts), unit // parts):
            copy.wait()
    for k in range(max(0, parts - 2), parts):
        for copy in ffn_copies(k):
            copy.wait()
    for b in range(blocks):
        for copy in norm_copies(b):
            copy.wait()
    for copy in final_copies():
        copy.wait()


def forward(arrays, layout, inputs, cotangent, parts, dp_count, slot_count, micro_count, per_micro):
    bits = dp_count.bit_length() - 1
    slab_count = 3
    rows, cols = arrays[2].shape
    width = rows * dp_count
    places = 2 * parts - 1
    blocks = micro_count * per_micro
    heads = parts * CHUNK_HEADS
    spread = (slab_count, parts) + (2,) * bits + (rows, cols)
    shape = jax.ShapeDtypeStruct
    dma = pltpu.SemaphoreType.DMA
    hbm, vmem, smem = [pl.BlockSpec(memory_space=space) for space in (pl.ANY, pltpu.VMEM, pltpu.SMEM)]
    slab = (slot_count, cols)
    rows_of = (slot_count, width)
    outs = [
        (spread, LOW, hbm),
        ((8, width), WIDE, vmem),
        ((parts, 1, cols), WIDE, vmem),
        ((parts, 1, cols), WIDE, vmem),
        ((blocks,) + rows_of, WIDE, hbm),
        ((blocks, slot_count, 128), WIDE, hbm),
        ((blocks, parts) + slab, LOW, hbm),
        ((blocks, heads, slot_count, slot_count), LOW, hbm),
        ((blocks, parts, slot_count, 4 * HEAD_DIM), LOW, hbm),
        ((parts,) + slab, LOW, hbm),
        ((parts,) + slab, LOW, hbm),
        (rows_of, LOW, hbm),
        (rows_of, WIDE, hbm),
        (rows_of, LOW, hbm),
        ((8, width), WIDE, vmem),
    ]
    result = pl.pallas_call(
        functools.partial(forward_kernel, parts, bits, micro_count, per_micro, slot_count),
        out_shape=[shape(dims, kind) for dims, kind, _ in outs],
        in_specs=[vmem] * len(arrays) + [smem, smem, smem, hbm, hbm],
        out_specs=[space for _, _, space in outs],
        scratch_shapes=[
            pltpu.VMEM((slab_count, rows, cols), LOW),
            pltpu.VMEM((2, 16, cols), LOW),
            pltpu.VMEM(spread, LOW),
            pltpu.VMEM((2,) * bits + (16, cols), LOW),
            pltpu.VMEM((parts, 16, cols), LOW),
            pltpu.VMEM((blocks,) + rows_of, LOW),
            pltpu.VMEM(rows_of, LOW),
            pltpu.VMEM(rows_of, WIDE),
            pltpu.VMEM((blocks,) + rows_of, WIDE),
            pltpu.VMEM((blocks, slot_count, 128), WIDE),
            pltpu.VMEM((2,) + slab, LOW),
            pltpu.VMEM((2, CHUNK_HEADS, slot_count, slot_count), LOW),
            pltpu.VMEM((2, slot_count, 4 * HEAD_DIM), LOW),
            pltpu.VMEM((2,) + slab, LOW),
            pltpu.VMEM((2,) + slab, LOW),
            pltpu.VMEM(rows_of, LOW),
            pltpu.VMEM(rows_of, WIDE),
            pltpu.VMEM(rows_of, LOW),
            pltpu.VMEM(rows_of, WIDE),
            pltpu.VMEM(rows_of, LOW),
            dma((slab_count, parts, 2)),
            dma((slab_count, parts)),
            dma((slab_count, places, bits)),
            dma((slab_count, places, bits)),
            dma((bits + parts - 1,)),
            dma((bits + parts - 1,)),
            dma((slab_count + 2,)),
            dma((blocks + 1,)),
            dma((slab_count, parts)),
            dma((2, 3)),
            dma((2, 2)),
            dma((blocks + 2, 2)),
        ],
        compiler_params=pltpu.CompilerParams(collective_id=2, has_side_effects=True, vmem_limit_bytes=VMEM_LIMIT),
        name="forward",
    )(*arrays, *layout, inputs, cotangent)
    return (result[0].reshape(slab_count, parts, width, cols),) + tuple(result[1:])


def phase_index(step, parts, uses):
    block = jnp.int32(uses[0][1])
    part = jnp.clip(step - uses[0][0] * parts, 0, parts - 1)
    for phase, b in uses[1:]:
        later = step >= phase * parts
        block = jnp.where(later, b, block)
        part = jnp.where(later, jnp.clip(step - phase * parts, 0, parts - 1), part)
    return block, part


def line_events(send, hand_on, blocks, parts, chunks, start):
    events = []
    for b in range(blocks):
        for q in range(chunks):
            events.append((start[b][0], functools.partial(send, b, q)))
            for hop in range(1, parts - 1):
                events.append((start[b][hop] + q, functools.partial(hand_on, b, hop, q)))
            events.append((start[b][parts - 2] + q + chunks, functools.partial(hand_on, b, parts - 1, q)))
    return events


def backward_kernel(parts, micro_count, per_micro, slot_count, chunks, phases, bucket, lengths, counts, stat_first, vectors,
                    ffn_rows, first_out, cotangent, w_head, w_in, w_down, normed, inverse, slope_first, second_first,
                    second_low_first, proj, probs, context,
                    line_out, act_out, second_low_out, up_out, hidden_low_out, head_out, token_out, small_out,
                    first_low, total, slope_buf, second_buf, second_low_buf, hidden_buf, hidden_low_buf, out_buf, cot,
                    g_send, g_recv, g_keep, load):
    layout = (bucket, lengths, counts)
    d = lax.axis_index("dp")
    t = lax.axis_index("tensor")
    step = pl.program_id(0)
    blocks = micro_count * per_micro
    chunk_rows = slot_count // chunks

    def block_place(b):
        return b // per_micro, t * per_micro + b % per_micro

    def line_rows(b, at, q):
        place = at * per_micro + b % per_micro
        start = pl.multiple_of(place * slot_count + q * chunk_rows, chunk_rows)
        return line_out.at[b // per_micro, pl.ds(start, chunk_rows)]

    def own_rows(b, q):
        source = first_out if b == 0 else out_buf.at[b - 1]
        return source.at[pl.ds(q * chunk_rows, chunk_rows)]

    def line_copy(b, at, q, src, up):
        to = (d, t + 1) if up else (d, t - 1)
        return pltpu.make_async_remote_copy(src, line_rows(b, at, q), g_send.at[b, at, q, 0 if up else 1], g_recv.at[b, at, q],
                                            device_id=to, device_id_type=MESH)

    def keep_copy(b, q):
        return pltpu.make_async_copy(own_rows(b, q), line_rows(b, t, q), g_keep.at[b, q])

    def line_send(b, q):
        for up in (True, False):
            @pl.when((t < parts - 1) if up else (t > 0))
            def _():
                line_copy(b, t, q, own_rows(b, q), up).start()
        keep_copy(b, q).start()

    def line_pass(b, hop, q):
        for up in (True, False):
            at = t - hop if up else t + hop

            @pl.when((at >= 0) if up else (at < parts))
            def _():
                line_copy(b, at, q, own_rows(b, q), up).wait_recv()

                @pl.when((t < parts - 1) if up else (t > 0))
                def _():
                    line_copy(b, at, q, line_rows(b, at, q), up).start()

    def line_settle(b, hop, q):
        for up in (True, False):
            at = t - hop if up else t + hop

            @pl.when(((at >= 0) if up else (at < parts)) & ((t < parts - 1) if up else (t > 0)))
            def _():
                line_copy(b, at, q, own_rows(b, q), up).wait_send()

    def cot_copy(b):
        micro, place = block_place(b)
        rows = pl.ds(pl.multiple_of(place * slot_count, slot_count), slot_count)
        return pltpu.make_async_copy(cotangent.at[micro, rows], cot.at[b - 1], load.at[b - 1])

    @pl.when(step == 0)
    def _():
        greet(d, t, [], parts)
        for b in range(1, blocks):
            cot_copy(b).start()
        small_out[...] = jnp.zeros_like(small_out)
        small_out[1:2] = stat_first[0:1]
        small_out[5:6] = stat_first[1:2]
        small_out[4:5] = stat_first[2:3]

    events = line_events(line_send, line_pass, blocks, parts, chunks, LINE_START)
    last_step = len(phases) * parts
    for when in sorted(set(at for at, _ in events)):
        if when < last_step:
            @pl.when(step == when)
            def _():
                for at, event in events:
                    if at == when:
                        event()

    def collect(part, value):
        @pl.when(part == 0)
        def _():
            total[...] = value

        @pl.when(part > 0)
        def _():
            total[...] += value

    def ffn_phase(b, part):
        @pl.when(part == 0)
        def _():
            first_low[...] = (normed[...] * vectors[0:1] + vectors[3:4]).astype(LOW)

        down = ffn_unit(first_low[...], w_in[0, 0], w_down[0, 0], ffn_rows[part], act_out.at[0, 0], slope_buf.at[b - 1, part])
        collect(part, down)

        @pl.when(part == parts - 1)
        def _():
            cot_copy(b).wait()
            micro, place = block_place(b)
            out, second, stat = second_norm(layout, micro, place, normed[...], total[...], cot[b - 1], vectors)
            out_buf[b - 1] = out
            second_buf[b - 1] = second
            second_low_buf[b - 1] = second.astype(LOW)
            second_low_out[0] = second.astype(LOW)
            small_out[1:2] += stat[0:1]
            small_out[5:6] += stat[1:2]
            small_out[4:5] += stat[2:3]

    def ffn_back_phase(b, part):
        second_low = second_low_first[...] if b == 0 else second_low_buf[b - 1]
        slope = slope_first[0] if b == 0 else slope_buf[b - 1, part]
        grad_act = dot_nn(second_low, w_down[0, 0])
        grad_up = (grad_act * slope.astype(WIDE)).astype(LOW)
        up_out[0, 0] = grad_up
        small_out[pl.ds(6 + part, 1)] += row_sum(grad_up.astype(WIDE))
        collect(part, dot_nt(grad_up, w_in[0, 0]))

        @pl.when(part == parts - 1)
        def _():
            grad_first = total[...] + (second_first[...] if b == 0 else second_buf[b - 1])
            unit = normed[...]
            hidden = norm_pullback(grad_first, unit, inverse[:, :1], vectors[0:1])
            hidden_buf[...] = hidden
            hidden_low_buf[...] = hidden.astype(LOW)
            hidden_low_out[0] = hidden.astype(LOW)
            small_out[0:1] += row_sum(grad_first * unit)
            small_out[3:4] += row_sum(grad_first)
            small_out[2:3] += row_sum(hidden)

    def attend_back_phase(b, part):
        micro, place = block_place(b)
        slab, back, sums = attend_back_unit(layout, micro, place, hidden_low_buf[...], w_head[0, 0], proj[0, 0], probs[0],
                                            context[0, 0])
        head_out[0, 0] = slab
        small_out[pl.ds(6 + parts + part, 1)] += sums
        collect(part, back)

        @pl.when(part == parts - 1)
        def _():
            token_out[0] = (total[...] + hidden_buf[...]).astype(LOW)

    kinds = {"ffn": ffn_phase, "ffn_back": ffn_back_phase, "attend_back": attend_back_phase}
    for number, (kind, b) in enumerate(phases):
        @pl.when((step >= number * parts) & (step < (number + 1) * parts))
        def _():
            kinds[kind](b, step - number * parts)

    @pl.when(step == last_step - 1)
    def _():
        for at, event in events:
            if at >= last_step:
                event()
        for b in range(blocks):
            for q in range(chunks):
                keep_copy(b, q).wait()
                for hop in range(parts - 1):
                    line_settle(b, hop, q)


def backward(layout, stat_first, vectors, ffn_rows, first_out, cotangent, weights, normed, inverse, slope_first, second_first,
             second_low_first, proj, probs, context, micro_count, per_micro):
    parts, width, cols = weights.shape[1:]
    blocks, slot_count = normed.shape[:2]
    tokens = cotangent.shape[1]
    phases = [("ffn", b) for b in range(1, blocks)]
    for b in range(blocks):
        phases += [("ffn_back", b), ("attend_back", b)]

    def uses(*kinds):
        return [(number, b) for number, (kind, b) in enumerate(phases) if kind in kinds]

    def whole(*dims):
        return pl.BlockSpec(dims, lambda i: (0,) * len(dims))

    def stacked(dims, kinds, shift=0):
        def place(i):
            block, part = phase_index(i, parts, uses(*kinds))
            return (block - shift, part) + (0,) * len(dims)
        return pl.BlockSpec((1, 1) + dims, place)

    def by_block(dims, kinds, shift=0, squeeze=False):
        def place(i):
            return (phase_index(i, parts, uses(*kinds))[0] - shift,) + (0,) * len(dims)
        return pl.BlockSpec((None if squeeze else 1,) + dims, place)

    def slab(index, kinds):
        def place(i):
            return (index, phase_index(i, parts, uses(*kinds))[1], 0, 0)
        return pl.BlockSpec((1, 1, width, cols), place)

    def first_parts(i):
        return (phase_index(i, parts, [use for use in uses("ffn_back") if use[1] == 0])[1], 0, 0)

    shape = jax.ShapeDtypeStruct
    dma = pltpu.SemaphoreType.DMA
    hbm, smem = pl.BlockSpec(memory_space=pl.ANY), pl.BlockSpec(memory_space=pltpu.SMEM)
    rows_of = (slot_count, width)
    square = (slot_count, cols)
    later = max(blocks - 1, 1)
    both = ("ffn", "ffn_back")
    return pl.pallas_call(
        functools.partial(backward_kernel, parts, micro_count, per_micro, slot_count, LINE_CHUNKS, phases),
        grid=(len(phases) * parts,),
        in_specs=[
            smem, smem, smem,
            whole(*stat_first.shape),
            whole(*vectors.shape),
            whole(*ffn_rows.shape),
            hbm,
            hbm,
            slab(0, ("attend_back",)),
            slab(1, both),
            slab(2, both),
            by_block(rows_of, both, squeeze=True),
            by_block((slot_count, 128), ("ffn_back",), squeeze=True),
            pl.BlockSpec((1,) + square, first_parts),
            whole(*rows_of),
            whole(*rows_of),
            stacked(square, ("attend_back",)),
            pl.BlockSpec((1, CHUNK_HEADS, slot_count, slot_count),
                         lambda i: phase_index(i, parts, uses("attend_back")) + (0, 0)),
            stacked((slot_count, 4 * HEAD_DIM), ("attend_back",)),
        ],
        out_specs=[
            hbm,
            stacked(square, ("ffn",), 1),
            by_block(rows_of, ("ffn",), 1),
            stacked(square, ("ffn_back",)),
            by_block(rows_of, ("ffn_back",)),
            stacked(square, ("attend_back",)),
            by_block(rows_of, ("attend_back",)),
            whole(16, width),
        ],
        out_shape=[
            shape((micro_count, tokens, width), LOW),
            shape((later, parts) + square, LOW),
            shape((later,) + rows_of, LOW),
            shape((blocks, parts) + square, LOW),
            shape((blocks,) + rows_of, LOW),
            shape((blocks, parts) + square, LOW),
            shape((blocks,) + rows_of, LOW),
            shape((16, width), WIDE),
        ],
        scratch_shapes=[
            pltpu.VMEM(rows_of, LOW),
            pltpu.VMEM(rows_of, WIDE),
            pltpu.VMEM((later, parts) + square, LOW),
            pltpu.VMEM((later,) + rows_of, WIDE),
            pltpu.VMEM((later,) + rows_of, LOW),
            pltpu.VMEM(rows_of, WIDE),
            pltpu.VMEM(rows_of, LOW),
            pltpu.VMEM((later,) + rows_of, LOW),
            pltpu.VMEM((later,) + rows_of, LOW),
            dma((blocks, parts, LINE_CHUNKS, 2)),
            dma((blocks, parts, LINE_CHUNKS)),
            dma((blocks, LINE_CHUNKS)),
            dma((later,)),
        ],
        compiler_params=pltpu.CompilerParams(
            dimension_semantics=("arbitrary",), collective_id=4, has_side_effects=True, vmem_limit_bytes=VMEM_LIMIT
        ),
        name="backward",
        cost_estimate=takes(100),
    )(*layout, stat_first, vectors, ffn_rows, first_out, cotangent, weights, weights, weights, normed, inverse, slope_first,
      second_first, second_low_first, proj, probs, context)


def finish_kernel(parts, bits, micro_count, per_micro, slot_count, chunks, vectors, small, inputs, normed, second_low_first,
                  second_low_later, hidden_low, act_first, act_later, grad_up, head_grads, token_grad, *rest):
    blocks = micro_count * per_micro
    second_low = [second_low_first] + [second_low_later.at[b - 1] for b in range(1, blocks)]
    act = [act_first] + [act_later.at[b - 1] for b in range(1, blocks)]
    hidden_low, grad_up, head_grads, token_grad = [
        [array.at[b] for b in range(blocks)] for array in (hidden_low, grad_up, head_grads, token_grad)
    ]
    gathered, out, small_out = rest[:3]
    (grads, operand, turned, staged, staged_wide, small_buf, small_sum, z_up, z_down) = rest[3:12]
    bufs = rest[12 : 12 + bits]
    (h_send, h_recv, up_send, up_recv, down_send, down_recv, s_send, s_recv, g_send, g_recv, g_keep, load, load_wide, fetch) = rest[
        12 + bits :
    ]
    d, t, digits, mates = mesh_place(bits)
    slab_count = grads.shape[0]
    rows = grads.shape[-2]
    width = inputs.shape[2]
    items = [(s, at) for s in range(slab_count) for at in range(parts)]
    small_bits = bits + parts.bit_length() - 1
    chunk_rows = slot_count // chunks

    def remote(src, dst, send, recv, to):
        return pltpu.make_async_remote_copy(src, dst, send, recv, device_id=to, device_id_type=MESH)

    def token_rows(b):
        place = t * per_micro + b % per_micro
        return inputs.at[b // per_micro, pl.ds(pl.multiple_of(place * slot_count, slot_count), slot_count)]

    def span(b):
        return pl.ds(b * slot_count, slot_count)

    def stage_loads(which):
        if which == 3:
            return [pltpu.make_async_copy(normed.at[b], staged_wide.at[span(b)], load_wide.at[b]) for b in range(blocks)]
        source = ([token_rows(b) for b in range(blocks)], hidden_low, second_low)[which]
        return [pltpu.make_async_copy(source[b], staged.at[which, span(b)], load.at[which, b]) for b in range(blocks)]

    def operand_loads(number):
        s, at = items[number]
        source = (head_grads, grad_up, act)[s]
        slot = number % 3
        return [pltpu.make_async_copy(source[b].at[at], operand.at[slot, span(b)], fetch.at[slot, b]) for b in range(blocks)]

    def grads_job(number):
        s, at = items[number]
        if number == 0:
            for copy in stage_loads(0) + stage_loads(1):
                copy.wait()
            turned[0] = staged[0].T
            turned[1] = staged[1].T
        elif at == 0 and s == 1:
            for copy in stage_loads(3):
                copy.wait()
            turned[0] = (staged_wide[...] * vectors[0:1] + vectors[3:4]).astype(LOW).T
        elif at == 0:
            for copy in stage_loads(2):
                copy.wait()
            turned[1] = staged[2].T
        for copy in operand_loads(number):
            copy.wait()
        right = operand[number % 3]
        if s == 0:
            qkv = dot_nn(turned[0], right)
            outs = dot_nn(turned[1], right[:, 8 * HEAD_DIM :])
            lane = lax.broadcasted_iota(jnp.int32, (1, 2 * HEAD_DIM), 1)
            last = jnp.where(lane < HEAD_DIM, qkv[:, 10 * HEAD_DIM :], outs[:, 2 * HEAD_DIM :])
            total = jnp.concatenate([qkv[:, : 8 * HEAD_DIM], outs[:, : 2 * HEAD_DIM], last], axis=1)
        else:
            total = dot_nn(turned[s - 1], right)
        grads[s, at] = total.astype(LOW).reshape(grads.shape[2:])
        if number + 3 < len(items):
            for copy in operand_loads(number + 3):
                copy.start()

    def order_of(number):
        s, at = items[number]
        return bit_order(bits, (s + at) % 2 == 1)[::-1]

    def held(number, step):
        s, at = items[number]
        return grads.at[s, at] if step == 0 else bufs[step - 1].at[number]

    def part_of(number, step, side):
        order = order_of(number)
        left = [k for k in reversed(range(bits)) if k not in order[:step]]
        pick = tuple(side if k == order[step] else slice(None) for k in left)
        return held(number, step).at[pick]

    def h_copy(number, step):
        order = order_of(number)
        digit = digits[order[step]]
        return remote(part_of(number, step, 1 - digit), bufs[step].at[number],
                      h_send.at[number, step], h_recv.at[number, step], (mates[order[step]], t))

    def fold(number, step):
        h_copy(number, step).wait_recv()
        digit = digits[order_of(number)[step]]
        add_rows(bufs[step].at[number], bufs[step].at[number], part_of(number, step, digit), rows)

    def summed(s, at):
        return bufs[bits - 1].at[s * parts + at]

    def z_copy(s, at, up, src):
        buf, send, recv = (z_up, up_send, up_recv) if up else (z_down, down_send, down_recv)
        to = (d, t + 1) if up else (d, t - 1)
        return remote(src, buf.at[s, at], send.at[s, at], recv.at[s, at], to)

    def z_pass(s, hop, up):
        at = t + hop if up else t - hop
        edge = (t == 0) if up else (t == parts - 1)
        buf = z_up if up else z_down

        @pl.when((at < parts) if up else (at >= 0))
        def _():
            @pl.when(edge)
            def _():
                z_copy(s, at, up, summed(s, at)).start()

            @pl.when(jnp.logical_not(edge))
            def _():
                z_copy(s, at, up, summed(s, at)).wait_recv()
                add_rows(buf.at[s, at], buf.at[s, at], summed(s, at), rows)
                z_copy(s, at, up, buf.at[s, at]).start()

    def z_finish(s):
        @pl.when(t > 0)
        def _():
            z_copy(s, t, True, summed(s, t)).wait_recv()
            add_rows(out.at[s], summed(s, t), z_up.at[s, t], rows)

        @pl.when(t < parts - 1)
        def _():
            z_copy(s, t, False, summed(s, t)).wait_recv()

            @pl.when(t > 0)
            def _():
                add_rows(out.at[s], out.at[s], z_down.at[s, t], rows)

            @pl.when(t == 0)
            def _():
                add_rows(out.at[s], summed(s, t), z_down.at[s, t], rows)

    def small_copy(step):
        if step < bits:
            to = (mates[step], t)
        else:
            gap = 1 << (step - bits)
            to = (d, t + (1 - 2 * ((t // gap) % 2)) * gap)
        src = small if step == 0 else small_sum.at[step - 1]
        return remote(src, small_buf.at[step], s_send.at[step], s_recv.at[step], to)

    def small_fold(step):
        small_copy(step).wait_recv()
        before = small[...] if step == 0 else small_sum[step - 1]
        small_sum[step] = before + small_buf[step]
        if step + 1 < small_bits:
            small_copy(step + 1).start()

    def line_rows(b, at, q):
        place = at * per_micro + b % per_micro
        start = pl.multiple_of(place * slot_count + q * chunk_rows, chunk_rows)
        return gathered.at[b // per_micro, pl.ds(start, chunk_rows)]

    def own_rows(b, q):
        return token_grad[b].at[pl.ds(q * chunk_rows, chunk_rows)]

    def line_copy(b, at, q, src, up):
        to = (d, t + 1) if up else (d, t - 1)
        return remote(src, line_rows(b, at, q), g_send.at[b, at, q, 0 if up else 1], g_recv.at[b, at, q], to)

    def line_send(b, q):
        for up in (True, False):
            @pl.when((t < parts - 1) if up else (t > 0))
            def _():
                line_copy(b, t, q, own_rows(b, q), up).start()

    def line_pass(b, hop, q):
        for up in (True, False):
            at = t - hop if up else t + hop

            @pl.when((at >= 0) if up else (at < parts))
            def _():
                line_copy(b, at, q, own_rows(b, q), up).wait_recv()

                @pl.when((t < parts - 1) if up else (t > 0))
                def _():
                    line_copy(b, at, q, line_rows(b, at, q), up).start()

    def line_settle(b, hop, q):
        for up in (True, False):
            at = t - hop if up else t + hop

            @pl.when(((at >= 0) if up else (at < parts)) & ((t < parts - 1) if up else (t > 0)))
            def _():
                line_copy(b, at, q, own_rows(b, q), up).wait_send()

    keeps = [pltpu.make_async_copy(own_rows(b, q), line_rows(b, t, q), g_keep.at[b, q])
             for b in range(blocks) for q in range(chunks)]
    events = []
    for turn in range(blocks + parts):
        for hop in range(parts + 1):
            b = turn - hop
            if 0 <= b < blocks and hop <= parts - 1:
                for q in range(chunks):
                    events.append(functools.partial(line_send, b, q) if hop == 0 else functools.partial(line_pass, b, hop, q))

    for copy in stage_loads(0) + stage_loads(1):
        copy.start()
    for number in range(min(3, len(items))):
        for copy in operand_loads(number):
            copy.start()
    for copy in stage_loads(3) + stage_loads(2):
        copy.start()
    greet(d, t, mates, parts)
    for copy in keeps:
        copy.start()
    small_copy(0).start()
    ahead = chunks

    waves = len(items) + bits * REDUCE_LAG + parts
    per_wave = LINE_PACE
    for wave in range(max(waves, len(events))):
        while events and wave * per_wave + ahead > total_done(events, blocks, parts, chunks):
            events.pop(0)()
        if wave < len(items):
            grads_job(wave)
            h_copy(wave, 0).start()
        for step in range(bits):
            number = wave - (step + 1) * REDUCE_LAG + 1
            if 0 <= number < len(items):
                fold(number, step)
                if step + 1 < bits:
                    h_copy(number, step + 1).start()
        for s in range(slab_count):
            phase = wave - ((s + 1) * parts + bits * REDUCE_LAG - 1)
            if 0 <= phase < parts - 1:
                z_pass(s, parts - 1 - phase, True)
                z_pass(s, parts - 1 - phase, False)
            elif phase == parts - 1:
                z_finish(s)
        if wave < small_bits:
            small_fold(wave)
    small_out[...] = small_sum[small_bits - 1]

    for copy in keeps:
        copy.wait()
    for b in range(blocks):
        for hop in range(parts - 1):
            for q in range(chunks):
                line_settle(b, hop, q)
    for step in range(small_bits):
        small_copy(step).wait_send()
    for number in range(len(items)):
        for step in range(bits):
            h_copy(number, step).wait_send()
    for s in range(slab_count):
        for hop in range(1, parts):
            @pl.when(t + hop < parts)
            def _():
                z_copy(s, t + hop, True, summed(s, t)).wait_send()

            @pl.when(t - hop >= 0)
            def _():
                z_copy(s, t - hop, False, summed(s, t)).wait_send()


def total_done(events, blocks, parts, chunks):
    return blocks * parts * chunks - len(events)


def finish(vectors, small, inputs, normed, second_low_first, second_low_later, hidden_low, act_first, act_later, grad_up,
           head_grads, token_grad, parts, dp_count):
    bits = dp_count.bit_length() - 1
    blocks = token_grad.shape[0]
    micro_count, tokens, width = inputs.shape
    per_micro = blocks // micro_count
    slot_count, cols = act_first.shape[1:]
    rows = width // dp_count
    slab_count = 3
    count = slab_count * parts
    small_bits = bits + parts.bit_length() - 1
    dma = pltpu.SemaphoreType.DMA
    hbm, vmem = pl.BlockSpec(memory_space=pl.ANY), pl.BlockSpec(memory_space=pltpu.VMEM)
    block = (rows, cols)
    return pl.pallas_call(
        functools.partial(finish_kernel, parts, bits, micro_count, per_micro, slot_count, LINE_CHUNKS),
        out_shape=[
            jax.ShapeDtypeStruct((micro_count, tokens, width), LOW),
            jax.ShapeDtypeStruct((slab_count,) + block, WIDE),
            jax.ShapeDtypeStruct(small.shape, WIDE),
        ],
        in_specs=[vmem, vmem] + [hbm] * 10,
        out_specs=[hbm, vmem, vmem],
        scratch_shapes=[
            pltpu.VMEM((slab_count, parts) + (2,) * bits + block, LOW),
            pltpu.VMEM((3, blocks * slot_count, cols), LOW),
            pltpu.VMEM((2, width, blocks * slot_count), LOW),
            pltpu.VMEM((3, blocks * slot_count, width), LOW),
            pltpu.VMEM((blocks * slot_count, width), WIDE),
            pltpu.VMEM((small_bits,) + small.shape, WIDE),
            pltpu.VMEM((small_bits,) + small.shape, WIDE),
            pltpu.VMEM((slab_count, parts) + block, LOW),
            pltpu.VMEM((slab_count, parts) + block, LOW),
        ]
        + [pltpu.VMEM((count,) + (2,) * (bits - 1 - step) + block, LOW) for step in range(bits)]
        + [dma((count, bits)), dma((count, bits))]
        + [dma((slab_count, parts))] * 4
        + [dma((small_bits,))] * 2
        + [dma((blocks, parts, LINE_CHUNKS, 2)), dma((blocks, parts, LINE_CHUNKS)), dma((blocks, LINE_CHUNKS))]
        + [dma((3, blocks)), dma((blocks,)), dma((3, blocks))],
        compiler_params=pltpu.CompilerParams(collective_id=3, has_side_effects=True, vmem_limit_bytes=VMEM_LIMIT),
        name="finish",
        cost_estimate=takes(100),
    )(vectors, small, inputs, normed, second_low_first, second_low_later, hidden_low, act_first, act_later, grad_up, head_grads,
      token_grad)


def place_kernel(parts, dp_count, shard, sums, grad_qkv, grad_out, grad_in, grad_down, grad_head, grad_ffn,
                 grad_gains, grad_shifts):
    dp_rank, rank = lax.axis_index("dp"), lax.axis_index("tensor")
    groups = slab_parts(shard[0])
    for i in range(3):
        grad_qkv[i] = groups[i]
    grad_out[...] = groups[3].T
    grad_in[...] = shard[1]
    grad_down[...] = shard[2]
    grad_ffn[...] = sums[pl.ds(6 + rank, 1), :].reshape(-1)
    head = slab_parts(sums[pl.ds(6 + parts + rank, 1), :])
    grad_head[...] = jnp.concatenate([head[0], head[2]], axis=0)
    rows = shard.shape[1]
    wide = sums[0:8, :]
    vectors = wide[:, :rows]
    for i in range(1, dp_count):
        vectors = jnp.where(dp_rank == i, wide[:, i * rows : (i + 1) * rows], vectors)
    grad_gains[...] = vectors[0:2]
    grad_shifts[...] = vectors[2:6]


def place_results(shard, sums, parts, dp_count):
    rows, cols = shard.shape[1:]
    head_cols = CHUNK_HEADS * HEAD_DIM
    smalls = [(3, rows, head_cols), (head_cols, rows), (rows, cols), (rows, cols), (2, head_cols), (cols,), (2, rows), (4, rows)]
    vmem = pl.BlockSpec(memory_space=pltpu.VMEM)
    return pl.pallas_call(
        functools.partial(place_kernel, parts, dp_count),
        in_specs=[vmem, vmem],
        out_specs=[vmem] * len(smalls),
        out_shape=[jax.ShapeDtypeStruct(dims, WIDE) for dims in smalls],
        compiler_params=pltpu.CompilerParams(vmem_limit_bytes=VMEM_LIMIT),
        name="place_results",
    )(shard, sums)


def add_all(terms):
    total = terms[0]
    for term in terms[1:]:
        total = total + term
    return total


def body(
    inputs,
    cotangent,
    bucket,
    lengths,
    counts,
    w_qkv,
    w_out,
    w_in,
    w_down,
    head_bias,
    ffn_bias,
    norm_gains,
    row_biases,
):
    micro_count, _, width = inputs.shape
    blocks_all = bucket.shape[1]
    slot_count = inputs.shape[1] // blocks_all
    parts, dp_count = lax.axis_size("tensor"), lax.axis_size("dp")
    rank, dp_rank = lax.axis_index("tensor"), lax.axis_index("dp")
    per_micro = blocks_all // parts
    cols = w_in.shape[1]
    rows = w_in.shape[0]

    vector_count = norm_gains.shape[0] + row_biases.shape[0]
    blocks = [(m, k) for m in range(micro_count) for k in range(per_micro)]
    places = [jnp.full((1,), rank * per_micro + k, jnp.int32) for k in range(per_micro)]
    layout = (bucket, lengths, counts)
    if rows % 16 == 0:
        (weights, vectors, _, ffn_rows, normed, inverse, proj, probs, context, act, slope, out, second, second_low, stat) = forward(
            (w_qkv, w_out, w_in, w_down.T, head_bias, ffn_bias, norm_gains, row_biases),
            layout, inputs, cotangent, parts, dp_count, slot_count, micro_count, per_micro
        )
        layer_output, act_later, second_low_later, grad_up, hidden_low, head_grads, token_grad, small_grads = backward(
            layout, stat, vectors, ffn_rows, out, cotangent, weights, normed, inverse, slope, second, second_low, proj, probs,
            context, micro_count, per_micro
        )
        input_grad, shard, sums = finish(
            vectors, small_grads, inputs, normed, second_low, second_low_later, hidden_low, act, act_later, grad_up, head_grads,
            token_grad, parts, dp_count
        )
        grad_w_qkv, grad_w_out, grad_w_in, grad_w_down, grad_head, grad_ffn, grad_gains, grad_shifts = place_results(
            shard, sums, parts, dp_count
        )
        grad_w_down = grad_w_down.T
    else:
        own = jnp.stack([slab_order(w_qkv[0], w_qkv[1], w_qkv[2], w_out.T), w_in, w_down.T])
        norm_rows = jnp.concatenate([norm_gains, row_biases], axis=0)
        no_bias = jnp.zeros_like(head_bias[:1])
        bias_rows = jnp.concatenate([slab_order(head_bias[:1], no_bias, head_bias[1:], no_bias), ffn_bias[None]], axis=0)
        small = jnp.stack([
            jnp.pad(norm_rows, ((0, 16 - vector_count), (0, cols - rows))),
            jnp.pad(bias_rows, ((0, 14), (0, 0))),
        ])
        weights, small_dp, small_t = gather_weights(own, small, parts, dp_count)
        vectors = small_dp[:, :8, :rows].transpose(1, 0, 2).reshape(8, width).astype(jnp.float32)
        head_rows = small_t[:, 0:1].astype(jnp.float32)
        ffn_rows = small_t[:, 1:2].astype(jnp.float32)
        outs, token_grads, saved = [], [], []
        for m, k in blocks:
            attended = attend(m, places[k], *layout, inputs, weights, head_rows, vectors, slot_count)
            normed, inverse, proj, probs, context = [(array[None], 0) for array in attended]
            act, slope, out, second, second_low, stat = ffn(m, places[k], *layout, normed, cotangent, weights, ffn_rows, vectors)
            grad_up, hidden, hidden_low, up_stat, first_stat = ffn_back(second, second_low, slope, weights, normed, inverse, vectors)
            head_grads, token_grad, head_stat = attend_back(
                m, places[k], *layout, hidden, hidden_low, weights, proj, probs, context
            )
            outs.append(out)
            token_grads.append(token_grad)
            saved.append((normed, second_low, hidden_low, act, grad_up, head_grads, stat, first_stat, up_stat, head_stat))

        def along_line(rows_of):
            return jnp.stack([
                lax.all_gather(jnp.concatenate(rows_of[m * per_micro : (m + 1) * per_micro], axis=0), "tensor", axis=0, tiled=True)
                for m in range(micro_count)
            ])

        layer_output, input_grad = along_line(outs), along_line(token_grads)
        columns = list(zip(*saved))
        stat, first_stat, up_stat, head_stat = [add_all(column) for column in columns[6:]]
        small_grads = jnp.concatenate(
            [
                jnp.stack([first_stat[0], stat[0], first_stat[2], first_stat[1], stat[2], stat[1]]),
                up_stat[:, 0],
                head_stat[:, 0],
            ],
            axis=0,
        )
        small_grads = jnp.pad(small_grads, ((0, -small_grads.shape[0] % 8), (0, 0)))
        grads = weight_grads(places[0], inputs, *columns[:6], vectors)
        shard, sums = reduce_grads(grads, small_grads, parts, dp_count)
        vector_sums = lax.dynamic_slice_in_dim(sums[:vector_count], dp_rank * rows, rows, 1)
        grad_gains, grad_shifts = vector_sums[:2], vector_sums[2:]
        grad_query, grad_key, grad_value, grad_out = slab_parts(shard[0])
        grad_w_qkv = jnp.stack([grad_query, grad_key, grad_value])
        grad_w_out, grad_w_in, grad_w_down = grad_out.T, shard[1], shard[2].T
        grad_ffn = lax.dynamic_slice_in_dim(sums, vector_count + rank, 1, 0)[0]
        head_sum = slab_parts(lax.dynamic_slice_in_dim(sums, vector_count + parts + rank, 1, 0))
        grad_head = jnp.concatenate([head_sum[0], head_sum[2]], axis=0)
    return (
        layer_output,
        input_grad,
        grad_w_qkv,
        grad_w_out,
        grad_w_in,
        grad_w_down,
        grad_head,
        grad_ffn,
        grad_gains,
        grad_shifts,
    )


def solution(mesh):
    in_specs = (
        P(None, "dp", None),
        P(None, "dp", None),
        P(None, "dp"),
        P(None, "dp", None),
        P(None, "dp"),
        P(None, "dp", "tensor"),
        P("tensor", "dp"),
        P("dp", "tensor"),
        P("tensor", "dp"),
        P(None, "tensor"),
        P("tensor"),
        P(None, "dp"),
        P(None, "dp"),
    )
    out_specs = (
        P(None, "dp", None),
        P(None, "dp", None),
        P(None, "dp", "tensor"),
        P("tensor", "dp"),
        P("dp", "tensor"),
        P("tensor", "dp"),
        P(None, "tensor"),
        P("tensor"),
        P(None, "dp"),
        P(None, "dp"),
    )
    return jax.shard_map(body, mesh=mesh, in_specs=in_specs, out_specs=out_specs, check_vma=False)
```
